32 devices in a mesh: ctx: 8 (over z, x), dp: 4 (over y, core).
Axes of the slice: x: 2, y: 2, z: 4, core: 2. Of those that a mesh axis runs over, the one named last changes fastest.
Arguments:
- xbc_raw: bfloat16 [4, 2048, 512], P('dp', 'ctx'), may hold values from -6 to 6
- conv_weight: float32 [4, 512], replicated, may hold values from -3 to 3
- conv_bias: float32 [512], replicated, may hold values from -3 to 3
- dt_raw: float32 [4, 2048, 4], P('dp', 'ctx'), may hold values from -1 to 10
- dt_bias: float32 [4], replicated, may hold values from -7.3 to -0.15
- a_log: float32 [4], replicated, may hold values from -3.5 to -2.5
- d_skip: float32 [4], replicated, may hold values from 0.5 to 1.5
- grad_out: bfloat16 [4, 2048, 256], P('dp', 'ctx'), may hold values from -6 to 6
Outputs:
- grad_xbc: bfloat16 [4, 2048, 512], P('dp', 'ctx')
- grad_dt: float32 [4, 2048, 4], P('dp', 'ctx')
- grad_conv_weight: float32 [4, 512], replicated
- grad_conv_bias: float32 [512], replicated
- grad_dt_bias: float32 [4], replicated
- grad_a_log: float32 [4], replicated
- grad_d_skip: float32 [4], replicated
The draws below stay inside these ranges and needn't reach their ends.
All inputs are finite; a program needn't handle non-finite values.
Results may differ from the reference program's by a relative error of at most 0.0025.
The reference program's roundings to bfloat16 on the way count: a program that leaves them out, or rounds other values in their place, can miss the bound.
Values may be sent and summed in bfloat16 or wider, within the bound.
No kernel may reach another device: no remote copies, remote signals or barrier semaphores. Data moves between devices by JAX's collectives and lax.ppermute only.
A program may use at most 64 MiB of HBM per device.

```python
import jax
import jax.numpy as jnp
from jax import lax

H = 4
P_SIZE = 64
N = 128
K = 4
L = 256
CH = 512
CONTEXT_TOKENS = 2048
CONTEXT_COUNT = 4
N_CTX = 8


def draw_dt_raw(key, part):
    key_noise, key_position = jax.random.split(key)
    random_noise = jax.random.uniform(key_noise, (CONTEXT_COUNT, CONTEXT_TOKENS, H), jnp.float32, -0.7, 0.7)
    spike_position = jax.random.randint(key_position, (CONTEXT_COUNT, 3), 0, CONTEXT_TOKENS)
    token_positions = jnp.arange(CONTEXT_TOKENS)[None, :, None]
    spike_mask = jnp.any(token_positions == spike_position[:, None, :], axis=2).astype(jnp.float32)
    return random_noise + spike_mask[:, :, None] * 8.8


def draw_dt_bias(key, part):
    key_kind, key_level = jax.random.split(key)
    head_draw = jax.random.randint(key_kind, (H,), 0, 10)
    slow_heads = head_draw < 5
    level = jax.random.uniform(key_level, (H,), jnp.float32, -0.3, 0.3)
    return jnp.where(slow_heads, -7.0 + level, -0.45 + level)


def block_scale(stream_key, shape, cuts, low, top_value):
    level, own = 1.0, jax.random.fold_in(stream_key, 6)
    for axis_at, shards_of in cuts:
        draws = jnp.exp(jax.random.uniform(jax.random.fold_in(own, axis_at), (shards_of,), jnp.float32, low / len(cuts), top_value / len(cuts)))
        level = level * jnp.repeat(draws, shape[axis_at] // shards_of).reshape([-1 if axis == axis_at else 1 for axis in range(len(shape))])
    return level


def normal_values(own_key, shape, scale, reach, cuts=(), held_as=jnp.bfloat16):
    loudness = block_scale(own_key, shape, cuts, -0.22, 0.18) if cuts else 1.0
    entries = jax.random.normal(own_key, shape, jnp.float32) * scale * loudness
    return jnp.minimum(jnp.maximum(entries, -reach), reach).astype(held_as)


def setup_inputs(seed: int = 0) -> dict:
    streams_of = jax.random.split(jax.random.key(seed), 9)
    xbc_raw = normal_values(streams_of[0], (CONTEXT_COUNT, CONTEXT_TOKENS, CH), 1.0, 6.0, ((0, 4), (1, 8)))
    conv_weight = normal_values(streams_of[1], (K, CH), K ** -0.5, 3.0, (), jnp.float32)
    conv_bias = normal_values(streams_of[2], (CH,), 0.5, 3.0, (), jnp.float32)
    dt_raw = draw_dt_raw(jax.random.fold_in(streams_of[8], 71), 0)
    dt_bias = draw_dt_bias(jax.random.fold_in(streams_of[8], 71), 0)
    a_log = jnp.clip(jax.random.uniform(streams_of[5], (H,), jnp.float32, -3.5, -2.5), -3.5, -2.5)
    d_skip = jnp.clip(jax.random.uniform(streams_of[6], (H,), jnp.float32, 0.5, 1.5), 0.5, 1.5)
    grad_out = normal_values(streams_of[7], (CONTEXT_COUNT, CONTEXT_TOKENS, H * P_SIZE), 1.0, 6.0, ((0, 4), (1, 8)))
    return dict(xbc_raw=xbc_raw, conv_weight=conv_weight, conv_bias=conv_bias, dt_raw=dt_raw, dt_bias=dt_bias, a_log=a_log, d_skip=d_skip, grad_out=grad_out)


highest = lax.Precision.HIGHEST

def seq_forward(raw_rows, conv_weight, conv_bias, dt_seq, dt_bias, a_log, d_skip):
    length = raw_rows.shape[0]
    padded = jnp.pad(raw_rows.astype(jnp.float32), ((K - 1, 0), (0, 0)))
    pre_conv = conv_bias + sum((conv_weight[tap_idx] * padded[tap_idx:tap_idx + length] for tap_idx in range(K)))
    xbc_low = lax.optimization_barrier(jax.nn.silu(pre_conv).astype(jnp.bfloat16))
    xbc = xbc_low.astype(jnp.float32)
    inner_width = H * P_SIZE
    values = xbc[:, :inner_width].reshape(N_CTX, L, H, P_SIZE)
    b_proj = xbc[:, inner_width:inner_width + N].reshape(N_CTX, L, N)
    c_proj = xbc[:, inner_width + N:].reshape(N_CTX, L, N)
    step_size = jax.nn.softplus(dt_seq + dt_bias).reshape(N_CTX, L, H)
    decay_rate = -jnp.exp(a_log)
    causal = jnp.tril(jnp.ones((L, L), dtype=jnp.bool_))

    def block_step(carried, pieces):
        block_vals, block_b, block_c, block_size = pieces
        cum_log = jnp.cumsum(block_size * decay_rate, axis=0)
        cum_log_t = cum_log.T
        log_gaps = cum_log_t[:, :, None] - cum_log_t[:, None, :]
        within = jnp.where(causal, jnp.exp(jnp.where(causal, log_gaps, 0.0)), 0.0)
        gram_mat = jnp.dot(block_c, block_b.T, precision=highest)
        mixing = gram_mat[None] * within * block_size.T[:, None, :]
        local_out = jnp.einsum('hts,shp->thp', mixing, block_vals, precision=highest)
        state_out = jnp.einsum('tn,hpn->thp', block_c, carried, precision=highest)
        output = local_out + jnp.exp(cum_log)[:, :, None] * state_out + d_skip[:, None] * block_vals
        tail_w = jnp.exp(cum_log[-1:] - cum_log) * block_size
        new_state = jnp.exp(cum_log[-1])[:, None, None] * carried + jnp.einsum('shp,sn->hpn', block_vals * tail_w[:, :, None], block_b, precision=highest)
        return (new_state, output.reshape(L, H * P_SIZE))
    start_state = jnp.zeros((H, P_SIZE, N), jnp.float32)
    _, outputs = lax.scan(jax.checkpoint(block_step), start_state, (values, b_proj, c_proj, step_size))
    return outputs.reshape(length, H * P_SIZE)

def reference(xbc_raw, conv_weight, conv_bias, dt_raw, dt_bias, a_log, d_skip, grad_out):
    zeros_init = (jnp.zeros_like(conv_weight), jnp.zeros_like(conv_bias), jnp.zeros_like(dt_bias), jnp.zeros_like(a_log), jnp.zeros_like(d_skip))

    def per_context(totals, inputs):
        raw_rows, dt_seq, cotangent = inputs
        _, pullback = jax.vjp(seq_forward, raw_rows, conv_weight, conv_bias, dt_seq, dt_bias, a_log, d_skip)
        gradients = pullback(cotangent.astype(jnp.float32))
        totals = (totals[0] + gradients[1], totals[1] + gradients[2], totals[2] + gradients[4], totals[3] + gradients[5], totals[4] + gradients[6])
        return (totals, (gradients[0], gradients[3]))
    totals, outs_pair = lax.scan(per_context, zeros_init, (xbc_raw, dt_raw, grad_out))
    return (outs_pair[0], outs_pair[1], totals[0], totals[1], totals[2], totals[3], totals[4])
```

```python
import functools

import jax
import jax.numpy as jnp
from jax import lax
from jax.experimental import pallas as pl
from jax.experimental.pallas import tpu as pltpu
from jax.sharding import PartitionSpec as P

H = 4
P_SIZE = 64
N = 128
K = 4
INNER = H * P_SIZE
HEAD_ROWS = 8
TAIL_ROWS = 16
HALO_ROWS = 16
END_ROWS = 16
LANE_BLOCKS = (INNER + 2 * N) // 128
TOTAL_ROWS = 24

f32 = jnp.float32
bf16 = jnp.bfloat16

VMEM = pl.BlockSpec(memory_space=pltpu.VMEM)
SMEM = pl.BlockSpec(memory_space=pltpu.SMEM)
HBM = pl.BlockSpec(memory_space=pltpu.HBM)


def dot(a, b, a_dim=1, b_dim=0):
    return lax.dot_general(a, b, (((a_dim,), (b_dim,)), ((), ())), preferred_element_type=f32)


def split2(x):
    high = x.astype(bf16)
    return high, (x - high.astype(f32)).astype(bf16)


def split3(x):
    high = x.astype(bf16).astype(f32)
    rest = x - high
    middle = rest.astype(bf16).astype(f32)
    return high, middle, rest - middle


def iota(shape, dim):
    return lax.broadcasted_iota(jnp.int32, shape, dim)


def stacked(rows):
    return jnp.concatenate([*split3(rows), jnp.zeros_like(rows)], 0).astype(bf16)


def unstacked(rows):
    return rows[0:8] + rows[8:16] + rows[16:24]


def head_selector(rows):
    shape = (rows, INNER)
    return jnp.where(iota(shape, 1) // P_SIZE == iota(shape, 0) % HEAD_ROWS, 1.0, 0.0).astype(bf16)


def over_channels(rows):
    return dot(stacked(rows), head_selector(4 * HEAD_ROWS), 0, 0)


def head_sums(x):
    high, low = split2(x)
    selector = head_selector(HEAD_ROWS * 2)
    return (dot(selector, high, 1, 1) + dot(selector, low, 1, 1))[:HEAD_ROWS]


def by_head(ref, width):
    row = iota((HEAD_ROWS, width), 0)
    out = jnp.zeros((HEAD_ROWS, width), f32)
    for h in range(H):
        out = jnp.where(row == h, ref[h], out)
    return out


def shifted_down(x, first, count):
    moved = pltpu.roll(x, count, 0)
    top = jnp.where(iota(first.shape, 0) < count, pltpu.roll(first, count, 0), moved[:8])
    return jnp.concatenate([top, moved[8:]], 0)


def quantized_log(size):
    return jnp.log(jnp.maximum(size, 1e-30)).astype(bf16).astype(f32)


def scaled_columns(x):
    log_size = quantized_log(jnp.max(jnp.abs(x), axis=0, keepdims=True))
    return x * jnp.exp(-log_size), log_size


def write_message(msg_ref, state, grad, log_decay, last, upper):
    row = iota((TAIL_ROWS, INNER), 0)
    if last:
        body, log_size = scaled_columns(jnp.where(upper, grad, state))
        msg_ref[0:N] = body
        msg_ref[N : N + TAIL_ROWS] = jnp.where(row == 0, log_size, 0.0)
        return
    state, state_size = scaled_columns(state)
    grad, grad_size = scaled_columns(grad)
    high, middle, low = split3(log_decay)
    tail = jnp.where(row == 2, state_size, jnp.where(row == 3, grad_size, 0.0))
    tail = jnp.where(row == 4, high, jnp.where(row == 5, middle * 256.0, jnp.where(row == 6, low * 65536.0, tail)))
    msg_ref[0:N] = state
    msg_ref[N : 2 * N] = grad
    msg_ref[2 * N : 2 * N + TAIL_ROWS] = tail


def pack_totals(x):
    log_size = quantized_log(jnp.max(jnp.abs(x), axis=1, keepdims=True))
    shape = x.shape
    logs = jnp.sum(jnp.where(iota(shape, 0) == iota(shape, 1), log_size, 0.0), axis=0, keepdims=True)
    return jnp.where(iota(shape, 0) == shape[0] - 1, logs, x * jnp.exp(-log_size))


def start_kernel(
    raw_hbm, cot_hbm, weight_hbm, bias_hbm, dt_hbm, dt_bias_hbm, alog_hbm, skip_hbm,
    raw_ref, cot_ref, weight_ref, pre_ref, scaled_ref, tail_ref, rows_ref, logs_ref,
    bias_ref, dt_ref, dt8_ref, dt_bias_ref, alog_ref, skip_ref, sems,
):
    pairs = [
        (dt_hbm, dt_ref), (dt_bias_hbm, dt_bias_ref), (alog_hbm, alog_ref), (skip_hbm, skip_ref),
        (cot_hbm, cot_ref), (raw_hbm, raw_ref), (weight_hbm, weight_ref), (bias_hbm, bias_ref),
    ]
    copies = [pltpu.make_async_copy(src, dst, sems.at[i]) for i, (src, dst) in enumerate(pairs)]
    for copy in copies:
        copy.start()
    tok = raw_ref.shape[0]
    dt8_ref[...] = jnp.zeros_like(dt8_ref)
    for copy in copies[:4]:
        copy.wait()
    dt8_ref[0:H] = dt_ref[...]
    dt_pre = dt8_ref[...] + by_head(dt_bias_ref, tok)
    step = jnp.maximum(dt_pre, 0.0) + jnp.log1p(jnp.exp(-jnp.abs(dt_pre)))
    decay_rate = -jnp.exp(by_head(alog_ref, tok))
    until = jnp.where(iota((tok, tok), 0) <= iota((tok, tok), 1), 1.0, 0.0).astype(bf16)
    cum = unstacked(dot(stacked(step * decay_rate), until))
    left = jnp.exp(cum[:, tok - 1 : tok] - cum)
    reach = jnp.exp(cum)
    rows_ref[0:8] = cum
    rows_ref[8:16] = step
    rows_ref[16:24] = left
    rows_ref[24:32] = reach
    rows_ref[32:40] = 1.0 / (1.0 + jnp.exp(-dt_pre))
    rows_ref[40:48] = decay_rate
    tail_ref[...] = over_channels(left * step)
    log_total = over_channels(cum)[tok - 1 : tok]
    skip = jnp.zeros((1, INNER), f32)
    for h in range(H):
        skip = jnp.where(iota((1, INNER), 1) // P_SIZE == h, skip_ref[h], skip)
    row = iota((8, INNER), 0)
    logs_ref[...] = jnp.where(row == 2, log_total, jnp.where(row == 3, skip, 0.0))
    copies[4].wait()
    scaled_ref[...] = jnp.concatenate(split2(cot_ref[...].astype(f32) * over_channels(reach)), 1)
    for copy in copies[5:]:
        copy.wait()
    raw = raw_ref[...].astype(f32)
    zeros = jnp.zeros((8, raw.shape[1]), f32)
    pre = bias_ref[...] + weight_ref[K - 1 : K] * raw
    for back in range(1, K):
        pre = pre + weight_ref[K - 1 - back : K - back] * shifted_down(raw, zeros, back)
    pre_ref[...] = pre


def enter_kernel(
    last, pre_ref, halo_ref, weight_ref, scaled_ref, tail_ref, logs_ref, upper_ref,
    xbc_ref, slope_ref, weighted_ref, state_ref, grad_ref, msg_ref,
):
    tok = pre_ref.shape[0]
    halo = halo_ref[HALO_ROWS - 8 :].astype(f32)
    top = pre_ref[0:8]
    for back in range(1, K):
        tap = weight_ref[K - 1 - back : K - back]
        top = top + jnp.where(iota(top.shape, 0) < back, tap * pltpu.roll(halo, back, 0), 0.0)
    pre = jnp.concatenate([top, pre_ref[8:]], 0)
    gate = 1.0 / (1.0 + jnp.exp(-pre))
    xbc = (pre * gate).astype(bf16)
    xbc_ref[...] = xbc
    slope_ref[...] = gate * (1.0 + pre * (1.0 - gate))
    weighted = jnp.concatenate(split2(xbc[:, :INNER].astype(f32) * tail_ref[...]), 1)
    weighted_ref[...] = weighted
    state = dot(xbc[:, INNER : INNER + N], weighted, 0, 0)
    state = state[:, :INNER] + state[:, INNER:]
    grad = dot(xbc[:, INNER + N :], scaled_ref[...], 0, 0)
    grad = grad[:, :INNER] + grad[:, INNER:]
    state_ref[...] = state
    grad_ref[...] = grad
    write_message(msg_ref, state, grad, logs_ref[2:3], last, upper_ref[0] == 1)


def merge_kernel(first, last, state_ref, grad_ref, logs_ref, got_ref, upper_ref, *refs):
    if first:
        prior = after = 0.0
    else:
        prior, after = refs[0][...], refs[1][...]
        refs = refs[2:]
    logs_out, msg_ref, prior_out, after_out, *refs = refs
    upper = upper_ref[0] == 1
    log_prior, log_after, log_total = logs_ref[0:1], logs_ref[1:2], logs_ref[2:3]
    tail = got_ref[2 * N : 2 * N + TAIL_ROWS]
    got_state = got_ref[0:N] * jnp.exp(tail[2:3])
    got_grad = got_ref[N : 2 * N] * jnp.exp(tail[3:4])
    got_log = tail[4:5] + tail[5:6] * (1 / 256.0) + tail[6:7] * (1 / 65536.0)
    mine, theirs = jnp.exp(log_total), jnp.exp(got_log)
    own_state, own_grad = state_ref[...], grad_ref[...]
    state = jnp.where(upper, own_state + mine * got_state, got_state + theirs * own_state)
    grad = jnp.where(upper, got_grad + theirs * own_grad, own_grad + mine * got_grad)
    prior_out[...] = prior + jnp.where(upper, jnp.exp(log_prior) * got_state, 0.0)
    after_out[...] = after + jnp.where(upper, 0.0, jnp.exp(log_after) * got_grad)
    log_prior = jnp.where(upper, log_prior + got_log, log_prior)
    log_after = jnp.where(upper, log_after, log_after + got_log)
    log_total = log_total + got_log
    row = iota((8, INNER), 0)
    logs_out[...] = jnp.where(row == 0, log_prior, jnp.where(row == 1, log_after, jnp.where(row == 2, log_total, 0.0)))
    if refs:
        refs[0][...] = state
        refs[1][...] = grad
    write_message(msg_ref, state, grad, log_total, last, upper_ref[1] == 1)


def local_kernel(xbc_ref, cot_ref, rows_ref, logs_ref, local_ref, sums_ref):
    tok = xbc_ref.shape[0]
    cot = cot_ref[...]
    values = xbc_ref[:, :INNER]
    b_proj = xbc_ref[:, INNER : INNER + N]
    c_proj = xbc_ref[:, INNER + N :]
    cum, step = rows_ref[0:8], rows_ref[8:16]
    step_wide = over_channels(step)
    values_f = values.astype(f32)
    cot_f = cot.astype(f32)
    stepped = split2(values_f * step_wide)
    gram = dot(b_proj, c_proj, 1, 1)
    reached = iota((tok, tok), 0) <= iota((tok, tok), 1)
    pieces = stacked(cum)
    piece_head = iota((4 * HEAD_ROWS, tok), 0) % HEAD_ROWS
    dgram = jnp.zeros((tok, tok), f32)
    grads, sums = [], []
    for h in range(H):
        of = slice(h * P_SIZE, (h + 1) * P_SIZE)
        column = dot(pieces, jnp.where(piece_head == h, 1.0, 0.0).astype(bf16), 0, 0)
        within = jnp.exp(jnp.where(reached, cum[h : h + 1] - column, -1e30))
        cot_h = cot[:, of]
        high, low = split2(gram * within)
        grads.append(dot(high, cot_h) + dot(low, cot_h))
        dmix = dot(stepped[0][:, of], cot_h, 1, 1) + dot(stepped[1][:, of], cot_h, 1, 1)
        dmix = dmix * within
        dgram = dgram + dmix
        sums.append(jnp.sum(dmix * gram, axis=0, keepdims=True))
    grad_stepped = jnp.concatenate(grads, 1)
    local_ref[:, :INNER] = grad_stepped * step_wide + logs_ref[3:4] * cot_f
    high, low = split2(dgram)
    local_ref[:, INNER : INNER + N] = dot(high, c_proj) + dot(low, c_proj)
    local_ref[:, INNER + N :] = dot(high, b_proj, 0, 0) + dot(low, b_proj, 0, 0)
    row = iota((HEAD_ROWS, tok), 0)
    pairs = jnp.zeros((HEAD_ROWS, tok), f32)
    for h in range(H):
        pairs = jnp.where(row == h, sums[h], pairs)
    sums_ref[0:8] = pairs
    sums_ref[8:16] = head_sums(values_f * grad_stepped)
    sums_ref[16:24] = head_sums(values_f * cot_f)


def leave_kernel(
    raw_ref, halo_ref, weight_ref, xbc_ref, slope_ref, scaled_ref, weighted_ref, tail_ref, rows_ref, local_ref, sums_ref,
    logs_ref, got_ref, upper_ref, *refs
):
    prior, after = 0.0, 0.0
    if len(refs) > 8:
        prior, after = refs[0][...], refs[1][...]
        refs = refs[2:]
    out_hbm, dt_out_ref, end_ref, spill_ref, totals_ref, out_ref, totals_scratch, sem = refs
    tok = raw_ref.shape[0]
    upper = upper_ref[0] == 1
    got = got_ref[0:N] * jnp.exp(got_ref[N : N + 1])
    prior = prior + jnp.where(upper, jnp.exp(logs_ref[0:1]) * got, 0.0)
    after = after + jnp.where(upper, 0.0, jnp.exp(logs_ref[1:2]) * got)

    step, left, reach = rows_ref[8:16], rows_ref[16:24], rows_ref[24:32]
    dt_gate, decay_rate = rows_ref[32:40], rows_ref[40:48]
    b_proj = xbc_ref[:, INNER : INNER + N]
    c_proj = xbc_ref[:, INNER + N :]
    prior2 = jnp.concatenate(split2(prior), 0)
    after2 = jnp.concatenate(split2(after), 0)
    seen = dot(jnp.concatenate([c_proj, c_proj], 1), prior2)
    back = dot(jnp.concatenate([b_proj, b_proj], 1), after2)
    grad_c = dot(scaled_ref[:, :INNER], prior2, 1, 1)
    grad_c = grad_c[:, :N] + grad_c[:, N:] + dot(scaled_ref[:, INNER:], prior2[:N], 1, 1)
    grad_b = dot(weighted_ref[:, :INNER], after2, 1, 1)
    grad_b = grad_b[:, :N] + grad_b[:, N:] + dot(weighted_ref[:, INNER:], after2[:N], 1, 1)
    grad_low = (local_ref[...] + jnp.concatenate([tail_ref[...] * back, grad_b, grad_c], 1)).astype(bf16)
    grad_conv = grad_low.astype(f32) * slope_ref[...]

    raw = raw_ref[...].astype(f32)
    halo = halo_ref[HALO_ROWS - 8 :].astype(f32)
    sums = [None] * (K + 1)
    sums[K - 1] = jnp.sum(grad_conv * raw, axis=0, keepdims=True)
    sums[K] = jnp.sum(grad_conv, axis=0, keepdims=True)
    grad_in = weight_ref[K - 1 : K] * grad_conv
    spill = jnp.zeros((8, raw.shape[1]), f32)
    row8 = iota(spill.shape, 0)
    for ahead in range(1, K):
        tap = weight_ref[K - 1 - ahead : K - ahead]
        sums[K - 1 - ahead] = jnp.sum(grad_conv * shifted_down(raw, halo, ahead), axis=0, keepdims=True)
        moved = pltpu.roll(grad_conv, tok - ahead, 0)
        last8 = moved[tok - 8 :]
        inside = row8 < 8 - ahead
        grad_in = grad_in + tap * jnp.concatenate([moved[: tok - 8], jnp.where(inside, last8, 0.0)], 0)
        spill = spill + tap * jnp.where(inside, 0.0, last8)
    out_ref[...] = grad_in.astype(bf16)
    copy = pltpu.make_async_copy(out_ref, out_hbm, sem)
    copy.start()
    end_ref[...] = grad_in[tok - END_ROWS :]
    spill_ref[...] = spill
    totals_scratch[...] = jnp.zeros_like(totals_scratch)
    for k in range(K + 1):
        for j in range(LANE_BLOCKS):
            at = k * LANE_BLOCKS + j
            totals_scratch[at : at + 1] = sums[k][:, j * 128 : (j + 1) * 128]

    values = xbc_ref[:, :INNER].astype(f32)
    pairs, from_values, skip_rows = sums_ref[0:8], sums_ref[8:16], sums_ref[16:24]
    scaled_f = scaled_ref[:, :INNER].astype(f32) + scaled_ref[:, INNER:].astype(f32)
    seen_rows = head_sums(scaled_f * seen)
    tail_rows = head_sums(values * back)
    tail_term = tail_rows * left * step
    selector = head_selector(HEAD_ROWS * 2)[:HEAD_ROWS].astype(f32)
    through = jnp.sum(prior * after, axis=0, keepdims=True)
    through = jnp.sum(selector * through, axis=1, keepdims=True) * reach[:, tok - 1 : tok]
    last_extra = jnp.sum(tail_term, axis=1, keepdims=True) + through
    from_on = jnp.where(iota((tok, tok), 0) >= iota((tok, tok), 1), 1.0, 0.0).astype(bf16)
    grad_cum = pairs - from_values * step + seen_rows - tail_term
    grad_log = unstacked(dot(stacked(grad_cum), from_on)) + last_extra
    grad_step = from_values + tail_rows * left + decay_rate * grad_log
    grad_pre = grad_step * dt_gate
    dt_out_ref[...] = grad_pre[0:H]
    row, lane = iota((HEAD_ROWS, 128), 0), iota((HEAD_ROWS, 128), 1)
    small = jnp.zeros((HEAD_ROWS, 128), f32)
    for i, each in enumerate((grad_pre, grad_log * step * decay_rate, skip_rows)):
        column = jnp.sum(each, axis=1, keepdims=True)
        small = jnp.where((row < H) & (lane == row + i * H), column, small)
    at = (K + 1) * LANE_BLOCKS
    totals_scratch[at : at + 1] = jnp.sum(small, axis=0, keepdims=True)
    totals_ref[...] = pack_totals(totals_scratch[...])
    copy.wait()


def summed(parts):
    shape = parts.shape
    logs = parts[:, shape[1] - 1 :]
    logs = jnp.sum(jnp.where(iota(shape, 1) == iota(shape, 2), logs, 0.0), axis=2, keepdims=True)
    return jnp.sum(parts * jnp.exp(logs), axis=0)


def repack_kernel(parts_ref, out_ref):
    total = summed(parts_ref[...])
    out_ref[...] = pack_totals(jnp.where(iota(total.shape, 0) == total.shape[0] - 1, 0.0, total))


def finish_kernel(
    parts_ref, end_ref, spilled_ref, main_hbm, out_hbm, weight_ref, bias_ref, dt_bias_ref, alog_ref, skip_ref, rows_ref, sem
):
    end = end_ref[...]
    fixed = end[END_ROWS - 8 :] + spilled_ref[...]
    rows_ref[...] = jnp.concatenate([end[: END_ROWS - 8], fixed], 0).astype(bf16)
    tok = out_hbm.shape[0]
    copy = pltpu.make_async_copy(rows_ref, out_hbm.at[pl.ds(tok - END_ROWS, END_ROWS)], sem)
    copy.start()
    total = summed(parts_ref[...])
    for k in range(K + 1):
        for j in range(LANE_BLOCKS):
            at = k * LANE_BLOCKS + j
            if k < K:
                weight_ref[k : k + 1, j * 128 : (j + 1) * 128] = total[at : at + 1]
            else:
                bias_ref[:, j * 128 : (j + 1) * 128] = total[at : at + 1]
    at = (K + 1) * LANE_BLOCKS
    for i, ref in enumerate((dt_bias_ref, alog_ref, skip_ref)):
        ref[...] = total[at : at + 1, i * H : (i + 1) * H]
    copy.wait()


def call(kernel, outs, in_specs, out_specs=None, scratch=(), flops=0, limit=16 << 20, aliases=None):
    return pl.pallas_call(
        kernel,
        out_shape=outs,
        in_specs=in_specs,
        out_specs=out_specs or jax.tree.map(lambda _: VMEM, outs),
        scratch_shapes=list(scratch),
        input_output_aliases=aliases or {},
        compiler_params=pltpu.CompilerParams(vmem_limit_bytes=limit),
        cost_estimate=pl.CostEstimate(flops=flops, bytes_accessed=1 << 20, transcendentals=0),
    )


def struct(shape, dtype=f32):
    return jax.ShapeDtypeStruct(shape, dtype)


def exchange(message, distance, slabs):
    message = message.astype(jnp.float16)
    return lax.ppermute(message, "ctx", [(i, i ^ distance) for i in range(slabs)]).astype(f32)


def everyones(packed, axes, count):
    packed = jnp.broadcast_to(packed.astype(jnp.float16)[None], (count, *packed.shape))
    return lax.all_to_all(packed, axes, 0, 0).astype(f32)


def on_device(xbc_raw, conv_weight, conv_bias, dt_raw, dt_bias, a_log, d_skip, grad_out):
    raw = xbc_raw[0]
    tok, channels = raw.shape
    slabs = lax.axis_size("ctx")
    rounds = slabs.bit_length() - 1
    assert slabs == 1 << rounds and rounds > 0
    place = lax.axis_index("ctx")
    bits = [(place >> r) & 1 for r in range(rounds)]

    halo = lax.ppermute(raw[tok - HALO_ROWS :], "ctx", [(i, i + 1) for i in range(slabs - 1)])

    def message(r):
        return struct((N + TAIL_ROWS if r == rounds - 1 else 2 * N + TAIL_ROWS, INNER))

    state_like = struct((N, INNER))
    logs_like = struct((8, INNER))
    raw_near, cot, weight, pre, scaled, tail, rows, logs = call(
        start_kernel,
        (
            struct((tok, channels), bf16), struct((tok, INNER), bf16), struct((K, channels)), struct((tok, channels)),
            struct((tok, 2 * INNER), bf16), struct((tok, INNER)), struct((6 * HEAD_ROWS, tok)), logs_like,
        ),
        [HBM] * 8,
        scratch=[
            pltpu.VMEM((1, channels), f32), pltpu.VMEM((H, tok), f32), pltpu.VMEM((HEAD_ROWS, tok), f32),
            pltpu.SMEM((H,), f32), pltpu.SMEM((H,), f32), pltpu.SMEM((H,), f32), pltpu.SemaphoreType.DMA((8,)),
        ],
        flops=100_000_000,
    )(raw, grad_out[0], conv_weight, conv_bias[None], dt_raw[0].T, dt_bias, a_log, d_skip)

    xbc, slope, weighted, state, grad, msg = call(
        functools.partial(enter_kernel, rounds == 1),
        (
            struct((tok, channels), bf16), struct((tok, channels)), struct((tok, 2 * INNER), bf16),
            state_like, state_like, message(0),
        ),
        [VMEM] * 6 + [SMEM],
        flops=200_000_000,
    )(pre, halo, weight, scaled, tail, logs, jnp.stack([bits[0]]))

    local, sums = call(
        local_kernel,
        (struct((tok, channels)), struct((3 * HEAD_ROWS, tok))),
        [VMEM] * 4,
        flops=1_000_000_000,
    )(xbc, cot, rows, logs)

    carried = ()
    for r in range(rounds - 1):
        got = exchange(msg, 1 << r, slabs)
        if r == 0:
            got, local, sums = lax.optimization_barrier((got, local, sums))
        last = r + 1 == rounds - 1
        logs, msg, *carried = call(
            functools.partial(merge_kernel, r == 0, last),
            (logs_like, message(r + 1)) + (state_like,) * (2 if last else 4),
            [VMEM] * 4 + [SMEM] + [VMEM] * len(carried),
            flops=1_000_000,
        )(state, grad, logs, got, jnp.stack([bits[r], bits[r + 1]]), *carried)
        if not last:
            *carried, state, grad = carried
    got = exchange(msg, 1 << (rounds - 1), slabs)

    grad_main, grad_dt, end, spill, packed = call(
        leave_kernel,
        (
            struct((tok, channels), bf16), struct((H, tok)), struct((END_ROWS, channels)), struct((8, channels)),
            struct((TOTAL_ROWS, 128)),
        ),
        [VMEM] * 13 + [SMEM] + [VMEM] * len(carried),
        (HBM, VMEM, VMEM, VMEM, VMEM),
        [pltpu.VMEM((tok, channels), bf16), pltpu.VMEM((TOTAL_ROWS, 128), f32), pltpu.SemaphoreType.DMA],
        flops=200_000_000,
    )(raw_near, halo, weight, xbc, slope, scaled, weighted, tail, rows, local, sums, logs, got, jnp.stack([bits[-1]]), *carried)

    spilled = lax.ppermute(spill, "ctx", [(i + 1, i) for i in range(slabs - 1)])

    contexts = lax.axis_size("dp")
    if slabs * contexts <= 64:
        parts = everyones(packed, ("ctx", "dp"), slabs * contexts)
    else:
        packed = call(repack_kernel, struct((TOTAL_ROWS, 128)), [VMEM])(everyones(packed, "ctx", slabs))
        parts = everyones(packed, "dp", contexts)
    grad_input, grad_weight, grad_bias, *small = call(
        finish_kernel,
        (
            struct((tok, channels), bf16), struct((K, channels)), struct((1, channels)),
            struct((1, H)), struct((1, H)), struct((1, H)),
        ),
        [VMEM] * 3 + [HBM],
        (HBM,) + (VMEM,) * 5,
        [pltpu.VMEM((END_ROWS, channels), bf16), pltpu.SemaphoreType.DMA],
        aliases={3: 0},
    )(parts, end, spilled, grad_main)
    return (grad_input[None], grad_dt.T[None], grad_weight, grad_bias[0], *(each[0] for each in small))


def solution(mesh):
    in_specs = (
        P("dp", "ctx", None),
        P(),
        P(),
        P("dp", "ctx", None),
        P(),
        P(),
        P(),
        P("dp", "ctx", None),
    )
    out_specs = (P("dp", "ctx", None), P("dp", "ctx", None), P(), P(), P(), P(), P())
    return jax.shard_map(
        on_device, mesh=mesh, in_specs=in_specs, out_specs=out_specs, check_vma=False
    )
```

```python
import functools

import jax
import jax.numpy as jnp
from jax import lax
from jax.experimental import pallas as pl
from jax.experimental.pallas import tpu as pltpu
from jax.sharding import PartitionSpec as P

H = 4
P_SIZE = 64
N = 128
K = 4
INNER = H * P_SIZE
HEAD_ROWS = 8
TAIL_ROWS = 16
HALO_ROWS = 16
END_ROWS = 16
LANE_BLOCKS = (INNER + 2 * N) // 128
SMALL_ROW = (K + 1) * LANE_BLOCKS
TOTAL_ROWS = 24

f32 = jnp.float32
bf16 = jnp.bfloat16

VMEM = pl.BlockSpec(memory_space=pltpu.VMEM)
HBM = pl.BlockSpec(memory_space=pltpu.HBM)


def dot(a, b, a_dim=1, b_dim=0):
    return lax.dot_general(a, b, (((a_dim,), (b_dim,)), ((), ())), preferred_element_type=f32)


def split2(x):
    high = x.astype(bf16)
    return high, (x - high.astype(f32)).astype(bf16)


def split3(x):
    high = x.astype(bf16).astype(f32)
    rest = x - high
    middle = rest.astype(bf16).astype(f32)
    return high, middle, rest - middle


def iota(shape, dim):
    return lax.broadcasted_iota(jnp.int32, shape, dim)


def stacked(rows):
    return jnp.concatenate([*split3(rows), jnp.zeros_like(rows)], 0).astype(bf16)


def unstacked(rows):
    return rows[0:8] + rows[8:16] + rows[16:24]


def head_selector(rows):
    shape = (rows, INNER)
    return jnp.where(iota(shape, 1) // P_SIZE == iota(shape, 0) % HEAD_ROWS, 1.0, 0.0).astype(bf16)


def over_channels(rows):
    return dot(stacked(rows), head_selector(4 * HEAD_ROWS), 0, 0)


def head_sums(x):
    high, low = split2(x)
    selector = head_selector(HEAD_ROWS * 2)
    return (dot(selector, high, 1, 1) + dot(selector, low, 1, 1))[:HEAD_ROWS]


def by_head(ref, width):
    row = iota((HEAD_ROWS, width), 0)
    out = jnp.zeros((HEAD_ROWS, width), f32)
    for h in range(H):
        out = jnp.where(row == h, ref[:, h : h + 1], out)
    return out


def shifted_down(x, first, count):
    moved = pltpu.roll(x, count, 0)
    top = jnp.where(iota(first.shape, 0) < count, pltpu.roll(first, count, 0), moved[:8])
    return jnp.concatenate([top, moved[8:]], 0)


def is_upper(bits_ref, r):
    return bits_ref[8 * r : 8 * r + 1] > 0.5


def quantized_log(size):
    return jnp.log(jnp.maximum(size, 1e-30)).astype(bf16).astype(f32)


def scaled_columns(x):
    log_size = quantized_log(jnp.max(jnp.abs(x), axis=0, keepdims=True))
    return x * jnp.exp(-log_size), log_size


def write_message(msg_ref, state, grad, log_decay, last, upper):
    row = iota((TAIL_ROWS, INNER), 0)
    if last:
        body, log_size = scaled_columns(jnp.where(upper, grad, state))
        msg_ref[0:N] = body
        msg_ref[N : N + TAIL_ROWS] = jnp.where(row == 0, log_size, 0.0)
        return
    state, state_size = scaled_columns(state)
    grad, grad_size = scaled_columns(grad)
    high, middle, low = split3(log_decay)
    tail = jnp.where(row == 2, state_size, jnp.where(row == 3, grad_size, 0.0))
    tail = jnp.where(row == 4, high, jnp.where(row == 5, middle * 256.0, jnp.where(row == 6, low * 65536.0, tail)))
    msg_ref[0:N] = state
    msg_ref[N : 2 * N] = grad
    msg_ref[2 * N : 2 * N + TAIL_ROWS] = tail


def pack_totals(x):
    row = iota(x.shape, 0)
    large = jnp.where(row < SMALL_ROW, x, 0.0)
    large_size = quantized_log(jnp.max(jnp.abs(large), axis=0, keepdims=True))
    small = x[SMALL_ROW : SMALL_ROW + 1]
    small_size = quantized_log(jnp.abs(small))
    out = jnp.where(row == SMALL_ROW, small * jnp.exp(-small_size), large * jnp.exp(-large_size))
    return jnp.where(row == SMALL_ROW + 1, large_size, jnp.where(row == SMALL_ROW + 2, small_size, out))


def triangle_kernel(until_ref):
    shape = until_ref.shape
    until_ref[...] = jnp.where(iota(shape, 0) <= iota(shape, 1), 1.0, 0.0).astype(bf16)


def start_kernel(
    rounds, raw_ref, cot_ref, weight_ref, bias_ref, dt_ref, dt_bias_ref, alog_ref, skip_ref, until_ref,
    pre_ref, scaled_ref, tail_ref, rows_ref, logs_ref, bits_ref, dt8_ref,
):
    tok = raw_ref.shape[0]
    place = lax.axis_index("ctx")
    for r in range(rounds):
        bits_ref[8 * r : 8 * r + 8] = jnp.full((8, INNER), (place >> r) & 1, jnp.int32).astype(f32)
    dt8_ref[...] = jnp.zeros_like(dt8_ref)
    dt8_ref[0:H] = dt_ref[...]
    dt_pre = dt8_ref[...] + by_head(dt_bias_ref, tok)
    step = jnp.maximum(dt_pre, 0.0) + jnp.log1p(jnp.exp(-jnp.abs(dt_pre)))
    real = iota((HEAD_ROWS, tok), 0) < H
    decay_rate = jnp.where(real, -jnp.exp(by_head(alog_ref, tok)), 0.0)
    cum = unstacked(dot(stacked(step * decay_rate), until_ref[...]))
    left = jnp.exp(cum[:, tok - 1 : tok] - cum)
    reach = jnp.exp(cum)
    rows_ref[0:8] = cum
    rows_ref[8:16] = step
    rows_ref[16:24] = left
    rows_ref[24:32] = reach
    rows_ref[32:40] = 1.0 / (1.0 + jnp.exp(-dt_pre))
    rows_ref[40:48] = decay_rate
    tail_ref[...] = over_channels(left * step)
    log_total = over_channels(cum)[tok - 1 : tok]
    skip = over_channels(by_head(skip_ref, HEAD_ROWS))[0:1]
    row = iota((8, INNER), 0)
    logs_ref[...] = jnp.where(row == 2, log_total, jnp.where(row == 3, skip, 0.0))
    scaled_ref[...] = jnp.concatenate(split2(cot_ref[...].astype(f32) * over_channels(reach)), 1)
    raw = raw_ref[...].astype(f32)
    zeros = jnp.zeros((8, raw.shape[1]), f32)
    pre = bias_ref[...] + weight_ref[K - 1 : K] * raw
    for back in range(1, K):
        pre = pre + weight_ref[K - 1 - back : K - back] * shifted_down(raw, zeros, back)
    pre_ref[...] = pre


def enter_kernel(
    last, pre_ref, halo_ref, weight_ref, scaled_ref, tail_ref, logs_ref, bits_ref,
    xbc_ref, slope_ref, weighted_ref, state_ref, grad_ref, msg_ref,
):
    tok = pre_ref.shape[0]
    halo = halo_ref[HALO_ROWS - 8 :].astype(f32)
    top = pre_ref[0:8]
    for back in range(1, K):
        tap = weight_ref[K - 1 - back : K - back]
        top = top + jnp.where(iota(top.shape, 0) < back, tap * pltpu.roll(halo, back, 0), 0.0)
    pre = jnp.concatenate([top, pre_ref[8:]], 0)
    gate = 1.0 / (1.0 + jnp.exp(-pre))
    xbc = (pre * gate).astype(bf16)
    xbc_ref[...] = xbc
    slope_ref[...] = gate * (1.0 + pre * (1.0 - gate))
    weighted = jnp.concatenate(split2(xbc[:, :INNER].astype(f32) * tail_ref[...]), 1)
    weighted_ref[...] = weighted
    state = dot(xbc[:, INNER : INNER + N], weighted, 0, 0)
    state = state[:, :INNER] + state[:, INNER:]
    grad = dot(xbc[:, INNER + N :], scaled_ref[...], 0, 0)
    grad = grad[:, :INNER] + grad[:, INNER:]
    state_ref[...] = state
    grad_ref[...] = grad
    write_message(msg_ref, state, grad, logs_ref[2:3], last, is_upper(bits_ref, 0))


def merge_kernel(r, first, last, state_ref, grad_ref, logs_ref, got_ref, bits_ref, *refs):
    if first:
        prior = after = 0.0
    else:
        prior, after = refs[0][...], refs[1][...]
        refs = refs[2:]
    logs_out, msg_ref, prior_out, after_out, *refs = refs
    upper = is_upper(bits_ref, r)
    log_prior, log_after, log_total = logs_ref[0:1], logs_ref[1:2], logs_ref[2:3]
    tail = got_ref[2 * N : 2 * N + TAIL_ROWS]
    got_state = got_ref[0:N] * jnp.exp(tail[2:3])
    got_grad = got_ref[N : 2 * N] * jnp.exp(tail[3:4])
    got_log = tail[4:5] + tail[5:6] * (1 / 256.0) + tail[6:7] * (1 / 65536.0)
    mine, theirs = jnp.exp(log_total), jnp.exp(got_log)
    own_state, own_grad = state_ref[...], grad_ref[...]
    state = jnp.where(upper, own_state + mine * got_state, got_state + theirs * own_state)
    grad = jnp.where(upper, got_grad + theirs * own_grad, own_grad + mine * got_grad)
    prior_out[...] = prior + jnp.where(upper, jnp.exp(log_prior) * got_state, 0.0)
    after_out[...] = after + jnp.where(upper, 0.0, jnp.exp(log_after) * got_grad)
    log_prior = jnp.where(upper, log_prior + got_log, log_prior)
    log_after = jnp.where(upper, log_after, log_after + got_log)
    log_total = log_total + got_log
    row = iota((8, INNER), 0)
    logs_out[...] = jnp.where(row == 0, log_prior, jnp.where(row == 1, log_after, jnp.where(row == 2, log_total, 0.0)))
    if refs:
        refs[0][...] = state
        refs[1][...] = grad
    write_message(msg_ref, state, grad, log_total, last, is_upper(bits_ref, r + 1))


def local_kernel(xbc_ref, cot_ref, rows_ref, logs_ref, local_ref, sums_ref):
    tok = xbc_ref.shape[0]
    cot = cot_ref[...]
    values = xbc_ref[:, :INNER]
    b_proj = xbc_ref[:, INNER : INNER + N]
    c_proj = xbc_ref[:, INNER + N :]
    cum, step = rows_ref[0:8], rows_ref[8:16]
    step_wide = over_channels(step)
    values_f = values.astype(f32)
    cot_f = cot.astype(f32)
    stepped = split2(values_f * step_wide)
    gram = dot(b_proj, c_proj, 1, 1)
    reached = iota((tok, tok), 0) <= iota((tok, tok), 1)
    pieces = stacked(cum)
    piece_head = iota((4 * HEAD_ROWS, tok), 0) % HEAD_ROWS
    dgram = jnp.zeros((tok, tok), f32)
    grads, sums = [], []
    for h in range(H):
        of = slice(h * P_SIZE, (h + 1) * P_SIZE)
        column = dot(pieces, jnp.where(piece_head == h, 1.0, 0.0).astype(bf16), 0, 0)
        within = jnp.exp(jnp.where(reached, cum[h : h + 1] - column, -1e30))
        cot_h = cot[:, of]
        high, low = split2(gram * within)
        grads.append(dot(high, cot_h) + dot(low, cot_h))
        dmix = dot(stepped[0][:, of], cot_h, 1, 1) + dot(stepped[1][:, of], cot_h, 1, 1)
        dmix = dmix * within
        dgram = dgram + dmix
        sums.append(jnp.sum(dmix * gram, axis=0, keepdims=True))
    grad_stepped = jnp.concatenate(grads, 1)
    local_ref[:, :INNER] = grad_stepped * step_wide + logs_ref[3:4] * cot_f
    high, low = split2(dgram)
    local_ref[:, INNER : INNER + N] = dot(high, c_proj) + dot(low, c_proj)
    local_ref[:, INNER + N :] = dot(high, b_proj, 0, 0) + dot(low, b_proj, 0, 0)
    row = iota((HEAD_ROWS, tok), 0)
    pairs = jnp.zeros((HEAD_ROWS, tok), f32)
    for h in range(H):
        pairs = jnp.where(row == h, sums[h], pairs)
    sums_ref[0:8] = pairs
    sums_ref[8:16] = head_sums(values_f * grad_stepped)
    sums_ref[16:24] = head_sums(values_f * cot_f)


def totals_kernel(
    r, raw_ref, halo_ref, xbc_ref, slope_ref, scaled_ref, weighted_ref, tail_ref, rows_ref, local_ref, sums_ref,
    logs_ref, got_ref, bits_ref, until_ref, weight_ref, *refs
):
    prior, after = 0.0, 0.0
    if len(refs) > 5:
        prior, after = refs[0][...], refs[1][...]
        refs = refs[2:]
    conv_ref, dt_out_ref, totals_ref, spill_ref, totals_scratch = refs
    tok = raw_ref.shape[0]
    upper = is_upper(bits_ref, r)
    got = got_ref[0:N] * jnp.exp(got_ref[N : N + 1])
    prior = prior + jnp.where(upper, jnp.exp(logs_ref[0:1]) * got, 0.0)
    after = after + jnp.where(upper, 0.0, jnp.exp(logs_ref[1:2]) * got)

    step, left, reach = rows_ref[8:16], rows_ref[16:24], rows_ref[24:32]
    dt_gate, decay_rate = rows_ref[32:40], rows_ref[40:48]
    b_proj = xbc_ref[:, INNER : INNER + N]
    c_proj = xbc_ref[:, INNER + N :]
    prior2 = jnp.concatenate(split2(prior), 0)
    after2 = jnp.concatenate(split2(after), 0)
    seen = dot(jnp.concatenate([c_proj, c_proj], 1), prior2)
    back = dot(jnp.concatenate([b_proj, b_proj], 1), after2)
    grad_c = dot(scaled_ref[:, :INNER], prior2, 1, 1)
    grad_c = grad_c[:, :N] + grad_c[:, N:] + dot(scaled_ref[:, INNER:], prior2[:N], 1, 1)
    grad_b = dot(weighted_ref[:, :INNER], after2, 1, 1)
    grad_b = grad_b[:, :N] + grad_b[:, N:] + dot(weighted_ref[:, INNER:], after2[:N], 1, 1)
    grad_low = (local_ref[...] + jnp.concatenate([tail_ref[...] * back, grad_b, grad_c], 1)).astype(bf16)
    grad_conv = grad_low.astype(f32) * slope_ref[...]
    conv_ref[...] = grad_conv
    top = grad_conv[:8]
    spill = jnp.zeros_like(top)
    for ahead in range(1, K):
        tap = weight_ref[K - 1 - ahead : K - ahead]
        spill = spill + tap * jnp.where(iota(top.shape, 0) < 8 - ahead, 0.0, pltpu.roll(top, 8 - ahead, 0))
    spill_ref[...] = spill

    raw = raw_ref[...].astype(f32)
    halo = halo_ref[HALO_ROWS - 8 :].astype(f32)
    sums = [grad_conv * shifted_down(raw, halo, K - 1 - k) for k in range(K - 1)] + [grad_conv * raw, grad_conv]
    totals_scratch[...] = jnp.zeros_like(totals_scratch)
    for k, each in enumerate(sums):
        each = jnp.sum(each, axis=0, keepdims=True)
        for j in range(LANE_BLOCKS):
            at = k * LANE_BLOCKS + j
            totals_scratch[at : at + 1] = each[:, j * 128 : (j + 1) * 128]

    values = xbc_ref[:, :INNER].astype(f32)
    pairs, from_values, skip_rows = sums_ref[0:8], sums_ref[8:16], sums_ref[16:24]
    scaled_f = scaled_ref[:, :INNER].astype(f32) + scaled_ref[:, INNER:].astype(f32)
    seen_rows = head_sums(scaled_f * seen)
    tail_rows = head_sums(values * back)
    tail_term = tail_rows * left * step
    selector = head_selector(HEAD_ROWS * 2)[:HEAD_ROWS].astype(f32)
    through = jnp.sum(prior * after, axis=0, keepdims=True)
    through = jnp.sum(selector * through, axis=1, keepdims=True) * reach[:, tok - 1 : tok]
    last_extra = jnp.sum(tail_term, axis=1, keepdims=True) + through
    grad_cum = pairs - from_values * step + seen_rows - tail_term
    grad_log = unstacked(dot(stacked(grad_cum), until_ref[...], 1, 1)) + last_extra
    grad_step = from_values + tail_rows * left + decay_rate * grad_log
    grad_pre = grad_step * dt_gate
    dt_out_ref[...] = grad_pre[0:H]
    row, lane = iota((HEAD_ROWS, 128), 0), iota((HEAD_ROWS, 128), 1)
    small = jnp.zeros((HEAD_ROWS, 128), f32)
    for i, each in enumerate((grad_pre, grad_log * step * decay_rate, skip_rows)):
        column = jnp.sum(each, axis=1, keepdims=True)
        small = jnp.where((row < H) & (lane == row + i * H), column, small)
    totals_scratch[SMALL_ROW : SMALL_ROW + 1] = jnp.sum(small, axis=0, keepdims=True)
    totals_ref[...] = pack_totals(totals_scratch[...])


def input_kernel(conv_ref, weight_ref, out_hbm, end_ref, out_ref, sem):
    grad_conv = conv_ref[...]
    tok, channels = grad_conv.shape
    grad_in = weight_ref[K - 1 : K] * grad_conv
    row8 = iota((8, channels), 0)
    for ahead in range(1, K):
        tap = weight_ref[K - 1 - ahead : K - ahead]
        moved = pltpu.roll(grad_conv, tok - ahead, 0)
        last8 = moved[tok - 8 :]
        inside = row8 < 8 - ahead
        grad_in = grad_in + tap * jnp.concatenate([moved[: tok - 8], jnp.where(inside, last8, 0.0)], 0)
    out_ref[...] = grad_in.astype(bf16)
    copy = pltpu.make_async_copy(out_ref, out_hbm, sem)
    copy.start()
    end_ref[...] = grad_in[tok - END_ROWS :]
    copy.wait()


def end_kernel(end_ref, spilled_ref, main_hbm, out_hbm, rows_ref, sem):
    end = end_ref[...]
    fixed = end[END_ROWS - 8 :] + spilled_ref[...]
    rows_ref[...] = jnp.concatenate([end[: END_ROWS - 8], fixed], 0).astype(bf16)
    tok = out_hbm.shape[0]
    copy = pltpu.make_async_copy(rows_ref, out_hbm.at[pl.ds(tok - END_ROWS, END_ROWS)], sem)
    copy.start()
    copy.wait()


def summed(parts):
    large = jnp.sum(parts * jnp.exp(parts[:, SMALL_ROW + 1 : SMALL_ROW + 2]), axis=0)
    small = parts[:, SMALL_ROW : SMALL_ROW + 1] * jnp.exp(parts[:, SMALL_ROW + 2 : SMALL_ROW + 3])
    return large, jnp.sum(small, axis=0)


def repack_kernel(parts_ref, out_ref):
    large, small = summed(parts_ref[...])
    out_ref[...] = pack_totals(jnp.where(iota(large.shape, 0) == SMALL_ROW, small, large))


def finish_kernel(parts_ref, weight_ref, bias_ref, dt_bias_ref, alog_ref, skip_ref):
    large, small = summed(parts_ref[...])
    for k in range(K + 1):
        for j in range(LANE_BLOCKS):
            at = k * LANE_BLOCKS + j
            if k < K:
                weight_ref[k : k + 1, j * 128 : (j + 1) * 128] = large[at : at + 1]
            else:
                bias_ref[:, j * 128 : (j + 1) * 128] = large[at : at + 1]
    for i, ref in enumerate((dt_bias_ref, alog_ref, skip_ref)):
        ref[...] = small[:, i * H : (i + 1) * H]


def call(kernel, outs, in_specs, out_specs=None, scratch=(), flops=0, limit=16 << 20, aliases=None):
    return pl.pallas_call(
        kernel,
        out_shape=outs,
        in_specs=in_specs,
        out_specs=out_specs or jax.tree.map(lambda _: VMEM, outs),
        scratch_shapes=list(scratch),
        input_output_aliases=aliases or {},
        compiler_params=pltpu.CompilerParams(vmem_limit_bytes=limit),
        cost_estimate=pl.CostEstimate(flops=flops, bytes_accessed=1 << 20, transcendentals=0),
    )


def struct(shape, dtype=f32):
    return jax.ShapeDtypeStruct(shape, dtype)


def exchange(message, distance, slabs):
    message = message.astype(jnp.float16)
    return lax.ppermute(message, "ctx", [(i, i ^ distance) for i in range(slabs)]).astype(f32)


def everyones(packed, axes, count):
    packed = jnp.broadcast_to(packed.astype(jnp.float16)[None], (count, *packed.shape))
    return lax.all_to_all(packed, axes, 0, 0).astype(f32)


def on_device(xbc_raw, conv_weight, conv_bias, dt_raw, dt_bias, a_log, d_skip, grad_out):
    tok, channels = xbc_raw.shape[1:]
    slabs = lax.axis_size("ctx")
    contexts = lax.axis_size("dp")
    rounds = slabs.bit_length() - 1
    assert slabs == 1 << rounds and rounds > 0

    raw, cot, dt_rows = xbc_raw[0], grad_out[0], dt_raw[0].T
    until = call(triangle_kernel, struct((tok, tok), bf16), [], flops=10**10)()
    early_raw, until = lax.optimization_barrier((raw, until))
    halo = lax.ppermute(early_raw[tok - HALO_ROWS :], "ctx", [(i, i + 1) for i in range(slabs - 1)])

    def message(r):
        return struct((N + TAIL_ROWS if r == rounds - 1 else 2 * N + TAIL_ROWS, INNER))

    state_like = struct((N, INNER))
    logs_like = struct((8, INNER))
    pre, scaled, tail, rows, logs, bits = call(
        functools.partial(start_kernel, rounds),
        (
            struct((tok, channels)), struct((tok, 2 * INNER), bf16), struct((tok, INNER)), struct((6 * HEAD_ROWS, tok)),
            logs_like, struct((8 * rounds, INNER)),
        ),
        [VMEM] * 9,
        scratch=[pltpu.VMEM((HEAD_ROWS, tok), f32)],
        flops=100_000_000,
    )(raw, cot, conv_weight, conv_bias[None], dt_rows, dt_bias[None], a_log[None], d_skip[None], until)

    xbc, slope, weighted, state, grad, msg = call(
        functools.partial(enter_kernel, rounds == 1),
        (
            struct((tok, channels), bf16), struct((tok, channels)), struct((tok, 2 * INNER), bf16),
            state_like, state_like, message(0),
        ),
        [VMEM] * 7,
        flops=200_000_000,
    )(pre, halo, conv_weight, scaled, tail, logs, bits)

    local, sums = call(
        local_kernel,
        (struct((tok, channels)), struct((3 * HEAD_ROWS, tok))),
        [VMEM] * 4,
        flops=1_000_000_000,
    )(xbc, cot, rows, logs)

    carried = ()
    for r in range(rounds - 1):
        got = exchange(msg, 1 << r, slabs)
        if r == 0:
            got, local, sums = lax.optimization_barrier((got, local, sums))
        last = r + 1 == rounds - 1
        logs, msg, *carried = call(
            functools.partial(merge_kernel, r, r == 0, last),
            (logs_like, message(r + 1)) + (state_like,) * (2 if last else 4),
            [VMEM] * (5 + len(carried)),
            flops=1_000_000,
        )(state, grad, logs, got, bits, *carried)
        if not last:
            *carried, state, grad = carried
    got = exchange(msg, 1 << (rounds - 1), slabs)

    grad_conv, grad_dt, packed, spill = call(
        functools.partial(totals_kernel, rounds - 1),
        (struct((tok, channels)), struct((H, tok)), struct((TOTAL_ROWS, 128)), struct((8, channels))),
        [VMEM] * (15 + len(carried)),
        scratch=[pltpu.VMEM((TOTAL_ROWS, 128), f32)],
        flops=200_000_000,
    )(raw, halo, xbc, slope, scaled, weighted, tail, rows, local, sums, logs, got, bits, until, conv_weight, *carried)

    spilled = lax.ppermute(spill, "ctx", [(i + 1, i) for i in range(slabs - 1)])
    if slabs * contexts <= 64:
        parts = everyones(packed, ("ctx", "dp"), slabs * contexts)
    else:
        packed = call(repack_kernel, struct((TOTAL_ROWS, 128)), [VMEM])(everyones(packed, "ctx", slabs))
        parts = everyones(packed, "dp", contexts)

    grad_main, end = call(
        input_kernel,
        (struct((tok, channels), bf16), struct((END_ROWS, channels))),
        [VMEM] * 2,
        (HBM, VMEM),
        [pltpu.VMEM((tok, channels), bf16), pltpu.SemaphoreType.DMA],
        flops=1_000_000,
    )(grad_conv, conv_weight)
    grad_input = call(
        end_kernel,
        struct((tok, channels), bf16),
        [VMEM] * 2 + [HBM],
        HBM,
        [pltpu.VMEM((END_ROWS, channels), bf16), pltpu.SemaphoreType.DMA],
        aliases={2: 0},
    )(end, spilled, grad_main)

    grad_weight, grad_bias, *small = call(
        finish_kernel,
        (struct((K, channels)), struct((1, channels)), struct((1, H)), struct((1, H)), struct((1, H))),
        [VMEM],
    )(parts)
    return (grad_input[None], grad_dt.T[None], grad_weight, grad_bias[0], *(each[0] for each in small))


def solution(mesh):
    in_specs = (
        P("dp", "ctx", None),
        P(),
        P(),
        P("dp", "ctx", None),
        P(),
        P(),
        P(),
        P("dp", "ctx", None),
    )
    out_specs = (P("dp", "ctx", None), P("dp", "ctx", None), P(), P(), P(), P(), P())
    return jax.shard_map(
        on_device, mesh=mesh, in_specs=in_specs, out_specs=out_specs, check_vma=False
    )
```

```python
import functools

import jax
import jax.numpy as jnp
from jax import lax
from jax.experimental import pallas as pl
from jax.experimental.pallas import tpu as pltpu
from jax.sharding import PartitionSpec as P

H = 4
P_SIZE = 64
N = 128
K = 4
INNER = H * P_SIZE
HEAD_ROWS = 8
TAIL_ROWS = 16
HALO_ROWS = 16
END_ROWS = 16
LANE_BLOCKS = (INNER + 2 * N) // 128
SMALL_ROW = (K + 1) * LANE_BLOCKS
TOTAL_ROWS = 24

f32 = jnp.float32
bf16 = jnp.bfloat16

VMEM = pl.BlockSpec(memory_space=pltpu.VMEM)
HBM = pl.BlockSpec(memory_space=pltpu.HBM)


def dot(a, b, a_dim=1, b_dim=0):
    return lax.dot_general(a, b, (((a_dim,), (b_dim,)), ((), ())), preferred_element_type=f32)


def split2(x):
    high = x.astype(bf16)
    return high, (x - high.astype(f32)).astype(bf16)


def split3(x):
    high = x.astype(bf16).astype(f32)
    rest = x - high
    middle = rest.astype(bf16).astype(f32)
    return high, middle, rest - middle


def iota(shape, dim):
    return lax.broadcasted_iota(jnp.int32, shape, dim)


def stacked(rows):
    return jnp.concatenate([*split3(rows), jnp.zeros_like(rows)], 0).astype(bf16)


def unstacked(rows):
    return rows[0:8] + rows[8:16] + rows[16:24]


def head_selector(rows):
    shape = (rows, INNER)
    return jnp.where(iota(shape, 1) // P_SIZE == iota(shape, 0) % HEAD_ROWS, 1.0, 0.0).astype(bf16)


def over_channels(rows):
    return dot(stacked(rows), head_selector(4 * HEAD_ROWS), 0, 0)


def head_sums(x):
    high, low = split2(x)
    selector = head_selector(HEAD_ROWS * 2)
    return (dot(selector, high, 1, 1) + dot(selector, low, 1, 1))[:HEAD_ROWS]


def by_head(ref, width):
    row = iota((HEAD_ROWS, width), 0)
    out = jnp.zeros((HEAD_ROWS, width), f32)
    for h in range(H):
        out = jnp.where(row == h, ref[:, h : h + 1], out)
    return out


def shifted_down(x, first, count):
    moved = pltpu.roll(x, count, 0)
    top = jnp.where(iota(first.shape, 0) < count, pltpu.roll(first, count, 0), moved[:8])
    return jnp.concatenate([top, moved[8:]], 0)


def quantized_log(size):
    return jnp.log(jnp.maximum(size, 1e-30)).astype(bf16).astype(f32)


def scaled_columns(x):
    log_size = quantized_log(jnp.max(jnp.abs(x), axis=0, keepdims=True))
    return x * jnp.exp(-log_size), log_size


def write_messages(msg_refs, state, grad, log_total, place, radix):
    row = iota((TAIL_ROWS, INNER), 0)
    high, middle, low = split3(log_total)
    tail = jnp.where(row == 4, high, jnp.where(row == 5, middle * 256.0, jnp.where(row == 6, low * 65536.0, 0.0)))
    state, state_size = scaled_columns(state)
    grad, grad_size = scaled_columns(grad)
    if radix:
        for s, msg_ref in enumerate(msg_refs, 1):
            on = place + s < radix
            msg_ref[0:N] = jnp.where(on, state, grad)
            msg_ref[N : N + TAIL_ROWS] = jnp.where(row == 0, jnp.where(on, state_size, grad_size), tail)
    else:
        (msg_ref,) = msg_refs
        msg_ref[0:N] = state
        msg_ref[N : 2 * N] = grad
        msg_ref[2 * N : 2 * N + TAIL_ROWS] = jnp.where(row == 0, state_size, jnp.where(row == 1, grad_size, tail))


def message_log(got_ref):
    rows = got_ref.shape[0] - TAIL_ROWS
    tail = got_ref[rows : rows + 8]
    return tail[4:5] + tail[5:6] * (1 / 256.0) + tail[6:7] * (1 / 65536.0)


def message_block(got_ref, which=0):
    rows = got_ref.shape[0] - TAIL_ROWS
    return got_ref[which * N : (which + 1) * N] * jnp.exp(got_ref[rows + which : rows + which + 1])


def chained(blocks, logs, used):
    total, log_sum = 0.0, 0.0
    for block, log, use in zip(blocks, logs, used):
        total = total + jnp.where(use, jnp.exp(log_sum) * block, 0.0)
        log_sum = log_sum + jnp.where(use, log, 0.0)
    return total, log_sum


def pack_totals(x):
    row = iota(x.shape, 0)
    large = jnp.where(row < SMALL_ROW, x, 0.0)
    large_size = quantized_log(jnp.max(jnp.abs(large), axis=0, keepdims=True))
    small = x[SMALL_ROW : SMALL_ROW + 1]
    small_size = quantized_log(jnp.abs(small))
    small = small * jnp.exp(-small_size)
    small_high = small.astype(bf16).astype(f32)
    out = jnp.where(row == SMALL_ROW, small_high, large * jnp.exp(-large_size))
    out = jnp.where(row == SMALL_ROW + 3, (small - small_high) * 256.0, out)
    return jnp.where(row == SMALL_ROW + 1, large_size, jnp.where(row == SMALL_ROW + 2, small_size, out))


def triangle_kernel(until_ref):
    shape = until_ref.shape
    until_ref[...] = jnp.where(iota(shape, 0) <= iota(shape, 1), 1.0, 0.0).astype(bf16)


def start_kernel(
    stages, raw_ref, cot_ref, weight_ref, bias_ref, dt_ref, dt_bias_ref, alog_ref, skip_ref, until_ref,
    pre_ref, scaled_ref, tail_ref, rows_ref, logs_ref, places_ref, dt8_ref,
):
    tok = raw_ref.shape[0]
    place = lax.axis_index("ctx")
    for t, (size, radix) in enumerate(stages):
        places_ref[8 * t : 8 * t + 8] = jnp.full((8, INNER), lax.rem(lax.div(place, size), radix), jnp.int32).astype(f32)
    dt8_ref[...] = jnp.zeros_like(dt8_ref)
    dt8_ref[0:H] = dt_ref[...]
    dt_pre = dt8_ref[...] + by_head(dt_bias_ref, tok)
    step = jnp.maximum(dt_pre, 0.0) + jnp.log1p(jnp.exp(-jnp.abs(dt_pre)))
    real = iota((HEAD_ROWS, tok), 0) < H
    decay_rate = jnp.where(real, -jnp.exp(by_head(alog_ref, tok)), 0.0)
    cum = unstacked(dot(stacked(step * decay_rate), until_ref[...]))
    left = jnp.exp(cum[:, tok - 1 : tok] - cum)
    reach = jnp.exp(cum)
    rows_ref[0:8] = cum
    rows_ref[8:16] = step
    rows_ref[16:24] = left
    rows_ref[24:32] = reach
    rows_ref[32:40] = 1.0 / (1.0 + jnp.exp(-dt_pre))
    rows_ref[40:48] = decay_rate
    tail_ref[...] = over_channels(left * step)
    log_total = over_channels(cum)[tok - 1 : tok]
    skip = over_channels(by_head(skip_ref, HEAD_ROWS))[0:1]
    row = iota((8, INNER), 0)
    logs_ref[...] = jnp.where(row == 2, log_total, jnp.where(row == 3, skip, 0.0))
    scaled_ref[...] = jnp.concatenate(split2(cot_ref[...].astype(f32) * over_channels(reach)), 1)
    raw = raw_ref[...].astype(f32)
    zeros = jnp.zeros((8, raw.shape[1]), f32)
    pre = bias_ref[...] + weight_ref[K - 1 : K] * raw
    for back in range(1, K):
        pre = pre + weight_ref[K - 1 - back : K - back] * shifted_down(raw, zeros, back)
    pre_ref[...] = pre


def enter_kernel(
    radix, pre_ref, halo_ref, weight_ref, scaled_ref, tail_ref, logs_ref, places_ref,
    xbc_ref, slope_ref, weighted_ref, state_ref, grad_ref, *msg_refs
):
    tok = pre_ref.shape[0]
    halo = halo_ref[HALO_ROWS - 8 :].astype(f32)
    top = pre_ref[0:8]
    for back in range(1, K):
        tap = weight_ref[K - 1 - back : K - back]
        top = top + jnp.where(iota(top.shape, 0) < back, tap * pltpu.roll(halo, back, 0), 0.0)
    pre = jnp.concatenate([top, pre_ref[8:]], 0)
    gate = 1.0 / (1.0 + jnp.exp(-pre))
    xbc = (pre * gate).astype(bf16)
    xbc_ref[...] = xbc
    slope_ref[...] = gate * (1.0 + pre * (1.0 - gate))
    weighted = jnp.concatenate(split2(xbc[:, :INNER].astype(f32) * tail_ref[...]), 1)
    weighted_ref[...] = weighted
    state = dot(xbc[:, INNER : INNER + N], weighted, 0, 0)
    state = state[:, :INNER] + state[:, INNER:]
    grad = dot(xbc[:, INNER + N :], scaled_ref[...], 0, 0)
    grad = grad[:, :INNER] + grad[:, INNER:]
    state_ref[...] = state
    grad_ref[...] = grad
    write_messages(msg_refs, state, grad, logs_ref[2:3], places_ref[0:1], radix)


def merge_kernel(t, radix, next_radix, state_ref, grad_ref, logs_ref, places_ref, *refs):
    got, refs = refs[: radix - 1], refs[radix - 1 :]
    prior = after = 0.0
    if t > 0:
        prior, after = refs[0][...], refs[1][...]
        refs = refs[2:]
    logs_out, prior_out, after_out, *refs = refs
    if not next_radix:
        state_out, grad_out, *refs = refs
    place = places_ref[8 * t : 8 * t + 1]
    log_prior, log_after, log_total = logs_ref[0:1], logs_ref[1:2], logs_ref[2:3]
    states = [message_block(ref, 0) for ref in got]
    grads = [message_block(ref, 1) for ref in got]
    logs = [message_log(ref) for ref in got]
    earlier = [s <= place for s in range(1, radix)]
    later = [s > place for s in range(1, radix)]
    before, log_before = chained(states, logs, earlier)
    beyond, log_beyond = chained(grads[::-1], logs[::-1], later[::-1])
    above, _ = chained(states, logs, later)
    below, _ = chained(grads[::-1], logs[::-1], earlier[::-1])
    mine = jnp.exp(log_total)
    state = above + jnp.exp(log_beyond) * (state_ref[...] + mine * before)
    grad = below + jnp.exp(log_before) * (grad_ref[...] + mine * beyond)
    prior_out[...] = prior + jnp.exp(log_prior) * before
    after_out[...] = after + jnp.exp(log_after) * beyond
    log_prior = log_prior + log_before
    log_after = log_after + log_beyond
    log_total = log_total + log_before + log_beyond
    row = iota((8, INNER), 0)
    logs_out[...] = jnp.where(row == 0, log_prior, jnp.where(row == 1, log_after, jnp.where(row == 2, log_total, 0.0)))
    if not next_radix:
        state_out[...] = state
        grad_out[...] = grad
    write_messages(refs, state, grad, log_total, places_ref[8 * t + 8 : 8 * t + 9], next_radix)


def local_kernel(xbc_ref, cot_ref, rows_ref, logs_ref, local_ref, sums_ref):
    tok = xbc_ref.shape[0]
    cot = cot_ref[...]
    values = xbc_ref[:, :INNER]
    b_proj = xbc_ref[:, INNER : INNER + N]
    c_proj = xbc_ref[:, INNER + N :]
    cum, step = rows_ref[0:8], rows_ref[8:16]
    step_wide = over_channels(step)
    values_f = values.astype(f32)
    cot_f = cot.astype(f32)
    stepped = split2(values_f * step_wide)
    gram = dot(b_proj, c_proj, 1, 1)
    reached = iota((tok, tok), 0) <= iota((tok, tok), 1)
    pieces = stacked(cum)
    piece_head = iota((4 * HEAD_ROWS, tok), 0) % HEAD_ROWS
    dgram = jnp.zeros((tok, tok), f32)
    grads, sums = [], []
    for h in range(H):
        of = slice(h * P_SIZE, (h + 1) * P_SIZE)
        column = dot(pieces, jnp.where(piece_head == h, 1.0, 0.0).astype(bf16), 0, 0)
        within = jnp.exp(jnp.where(reached, cum[h : h + 1] - column, -1e30))
        cot_h = cot[:, of]
        high, low = split2(gram * within)
        grads.append(dot(high, cot_h) + dot(low, cot_h))
        dmix = dot(stepped[0][:, of], cot_h, 1, 1) + dot(stepped[1][:, of], cot_h, 1, 1)
        dmix = dmix * within
        dgram = dgram + dmix
        sums.append(jnp.sum(dmix * gram, axis=0, keepdims=True))
    grad_stepped = jnp.concatenate(grads, 1)
    local_ref[:, :INNER] = grad_stepped * step_wide + logs_ref[3:4] * cot_f
    high, low = split2(dgram)
    local_ref[:, INNER : INNER + N] = dot(high, c_proj) + dot(low, c_proj)
    local_ref[:, INNER + N :] = dot(high, b_proj, 0, 0) + dot(low, b_proj, 0, 0)
    row = iota((HEAD_ROWS, tok), 0)
    pairs = jnp.zeros((HEAD_ROWS, tok), f32)
    for h in range(H):
        pairs = jnp.where(row == h, sums[h], pairs)
    sums_ref[0:8] = pairs
    sums_ref[8:16] = head_sums(values_f * grad_stepped)
    sums_ref[16:24] = head_sums(values_f * cot_f)


def totals_kernel(
    t, radix, raw_ref, halo_ref, xbc_ref, slope_ref, scaled_ref, weighted_ref, tail_ref, rows_ref, local_ref, sums_ref,
    logs_ref, places_ref, until_ref, weight_ref, *refs
):
    got, refs = refs[: radix - 1], refs[radix - 1 :]
    prior = after = 0.0
    if t > 0:
        prior, after = refs[0][...], refs[1][...]
        refs = refs[2:]
    conv_ref, dt_out_ref, totals_ref, spill_ref, totals_scratch = refs
    tok = raw_ref.shape[0]
    place = places_ref[8 * t : 8 * t + 1]
    blocks = [message_block(ref) for ref in got]
    logs = [message_log(ref) for ref in got]
    before, _ = chained(blocks, logs, [s <= place for s in range(1, radix)])
    beyond, _ = chained(blocks[::-1], logs[::-1], [s > place for s in range(radix - 1, 0, -1)])
    prior = prior + jnp.exp(logs_ref[0:1]) * before
    after = after + jnp.exp(logs_ref[1:2]) * beyond

    step, left, reach = rows_ref[8:16], rows_ref[16:24], rows_ref[24:32]
    dt_gate, decay_rate = rows_ref[32:40], rows_ref[40:48]
    b_proj = xbc_ref[:, INNER : INNER + N]
    c_proj = xbc_ref[:, INNER + N :]
    prior2 = jnp.concatenate(split2(prior), 0)
    after2 = jnp.concatenate(split2(after), 0)
    seen = dot(jnp.concatenate([c_proj, c_proj], 1), prior2)
    back = dot(jnp.concatenate([b_proj, b_proj], 1), after2)
    grad_c = dot(scaled_ref[:, :INNER], prior2, 1, 1)
    grad_c = grad_c[:, :N] + grad_c[:, N:] + dot(scaled_ref[:, INNER:], prior2[:N], 1, 1)
    grad_b = dot(weighted_ref[:, :INNER], after2, 1, 1)
    grad_b = grad_b[:, :N] + grad_b[:, N:] + dot(weighted_ref[:, INNER:], after2[:N], 1, 1)
    grad_low = (local_ref[...] + jnp.concatenate([tail_ref[...] * back, grad_b, grad_c], 1)).astype(bf16)
    grad_conv = grad_low.astype(f32) * slope_ref[...]
    conv_ref[...] = grad_conv
    top = grad_conv[:8]
    spill = jnp.zeros_like(top)
    for ahead in range(1, K):
        tap = weight_ref[K - 1 - ahead : K - ahead]
        spill = spill + tap * jnp.where(iota(top.shape, 0) < 8 - ahead, 0.0, pltpu.roll(top, 8 - ahead, 0))
    spill_ref[...] = spill

    raw = raw_ref[...].astype(f32)
    halo = halo_ref[HALO_ROWS - 8 :].astype(f32)
    sums = [grad_conv * shifted_down(raw, halo, K - 1 - k) for k in range(K - 1)] + [grad_conv * raw, grad_conv]
    totals_scratch[...] = jnp.zeros_like(totals_scratch)
    for k, each in enumerate(sums):
        each = jnp.sum(each, axis=0, keepdims=True)
        for j in range(LANE_BLOCKS):
            at = k * LANE_BLOCKS + j
            totals_scratch[at : at + 1] = each[:, j * 128 : (j + 1) * 128]

    values = xbc_ref[:, :INNER].astype(f32)
    pairs, from_values, skip_rows = sums_ref[0:8], sums_ref[8:16], sums_ref[16:24]
    scaled_f = scaled_ref[:, :INNER].astype(f32) + scaled_ref[:, INNER:].astype(f32)
    seen_rows = head_sums(scaled_f * seen)
    tail_rows = head_sums(values * back)
    tail_term = tail_rows * left * step
    selector = head_selector(HEAD_ROWS * 2)[:HEAD_ROWS].astype(f32)
    through = jnp.sum(prior * after, axis=0, keepdims=True)
    through = jnp.sum(selector * through, axis=1, keepdims=True) * reach[:, tok - 1 : tok]
    last_extra = jnp.sum(tail_term, axis=1, keepdims=True) + through
    grad_cum = pairs - from_values * step + seen_rows - tail_term
    grad_log = unstacked(dot(stacked(grad_cum), until_ref[...], 1, 1)) + last_extra
    grad_step = from_values + tail_rows * left + decay_rate * grad_log
    grad_pre = grad_step * dt_gate
    dt_out_ref[...] = grad_pre[0:H]
    row, lane = iota((HEAD_ROWS, 128), 0), iota((HEAD_ROWS, 128), 1)
    small = jnp.zeros((HEAD_ROWS, 128), f32)
    for i, each in enumerate((grad_pre, grad_log * step * decay_rate, skip_rows)):
        column = jnp.sum(each, axis=1, keepdims=True)
        small = jnp.where((row < H) & (lane == row + i * H), column, small)
    totals_scratch[SMALL_ROW : SMALL_ROW + 1] = jnp.sum(small, axis=0, keepdims=True)
    totals_ref[...] = pack_totals(totals_scratch[...])


def input_kernel(conv_ref, weight_ref, out_hbm, end_ref, out_ref, sem):
    grad_conv = conv_ref[...]
    tok, channels = grad_conv.shape
    grad_in = weight_ref[K - 1 : K] * grad_conv
    row8 = iota((8, channels), 0)
    for ahead in range(1, K):
        tap = weight_ref[K - 1 - ahead : K - ahead]
        moved = pltpu.roll(grad_conv, tok - ahead, 0)
        last8 = moved[tok - 8 :]
        inside = row8 < 8 - ahead
        grad_in = grad_in + tap * jnp.concatenate([moved[: tok - 8], jnp.where(inside, last8, 0.0)], 0)
    out_ref[...] = grad_in.astype(bf16)
    copy = pltpu.make_async_copy(out_ref, out_hbm, sem)
    copy.start()
    end_ref[...] = grad_in[tok - END_ROWS :]
    copy.wait()


def end_kernel(end_ref, spilled_ref, main_hbm, out_hbm, rows_ref, sem):
    end = end_ref[...]
    fixed = end[END_ROWS - 8 :] + spilled_ref[...]
    rows_ref[...] = jnp.concatenate([end[: END_ROWS - 8], fixed], 0).astype(bf16)
    tok = out_hbm.shape[0]
    copy = pltpu.make_async_copy(rows_ref, out_hbm.at[pl.ds(tok - END_ROWS, END_ROWS)], sem)
    copy.start()
    copy.wait()


def summed(parts):
    large = jnp.sum(parts * jnp.exp(parts[:, SMALL_ROW + 1 : SMALL_ROW + 2]), axis=0)
    small = parts[:, SMALL_ROW : SMALL_ROW + 1] + parts[:, SMALL_ROW + 3 : SMALL_ROW + 4] * (1 / 256.0)
    small = small * jnp.exp(parts[:, SMALL_ROW + 2 : SMALL_ROW + 3])
    return large, jnp.sum(small, axis=0)


def repack_kernel(parts_ref, out_ref):
    large, small = summed(parts_ref[...])
    out_ref[...] = pack_totals(jnp.where(iota(large.shape, 0) == SMALL_ROW, small, large))


def finish_kernel(parts_ref, weight_ref, bias_ref, dt_bias_ref, alog_ref, skip_ref):
    large, small = summed(parts_ref[...])
    for k in range(K + 1):
        for j in range(LANE_BLOCKS):
            at = k * LANE_BLOCKS + j
            if k < K:
                weight_ref[k : k + 1, j * 128 : (j + 1) * 128] = large[at : at + 1]
            else:
                bias_ref[:, j * 128 : (j + 1) * 128] = large[at : at + 1]
    for i, ref in enumerate((dt_bias_ref, alog_ref, skip_ref)):
        ref[...] = small[:, i * H : (i + 1) * H]


def call(kernel, outs, in_specs, out_specs=None, scratch=(), flops=0, limit=16 << 20, aliases=None):
    return pl.pallas_call(
        kernel,
        out_shape=outs,
        in_specs=in_specs,
        out_specs=out_specs or jax.tree.map(lambda _: VMEM, outs),
        scratch_shapes=list(scratch),
        input_output_aliases=aliases or {},
        compiler_params=pltpu.CompilerParams(vmem_limit_bytes=limit),
        cost_estimate=pl.CostEstimate(flops=flops, bytes_accessed=1 << 20, transcendentals=0),
    )


def struct(shape, dtype=f32):
    return jax.ShapeDtypeStruct(shape, dtype)


def from_groups(messages, slabs, size, radix):
    got = []
    for s in range(1, radix):
        message = messages[s - 1 if len(messages) > 1 else 0]
        route = [(p, p - p % (size * radix) + (p + s * size) % (size * radix)) for p in range(slabs)]
        got.append(lax.ppermute(message.astype(jnp.float16), "ctx", route).astype(f32))
    return got


def stages_of(slabs):
    stages, size = [], 1
    while size < slabs:
        radix = 2 if (slabs // size).bit_length() % 2 == 0 else 4
        stages.append((size, radix))
        size *= radix
    assert size == slabs and stages
    return stages


def everyones(packed, axes, count):
    packed = jnp.broadcast_to(packed.astype(jnp.float16)[None], (count, *packed.shape))
    return lax.all_to_all(packed, axes, 0, 0).astype(f32)


def on_device(xbc_raw, conv_weight, conv_bias, dt_raw, dt_bias, a_log, d_skip, grad_out):
    tok, channels = xbc_raw.shape[1:]
    slabs = lax.axis_size("ctx")
    contexts = lax.axis_size("dp")
    stages = stages_of(slabs)

    raw, cot, dt_rows = xbc_raw[0], grad_out[0], dt_raw[0].T
    until = call(triangle_kernel, struct((tok, tok), bf16), [], flops=10**10)()
    early_raw, until = lax.optimization_barrier((raw, until))
    halo = lax.ppermute(early_raw[tok - HALO_ROWS :], "ctx", [(i, i + 1) for i in range(slabs - 1)])

    def last_radix(t):
        return stages[t][1] if t == len(stages) - 1 else 0

    def messages(t):
        if last_radix(t):
            return (struct((N + TAIL_ROWS, INNER)),) * (last_radix(t) - 1)
        return (struct((2 * N + TAIL_ROWS, INNER)),)

    state_like = struct((N, INNER))
    logs_like = struct((8, INNER))
    pre, scaled, tail, rows, logs, places = call(
        functools.partial(start_kernel, stages),
        (
            struct((tok, channels)), struct((tok, 2 * INNER), bf16), struct((tok, INNER)), struct((6 * HEAD_ROWS, tok)),
            logs_like, struct((8 * len(stages), INNER)),
        ),
        [VMEM] * 9,
        scratch=[pltpu.VMEM((HEAD_ROWS, tok), f32)],
        flops=100_000_000,
    )(raw, cot, conv_weight, conv_bias[None], dt_rows, dt_bias[None], a_log[None], d_skip[None], until)

    xbc, slope, weighted, state, grad, *outgoing = call(
        functools.partial(enter_kernel, last_radix(0)),
        (
            struct((tok, channels), bf16), struct((tok, channels)), struct((tok, 2 * INNER), bf16),
            state_like, state_like, *messages(0),
        ),
        [VMEM] * 7,
        flops=200_000_000,
    )(pre, halo, conv_weight, scaled, tail, logs, places)

    local, sums = call(
        local_kernel,
        (struct((tok, channels)), struct((3 * HEAD_ROWS, tok))),
        [VMEM] * 4,
        flops=1_000_000_000,
    )(xbc, cot, rows, logs)

    carried = ()
    for t, (size, radix) in enumerate(stages):
        got = from_groups(outgoing, slabs, size, radix)
        if t == 0:
            got, local, sums = lax.optimization_barrier((got, local, sums))
        if t == len(stages) - 1:
            break
        last = last_radix(t + 1)
        outs = (logs_like, state_like, state_like) + (() if last else (state_like, state_like))
        logs, *outgoing = call(
            functools.partial(merge_kernel, t, radix, last),
            outs + messages(t + 1),
            [VMEM] * (4 + len(got) + len(carried)),
            flops=1_000_000,
        )(state, grad, logs, places, *got, *carried)
        carried, outgoing = outgoing[:2], outgoing[2:]
        if not last:
            (state, grad), outgoing = outgoing[:2], outgoing[2:]

    grad_conv, grad_dt, packed, spill = call(
        functools.partial(totals_kernel, len(stages) - 1, radix),
        (struct((tok, channels)), struct((H, tok)), struct((TOTAL_ROWS, 128)), struct((8, channels))),
        [VMEM] * (14 + len(got) + len(carried)),
        scratch=[pltpu.VMEM((TOTAL_ROWS, 128), f32)],
        flops=200_000_000,
    )(raw, halo, xbc, slope, scaled, weighted, tail, rows, local, sums, logs, places, until, conv_weight, *got, *carried)

    spilled = lax.ppermute(spill, "ctx", [(i + 1, i) for i in range(slabs - 1)])
    if slabs * contexts <= 64:
        parts = everyones(packed, ("ctx", "dp"), slabs * contexts)
    else:
        packed = call(repack_kernel, struct((TOTAL_ROWS, 128)), [VMEM])(everyones(packed, "ctx", slabs))
        parts = everyones(packed, "dp", contexts)

    grad_main, end = call(
        input_kernel,
        (struct((tok, channels), bf16), struct((END_ROWS, channels))),
        [VMEM] * 2,
        (HBM, VMEM),
        [pltpu.VMEM((tok, channels), bf16), pltpu.SemaphoreType.DMA],
        flops=1_000_000,
    )(grad_conv, conv_weight)
    grad_input = call(
        end_kernel,
        struct((tok, channels), bf16),
        [VMEM] * 2 + [HBM],
        HBM,
        [pltpu.VMEM((END_ROWS, channels), bf16), pltpu.SemaphoreType.DMA],
        aliases={2: 0},
    )(end, spilled, grad_main)

    grad_weight, grad_bias, *small = call(
        finish_kernel,
        (struct((K, channels)), struct((1, channels)), struct((1, H)), struct((1, H)), struct((1, H))),
        [VMEM],
    )(parts)
    return (grad_input[None], grad_dt.T[None], grad_weight, grad_bias[0], *(each[0] for each in small))


def solution(mesh):
    in_specs = (
        P("dp", "ctx", None),
        P(),
        P(),
        P("dp", "ctx", None),
        P(),
        P(),
        P(),
        P("dp", "ctx", None),
    )
    out_specs = (P("dp", "ctx", None), P("dp", "ctx", None), P(), P(), P(), P(), P())
    return jax.shard_map(
        on_device, mesh=mesh, in_specs=in_specs, out_specs=out_specs, check_vma=False
    )
```

```python
import functools

import jax
import jax.numpy as jnp
from jax import lax
from jax.experimental import pallas as pl
from jax.experimental.pallas import tpu as pltpu
from jax.sharding import PartitionSpec as P

H = 4
P_SIZE = 64
N = 128
K = 4
INNER = H * P_SIZE
HEAD_ROWS = 8
TAIL_ROWS = 16
HALO_ROWS = 16
END_ROWS = 16
LANE_BLOCKS = (INNER + 2 * N) // 128
SMALL_ROW = (K + 1) * LANE_BLOCKS
TOTAL_ROWS = 24

f32 = jnp.float32
bf16 = jnp.bfloat16

VMEM = pl.BlockSpec(memory_space=pltpu.VMEM)
HBM = pl.BlockSpec(memory_space=pltpu.HBM)


def dot(a, b, a_dim=1, b_dim=0):
    return lax.dot_general(a, b, (((a_dim,), (b_dim,)), ((), ())), preferred_element_type=f32)


def split2(x):
    high = x.astype(bf16)
    return high, (x - high.astype(f32)).astype(bf16)


def split3(x):
    high = x.astype(bf16).astype(f32)
    rest = x - high
    middle = rest.astype(bf16).astype(f32)
    return high, middle, rest - middle


def iota(shape, dim):
    return lax.broadcasted_iota(jnp.int32, shape, dim)


def stacked(rows):
    return jnp.concatenate([*split3(rows), jnp.zeros_like(rows)], 0).astype(bf16)


def unstacked(rows):
    return rows[0:8] + rows[8:16] + rows[16:24]


def head_selector(rows):
    shape = (rows, INNER)
    return jnp.where(iota(shape, 1) // P_SIZE == iota(shape, 0) % HEAD_ROWS, 1.0, 0.0).astype(bf16)


def over_channels(rows):
    return dot(stacked(rows), head_selector(4 * HEAD_ROWS), 0, 0)


def head_sums(x):
    high, low = split2(x)
    selector = head_selector(HEAD_ROWS * 2)
    return (dot(selector, high, 1, 1) + dot(selector, low, 1, 1))[:HEAD_ROWS]


def by_head(ref, width):
    row = iota((HEAD_ROWS, width), 0)
    out = jnp.zeros((HEAD_ROWS, width), f32)
    for h in range(H):
        out = jnp.where(row == h, ref[:, h : h + 1], out)
    return out


def shifted_down(x, first, count):
    moved = pltpu.roll(x, count, 0)
    top = jnp.where(iota(first.shape, 0) < count, pltpu.roll(first, count, 0), moved[:8])
    return jnp.concatenate([top, moved[8:]], 0)


def quantized_log(size):
    return jnp.log(jnp.maximum(size, 1e-30)).astype(bf16).astype(f32)


def scaled_columns(x):
    log_size = quantized_log(jnp.max(jnp.abs(x), axis=0, keepdims=True))
    return x * jnp.exp(-log_size), log_size


def write_messages(msg_refs, state, grad, log_total, place, radix):
    row = iota((TAIL_ROWS, INNER), 0)
    high, middle, low = split3(log_total)
    tail = jnp.where(row == 4, high, jnp.where(row == 5, middle * 256.0, jnp.where(row == 6, low * 65536.0, 0.0)))
    state, state_size = scaled_columns(state)
    grad, grad_size = scaled_columns(grad)
    if radix:
        for s, msg_ref in enumerate(msg_refs, 1):
            on = place + s < radix
            msg_ref[0:N] = jnp.where(on, state, grad)
            msg_ref[N : N + TAIL_ROWS] = jnp.where(row == 0, jnp.where(on, state_size, grad_size), tail)
    else:
        (msg_ref,) = msg_refs
        msg_ref[0:N] = state
        msg_ref[N : 2 * N] = grad
        msg_ref[2 * N : 2 * N + TAIL_ROWS] = jnp.where(row == 0, state_size, jnp.where(row == 1, grad_size, tail))


def message_log(got_ref):
    rows = got_ref.shape[0] - TAIL_ROWS
    tail = got_ref[rows : rows + 8]
    return tail[4:5] + tail[5:6] * (1 / 256.0) + tail[6:7] * (1 / 65536.0)


def message_block(got_ref, which=0):
    rows = got_ref.shape[0] - TAIL_ROWS
    return got_ref[which * N : (which + 1) * N] * jnp.exp(got_ref[rows + which : rows + which + 1])


def chained(blocks, logs, used):
    total, log_sum = 0.0, 0.0
    for block, log, use in zip(blocks, logs, used):
        total = total + jnp.where(use, jnp.exp(log_sum) * block, 0.0)
        log_sum = log_sum + jnp.where(use, log, 0.0)
    return total, log_sum


def pack_totals(x):
    row = iota(x.shape, 0)
    large = jnp.where(row < SMALL_ROW, x, 0.0)
    large_size = quantized_log(jnp.max(jnp.abs(large), axis=0, keepdims=True))
    small = x[SMALL_ROW : SMALL_ROW + 1]
    small_size = quantized_log(jnp.abs(small))
    small = small * jnp.exp(-small_size)
    small_high = small.astype(bf16).astype(f32)
    out = jnp.where(row == SMALL_ROW, small_high, large * jnp.exp(-large_size))
    out = jnp.where(row == SMALL_ROW + 3, (small - small_high) * 256.0, out)
    return jnp.where(row == SMALL_ROW + 1, large_size, jnp.where(row == SMALL_ROW + 2, small_size, out))


def triangle_kernel(until_ref):
    shape = until_ref.shape
    until_ref[...] = jnp.where(iota(shape, 0) <= iota(shape, 1), 1.0, 0.0).astype(bf16)


def start_kernel(
    stages, raw_ref, cot_ref, weight_ref, bias_ref, dt_ref, dt_bias_ref, alog_ref, skip_ref, until_ref,
    pre_ref, scaled_ref, tail_ref, rows_ref, logs_ref, places_ref, dt8_ref,
):
    tok = raw_ref.shape[0]
    place = lax.axis_index("ctx")
    for t, (size, radix) in enumerate(stages):
        places_ref[8 * t : 8 * t + 8] = jnp.full((8, INNER), lax.rem(lax.div(place, size), radix), jnp.int32).astype(f32)
    at = 8 * len(stages)
    slabs = stages[-1][0] * stages[-1][1]
    places_ref[at : at + 8] = jnp.full((8, INNER), jnp.where(place == 0, 1, 0), jnp.int32).astype(f32)
    places_ref[at + 8 : at + 16] = jnp.full((8, INNER), jnp.where(place == slabs - 1, 1, 0), jnp.int32).astype(f32)
    dt8_ref[...] = jnp.zeros_like(dt8_ref)
    dt8_ref[0:H] = dt_ref[...]
    dt_pre = dt8_ref[...] + by_head(dt_bias_ref, tok)
    step = jnp.maximum(dt_pre, 0.0) + jnp.log1p(jnp.exp(-jnp.abs(dt_pre)))
    real = iota((HEAD_ROWS, tok), 0) < H
    decay_rate = jnp.where(real, -jnp.exp(by_head(alog_ref, tok)), 0.0)
    cum = unstacked(dot(stacked(step * decay_rate), until_ref[...]))
    left = jnp.exp(cum[:, tok - 1 : tok] - cum)
    reach = jnp.exp(cum)
    rows_ref[0:8] = cum
    rows_ref[8:16] = step
    rows_ref[16:24] = left
    rows_ref[24:32] = reach
    rows_ref[32:40] = 1.0 / (1.0 + jnp.exp(-dt_pre))
    rows_ref[40:48] = decay_rate
    tail_ref[...] = over_channels(left * step)
    log_total = over_channels(cum)[tok - 1 : tok]
    skip = over_channels(by_head(skip_ref, HEAD_ROWS))[0:1]
    row = iota((8, INNER), 0)
    logs_ref[...] = jnp.where(row == 2, log_total, jnp.where(row == 3, skip, 0.0))
    scaled_ref[...] = jnp.concatenate(split2(cot_ref[...].astype(f32) * over_channels(reach)), 1)
    raw = raw_ref[...].astype(f32)
    zeros = jnp.zeros((8, raw.shape[1]), f32)
    pre = bias_ref[...] + weight_ref[K - 1 : K] * raw
    for back in range(1, K):
        pre = pre + weight_ref[K - 1 - back : K - back] * shifted_down(raw, zeros, back)
    pre_ref[...] = pre


def real_halo(halo_ref, places_ref):
    first = places_ref[places_ref.shape[0] - 16 :][:1, :1]
    return jnp.where(first > 0.5, 0.0, halo_ref[HALO_ROWS - 8 :].astype(f32))


def enter_kernel(
    radix, pre_ref, halo_ref, weight_ref, scaled_ref, tail_ref, logs_ref, places_ref,
    xbc_ref, slope_ref, weighted_ref, state_ref, grad_ref, *msg_refs
):
    tok = pre_ref.shape[0]
    halo = real_halo(halo_ref, places_ref)
    top = pre_ref[0:8]
    for back in range(1, K):
        tap = weight_ref[K - 1 - back : K - back]
        top = top + jnp.where(iota(top.shape, 0) < back, tap * pltpu.roll(halo, back, 0), 0.0)
    pre = jnp.concatenate([top, pre_ref[8:]], 0)
    gate = 1.0 / (1.0 + jnp.exp(-pre))
    xbc = (pre * gate).astype(bf16)
    xbc_ref[...] = xbc
    slope_ref[...] = gate * (1.0 + pre * (1.0 - gate))
    weighted = jnp.concatenate(split2(xbc[:, :INNER].astype(f32) * tail_ref[...]), 1)
    weighted_ref[...] = weighted
    state = dot(xbc[:, INNER : INNER + N], weighted, 0, 0)
    state = state[:, :INNER] + state[:, INNER:]
    grad = dot(xbc[:, INNER + N :], scaled_ref[...], 0, 0)
    grad = grad[:, :INNER] + grad[:, INNER:]
    state_ref[...] = state
    grad_ref[...] = grad
    write_messages(msg_refs, state, grad, logs_ref[2:3], places_ref[0:1], radix)


def merge_kernel(t, radix, next_radix, state_ref, grad_ref, logs_ref, places_ref, *refs):
    got, refs = refs[: radix - 1], refs[radix - 1 :]
    prior = after = 0.0
    if t > 0:
        prior, after = refs[0][...], refs[1][...]
        refs = refs[2:]
    logs_out, prior_out, after_out, *refs = refs
    if not next_radix:
        state_out, grad_out, *refs = refs
    place = places_ref[8 * t : 8 * t + 1]
    log_prior, log_after, log_total = logs_ref[0:1], logs_ref[1:2], logs_ref[2:3]
    states = [message_block(ref, 0) for ref in got]
    grads = [message_block(ref, 1) for ref in got]
    logs = [message_log(ref) for ref in got]
    earlier = [s <= place for s in range(1, radix)]
    later = [s > place for s in range(1, radix)]
    before, log_before = chained(states, logs, earlier)
    beyond, log_beyond = chained(grads[::-1], logs[::-1], later[::-1])
    above, _ = chained(states, logs, later)
    below, _ = chained(grads[::-1], logs[::-1], earlier[::-1])
    mine = jnp.exp(log_total)
    state = above + jnp.exp(log_beyond) * (state_ref[...] + mine * before)
    grad = below + jnp.exp(log_before) * (grad_ref[...] + mine * beyond)
    prior_out[...] = prior + jnp.exp(log_prior) * before
    after_out[...] = after + jnp.exp(log_after) * beyond
    log_prior = log_prior + log_before
    log_after = log_after + log_beyond
    log_total = log_total + log_before + log_beyond
    row = iota((8, INNER), 0)
    logs_out[...] = jnp.where(row == 0, log_prior, jnp.where(row == 1, log_after, jnp.where(row == 2, log_total, 0.0)))
    if not next_radix:
        state_out[...] = state
        grad_out[...] = grad
    write_messages(refs, state, grad, log_total, places_ref[8 * t + 8 : 8 * t + 9], next_radix)


def local_kernel(xbc_ref, cot_ref, rows_ref, logs_ref, local_ref, sums_ref):
    tok = xbc_ref.shape[0]
    cot = cot_ref[...]
    values = xbc_ref[:, :INNER]
    b_proj = xbc_ref[:, INNER : INNER + N]
    c_proj = xbc_ref[:, INNER + N :]
    cum, step = rows_ref[0:8], rows_ref[8:16]
    step_wide = over_channels(step)
    values_f = values.astype(f32)
    cot_f = cot.astype(f32)
    stepped = split2(values_f * step_wide)
    gram = dot(b_proj, c_proj, 1, 1)
    reached = iota((tok, tok), 0) <= iota((tok, tok), 1)
    pieces = stacked(cum)
    piece_head = iota((4 * HEAD_ROWS, tok), 0) % HEAD_ROWS
    dgram = jnp.zeros((tok, tok), f32)
    grads, sums = [], []
    for h in range(H):
        of = slice(h * P_SIZE, (h + 1) * P_SIZE)
        column = dot(pieces, jnp.where(piece_head == h, 1.0, 0.0).astype(bf16), 0, 0)
        within = jnp.exp(jnp.where(reached, cum[h : h + 1] - column, -1e30))
        cot_h = cot[:, of]
        high, low = split2(gram * within)
        grads.append(dot(high, cot_h) + dot(low, cot_h))
        dmix = dot(stepped[0][:, of], cot_h, 1, 1) + dot(stepped[1][:, of], cot_h, 1, 1)
        dmix = dmix * within
        dgram = dgram + dmix
        sums.append(jnp.sum(dmix * gram, axis=0, keepdims=True))
    grad_stepped = jnp.concatenate(grads, 1)
    local_ref[:, :INNER] = grad_stepped * step_wide + logs_ref[3:4] * cot_f
    high, low = split2(dgram)
    local_ref[:, INNER : INNER + N] = dot(high, c_proj) + dot(low, c_proj)
    local_ref[:, INNER + N :] = dot(high, b_proj, 0, 0) + dot(low, b_proj, 0, 0)
    row = iota((HEAD_ROWS, tok), 0)
    pairs = jnp.zeros((HEAD_ROWS, tok), f32)
    for h in range(H):
        pairs = jnp.where(row == h, sums[h], pairs)
    sums_ref[0:8] = pairs
    sums_ref[8:16] = head_sums(values_f * grad_stepped)
    sums_ref[16:24] = head_sums(values_f * cot_f)


def totals_kernel(
    t, radix, raw_ref, halo_ref, xbc_ref, slope_ref, scaled_ref, weighted_ref, tail_ref, rows_ref, local_ref, sums_ref,
    logs_ref, places_ref, until_ref, weight_ref, *refs
):
    got, refs = refs[: radix - 1], refs[radix - 1 :]
    prior = after = 0.0
    if t > 0:
        prior, after = refs[0][...], refs[1][...]
        refs = refs[2:]
    conv_ref, dt_out_ref, totals_ref, spill_ref, totals_scratch = refs
    tok = raw_ref.shape[0]
    place = places_ref[8 * t : 8 * t + 1]
    blocks = [message_block(ref) for ref in got]
    logs = [message_log(ref) for ref in got]
    before, _ = chained(blocks, logs, [s <= place for s in range(1, radix)])
    beyond, _ = chained(blocks[::-1], logs[::-1], [s > place for s in range(radix - 1, 0, -1)])
    prior = prior + jnp.exp(logs_ref[0:1]) * before
    after = after + jnp.exp(logs_ref[1:2]) * beyond

    step, left, reach = rows_ref[8:16], rows_ref[16:24], rows_ref[24:32]
    dt_gate, decay_rate = rows_ref[32:40], rows_ref[40:48]
    b_proj = xbc_ref[:, INNER : INNER + N]
    c_proj = xbc_ref[:, INNER + N :]
    prior2 = jnp.concatenate(split2(prior), 0)
    after2 = jnp.concatenate(split2(after), 0)
    seen = dot(jnp.concatenate([c_proj, c_proj], 1), prior2)
    back = dot(jnp.concatenate([b_proj, b_proj], 1), after2)
    grad_c = dot(scaled_ref[:, :INNER], prior2, 1, 1)
    grad_c = grad_c[:, :N] + grad_c[:, N:] + dot(scaled_ref[:, INNER:], prior2[:N], 1, 1)
    grad_b = dot(weighted_ref[:, :INNER], after2, 1, 1)
    grad_b = grad_b[:, :N] + grad_b[:, N:] + dot(weighted_ref[:, INNER:], after2[:N], 1, 1)
    grad_low = (local_ref[...] + jnp.concatenate([tail_ref[...] * back, grad_b, grad_c], 1)).astype(bf16)
    grad_conv = grad_low.astype(f32) * slope_ref[...]
    conv_ref[...] = grad_conv
    top = grad_conv[:8]
    spill = jnp.zeros_like(top)
    for ahead in range(1, K):
        tap = weight_ref[K - 1 - ahead : K - ahead]
        spill = spill + tap * jnp.where(iota(top.shape, 0) < 8 - ahead, 0.0, pltpu.roll(top, 8 - ahead, 0))
    spill_ref[...] = spill

    raw = raw_ref[...].astype(f32)
    halo = real_halo(halo_ref, places_ref)
    sums = [grad_conv * shifted_down(raw, halo, K - 1 - k) for k in range(K - 1)] + [grad_conv * raw, grad_conv]
    totals_scratch[...] = jnp.zeros_like(totals_scratch)
    for k, each in enumerate(sums):
        each = jnp.sum(each, axis=0, keepdims=True)
        for j in range(LANE_BLOCKS):
            at = k * LANE_BLOCKS + j
            totals_scratch[at : at + 1] = each[:, j * 128 : (j + 1) * 128]

    values = xbc_ref[:, :INNER].astype(f32)
    pairs, from_values, skip_rows = sums_ref[0:8], sums_ref[8:16], sums_ref[16:24]
    scaled_f = scaled_ref[:, :INNER].astype(f32) + scaled_ref[:, INNER:].astype(f32)
    seen_rows = head_sums(scaled_f * seen)
    tail_rows = head_sums(values * back)
    tail_term = tail_rows * left * step
    selector = head_selector(HEAD_ROWS * 2)[:HEAD_ROWS].astype(f32)
    through = jnp.sum(prior * after, axis=0, keepdims=True)
    through = jnp.sum(selector * through, axis=1, keepdims=True) * reach[:, tok - 1 : tok]
    last_extra = jnp.sum(tail_term, axis=1, keepdims=True) + through
    grad_cum = pairs - from_values * step + seen_rows - tail_term
    grad_log = unstacked(dot(stacked(grad_cum), until_ref[...], 1, 1)) + last_extra
    grad_step = from_values + tail_rows * left + decay_rate * grad_log
    grad_pre = grad_step * dt_gate
    dt_out_ref[...] = grad_pre[0:H]
    row, lane = iota((HEAD_ROWS, 128), 0), iota((HEAD_ROWS, 128), 1)
    small = jnp.zeros((HEAD_ROWS, 128), f32)
    for i, each in enumerate((grad_pre, grad_log * step * decay_rate, skip_rows)):
        column = jnp.sum(each, axis=1, keepdims=True)
        small = jnp.where((row < H) & (lane == row + i * H), column, small)
    totals_scratch[SMALL_ROW : SMALL_ROW + 1] = jnp.sum(small, axis=0, keepdims=True)
    totals_ref[...] = pack_totals(totals_scratch[...])


def input_kernel(conv_ref, weight_ref, out_hbm, end_ref, out_ref, sem):
    grad_conv = conv_ref[...]
    tok, channels = grad_conv.shape
    grad_in = weight_ref[K - 1 : K] * grad_conv
    row8 = iota((8, channels), 0)
    for ahead in range(1, K):
        tap = weight_ref[K - 1 - ahead : K - ahead]
        moved = pltpu.roll(grad_conv, tok - ahead, 0)
        last8 = moved[tok - 8 :]
        inside = row8 < 8 - ahead
        grad_in = grad_in + tap * jnp.concatenate([moved[: tok - 8], jnp.where(inside, last8, 0.0)], 0)
    out_ref[...] = grad_in.astype(bf16)
    copy = pltpu.make_async_copy(out_ref, out_hbm, sem)
    copy.start()
    end_ref[...] = grad_in[tok - END_ROWS :]
    copy.wait()


def end_kernel(end_ref, spilled_ref, places_ref, main_hbm, out_hbm, rows_ref, sem):
    end = end_ref[...]
    last = places_ref[places_ref.shape[0] - 8 :][:1, :1]
    fixed = end[END_ROWS - 8 :] + jnp.where(last > 0.5, 0.0, spilled_ref[...])
    rows_ref[...] = jnp.concatenate([end[: END_ROWS - 8], fixed], 0).astype(bf16)
    tok = out_hbm.shape[0]
    copy = pltpu.make_async_copy(rows_ref, out_hbm.at[pl.ds(tok - END_ROWS, END_ROWS)], sem)
    copy.start()
    copy.wait()


def summed(parts):
    large = jnp.sum(parts * jnp.exp(parts[:, SMALL_ROW + 1 : SMALL_ROW + 2]), axis=0)
    small = parts[:, SMALL_ROW : SMALL_ROW + 1] + parts[:, SMALL_ROW + 3 : SMALL_ROW + 4] * (1 / 256.0)
    small = small * jnp.exp(parts[:, SMALL_ROW + 2 : SMALL_ROW + 3])
    return large, jnp.sum(small, axis=0)


def repack_kernel(parts_ref, out_ref):
    large, small = summed(parts_ref[...])
    out_ref[...] = pack_totals(jnp.where(iota(large.shape, 0) == SMALL_ROW, small, large))


def finish_kernel(parts_ref, weight_ref, bias_ref, dt_bias_ref, alog_ref, skip_ref):
    large, small = summed(parts_ref[...])
    for k in range(K + 1):
        for j in range(LANE_BLOCKS):
            at = k * LANE_BLOCKS + j
            if k < K:
                weight_ref[k : k + 1, j * 128 : (j + 1) * 128] = large[at : at + 1]
            else:
                bias_ref[:, j * 128 : (j + 1) * 128] = large[at : at + 1]
    for i, ref in enumerate((dt_bias_ref, alog_ref, skip_ref)):
        ref[...] = small[:, i * H : (i + 1) * H]


def call(kernel, outs, in_specs, out_specs=None, scratch=(), flops=0, limit=16 << 20, aliases=None):
    return pl.pallas_call(
        kernel,
        out_shape=outs,
        in_specs=in_specs,
        out_specs=out_specs or jax.tree.map(lambda _: VMEM, outs),
        scratch_shapes=list(scratch),
        input_output_aliases=aliases or {},
        compiler_params=pltpu.CompilerParams(vmem_limit_bytes=limit),
        cost_estimate=pl.CostEstimate(flops=flops, bytes_accessed=1 << 20, transcendentals=0),
    )


def struct(shape, dtype=f32):
    return jax.ShapeDtypeStruct(shape, dtype)


def from_groups(messages, slabs, size, radix):
    got = []
    for s in range(1, radix):
        message = messages[s - 1 if len(messages) > 1 else 0]
        route = [(p, p - p % (size * radix) + (p + s * size) % (size * radix)) for p in range(slabs)]
        got.append(lax.ppermute(message.astype(jnp.float16), "ctx", route).astype(f32))
    return got


def stages_of(slabs):
    stages, size = [], 1
    while size < slabs:
        radix = 2 if (slabs // size).bit_length() % 2 == 0 else 4
        stages.append((size, radix))
        size *= radix
    assert size == slabs and stages
    return stages


def everyones(packed, axes, count):
    packed = jnp.broadcast_to(packed.astype(jnp.float16)[None], (count, *packed.shape))
    return lax.all_to_all(packed, axes, 0, 0).astype(f32)


def on_device(xbc_raw, conv_weight, conv_bias, dt_raw, dt_bias, a_log, d_skip, grad_out):
    tok, channels = xbc_raw.shape[1:]
    slabs = lax.axis_size("ctx")
    contexts = lax.axis_size("dp")
    stages = stages_of(slabs)

    raw, cot, dt_rows = xbc_raw[0], grad_out[0], dt_raw[0].T
    until = call(triangle_kernel, struct((tok, tok), bf16), [], flops=10**10)()
    early_raw, until = lax.optimization_barrier((raw, until))
    halo = lax.ppermute(early_raw[tok - HALO_ROWS :], "ctx", [(i, (i + 1) % slabs) for i in range(slabs)])

    def last_radix(t):
        return stages[t][1] if t == len(stages) - 1 else 0

    def messages(t):
        if last_radix(t):
            return (struct((N + TAIL_ROWS, INNER)),) * (last_radix(t) - 1)
        return (struct((2 * N + TAIL_ROWS, INNER)),)

    state_like = struct((N, INNER))
    logs_like = struct((8, INNER))
    pre, scaled, tail, rows, logs, places = call(
        functools.partial(start_kernel, stages),
        (
            struct((tok, channels)), struct((tok, 2 * INNER), bf16), struct((tok, INNER)), struct((6 * HEAD_ROWS, tok)),
            logs_like, struct((8 * len(stages) + 16, INNER)),
        ),
        [VMEM] * 9,
        scratch=[pltpu.VMEM((HEAD_ROWS, tok), f32)],
        flops=100_000_000,
    )(raw, cot, conv_weight, conv_bias[None], dt_rows, dt_bias[None], a_log[None], d_skip[None], until)

    xbc, slope, weighted, state, grad, *outgoing = call(
        functools.partial(enter_kernel, last_radix(0)),
        (
            struct((tok, channels), bf16), struct((tok, channels)), struct((tok, 2 * INNER), bf16),
            state_like, state_like, *messages(0),
        ),
        [VMEM] * 7,
        flops=200_000_000,
    )(pre, halo, conv_weight, scaled, tail, logs, places)

    local, sums = call(
        local_kernel,
        (struct((tok, channels)), struct((3 * HEAD_ROWS, tok))),
        [VMEM] * 4,
        flops=1_000_000_000,
    )(xbc, cot, rows, logs)

    carried = ()
    for t, (size, radix) in enumerate(stages):
        got = from_groups(outgoing, slabs, size, radix)
        if t == 0:
            got, local, sums = lax.optimization_barrier((got, local, sums))
        if t == len(stages) - 1:
            break
        last = last_radix(t + 1)
        outs = (logs_like, state_like, state_like) + (() if last else (state_like, state_like))
        logs, *outgoing = call(
            functools.partial(merge_kernel, t, radix, last),
            outs + messages(t + 1),
            [VMEM] * (4 + len(got) + len(carried)),
            flops=1_000_000,
        )(state, grad, logs, places, *got, *carried)
        carried, outgoing = outgoing[:2], outgoing[2:]
        if not last:
            (state, grad), outgoing = outgoing[:2], outgoing[2:]

    grad_conv, grad_dt, packed, spill = call(
        functools.partial(totals_kernel, len(stages) - 1, radix),
        (struct((tok, channels)), struct((H, tok)), struct((TOTAL_ROWS, 128)), struct((8, channels))),
        [VMEM] * (14 + len(got) + len(carried)),
        scratch=[pltpu.VMEM((TOTAL_ROWS, 128), f32)],
        flops=200_000_000,
    )(raw, halo, xbc, slope, scaled, weighted, tail, rows, local, sums, logs, places, until, conv_weight, *got, *carried)

    spilled = lax.ppermute(spill, "ctx", [((i + 1) % slabs, i) for i in range(slabs)])
    if slabs * contexts <= 64:
        parts = everyones(packed, ("ctx", "dp"), slabs * contexts)
    else:
        packed = call(repack_kernel, struct((TOTAL_ROWS, 128)), [VMEM])(everyones(packed, "ctx", slabs))
        parts = everyones(packed, "dp", contexts)

    grad_main, end = call(
        input_kernel,
        (struct((tok, channels), bf16), struct((END_ROWS, channels))),
        [VMEM] * 2,
        (HBM, VMEM),
        [pltpu.VMEM((tok, channels), bf16), pltpu.SemaphoreType.DMA],
        flops=1_000_000,
    )(grad_conv, conv_weight)
    grad_input = call(
        end_kernel,
        struct((tok, channels), bf16),
        [VMEM] * 3 + [HBM],
        HBM,
        [pltpu.VMEM((END_ROWS, channels), bf16), pltpu.SemaphoreType.DMA],
        aliases={3: 0},
    )(end, spilled, places, grad_main)

    grad_weight, grad_bias, *small = call(
        finish_kernel,
        (struct((K, channels)), struct((1, channels)), struct((1, H)), struct((1, H)), struct((1, H))),
        [VMEM],
    )(parts)
    return (grad_input[None], grad_dt.T[None], grad_weight, grad_bias[0], *(each[0] for each in small))


def solution(mesh):
    in_specs = (
        P("dp", "ctx", None),
        P(),
        P(),
        P("dp", "ctx", None),
        P(),
        P(),
        P(),
        P("dp", "ctx", None),
    )
    out_specs = (P("dp", "ctx", None), P("dp", "ctx", None), P(), P(), P(), P(), P())
    return jax.shard_map(
        on_device, mesh=mesh, in_specs=in_specs, out_specs=out_specs, check_vma=False
    )
```

```python
import functools

import jax
import jax.numpy as jnp
from jax import lax
from jax.experimental import pallas as pl
from jax.experimental.pallas import tpu as pltpu
from jax.sharding import PartitionSpec as P

H = 4
P_SIZE = 64
N = 128
K = 4
INNER = H * P_SIZE
HEAD_ROWS = 8
TAIL_ROWS = 16
HALO_ROWS = 16
FIX_ROWS = 16
END_ROWS = 16
LANE_BLOCKS = (INNER + 2 * N) // 128
SMALL_ROW = (K + 1) * LANE_BLOCKS
TOTAL_ROWS = 24

f32 = jnp.float32
bf16 = jnp.bfloat16

VMEM = pl.BlockSpec(memory_space=pltpu.VMEM)
HBM = pl.BlockSpec(memory_space=pltpu.HBM)


def dot(a, b, a_dim=1, b_dim=0):
    return lax.dot_general(a, b, (((a_dim,), (b_dim,)), ((), ())), preferred_element_type=f32)


def split2(x):
    high = x.astype(bf16)
    return high, (x - high.astype(f32)).astype(bf16)


def split3(x):
    high = x.astype(bf16).astype(f32)
    rest = x - high
    middle = rest.astype(bf16).astype(f32)
    return high, middle, rest - middle


def iota(shape, dim):
    return lax.broadcasted_iota(jnp.int32, shape, dim)


def stacked(rows):
    return jnp.concatenate([*split3(rows), jnp.zeros_like(rows)], 0).astype(bf16)


def unstacked(rows):
    return rows[0:8] + rows[8:16] + rows[16:24]


def head_selector(rows):
    shape = (rows, INNER)
    return jnp.where(iota(shape, 1) // P_SIZE == iota(shape, 0) % HEAD_ROWS, 1.0, 0.0).astype(bf16)


def over_channels(rows):
    return dot(stacked(rows), head_selector(4 * HEAD_ROWS), 0, 0)


def head_sums(x):
    high, low = split2(x)
    selector = head_selector(HEAD_ROWS * 2)
    return (dot(selector, high, 1, 1) + dot(selector, low, 1, 1))[:HEAD_ROWS]


def by_head(ref, width):
    row = iota((HEAD_ROWS, width), 0)
    out = jnp.zeros((HEAD_ROWS, width), f32)
    for h in range(H):
        out = jnp.where(row == h, ref[:, h : h + 1], out)
    return out


def shifted_down(x, first, count):
    moved = pltpu.roll(x, count, 0)
    top = jnp.where(iota(first.shape, 0) < count, pltpu.roll(first, count, 0), moved[:8])
    return jnp.concatenate([top, moved[8:]], 0)


def quantized_log(size):
    return jnp.log(jnp.maximum(size, 1e-30)).astype(bf16).astype(f32)


def scaled_columns(x):
    log_size = quantized_log(jnp.max(jnp.abs(x), axis=0, keepdims=True))
    return x * jnp.exp(-log_size), log_size


def write_messages(msg_refs, state, grad, log_total, place, radix):
    row = iota((TAIL_ROWS, INNER), 0)
    high, middle, low = split3(log_total)
    tail = jnp.where(row == 4, high, jnp.where(row == 5, middle * 256.0, jnp.where(row == 6, low * 65536.0, 0.0)))
    state, state_size = scaled_columns(state)
    grad, grad_size = scaled_columns(grad)
    if radix:
        for s, msg_ref in enumerate(msg_refs, 1):
            on = place + s < radix
            msg_ref[0:N] = jnp.where(on, state, grad)
            msg_ref[N : N + TAIL_ROWS] = jnp.where(row == 0, jnp.where(on, state_size, grad_size), tail)
    else:
        (msg_ref,) = msg_refs
        msg_ref[0:N] = state
        msg_ref[N : 2 * N] = grad
        msg_ref[2 * N : 2 * N + TAIL_ROWS] = jnp.where(row == 0, state_size, jnp.where(row == 1, grad_size, tail))


def message_log(got_ref):
    rows = got_ref.shape[0] - TAIL_ROWS
    tail = got_ref[rows : rows + 8]
    return tail[4:5] + tail[5:6] * (1 / 256.0) + tail[6:7] * (1 / 65536.0)


def message_block(got_ref, which=0):
    rows = got_ref.shape[0] - TAIL_ROWS
    return got_ref[which * N : (which + 1) * N] * jnp.exp(got_ref[rows + which : rows + which + 1])


def chained(blocks, logs, used):
    total, log_sum = 0.0, 0.0
    for block, log, use in zip(blocks, logs, used):
        total = total + jnp.where(use, jnp.exp(log_sum) * block, 0.0)
        log_sum = log_sum + jnp.where(use, log, 0.0)
    return total, log_sum


def pack_totals(x):
    row = iota(x.shape, 0)
    large = jnp.where(row < SMALL_ROW, x, 0.0)
    large_size = quantized_log(jnp.max(jnp.abs(large), axis=0, keepdims=True))
    small = x[SMALL_ROW : SMALL_ROW + 1]
    small_size = quantized_log(jnp.abs(small))
    small = small * jnp.exp(-small_size)
    small_high = small.astype(bf16).astype(f32)
    out = jnp.where(row == SMALL_ROW, small_high, large * jnp.exp(-large_size))
    out = jnp.where(row == SMALL_ROW + 3, (small - small_high) * 256.0, out)
    return jnp.where(row == SMALL_ROW + 1, large_size, jnp.where(row == SMALL_ROW + 2, small_size, out))


def triangle_kernel(until_ref):
    shape = until_ref.shape
    until_ref[...] = jnp.where(iota(shape, 0) <= iota(shape, 1), 1.0, 0.0).astype(bf16)


def heads_kernel(bias_ref, dt_bias_ref, alog_ref, skip_ref, until_in, until_ref, bias_out, heads_ref):
    bias_out[...] = bias_ref[...]
    for i, ref in enumerate((dt_bias_ref, alog_ref, skip_ref)):
        heads_ref[8 * i : 8 * i + 8] = by_head(ref, until_ref.shape[1])


def mask_first(x):
    top = jnp.where(iota((FIX_ROWS, x.shape[1]), 0) < K - 1, 0.0, x[:FIX_ROWS].astype(f32))
    return jnp.concatenate([top.astype(x.dtype), x[FIX_ROWS:]], 0)


def start_kernel(
    stages, raw_ref, cot_ref, weight_ref, bias_ref, dt_ref, heads_ref, until_ref,
    top_ref, xbc_ref, slope_ref, weighted_ref, scaled_ref, tail_ref, rows_ref, logs_ref, places_ref, state_ref, grad_ref, msg_ref, dt8_ref,
):
    tok = raw_ref.shape[0]
    place = lax.axis_index("ctx")
    for t, (size, radix) in enumerate(stages):
        places_ref[8 * t : 8 * t + 8] = jnp.full((8, INNER), lax.rem(lax.div(place, size), radix), jnp.int32).astype(f32)
    at = 8 * len(stages)
    slabs = stages[-1][0] * stages[-1][1]
    places_ref[at : at + 8] = jnp.full((8, INNER), jnp.where(place == 0, 1, 0), jnp.int32).astype(f32)
    places_ref[at + 8 : at + 16] = jnp.full((8, INNER), jnp.where(place == slabs - 1, 1, 0), jnp.int32).astype(f32)
    dt8_ref[...] = jnp.zeros_like(dt8_ref)
    dt8_ref[0:H] = dt_ref[...]
    dt_pre = dt8_ref[...] + heads_ref[0:8]
    step = jnp.maximum(dt_pre, 0.0) + jnp.log1p(jnp.exp(-jnp.abs(dt_pre)))
    real = iota((HEAD_ROWS, tok), 0) < H
    decay_rate = jnp.where(real, -jnp.exp(heads_ref[8:16]), 0.0)
    cum = unstacked(dot(stacked(step * decay_rate), until_ref[...]))
    left = jnp.exp(cum[:, tok - 1 : tok] - cum)
    reach = jnp.exp(cum)
    rows_ref[0:8] = cum
    rows_ref[8:16] = step
    rows_ref[16:24] = left
    rows_ref[24:32] = reach
    rows_ref[32:40] = 1.0 / (1.0 + jnp.exp(-dt_pre))
    rows_ref[40:48] = decay_rate
    tail = over_channels(left * step)
    tail_ref[...] = tail
    log_total = over_channels(cum)[tok - 1 : tok]
    skip = over_channels(heads_ref[16:24])[0:1]
    row = iota((8, INNER), 0)
    logs_ref[...] = jnp.where(row == 2, log_total, jnp.where(row == 3, skip, 0.0))
    scaled = jnp.concatenate(split2(cot_ref[...].astype(f32) * over_channels(reach)), 1)
    scaled_ref[...] = scaled

    raw = raw_ref[...].astype(f32)
    zeros = jnp.zeros((8, raw.shape[1]), f32)
    pre = bias_ref[...] + weight_ref[K - 1 : K] * raw
    for back in range(1, K):
        pre = pre + weight_ref[K - 1 - back : K - back] * shifted_down(raw, zeros, back)
    top_ref[...] = pre[:FIX_ROWS]
    gate = 1.0 / (1.0 + jnp.exp(-pre))
    xbc = (pre * gate).astype(bf16)
    xbc_ref[...] = xbc
    slope_ref[...] = gate * (1.0 + pre * (1.0 - gate))
    weighted = jnp.concatenate(split2(xbc[:, :INNER].astype(f32) * tail), 1)
    weighted_ref[...] = weighted
    later = mask_first(xbc[:, INNER:])
    state = dot(later[:, :N], weighted, 0, 0)
    state = state[:, :INNER] + state[:, INNER:]
    grad = dot(later[:, N:], scaled, 0, 0)
    grad = grad[:, :INNER] + grad[:, INNER:]
    state_ref[...] = state
    grad_ref[...] = grad
    write_messages((msg_ref,), state, grad, log_total, places_ref[0:1], 0)


def real_halo(halo_ref, places_ref):
    first = places_ref[places_ref.shape[0] - 16 :][:1, :1]
    return jnp.where(first > 0.5, 0.0, halo_ref[HALO_ROWS - 8 :].astype(f32))


def fix_kernel(
    top_ref, halo_ref, weight_ref, scaled_ref, tail_ref, places_ref, xbc_in, slope_in, weighted_in,
    xbc_ref, slope_ref, weighted_ref, factors_ref,
):
    halo = real_halo(halo_ref, places_ref)
    top = top_ref[0:8]
    for back in range(1, K):
        tap = weight_ref[K - 1 - back : K - back]
        top = top + jnp.where(iota(top.shape, 0) < back, tap * pltpu.roll(halo, back, 0), 0.0)
    pre = jnp.concatenate([top, top_ref[8:]], 0)
    gate = 1.0 / (1.0 + jnp.exp(-pre))
    xbc = (pre * gate).astype(bf16)
    xbc_ref[0:FIX_ROWS] = xbc
    slope_ref[0:FIX_ROWS] = gate * (1.0 + pre * (1.0 - gate))
    xbc = xbc.astype(f32)
    weighted = jnp.concatenate([each.astype(f32) for each in split2(xbc[:, :INNER] * tail_ref[0:FIX_ROWS])], 1)
    weighted_ref[0:FIX_ROWS] = weighted.astype(bf16)
    scaled = scaled_ref[0:FIX_ROWS].astype(f32)

    def placed(low, high):
        row = iota(low.shape, 0)
        moved = jnp.concatenate([high[8:], high[:8]], 0)
        return jnp.where(row < K - 1, low, jnp.where((row >= 8) & (row < 8 + K - 1), moved, 0.0)).astype(bf16)

    zero = jnp.zeros((FIX_ROWS, N), f32)
    factors_ref[:, : 2 * INNER] = placed(weighted, scaled)
    factors_ref[:, 2 * INNER : 2 * INNER + N] = placed(xbc[:, INNER : INNER + N], zero)
    factors_ref[:, 2 * INNER + N :] = placed(zero, xbc[:, INNER + N :])


def first_parts(factors_ref):
    both = dot(factors_ref[:, 2 * INNER :], factors_ref[:, : 2 * INNER], 0, 0)
    both = both[:, :INNER] + both[:, INNER:]
    return both[:N], both[N:]


def merge_kernel(t, radix, next_radix, state_ref, grad_ref, logs_ref, places_ref, *refs):
    got, refs = refs[: radix - 1], refs[radix - 1 :]
    prior = after = 0.0
    if t > 0:
        prior, after = refs[0][...], refs[1][...]
        refs = refs[2:]
    else:
        parts, refs = [first_parts(ref) for ref in refs[:radix]], refs[radix:]
    logs_out, prior_out, after_out, *refs = refs
    if not next_radix:
        state_out, grad_out, *refs = refs
    place = places_ref[8 * t : 8 * t + 1]
    log_prior, log_after, log_total = logs_ref[0:1], logs_ref[1:2], logs_ref[2:3]
    states = [message_block(ref, 0) for ref in got]
    grads = [message_block(ref, 1) for ref in got]
    logs = [message_log(ref) for ref in got]
    own_state, own_grad = state_ref[...], grad_ref[...]
    if t == 0:
        own_state, own_grad = own_state + parts[0][0], own_grad + parts[0][1]
        states = [each + part[0] for each, part in zip(states, parts[1:])]
        grads = [each + part[1] for each, part in zip(grads, parts[1:])]
    earlier = [s <= place for s in range(1, radix)]
    later = [s > place for s in range(1, radix)]
    before, log_before = chained(states, logs, earlier)
    beyond, log_beyond = chained(grads[::-1], logs[::-1], later[::-1])
    above, _ = chained(states, logs, later)
    below, _ = chained(grads[::-1], logs[::-1], earlier[::-1])
    mine = jnp.exp(log_total)
    state = above + jnp.exp(log_beyond) * (own_state + mine * before)
    grad = below + jnp.exp(log_before) * (own_grad + mine * beyond)
    prior_out[...] = prior + jnp.exp(log_prior) * before
    after_out[...] = after + jnp.exp(log_after) * beyond
    log_prior = log_prior + log_before
    log_after = log_after + log_beyond
    log_total = log_total + log_before + log_beyond
    row = iota((8, INNER), 0)
    logs_out[...] = jnp.where(row == 0, log_prior, jnp.where(row == 1, log_after, jnp.where(row == 2, log_total, 0.0)))
    if not next_radix:
        state_out[...] = state
        grad_out[...] = grad
    write_messages(refs, state, grad, log_total, places_ref[8 * t + 8 : 8 * t + 9], next_radix)


def local_kernel(xbc_ref, cot_ref, rows_ref, logs_ref, local_ref, sums_ref):
    tok = xbc_ref.shape[0]
    cot = cot_ref[...]
    values = xbc_ref[:, :INNER]
    b_proj = xbc_ref[:, INNER : INNER + N]
    c_proj = xbc_ref[:, INNER + N :]
    cum, step = rows_ref[0:8], rows_ref[8:16]
    step_wide = over_channels(step)
    values_f = values.astype(f32)
    cot_f = cot.astype(f32)
    stepped = split2(values_f * step_wide)
    gram = dot(b_proj, c_proj, 1, 1)
    reached = iota((tok, tok), 0) <= iota((tok, tok), 1)
    pieces = stacked(cum)
    piece_head = iota((4 * HEAD_ROWS, tok), 0) % HEAD_ROWS
    dgram = jnp.zeros((tok, tok), f32)
    grads, sums = [], []
    for h in range(H):
        of = slice(h * P_SIZE, (h + 1) * P_SIZE)
        column = dot(pieces, jnp.where(piece_head == h, 1.0, 0.0).astype(bf16), 0, 0)
        within = jnp.exp(jnp.where(reached, cum[h : h + 1] - column, -1e30))
        cot_h = cot[:, of]
        high, low = split2(gram * within)
        grads.append(dot(high, cot_h) + dot(low, cot_h))
        dmix = dot(stepped[0][:, of], cot_h, 1, 1) + dot(stepped[1][:, of], cot_h, 1, 1)
        dmix = dmix * within
        dgram = dgram + dmix
        sums.append(jnp.sum(dmix * gram, axis=0, keepdims=True))
    grad_stepped = jnp.concatenate(grads, 1)
    local_ref[:, :INNER] = grad_stepped * step_wide + logs_ref[3:4] * cot_f
    high, low = split2(dgram)
    local_ref[:, INNER : INNER + N] = dot(high, c_proj) + dot(low, c_proj)
    local_ref[:, INNER + N :] = dot(high, b_proj, 0, 0) + dot(low, b_proj, 0, 0)
    row = iota((HEAD_ROWS, tok), 0)
    pairs = jnp.zeros((HEAD_ROWS, tok), f32)
    for h in range(H):
        pairs = jnp.where(row == h, sums[h], pairs)
    sums_ref[0:8] = pairs
    sums_ref[8:16] = head_sums(values_f * grad_stepped)
    sums_ref[16:24] = head_sums(values_f * cot_f)


def totals_kernel(
    t, radix, raw_ref, halo_ref, xbc_ref, slope_ref, scaled_ref, weighted_ref, tail_ref, rows_ref, local_ref, sums_ref,
    logs_ref, places_ref, until_ref, weight_ref, *refs
):
    got, refs = refs[: radix - 1], refs[radix - 1 :]
    prior = after = 0.0
    if t > 0:
        prior, after = refs[0][...], refs[1][...]
        refs = refs[2:]
    conv_ref, dt_out_ref, totals_ref, spill_ref, totals_scratch = refs
    tok = raw_ref.shape[0]
    place = places_ref[8 * t : 8 * t + 1]
    blocks = [message_block(ref) for ref in got]
    logs = [message_log(ref) for ref in got]
    before, _ = chained(blocks, logs, [s <= place for s in range(1, radix)])
    beyond, _ = chained(blocks[::-1], logs[::-1], [s > place for s in range(radix - 1, 0, -1)])
    prior = prior + jnp.exp(logs_ref[0:1]) * before
    after = after + jnp.exp(logs_ref[1:2]) * beyond

    step, left, reach = rows_ref[8:16], rows_ref[16:24], rows_ref[24:32]
    dt_gate, decay_rate = rows_ref[32:40], rows_ref[40:48]
    b_proj = xbc_ref[:, INNER : INNER + N]
    c_proj = xbc_ref[:, INNER + N :]
    prior2 = jnp.concatenate(split2(prior), 0)
    after2 = jnp.concatenate(split2(after), 0)
    seen = dot(jnp.concatenate([c_proj, c_proj], 1), prior2)
    back = dot(jnp.concatenate([b_proj, b_proj], 1), after2)
    grad_c = dot(scaled_ref[:, :INNER], prior2, 1, 1)
    grad_c = grad_c[:, :N] + grad_c[:, N:] + dot(scaled_ref[:, INNER:], prior2[:N], 1, 1)
    grad_b = dot(weighted_ref[:, :INNER], after2, 1, 1)
    grad_b = grad_b[:, :N] + grad_b[:, N:] + dot(weighted_ref[:, INNER:], after2[:N], 1, 1)
    grad_low = (local_ref[...] + jnp.concatenate([tail_ref[...] * back, grad_b, grad_c], 1)).astype(bf16)
    grad_conv = grad_low.astype(f32) * slope_ref[...]
    conv_ref[...] = grad_conv
    top = grad_conv[:8]
    spill = jnp.zeros_like(top)
    for ahead in range(1, K):
        tap = weight_ref[K - 1 - ahead : K - ahead]
        spill = spill + tap * jnp.where(iota(top.shape, 0) < 8 - ahead, 0.0, pltpu.roll(top, 8 - ahead, 0))
    spill_ref[...] = spill

    raw = raw_ref[...].astype(f32)
    halo = real_halo(halo_ref, places_ref)
    sums = [grad_conv * shifted_down(raw, halo, K - 1 - k) for k in range(K - 1)] + [grad_conv * raw, grad_conv]
    totals_scratch[...] = jnp.zeros_like(totals_scratch)
    for k, each in enumerate(sums):
        each = jnp.sum(each, axis=0, keepdims=True)
        for j in range(LANE_BLOCKS):
            at = k * LANE_BLOCKS + j
            totals_scratch[at : at + 1] = each[:, j * 128 : (j + 1) * 128]

    values = xbc_ref[:, :INNER].astype(f32)
    pairs, from_values, skip_rows = sums_ref[0:8], sums_ref[8:16], sums_ref[16:24]
    scaled_f = scaled_ref[:, :INNER].astype(f32) + scaled_ref[:, INNER:].astype(f32)
    seen_rows = head_sums(scaled_f * seen)
    tail_rows = head_sums(values * back)
    tail_term = tail_rows * left * step
    selector = head_selector(HEAD_ROWS * 2)[:HEAD_ROWS].astype(f32)
    through = jnp.sum(prior * after, axis=0, keepdims=True)
    through = jnp.sum(selector * through, axis=1, keepdims=True) * reach[:, tok - 1 : tok]
    last_extra = jnp.sum(tail_term, axis=1, keepdims=True) + through
    grad_cum = pairs - from_values * step + seen_rows - tail_term
    grad_log = unstacked(dot(stacked(grad_cum), until_ref[...], 1, 1)) + last_extra
    grad_step = from_values + tail_rows * left + decay_rate * grad_log
    grad_pre = grad_step * dt_gate
    dt_out_ref[...] = grad_pre[0:H]
    row, lane = iota((HEAD_ROWS, 128), 0), iota((HEAD_ROWS, 128), 1)
    small = jnp.zeros((HEAD_ROWS, 128), f32)
    for i, each in enumerate((grad_pre, grad_log * step * decay_rate, skip_rows)):
        column = jnp.sum(each, axis=1, keepdims=True)
        small = jnp.where((row < H) & (lane == row + i * H), column, small)
    totals_scratch[SMALL_ROW : SMALL_ROW + 1] = jnp.sum(small, axis=0, keepdims=True)
    totals_ref[...] = pack_totals(totals_scratch[...])


def input_kernel(conv_ref, weight_ref, out_hbm, end_ref, out_ref, sem):
    grad_conv = conv_ref[...]
    tok, channels = grad_conv.shape
    grad_in = weight_ref[K - 1 : K] * grad_conv
    row8 = iota((8, channels), 0)
    for ahead in range(1, K):
        tap = weight_ref[K - 1 - ahead : K - ahead]
        moved = pltpu.roll(grad_conv, tok - ahead, 0)
        last8 = moved[tok - 8 :]
        inside = row8 < 8 - ahead
        grad_in = grad_in + tap * jnp.concatenate([moved[: tok - 8], jnp.where(inside, last8, 0.0)], 0)
    out_ref[...] = grad_in.astype(bf16)
    copy = pltpu.make_async_copy(out_ref, out_hbm, sem)
    copy.start()
    end_ref[...] = grad_in[tok - END_ROWS :]
    copy.wait()


def end_kernel(end_ref, spilled_ref, places_ref, main_hbm, out_hbm, rows_ref, sem):
    end = end_ref[...]
    last = places_ref[places_ref.shape[0] - 8 :][:1, :1]
    fixed = end[END_ROWS - 8 :] + jnp.where(last > 0.5, 0.0, spilled_ref[...])
    rows_ref[...] = jnp.concatenate([end[: END_ROWS - 8], fixed], 0).astype(bf16)
    tok = out_hbm.shape[0]
    copy = pltpu.make_async_copy(rows_ref, out_hbm.at[pl.ds(tok - END_ROWS, END_ROWS)], sem)
    copy.start()
    copy.wait()


def summed(parts):
    large = jnp.sum(parts * jnp.exp(parts[:, SMALL_ROW + 1 : SMALL_ROW + 2]), axis=0)
    small = parts[:, SMALL_ROW : SMALL_ROW + 1] + parts[:, SMALL_ROW + 3 : SMALL_ROW + 4] * (1 / 256.0)
    small = small * jnp.exp(parts[:, SMALL_ROW + 2 : SMALL_ROW + 3])
    return large, jnp.sum(small, axis=0)


def repack_kernel(parts_ref, out_ref):
    large, small = summed(parts_ref[...])
    out_ref[...] = pack_totals(jnp.where(iota(large.shape, 0) == SMALL_ROW, small, large))


def finish_kernel(parts_ref, weight_ref, bias_ref, dt_bias_ref, alog_ref, skip_ref):
    large, small = summed(parts_ref[...])
    for k in range(K + 1):
        for j in range(LANE_BLOCKS):
            at = k * LANE_BLOCKS + j
            if k < K:
                weight_ref[k : k + 1, j * 128 : (j + 1) * 128] = large[at : at + 1]
            else:
                bias_ref[:, j * 128 : (j + 1) * 128] = large[at : at + 1]
    for i, ref in enumerate((dt_bias_ref, alog_ref, skip_ref)):
        ref[...] = small[:, i * H : (i + 1) * H]


def call(kernel, outs, in_specs, out_specs=None, scratch=(), flops=0, limit=16 << 20, aliases=None):
    return pl.pallas_call(
        kernel,
        out_shape=outs,
        in_specs=in_specs,
        out_specs=out_specs or jax.tree.map(lambda _: VMEM, outs),
        scratch_shapes=list(scratch),
        input_output_aliases=aliases or {},
        compiler_params=pltpu.CompilerParams(vmem_limit_bytes=limit),
        cost_estimate=pl.CostEstimate(flops=flops, bytes_accessed=1 << 20, transcendentals=0),
    )


def struct(shape, dtype=f32):
    return jax.ShapeDtypeStruct(shape, dtype)


def from_groups(messages, slabs, size, radix):
    got = []
    for s in range(1, radix):
        message = messages[s - 1 if len(messages) > 1 else 0]
        route = [(p, p - p % (size * radix) + (p + s * size) % (size * radix)) for p in range(slabs)]
        got.append(lax.ppermute(message, "ctx", route))
    return got


def states_from_groups(messages, slabs, size, radix):
    got = from_groups([message.astype(jnp.float16) for message in messages], slabs, size, radix)
    return [each.astype(f32) for each in got]


def stages_of(slabs):
    stages, size = [], 1
    while size < slabs:
        radix = 2 if (slabs // size).bit_length() % 2 == 0 else 4
        stages.append((size, radix))
        size *= radix
    assert size == slabs and len(stages) > 1
    return stages


def everyones(packed, axes, count):
    packed = jnp.broadcast_to(packed.astype(jnp.float16)[None], (count, *packed.shape))
    return lax.all_to_all(packed, axes, 0, 0).astype(f32)


def on_device(xbc_raw, conv_weight, conv_bias, dt_raw, dt_bias, a_log, d_skip, grad_out):
    tok, channels = xbc_raw.shape[1:]
    slabs = lax.axis_size("ctx")
    contexts = lax.axis_size("dp")
    stages = stages_of(slabs)

    raw, cot, dt_rows = xbc_raw[0], grad_out[0], dt_raw[0].T
    until = call(triangle_kernel, struct((tok, tok), bf16), [], flops=10**11)()
    until, bias, heads = call(
        heads_kernel,
        (struct((tok, tok), bf16), struct((1, channels)), struct((3 * HEAD_ROWS, tok))),
        [VMEM] * 5,
        aliases={4: 0},
    )(conv_bias[None], dt_bias[None], a_log[None], d_skip[None], until)
    early_raw, until = lax.optimization_barrier((raw, until))
    halo = lax.ppermute(early_raw[tok - HALO_ROWS :], "ctx", [(i, (i + 1) % slabs) for i in range(slabs)])

    def last_radix(t):
        return stages[t][1] if t == len(stages) - 1 else 0

    def messages(t):
        if last_radix(t):
            return (struct((N + TAIL_ROWS, INNER)),) * (last_radix(t) - 1)
        return (struct((2 * N + TAIL_ROWS, INNER)),)

    state_like = struct((N, INNER))
    logs_like = struct((8, INNER))
    top, xbc, slope, weighted, scaled, tail, rows, logs, places, state, grad, *outgoing = call(
        functools.partial(start_kernel, stages),
        (
            struct((FIX_ROWS, channels)), struct((tok, channels), bf16), struct((tok, channels)), struct((tok, 2 * INNER), bf16),
            struct((tok, 2 * INNER), bf16), struct((tok, INNER)), struct((6 * HEAD_ROWS, tok)),
            logs_like, struct((8 * len(stages) + 16, INNER)), state_like, state_like, *messages(0),
        ),
        [VMEM] * 7,
        scratch=[pltpu.VMEM((HEAD_ROWS, tok), f32)],
        flops=10**11,
    )(raw, cot, conv_weight, bias, dt_rows, heads, until)
    xbc, slope, weighted, factors = call(
        fix_kernel,
        (
            struct((tok, channels), bf16), struct((tok, channels)), struct((tok, 2 * INNER), bf16),
            struct((FIX_ROWS, 2 * INNER + 2 * N), bf16),
        ),
        [VMEM] * 9,
        flops=1_000_000,
        aliases={6: 0, 7: 1, 8: 2},
    )(top, halo, conv_weight, scaled, tail, places, xbc, slope, weighted)

    local, sums = call(
        local_kernel,
        (struct((tok, channels)), struct((3 * HEAD_ROWS, tok))),
        [VMEM] * 4,
        flops=10**11,
    )(xbc, cot, rows, logs)

    carried = ()
    for t, (size, radix) in enumerate(stages):
        got = states_from_groups(outgoing, slabs, size, radix)
        if t == 0:
            got, local, sums = lax.optimization_barrier((got, local, sums))
            carried = [factors] + from_groups([factors], slabs, size, radix)
        if t == len(stages) - 1:
            break
        last = last_radix(t + 1)
        outs = (logs_like, state_like, state_like) + (() if last else (state_like, state_like))
        logs, *outgoing = call(
            functools.partial(merge_kernel, t, radix, last),
            outs + messages(t + 1),
            [VMEM] * (4 + len(got) + len(carried)),
            flops=1_000_000,
        )(state, grad, logs, places, *got, *carried)
        carried, outgoing = outgoing[:2], outgoing[2:]
        if not last:
            (state, grad), outgoing = outgoing[:2], outgoing[2:]

    grad_conv, grad_dt, packed, spill = call(
        functools.partial(totals_kernel, len(stages) - 1, radix),
        (struct((tok, channels)), struct((H, tok)), struct((TOTAL_ROWS, 128)), struct((8, channels))),
        [VMEM] * (14 + len(got) + len(carried)),
        scratch=[pltpu.VMEM((TOTAL_ROWS, 128), f32)],
        flops=200_000_000,
    )(raw, halo, xbc, slope, scaled, weighted, tail, rows, local, sums, logs, places, until, conv_weight, *got, *carried)

    spilled = lax.ppermute(spill, "ctx", [((i + 1) % slabs, i) for i in range(slabs)])
    if slabs * contexts <= 64:
        parts = everyones(packed, ("ctx", "dp"), slabs * contexts)
    else:
        packed = call(repack_kernel, struct((TOTAL_ROWS, 128)), [VMEM])(everyones(packed, "ctx", slabs))
        parts = everyones(packed, "dp", contexts)

    grad_main, end = call(
        input_kernel,
        (struct((tok, channels), bf16), struct((END_ROWS, channels))),
        [VMEM] * 2,
        (HBM, VMEM),
        [pltpu.VMEM((tok, channels), bf16), pltpu.SemaphoreType.DMA],
        flops=1_000_000,
    )(grad_conv, conv_weight)
    grad_input = call(
        end_kernel,
        struct((tok, channels), bf16),
        [VMEM] * 3 + [HBM],
        HBM,
        [pltpu.VMEM((END_ROWS, channels), bf16), pltpu.SemaphoreType.DMA],
        aliases={3: 0},
    )(end, spilled, places, grad_main)

    grad_weight, grad_bias, *small = call(
        finish_kernel,
        (struct((K, channels)), struct((1, channels)), struct((1, H)), struct((1, H)), struct((1, H))),
        [VMEM],
    )(parts)
    return (grad_input[None], grad_dt.T[None], grad_weight, grad_bias[0], *(each[0] for each in small))


def solution(mesh):
    in_specs = (
        P("dp", "ctx", None),
        P(),
        P(),
        P("dp", "ctx", None),
        P(),
        P(),
        P(),
        P("dp", "ctx", None),
    )
    out_specs = (P("dp", "ctx", None), P("dp", "ctx", None), P(), P(), P(), P(), P())
    return jax.shard_map(
        on_device, mesh=mesh, in_specs=in_specs, out_specs=out_specs, check_vma=False
    )
```

```python
import functools

import jax
import jax.numpy as jnp
from jax import lax
from jax.experimental import pallas as pl
from jax.experimental.pallas import tpu as pltpu
from jax.sharding import PartitionSpec as P

H = 4
P_SIZE = 64
N = 128
K = 4
INNER = H * P_SIZE
HEAD_ROWS = 8
TAIL_ROWS = 8
HALO_ROWS = 16
FIX_ROWS = 16
END_ROWS = 16
LANE_BLOCKS = (INNER + 2 * N) // 128
SMALL_ROW = (K + 1) * LANE_BLOCKS
TOTAL_ROWS = 24

f32 = jnp.float32
bf16 = jnp.bfloat16

VMEM = pl.BlockSpec(memory_space=pltpu.VMEM)
HBM = pl.BlockSpec(memory_space=pltpu.HBM)


def dot(a, b, a_dim=1, b_dim=0):
    return lax.dot_general(a, b, (((a_dim,), (b_dim,)), ((), ())), preferred_element_type=f32)


def split2(x):
    high = x.astype(bf16)
    return high, (x - high.astype(f32)).astype(bf16)


def split3(x):
    high = x.astype(bf16).astype(f32)
    rest = x - high
    middle = rest.astype(bf16).astype(f32)
    return high, middle, rest - middle


def iota(shape, dim):
    return lax.broadcasted_iota(jnp.int32, shape, dim)


def stacked(rows):
    return jnp.concatenate([*split3(rows), jnp.zeros_like(rows)], 0).astype(bf16)


def unstacked(rows):
    return rows[0:8] + rows[8:16] + rows[16:24]


def head_selector(rows):
    shape = (rows, INNER)
    return jnp.where(iota(shape, 1) // P_SIZE == iota(shape, 0) % HEAD_ROWS, 1.0, 0.0).astype(bf16)


def over_channels(rows):
    return dot(stacked(rows), head_selector(4 * HEAD_ROWS), 0, 0)


def head_sums(x):
    high, low = split2(x)
    selector = head_selector(HEAD_ROWS * 2)
    return (dot(selector, high, 1, 1) + dot(selector, low, 1, 1))[:HEAD_ROWS]


def by_head(ref, width):
    row = iota((HEAD_ROWS, width), 0)
    out = jnp.zeros((HEAD_ROWS, width), f32)
    for h in range(H):
        out = jnp.where(row == h, ref[:, h : h + 1], out)
    return out


def shifted_down(x, first, count):
    moved = pltpu.roll(x, count, 0)
    top = jnp.where(iota(first.shape, 0) < count, pltpu.roll(first, count, 0), moved[:8])
    return jnp.concatenate([top, moved[8:]], 0)


def quantized_log(size):
    return jnp.log(jnp.maximum(size, 1e-30)).astype(bf16).astype(f32)


def scaled_columns(x):
    log_size = quantized_log(jnp.max(jnp.abs(x), axis=0, keepdims=True))
    return x * jnp.exp(-log_size), log_size


def write_messages(msg_refs, state, grad, log_total, place, radix):
    row = iota((TAIL_ROWS, INNER), 0)
    high, middle, low = split3(log_total)
    tail = jnp.where(row == 4, high, jnp.where(row == 5, middle * 256.0, jnp.where(row == 6, low * 65536.0, 0.0)))
    state, state_size = scaled_columns(state)
    grad, grad_size = scaled_columns(grad)
    if radix:
        for s, msg_ref in enumerate(msg_refs, 1):
            on = place + s < radix
            msg_ref[0:N] = jnp.where(on, state, grad)
            msg_ref[N : N + TAIL_ROWS] = jnp.where(row == 0, jnp.where(on, state_size, grad_size), tail)
    else:
        (msg_ref,) = msg_refs
        msg_ref[0:N] = state
        msg_ref[N : 2 * N] = grad
        msg_ref[2 * N : 2 * N + TAIL_ROWS] = jnp.where(row == 0, state_size, jnp.where(row == 1, grad_size, tail))


def message_log(got_ref):
    rows = got_ref.shape[0] - TAIL_ROWS
    tail = got_ref[rows : rows + 8]
    return tail[4:5] + tail[5:6] * (1 / 256.0) + tail[6:7] * (1 / 65536.0)


def message_block(got_ref, which=0):
    rows = got_ref.shape[0] - TAIL_ROWS
    return got_ref[which * N : (which + 1) * N] * jnp.exp(got_ref[rows + which : rows + which + 1])


def chained(blocks, logs, used):
    total, log_sum = 0.0, 0.0
    for block, log, use in zip(blocks, logs, used):
        total = total + jnp.where(use, jnp.exp(log_sum) * block, 0.0)
        log_sum = log_sum + jnp.where(use, log, 0.0)
    return total, log_sum


def pack_totals(x):
    row = iota(x.shape, 0)
    large = jnp.where(row < SMALL_ROW, x, 0.0)
    large_size = quantized_log(jnp.max(jnp.abs(large), axis=0, keepdims=True))
    small = x[SMALL_ROW : SMALL_ROW + 1]
    small_size = quantized_log(jnp.abs(small))
    small = small * jnp.exp(-small_size)
    small_high = small.astype(bf16).astype(f32)
    out = jnp.where(row == SMALL_ROW, small_high, large * jnp.exp(-large_size))
    out = jnp.where(row == SMALL_ROW + 3, (small - small_high) * 256.0, out)
    return jnp.where(row == SMALL_ROW + 1, large_size, jnp.where(row == SMALL_ROW + 2, small_size, out))


def triangle_kernel(until_ref):
    shape = until_ref.shape
    until_ref[...] = jnp.where(iota(shape, 0) <= iota(shape, 1), 1.0, 0.0).astype(bf16)


def heads_kernel(bias_ref, dt_bias_ref, alog_ref, skip_ref, until_in, until_ref, bias_out, heads_ref):
    bias_out[...] = bias_ref[...]
    for i, ref in enumerate((dt_bias_ref, alog_ref, skip_ref)):
        heads_ref[8 * i : 8 * i + 8] = by_head(ref, until_ref.shape[1])


def mask_first(x):
    top = jnp.where(iota((FIX_ROWS, x.shape[1]), 0) < K - 1, 0.0, x[:FIX_ROWS].astype(f32))
    return jnp.concatenate([top.astype(x.dtype), x[FIX_ROWS:]], 0)


def start_kernel(
    stages, raw_ref, cot_ref, weight_ref, bias_ref, dt_ref, heads_ref, until_ref,
    top_ref, xbc_ref, slope_ref, weighted_ref, scaled_ref, tail_ref, rows_ref, logs_ref, places_ref, state_ref, grad_ref, msg_ref, dt8_ref,
):
    tok = raw_ref.shape[0]
    place = lax.axis_index("ctx")
    for t, (size, radix) in enumerate(stages):
        places_ref[8 * t : 8 * t + 8] = jnp.full((8, INNER), lax.rem(lax.div(place, size), radix), jnp.int32).astype(f32)
    at = 8 * len(stages)
    slabs = stages[-1][0] * stages[-1][1]
    places_ref[at : at + 8] = jnp.full((8, INNER), jnp.where(place == 0, 1, 0), jnp.int32).astype(f32)
    places_ref[at + 8 : at + 16] = jnp.full((8, INNER), jnp.where(place == slabs - 1, 1, 0), jnp.int32).astype(f32)
    dt8_ref[...] = jnp.zeros_like(dt8_ref)
    dt8_ref[0:H] = dt_ref[...]
    dt_pre = dt8_ref[...] + heads_ref[0:8]
    step = jnp.maximum(dt_pre, 0.0) + jnp.log1p(jnp.exp(-jnp.abs(dt_pre)))
    real = iota((HEAD_ROWS, tok), 0) < H
    decay_rate = jnp.where(real, -jnp.exp(heads_ref[8:16]), 0.0)
    cum = unstacked(dot(stacked(step * decay_rate), until_ref[...]))
    left = jnp.exp(cum[:, tok - 1 : tok] - cum)
    reach = jnp.exp(cum)
    rows_ref[0:8] = cum
    rows_ref[8:16] = step
    rows_ref[16:24] = left
    rows_ref[24:32] = reach
    rows_ref[32:40] = 1.0 / (1.0 + jnp.exp(-dt_pre))
    rows_ref[40:48] = decay_rate
    tail = over_channels(left * step)
    tail_ref[...] = tail
    log_total = over_channels(cum)[tok - 1 : tok]
    skip = over_channels(heads_ref[16:24])[0:1]
    row = iota((8, INNER), 0)
    logs_ref[...] = jnp.where(row == 2, log_total, jnp.where(row == 3, skip, 0.0))
    scaled = jnp.concatenate(split2(cot_ref[...].astype(f32) * over_channels(reach)), 1)
    scaled_ref[...] = scaled

    raw = raw_ref[...].astype(f32)
    zeros = jnp.zeros((8, raw.shape[1]), f32)
    pre = bias_ref[...] + weight_ref[K - 1 : K] * raw
    for back in range(1, K):
        pre = pre + weight_ref[K - 1 - back : K - back] * shifted_down(raw, zeros, back)
    top_ref[...] = pre[:FIX_ROWS]
    gate = 1.0 / (1.0 + jnp.exp(-pre))
    xbc = (pre * gate).astype(bf16)
    xbc_ref[...] = xbc
    slope_ref[...] = gate * (1.0 + pre * (1.0 - gate))
    weighted = jnp.concatenate(split2(xbc[:, :INNER].astype(f32) * tail), 1)
    weighted_ref[...] = weighted
    later = mask_first(xbc[:, INNER:])
    state = dot(later[:, :N], weighted, 0, 0)
    state = state[:, :INNER] + state[:, INNER:]
    grad = dot(later[:, N:], scaled, 0, 0)
    grad = grad[:, :INNER] + grad[:, INNER:]
    state_ref[...] = state
    grad_ref[...] = grad
    write_messages((msg_ref,), state, grad, log_total, places_ref[0:1], 0)


def real_halo(halo_ref, places_ref):
    first = places_ref[places_ref.shape[0] - 16 :][:1, :1]
    return jnp.where(first > 0.5, 0.0, halo_ref[HALO_ROWS - 8 :].astype(f32))


def fix_kernel(
    top_ref, halo_ref, weight_ref, scaled_ref, tail_ref, places_ref, xbc_in, slope_in, weighted_in,
    xbc_ref, slope_ref, weighted_ref, factors_ref,
):
    halo = real_halo(halo_ref, places_ref)
    top = top_ref[0:8]
    for back in range(1, K):
        tap = weight_ref[K - 1 - back : K - back]
        top = top + jnp.where(iota(top.shape, 0) < back, tap * pltpu.roll(halo, back, 0), 0.0)
    pre = jnp.concatenate([top, top_ref[8:]], 0)
    gate = 1.0 / (1.0 + jnp.exp(-pre))
    xbc = (pre * gate).astype(bf16)
    xbc_ref[0:FIX_ROWS] = xbc
    slope_ref[0:FIX_ROWS] = gate * (1.0 + pre * (1.0 - gate))
    xbc = xbc.astype(f32)
    weighted = jnp.concatenate([each.astype(f32) for each in split2(xbc[:, :INNER] * tail_ref[0:FIX_ROWS])], 1)
    weighted_ref[0:FIX_ROWS] = weighted.astype(bf16)
    scaled = scaled_ref[0:FIX_ROWS].astype(f32)

    def placed(low, high):
        row = iota(low.shape, 0)
        moved = jnp.concatenate([high[8:], high[:8]], 0)
        return jnp.where(row < K - 1, low, jnp.where((row >= 8) & (row < 8 + K - 1), moved, 0.0)).astype(bf16)

    zero = jnp.zeros((FIX_ROWS, N), f32)
    factors_ref[:, : 2 * INNER] = placed(weighted, scaled)
    factors_ref[:, 2 * INNER : 2 * INNER + N] = placed(xbc[:, INNER : INNER + N], zero)
    factors_ref[:, 2 * INNER + N :] = placed(zero, xbc[:, INNER + N :])


def first_parts(factors_ref):
    both = dot(factors_ref[:, 2 * INNER :], factors_ref[:, : 2 * INNER], 0, 0)
    both = both[:, :INNER] + both[:, INNER:]
    return both[:N], both[N:]


def merge_kernel(t, radix, next_radix, state_ref, grad_ref, logs_ref, places_ref, *refs):
    got, refs = refs[: radix - 1], refs[radix - 1 :]
    prior = after = 0.0
    if t > 0:
        prior, after = refs[0][...], refs[1][...]
        refs = refs[2:]
    else:
        parts, refs = [first_parts(ref) for ref in refs[:radix]], refs[radix:]
    logs_out, prior_out, after_out, *refs = refs
    if not next_radix:
        state_out, grad_out, *refs = refs
    place = places_ref[8 * t : 8 * t + 1]
    log_prior, log_after, log_total = logs_ref[0:1], logs_ref[1:2], logs_ref[2:3]
    states = [message_block(ref, 0) for ref in got]
    grads = [message_block(ref, 1) for ref in got]
    logs = [message_log(ref) for ref in got]
    own_state, own_grad = state_ref[...], grad_ref[...]
    if t == 0:
        own_state, own_grad = own_state + parts[0][0], own_grad + parts[0][1]
        states = [each + part[0] for each, part in zip(states, parts[1:])]
        grads = [each + part[1] for each, part in zip(grads, parts[1:])]
    earlier = [s <= place for s in range(1, radix)]
    later = [s > place for s in range(1, radix)]
    before, log_before = chained(states, logs, earlier)
    beyond, log_beyond = chained(grads[::-1], logs[::-1], later[::-1])
    above, _ = chained(states, logs, later)
    below, _ = chained(grads[::-1], logs[::-1], earlier[::-1])
    mine = jnp.exp(log_total)
    state = above + jnp.exp(log_beyond) * (own_state + mine * before)
    grad = below + jnp.exp(log_before) * (own_grad + mine * beyond)
    prior_out[...] = prior + jnp.exp(log_prior) * before
    after_out[...] = after + jnp.exp(log_after) * beyond
    log_prior = log_prior + log_before
    log_after = log_after + log_beyond
    log_total = log_total + log_before + log_beyond
    row = iota((8, INNER), 0)
    logs_out[...] = jnp.where(row == 0, log_prior, jnp.where(row == 1, log_after, jnp.where(row == 2, log_total, 0.0)))
    if not next_radix:
        state_out[...] = state
        grad_out[...] = grad
    write_messages(refs, state, grad, log_total, places_ref[8 * t + 8 : 8 * t + 9], next_radix)


def local_kernel(xbc_ref, cot_ref, rows_ref, logs_ref, local_ref, sums_ref):
    tok = xbc_ref.shape[0]
    cot = cot_ref[...]
    values = xbc_ref[:, :INNER]
    b_proj = xbc_ref[:, INNER : INNER + N]
    c_proj = xbc_ref[:, INNER + N :]
    cum, step = rows_ref[0:8], rows_ref[8:16]
    step_wide = over_channels(step)
    values_f = values.astype(f32)
    cot_f = cot.astype(f32)
    stepped = split2(values_f * step_wide)
    gram = dot(b_proj, c_proj, 1, 1)
    reached = iota((tok, tok), 0) <= iota((tok, tok), 1)
    pieces = stacked(cum)
    piece_head = iota((4 * HEAD_ROWS, tok), 0) % HEAD_ROWS
    dgram = jnp.zeros((tok, tok), f32)
    grads, sums = [], []
    for h in range(H):
        of = slice(h * P_SIZE, (h + 1) * P_SIZE)
        column = dot(pieces, jnp.where(piece_head == h, 1.0, 0.0).astype(bf16), 0, 0)
        within = jnp.exp(jnp.where(reached, cum[h : h + 1] - column, -1e30))
        cot_h = cot[:, of]
        high, low = split2(gram * within)
        grads.append(dot(high, cot_h) + dot(low, cot_h))
        dmix = dot(stepped[0][:, of], cot_h, 1, 1) + dot(stepped[1][:, of], cot_h, 1, 1)
        dmix = dmix * within
        dgram = dgram + dmix
        sums.append(jnp.sum(dmix * gram, axis=0, keepdims=True))
    grad_stepped = jnp.concatenate(grads, 1)
    local_ref[:, :INNER] = grad_stepped * step_wide + logs_ref[3:4] * cot_f
    high, low = split2(dgram)
    local_ref[:, INNER : INNER + N] = dot(high, c_proj) + dot(low, c_proj)
    local_ref[:, INNER + N :] = dot(high, b_proj, 0, 0) + dot(low, b_proj, 0, 0)
    row = iota((HEAD_ROWS, tok), 0)
    pairs = jnp.zeros((HEAD_ROWS, tok), f32)
    for h in range(H):
        pairs = jnp.where(row == h, sums[h], pairs)
    sums_ref[0:8] = pairs
    sums_ref[8:16] = head_sums(values_f * grad_stepped)
    sums_ref[16:24] = head_sums(values_f * cot_f)


def totals_kernel(
    t, radix, raw_ref, halo_ref, xbc_ref, slope_ref, scaled_ref, weighted_ref, tail_ref, rows_ref, local_ref, sums_ref,
    logs_ref, places_ref, until_ref, weight_ref, *refs
):
    got, refs = refs[: radix - 1], refs[radix - 1 :]
    prior = after = 0.0
    if t > 0:
        prior, after = refs[0][...], refs[1][...]
        refs = refs[2:]
    conv_ref, dt_out_ref, totals_ref, spill_ref, totals_scratch = refs
    tok = raw_ref.shape[0]
    place = places_ref[8 * t : 8 * t + 1]
    blocks = [message_block(ref) for ref in got]
    logs = [message_log(ref) for ref in got]
    before, _ = chained(blocks, logs, [s <= place for s in range(1, radix)])
    beyond, _ = chained(blocks[::-1], logs[::-1], [s > place for s in range(radix - 1, 0, -1)])
    prior = prior + jnp.exp(logs_ref[0:1]) * before
    after = after + jnp.exp(logs_ref[1:2]) * beyond

    step, left, reach = rows_ref[8:16], rows_ref[16:24], rows_ref[24:32]
    dt_gate, decay_rate = rows_ref[32:40], rows_ref[40:48]
    b_proj = xbc_ref[:, INNER : INNER + N]
    c_proj = xbc_ref[:, INNER + N :]
    prior2 = jnp.concatenate(split2(prior), 0)
    after2 = jnp.concatenate(split2(after), 0)
    seen = dot(jnp.concatenate([c_proj, c_proj], 1), prior2)
    back = dot(jnp.concatenate([b_proj, b_proj], 1), after2)
    grad_c = dot(scaled_ref[:, :INNER], prior2, 1, 1)
    grad_c = grad_c[:, :N] + grad_c[:, N:] + dot(scaled_ref[:, INNER:], prior2[:N], 1, 1)
    grad_b = dot(weighted_ref[:, :INNER], after2, 1, 1)
    grad_b = grad_b[:, :N] + grad_b[:, N:] + dot(weighted_ref[:, INNER:], after2[:N], 1, 1)
    grad_low = (local_ref[...] + jnp.concatenate([tail_ref[...] * back, grad_b, grad_c], 1)).astype(bf16)
    grad_conv = grad_low.astype(f32) * slope_ref[...]
    conv_ref[...] = grad_conv
    top = grad_conv[:8]
    spill = jnp.zeros_like(top)
    for ahead in range(1, K):
        tap = weight_ref[K - 1 - ahead : K - ahead]
        spill = spill + tap * jnp.where(iota(top.shape, 0) < 8 - ahead, 0.0, pltpu.roll(top, 8 - ahead, 0))
    spill_ref[...] = spill

    raw = raw_ref[...].astype(f32)
    halo = real_halo(halo_ref, places_ref)
    sums = [grad_conv * shifted_down(raw, halo, K - 1 - k) for k in range(K - 1)] + [grad_conv * raw, grad_conv]
    totals_scratch[...] = jnp.zeros_like(totals_scratch)
    for k, each in enumerate(sums):
        each = jnp.sum(each, axis=0, keepdims=True)
        for j in range(LANE_BLOCKS):
            at = k * LANE_BLOCKS + j
            totals_scratch[at : at + 1] = each[:, j * 128 : (j + 1) * 128]

    values = xbc_ref[:, :INNER].astype(f32)
    pairs, from_values, skip_rows = sums_ref[0:8], sums_ref[8:16], sums_ref[16:24]
    scaled_f = scaled_ref[:, :INNER].astype(f32) + scaled_ref[:, INNER:].astype(f32)
    seen_rows = head_sums(scaled_f * seen)
    tail_rows = head_sums(values * back)
    tail_term = tail_rows * left * step
    selector = head_selector(HEAD_ROWS * 2)[:HEAD_ROWS].astype(f32)
    through = jnp.sum(prior * after, axis=0, keepdims=True)
    through = jnp.sum(selector * through, axis=1, keepdims=True) * reach[:, tok - 1 : tok]
    last_extra = jnp.sum(tail_term, axis=1, keepdims=True) + through
    grad_cum = pairs - from_values * step + seen_rows - tail_term
    grad_log = unstacked(dot(stacked(grad_cum), until_ref[...], 1, 1)) + last_extra
    grad_step = from_values + tail_rows * left + decay_rate * grad_log
    grad_pre = grad_step * dt_gate
    dt_out_ref[...] = grad_pre[0:H]
    row, lane = iota((HEAD_ROWS, 128), 0), iota((HEAD_ROWS, 128), 1)
    small = jnp.zeros((HEAD_ROWS, 128), f32)
    for i, each in enumerate((grad_pre, grad_log * step * decay_rate, skip_rows)):
        column = jnp.sum(each, axis=1, keepdims=True)
        small = jnp.where((row < H) & (lane == row + i * H), column, small)
    totals_scratch[SMALL_ROW : SMALL_ROW + 1] = jnp.sum(small, axis=0, keepdims=True)
    totals_ref[...] = pack_totals(totals_scratch[...])


def input_kernel(conv_ref, weight_ref, out_hbm, end_ref, out_ref, sem):
    grad_conv = conv_ref[...]
    tok, channels = grad_conv.shape
    grad_in = weight_ref[K - 1 : K] * grad_conv
    row8 = iota((8, channels), 0)
    for ahead in range(1, K):
        tap = weight_ref[K - 1 - ahead : K - ahead]
        moved = pltpu.roll(grad_conv, tok - ahead, 0)
        last8 = moved[tok - 8 :]
        inside = row8 < 8 - ahead
        grad_in = grad_in + tap * jnp.concatenate([moved[: tok - 8], jnp.where(inside, last8, 0.0)], 0)
    out_ref[...] = grad_in.astype(bf16)
    copy = pltpu.make_async_copy(out_ref, out_hbm, sem)
    copy.start()
    end_ref[...] = grad_in[tok - END_ROWS :]
    copy.wait()


def end_kernel(end_ref, spilled_ref, places_ref, main_hbm, out_hbm, rows_ref, sem):
    end = end_ref[...]
    last = places_ref[places_ref.shape[0] - 8 :][:1, :1]
    fixed = end[END_ROWS - 8 :] + jnp.where(last > 0.5, 0.0, spilled_ref[...])
    rows_ref[...] = jnp.concatenate([end[: END_ROWS - 8], fixed], 0).astype(bf16)
    tok = out_hbm.shape[0]
    copy = pltpu.make_async_copy(rows_ref, out_hbm.at[pl.ds(tok - END_ROWS, END_ROWS)], sem)
    copy.start()
    copy.wait()


def summed(parts):
    large = jnp.sum(parts * jnp.exp(parts[:, SMALL_ROW + 1 : SMALL_ROW + 2]), axis=0)
    small = parts[:, SMALL_ROW : SMALL_ROW + 1] + parts[:, SMALL_ROW + 3 : SMALL_ROW + 4] * (1 / 256.0)
    small = small * jnp.exp(parts[:, SMALL_ROW + 2 : SMALL_ROW + 3])
    return large, jnp.sum(small, axis=0)


def repack_kernel(parts_ref, out_ref):
    large, small = summed(parts_ref[...])
    out_ref[...] = pack_totals(jnp.where(iota(large.shape, 0) == SMALL_ROW, small, large))


def finish_kernel(parts_ref, weight_ref, bias_ref, dt_bias_ref, alog_ref, skip_ref):
    large, small = summed(parts_ref[...])
    for k in range(K + 1):
        for j in range(LANE_BLOCKS):
            at = k * LANE_BLOCKS + j
            if k < K:
                weight_ref[k : k + 1, j * 128 : (j + 1) * 128] = large[at : at + 1]
            else:
                bias_ref[:, j * 128 : (j + 1) * 128] = large[at : at + 1]
    for i, ref in enumerate((dt_bias_ref, alog_ref, skip_ref)):
        ref[...] = small[:, i * H : (i + 1) * H]


def call(kernel, outs, in_specs, out_specs=None, scratch=(), flops=0, limit=16 << 20, aliases=None):
    return pl.pallas_call(
        kernel,
        out_shape=outs,
        in_specs=in_specs,
        out_specs=out_specs or jax.tree.map(lambda _: VMEM, outs),
        scratch_shapes=list(scratch),
        input_output_aliases=aliases or {},
        compiler_params=pltpu.CompilerParams(vmem_limit_bytes=limit),
        cost_estimate=pl.CostEstimate(flops=flops, bytes_accessed=1 << 20, transcendentals=0),
    )


def struct(shape, dtype=f32):
    return jax.ShapeDtypeStruct(shape, dtype)


def from_groups(messages, slabs, size, radix):
    got = []
    for s in range(1, radix):
        message = messages[s - 1 if len(messages) > 1 else 0]
        route = [(p, p - p % (size * radix) + (p + s * size) % (size * radix)) for p in range(slabs)]
        got.append(lax.ppermute(message, "ctx", route))
    return got


def states_from_groups(messages, slabs, size, radix):
    got = from_groups([message.astype(jnp.float16) for message in messages], slabs, size, radix)
    return [each.astype(f32) for each in got]


def stages_of(slabs):
    stages, size = [], 1
    while size < slabs:
        radix = 2 if (slabs // size).bit_length() % 2 == 0 else 4
        stages.append((size, radix))
        size *= radix
    assert size == slabs and len(stages) > 1
    return stages


def everyones(packed, axes, count):
    packed = jnp.broadcast_to(packed.astype(jnp.float16)[None], (count, *packed.shape))
    return lax.all_to_all(packed, axes, 0, 0).astype(f32)


def on_device(xbc_raw, conv_weight, conv_bias, dt_raw, dt_bias, a_log, d_skip, grad_out):
    tok, channels = xbc_raw.shape[1:]
    slabs = lax.axis_size("ctx")
    contexts = lax.axis_size("dp")
    stages = stages_of(slabs)

    raw, cot, dt_rows = xbc_raw[0], grad_out[0], dt_raw[0].T
    until = call(triangle_kernel, struct((tok, tok), bf16), [], flops=10**11)()
    until, bias, heads = call(
        heads_kernel,
        (struct((tok, tok), bf16), struct((1, channels)), struct((3 * HEAD_ROWS, tok))),
        [VMEM] * 5,
        aliases={4: 0},
    )(conv_bias[None], dt_bias[None], a_log[None], d_skip[None], until)
    early_raw, until = lax.optimization_barrier((raw, until))
    halo = lax.ppermute(early_raw[tok - HALO_ROWS :], "ctx", [(i, (i + 1) % slabs) for i in range(slabs)])

    def last_radix(t):
        return stages[t][1] if t == len(stages) - 1 else 0

    def messages(t):
        if last_radix(t):
            return (struct((N + TAIL_ROWS, INNER)),) * (last_radix(t) - 1)
        return (struct((2 * N + TAIL_ROWS, INNER)),)

    state_like = struct((N, INNER))
    logs_like = struct((8, INNER))
    top, xbc, slope, weighted, scaled, tail, rows, logs, places, state, grad, *outgoing = call(
        functools.partial(start_kernel, stages),
        (
            struct((FIX_ROWS, channels)), struct((tok, channels), bf16), struct((tok, channels)), struct((tok, 2 * INNER), bf16),
            struct((tok, 2 * INNER), bf16), struct((tok, INNER)), struct((6 * HEAD_ROWS, tok)),
            logs_like, struct((8 * len(stages) + 16, INNER)), state_like, state_like, *messages(0),
        ),
        [VMEM] * 7,
        scratch=[pltpu.VMEM((HEAD_ROWS, tok), f32)],
        flops=10**11,
    )(raw, cot, conv_weight, bias, dt_rows, heads, until)
    xbc, slope, weighted, factors = call(
        fix_kernel,
        (
            struct((tok, channels), bf16), struct((tok, channels)), struct((tok, 2 * INNER), bf16),
            struct((FIX_ROWS, 2 * INNER + 2 * N), bf16),
        ),
        [VMEM] * 9,
        flops=1_000_000,
        aliases={6: 0, 7: 1, 8: 2},
    )(top, halo, conv_weight, scaled, tail, places, xbc, slope, weighted)

    local, sums = call(
        local_kernel,
        (struct((tok, channels)), struct((3 * HEAD_ROWS, tok))),
        [VMEM] * 4,
        flops=10**11,
    )(xbc, cot, rows, logs)

    carried = ()
    for t, (size, radix) in enumerate(stages):
        got = states_from_groups(outgoing, slabs, size, radix)
        if t == 0:
            got, local, sums = lax.optimization_barrier((got, local, sums))
            carried = [factors] + from_groups([factors], slabs, size, radix)
        if t == len(stages) - 1:
            break
        last = last_radix(t + 1)
        outs = (logs_like, state_like, state_like) + (() if last else (state_like, state_like))
        logs, *outgoing = call(
            functools.partial(merge_kernel, t, radix, last),
            outs + messages(t + 1),
            [VMEM] * (4 + len(got) + len(carried)),
            flops=1_000_000,
        )(state, grad, logs, places, *got, *carried)
        carried, outgoing = outgoing[:2], outgoing[2:]
        if not last:
            (state, grad), outgoing = outgoing[:2], outgoing[2:]

    grad_conv, grad_dt, packed, spill = call(
        functools.partial(totals_kernel, len(stages) - 1, radix),
        (struct((tok, channels)), struct((H, tok)), struct((TOTAL_ROWS, 128)), struct((8, channels))),
        [VMEM] * (14 + len(got) + len(carried)),
        scratch=[pltpu.VMEM((TOTAL_ROWS, 128), f32)],
        flops=200_000_000,
    )(raw, halo, xbc, slope, scaled, weighted, tail, rows, local, sums, logs, places, until, conv_weight, *got, *carried)

    spilled = lax.ppermute(spill, "ctx", [((i + 1) % slabs, i) for i in range(slabs)])
    if slabs * contexts <= 64:
        parts = everyones(packed, ("ctx", "dp"), slabs * contexts)
    else:
        packed = call(repack_kernel, struct((TOTAL_ROWS, 128)), [VMEM])(everyones(packed, "ctx", slabs))
        parts = everyones(packed, "dp", contexts)

    grad_main, end = call(
        input_kernel,
        (struct((tok, channels), bf16), struct((END_ROWS, channels))),
        [VMEM] * 2,
        (HBM, VMEM),
        [pltpu.VMEM((tok, channels), bf16), pltpu.SemaphoreType.DMA],
        flops=1_000_000,
    )(grad_conv, conv_weight)
    grad_input = call(
        end_kernel,
        struct((tok, channels), bf16),
        [VMEM] * 3 + [HBM],
        HBM,
        [pltpu.VMEM((END_ROWS, channels), bf16), pltpu.SemaphoreType.DMA],
        aliases={3: 0},
    )(end, spilled, places, grad_main)

    grad_weight, grad_bias, *small = call(
        finish_kernel,
        (struct((K, channels)), struct((1, channels)), struct((1, H)), struct((1, H)), struct((1, H))),
        [VMEM],
    )(parts)
    return (grad_input[None], grad_dt.T[None], grad_weight, grad_bias[0], *(each[0] for each in small))


def solution(mesh):
    in_specs = (
        P("dp", "ctx", None),
        P(),
        P(),
        P("dp", "ctx", None),
        P(),
        P(),
        P(),
        P("dp", "ctx", None),
    )
    out_specs = (P("dp", "ctx", None), P("dp", "ctx", None), P(), P(), P(), P(), P())
    return jax.shard_map(
        on_device, mesh=mesh, in_specs=in_specs, out_specs=out_specs, check_vma=False
    )
```

```python
import functools

import jax
import jax.numpy as jnp
from jax import lax
from jax.experimental import pallas as pl
from jax.experimental.pallas import tpu as pltpu
from jax.sharding import PartitionSpec as P

H = 4
P_SIZE = 64
N = 128
K = 4
INNER = H * P_SIZE
HEAD_ROWS = 8
TAIL_ROWS = 8
HALO_ROWS = 16
FIX_ROWS = 16
END_ROWS = 16
LANE_BLOCKS = (INNER + 2 * N) // 128
SMALL_ROW = (K + 1) * LANE_BLOCKS
TOTAL_ROWS = 24

f32 = jnp.float32
bf16 = jnp.bfloat16

VMEM = pl.BlockSpec(memory_space=pltpu.VMEM)
HBM = pl.BlockSpec(memory_space=pltpu.HBM)


def dot(a, b, a_dim=1, b_dim=0):
    return lax.dot_general(a, b, (((a_dim,), (b_dim,)), ((), ())), preferred_element_type=f32)


def split2(x):
    high = x.astype(bf16)
    return high, (x - high.astype(f32)).astype(bf16)


def split3(x):
    high = x.astype(bf16).astype(f32)
    rest = x - high
    middle = rest.astype(bf16).astype(f32)
    return high, middle, rest - middle


def iota(shape, dim):
    return lax.broadcasted_iota(jnp.int32, shape, dim)


def stacked(rows):
    return jnp.concatenate([*split3(rows), jnp.zeros_like(rows)], 0).astype(bf16)


def unstacked(rows):
    return rows[0:8] + rows[8:16] + rows[16:24]


def head_selector(rows):
    shape = (rows, INNER)
    return jnp.where(iota(shape, 1) // P_SIZE == iota(shape, 0) % HEAD_ROWS, 1.0, 0.0).astype(bf16)


def over_channels(rows):
    return dot(stacked(rows), head_selector(4 * HEAD_ROWS), 0, 0)


def head_sums(x):
    high, low = split2(x)
    selector = head_selector(HEAD_ROWS * 2)
    return (dot(selector, high, 1, 1) + dot(selector, low, 1, 1))[:HEAD_ROWS]


def by_head(ref, width):
    row = iota((HEAD_ROWS, width), 0)
    out = jnp.zeros((HEAD_ROWS, width), f32)
    for h in range(H):
        out = jnp.where(row == h, ref[:, h : h + 1], out)
    return out


def shifted_down(x, first, count):
    moved = pltpu.roll(x, count, 0)
    top = jnp.where(iota(first.shape, 0) < count, pltpu.roll(first, count, 0), moved[:8])
    return jnp.concatenate([top, moved[8:]], 0)


def quantized_log(size):
    return jnp.log(jnp.maximum(size, 1e-30)).astype(bf16).astype(f32)


def scaled_columns(x):
    log_size = quantized_log(jnp.max(jnp.abs(x), axis=0, keepdims=True))
    return x * jnp.exp(-log_size), log_size


def write_messages(msg_refs, state, grad, log_total, place, radix):
    row = iota((TAIL_ROWS, INNER), 0)
    high, middle, low = split3(log_total)
    tail = jnp.where(row == 4, high, jnp.where(row == 5, middle * 256.0, jnp.where(row == 6, low * 65536.0, 0.0)))
    state, state_size = scaled_columns(state)
    grad, grad_size = scaled_columns(grad)
    if radix:
        for s, msg_ref in enumerate(msg_refs, 1):
            on = place + s < radix
            msg_ref[0:N] = jnp.where(on, state, grad)
            msg_ref[N : N + TAIL_ROWS] = jnp.where(row == 0, jnp.where(on, state_size, grad_size), tail)
    else:
        (msg_ref,) = msg_refs
        msg_ref[0:N] = state
        msg_ref[N : 2 * N] = grad
        msg_ref[2 * N : 2 * N + TAIL_ROWS] = jnp.where(row == 0, state_size, jnp.where(row == 1, grad_size, tail))


def message_log(got_ref):
    rows = got_ref.shape[0] - TAIL_ROWS
    tail = got_ref[rows : rows + 8]
    return tail[4:5] + tail[5:6] * (1 / 256.0) + tail[6:7] * (1 / 65536.0)


def message_block(got_ref, which=0):
    rows = got_ref.shape[0] - TAIL_ROWS
    return got_ref[which * N : (which + 1) * N] * jnp.exp(got_ref[rows + which : rows + which + 1])


def chained(blocks, logs, used):
    total, log_sum = 0.0, 0.0
    for block, log, use in zip(blocks, logs, used):
        total = total + jnp.where(use, jnp.exp(log_sum) * block, 0.0)
        log_sum = log_sum + jnp.where(use, log, 0.0)
    return total, log_sum


def pack_totals(x):
    row = iota(x.shape, 0)
    large = jnp.where(row < SMALL_ROW, x, 0.0)
    large_size = quantized_log(jnp.max(jnp.abs(large), axis=0, keepdims=True))
    small = x[SMALL_ROW : SMALL_ROW + 1]
    small_size = quantized_log(jnp.abs(small))
    small = small * jnp.exp(-small_size)
    small_high = small.astype(bf16).astype(f32)
    out = jnp.where(row == SMALL_ROW, small_high, large * jnp.exp(-large_size))
    out = jnp.where(row == SMALL_ROW + 3, (small - small_high) * 256.0, out)
    return jnp.where(row == SMALL_ROW + 1, large_size, jnp.where(row == SMALL_ROW + 2, small_size, out))


def triangle_kernel(until_ref):
    shape = until_ref.shape
    until_ref[...] = jnp.where(iota(shape, 0) <= iota(shape, 1), 1.0, 0.0).astype(bf16)


def heads_kernel(bias_ref, dt_bias_ref, alog_ref, skip_ref, until_in, until_ref, bias_out, heads_ref):
    bias_out[...] = bias_ref[...]
    for i, ref in enumerate((dt_bias_ref, alog_ref, skip_ref)):
        heads_ref[8 * i : 8 * i + 8] = by_head(ref, until_ref.shape[1])


def mask_first(x):
    top = jnp.where(iota((FIX_ROWS, x.shape[1]), 0) < K - 1, 0.0, x[:FIX_ROWS].astype(f32))
    return jnp.concatenate([top.astype(x.dtype), x[FIX_ROWS:]], 0)


def start_kernel(
    stages, raw_ref, cot_ref, weight_ref, bias_ref, dt_ref, heads_ref, until_ref,
    pre_ref, xbc_ref, weighted_ref, scaled_ref, tail_ref, rows_ref, logs_ref, places_ref, state_ref, grad_ref, msg_ref, dt8_ref,
):
    tok = raw_ref.shape[0]
    place = lax.axis_index("ctx")
    for t, (size, radix) in enumerate(stages):
        places_ref[8 * t : 8 * t + 8] = jnp.full((8, INNER), lax.rem(lax.div(place, size), radix), jnp.int32).astype(f32)
    at = 8 * len(stages)
    slabs = stages[-1][0] * stages[-1][1]
    places_ref[at : at + 8] = jnp.full((8, INNER), jnp.where(place == 0, 1, 0), jnp.int32).astype(f32)
    places_ref[at + 8 : at + 16] = jnp.full((8, INNER), jnp.where(place == slabs - 1, 1, 0), jnp.int32).astype(f32)
    dt8_ref[...] = jnp.zeros_like(dt8_ref)
    dt8_ref[0:H] = dt_ref[...]
    dt_pre = dt8_ref[...] + heads_ref[0:8]
    step = jnp.maximum(dt_pre, 0.0) + jnp.log1p(jnp.exp(-jnp.abs(dt_pre)))
    real = iota((HEAD_ROWS, tok), 0) < H
    decay_rate = jnp.where(real, -jnp.exp(heads_ref[8:16]), 0.0)
    cum = unstacked(dot(stacked(step * decay_rate), until_ref[...]))
    left = jnp.exp(cum[:, tok - 1 : tok] - cum)
    reach = jnp.exp(cum)
    rows_ref[0:8] = cum
    rows_ref[8:16] = step
    rows_ref[16:24] = left
    rows_ref[24:32] = reach
    rows_ref[32:40] = 1.0 / (1.0 + jnp.exp(-dt_pre))
    rows_ref[40:48] = decay_rate
    tail = over_channels(left * step)
    tail_ref[...] = tail
    log_total = over_channels(cum)[tok - 1 : tok]
    skip = over_channels(heads_ref[16:24])[0:1]
    row = iota((8, INNER), 0)
    logs_ref[...] = jnp.where(row == 2, log_total, jnp.where(row == 3, skip, 0.0))
    scaled = jnp.concatenate(split2(cot_ref[...].astype(f32) * over_channels(reach)), 1)
    scaled_ref[...] = scaled

    raw = raw_ref[...].astype(f32)
    zeros = jnp.zeros((8, raw.shape[1]), f32)
    pre = bias_ref[...] + weight_ref[K - 1 : K] * raw
    for back in range(1, K):
        pre = pre + weight_ref[K - 1 - back : K - back] * shifted_down(raw, zeros, back)
    pre_ref[...] = pre
    gate = 1.0 / (1.0 + jnp.exp(-pre))
    xbc = (pre * gate).astype(bf16)
    xbc_ref[...] = xbc
    weighted = jnp.concatenate(split2(xbc[:, :INNER].astype(f32) * tail), 1)
    weighted_ref[...] = weighted
    later = mask_first(xbc[:, INNER:])
    state = dot(later[:, :N], weighted, 0, 0)
    state = state[:, :INNER] + state[:, INNER:]
    grad = dot(later[:, N:], scaled, 0, 0)
    grad = grad[:, :INNER] + grad[:, INNER:]
    state_ref[...] = state
    grad_ref[...] = grad
    write_messages((msg_ref,), state, grad, log_total, places_ref[0:1], 0)


def real_halo(halo_ref, places_ref):
    first = places_ref[places_ref.shape[0] - 16 :][:1, :1]
    return jnp.where(first > 0.5, 0.0, halo_ref[HALO_ROWS - 8 :].astype(f32))


def fix_kernel(
    halo_ref, weight_ref, scaled_ref, tail_ref, places_ref, pre_in, xbc_in, weighted_in,
    pre_ref, xbc_ref, weighted_ref, factors_ref,
):
    halo = real_halo(halo_ref, places_ref)
    top = pre_in[0:8]
    for back in range(1, K):
        tap = weight_ref[K - 1 - back : K - back]
        top = top + jnp.where(iota(top.shape, 0) < back, tap * pltpu.roll(halo, back, 0), 0.0)
    pre = jnp.concatenate([top, pre_in[8:FIX_ROWS]], 0)
    pre_ref[0:FIX_ROWS] = pre
    gate = 1.0 / (1.0 + jnp.exp(-pre))
    xbc = (pre * gate).astype(bf16)
    xbc_ref[0:FIX_ROWS] = xbc
    xbc = xbc.astype(f32)
    weighted = jnp.concatenate([each.astype(f32) for each in split2(xbc[:, :INNER] * tail_ref[0:FIX_ROWS])], 1)
    weighted_ref[0:FIX_ROWS] = weighted.astype(bf16)
    scaled = scaled_ref[0:FIX_ROWS].astype(f32)

    def placed(low, high):
        row = iota(low.shape, 0)
        moved = jnp.concatenate([high[8:], high[:8]], 0)
        return jnp.where(row < K - 1, low, jnp.where((row >= 8) & (row < 8 + K - 1), moved, 0.0)).astype(bf16)

    zero = jnp.zeros((FIX_ROWS, N), f32)
    factors_ref[:, : 2 * INNER] = placed(weighted, scaled)
    factors_ref[:, 2 * INNER : 2 * INNER + N] = placed(xbc[:, INNER : INNER + N], zero)
    factors_ref[:, 2 * INNER + N :] = placed(zero, xbc[:, INNER + N :])


def first_parts(factors_ref):
    both = dot(factors_ref[:, 2 * INNER :], factors_ref[:, : 2 * INNER], 0, 0)
    both = both[:, :INNER] + both[:, INNER:]
    return both[:N], both[N:]


def merge_kernel(t, radix, next_radix, state_ref, grad_ref, logs_ref, places_ref, *refs):
    got, refs = refs[: radix - 1], refs[radix - 1 :]
    prior = after = 0.0
    if t > 0:
        prior, after = refs[0][...], refs[1][...]
        refs = refs[2:]
    else:
        parts, refs = [first_parts(ref) for ref in refs[: radix - 1]], refs[radix - 1 :]
    logs_out, prior_out, after_out, *refs = refs
    if not next_radix:
        state_out, grad_out, *refs = refs
    place = places_ref[8 * t : 8 * t + 1]
    log_prior, log_after, log_total = logs_ref[0:1], logs_ref[1:2], logs_ref[2:3]
    states = [message_block(ref, 0) for ref in got]
    grads = [message_block(ref, 1) for ref in got]
    logs = [message_log(ref) for ref in got]
    own_state, own_grad = state_ref[...], grad_ref[...]
    if t == 0:
        states = [each + part[0] for each, part in zip(states, parts)]
        grads = [each + part[1] for each, part in zip(grads, parts)]
    earlier = [s <= place for s in range(1, radix)]
    later = [s > place for s in range(1, radix)]
    before, log_before = chained(states, logs, earlier)
    beyond, log_beyond = chained(grads[::-1], logs[::-1], later[::-1])
    above, _ = chained(states, logs, later)
    below, _ = chained(grads[::-1], logs[::-1], earlier[::-1])
    mine = jnp.exp(log_total)
    state = above + jnp.exp(log_beyond) * (own_state + mine * before)
    grad = below + jnp.exp(log_before) * (own_grad + mine * beyond)
    prior_out[...] = prior + jnp.exp(log_prior) * before
    after_out[...] = after + jnp.exp(log_after) * beyond
    log_prior = log_prior + log_before
    log_after = log_after + log_beyond
    log_total = log_total + log_before + log_beyond
    row = iota((8, INNER), 0)
    logs_out[...] = jnp.where(row == 0, log_prior, jnp.where(row == 1, log_after, jnp.where(row == 2, log_total, 0.0)))
    if not next_radix:
        state_out[...] = state
        grad_out[...] = grad
    write_messages(refs, state, grad, log_total, places_ref[8 * t + 8 : 8 * t + 9], next_radix)


def local_kernel(
    xbc_ref, cot_ref, rows_ref, logs_ref, raw_ref, halo_ref, places_ref, scaled_ref, until_ref, pre_ref, factors_ref, state_in, grad_in,
    local_ref, sums_ref, weights_ref, moved_ref, slope_ref, state_ref, grad_ref,
):
    state, grad = first_parts(factors_ref)
    state_ref[...] = state_in[...] + state
    grad_ref[...] = grad_in[...] + grad
    pre = pre_ref[...]
    sigmoid = 1.0 / (1.0 + jnp.exp(-pre))
    slope_ref[...] = sigmoid * (1.0 + pre * (1.0 - sigmoid))
    tok = xbc_ref.shape[0]
    cot = cot_ref[...]
    values = xbc_ref[:, :INNER]
    b_proj = xbc_ref[:, INNER : INNER + N]
    c_proj = xbc_ref[:, INNER + N :]
    cum, step = rows_ref[0:8], rows_ref[8:16]
    step_wide = over_channels(step)
    values_f = values.astype(f32)
    cot_f = cot.astype(f32)
    stepped = split2(values_f * step_wide)
    gram = dot(b_proj, c_proj, 1, 1)
    reached = iota((tok, tok), 0) <= iota((tok, tok), 1)
    pieces = stacked(cum)
    piece_head = iota((4 * HEAD_ROWS, tok), 0) % HEAD_ROWS
    dgram = jnp.zeros((tok, tok), f32)
    grads, sums = [], []
    for h in range(H):
        of = slice(h * P_SIZE, (h + 1) * P_SIZE)
        column = dot(pieces, jnp.where(piece_head == h, 1.0, 0.0).astype(bf16), 0, 0)
        within = jnp.exp(jnp.where(reached, cum[h : h + 1] - column, -1e30))
        cot_h = cot[:, of]
        high, low = split2(gram * within)
        grads.append(dot(high, cot_h) + dot(low, cot_h))
        dmix = dot(stepped[0][:, of], cot_h, 1, 1) + dot(stepped[1][:, of], cot_h, 1, 1)
        dmix = dmix * within
        dgram = dgram + dmix
        sums.append(jnp.sum(dmix * gram, axis=0, keepdims=True))
    grad_stepped = jnp.concatenate(grads, 1)
    local_ref[:, :INNER] = grad_stepped * step_wide + logs_ref[3:4] * cot_f
    high, low = split2(dgram)
    local_ref[:, INNER : INNER + N] = dot(high, c_proj) + dot(low, c_proj)
    local_ref[:, INNER + N :] = dot(high, b_proj, 0, 0) + dot(low, b_proj, 0, 0)
    row = iota((HEAD_ROWS, tok), 0)
    pairs = jnp.zeros((HEAD_ROWS, tok), f32)
    for h in range(H):
        pairs = jnp.where(row == h, sums[h], pairs)
    left, gate, decay_rate = rows_ref[16:24], rows_ref[32:40], rows_ref[40:48]
    from_values = head_sums(values_f * grad_stepped)
    skip_rows = head_sums(values_f * cot_f)
    base = pairs - from_values * step
    sums_ref[0:8] = base
    sums_ref[8:16] = from_values

    bias_weight = decay_rate * unstacked(dot(stacked(gate), until_ref[...]))
    cum_last, bias_last = cum[:, tok - 1 : tok], bias_weight[:, tok - 1 : tok]
    tail = left * step
    scaled_f = scaled_ref[:, :INNER].astype(f32) + scaled_ref[:, INNER:].astype(f32)
    weights_ref[:, :INNER] = scaled_f * over_channels(cum)
    weights_ref[:, INNER : 2 * INNER] = values_f * over_channels(tail * (cum_last - cum))
    weights_ref[:, 2 * INNER : 3 * INNER] = scaled_f * over_channels(bias_weight)
    weights_ref[:, 3 * INNER :] = values_f * over_channels(left * gate + tail * (bias_last - bias_weight))
    lane = iota((HEAD_ROWS, tok), 1)
    fixed = jnp.zeros((HEAD_ROWS, tok), f32)
    for i, column in enumerate((
        jnp.sum(from_values * gate + base * bias_weight, axis=1, keepdims=True),
        jnp.sum(base * cum, axis=1, keepdims=True),
        jnp.sum(skip_rows, axis=1, keepdims=True),
        bias_last, cum_last,
    )):
        fixed = jnp.where(lane == i, column, fixed)
    sums_ref[16:24] = fixed
    raw = raw_ref[...].astype(f32)
    halo = real_halo(halo_ref, places_ref)
    for back in range(1, K):
        moved_ref[(back - 1) * tok : back * tok] = shifted_down(raw, halo, back)


def totals_kernel(
    t, radix, raw_ref, moved_ref, xbc_ref, slope_ref, scaled_ref, weighted_ref, tail_ref, rows_ref, local_ref, sums_ref, weights_ref,
    logs_ref, places_ref, weight_ref, *refs
):
    got, refs = refs[: radix - 1], refs[radix - 1 :]
    prior = after = 0.0
    if t > 0:
        prior, after = refs[0][...], refs[1][...]
        refs = refs[2:]
    conv_ref, states_ref, totals_ref, spill_ref, totals_scratch = refs
    tok = raw_ref.shape[0]
    place = places_ref[8 * t : 8 * t + 1]
    blocks = [message_block(ref) for ref in got]
    logs = [message_log(ref) for ref in got]
    before, _ = chained(blocks, logs, [s <= place for s in range(1, radix)])
    beyond, _ = chained(blocks[::-1], logs[::-1], [s > place for s in range(radix - 1, 0, -1)])
    prior = prior + jnp.exp(logs_ref[0:1]) * before
    after = after + jnp.exp(logs_ref[1:2]) * beyond

    b_proj = xbc_ref[:, INNER : INNER + N]
    c_proj = xbc_ref[:, INNER + N :]
    prior2 = jnp.concatenate(split2(prior), 0)
    after2 = jnp.concatenate(split2(after), 0)
    seen = dot(jnp.concatenate([c_proj, c_proj], 1), prior2)
    back = dot(jnp.concatenate([b_proj, b_proj], 1), after2)
    grad_c = dot(scaled_ref[:, :INNER], prior2, 1, 1)
    grad_c = grad_c[:, :N] + grad_c[:, N:] + dot(scaled_ref[:, INNER:], prior2[:N], 1, 1)
    grad_b = dot(weighted_ref[:, :INNER], after2, 1, 1)
    grad_b = grad_b[:, :N] + grad_b[:, N:] + dot(weighted_ref[:, INNER:], after2[:N], 1, 1)
    grad_low = (local_ref[...] + jnp.concatenate([tail_ref[...] * back, grad_b, grad_c], 1)).astype(bf16)
    grad_conv = grad_low.astype(f32) * slope_ref[...]
    conv_ref[...] = grad_conv
    top = grad_conv[:8]
    spill = jnp.zeros_like(top)
    for ahead in range(1, K):
        tap = weight_ref[K - 1 - ahead : K - ahead]
        spill = spill + tap * jnp.where(iota(top.shape, 0) < 8 - ahead, 0.0, pltpu.roll(top, 8 - ahead, 0))
    spill_ref[...] = spill

    sums = [grad_conv * moved_ref[back * tok : (back + 1) * tok] for back in range(K - 2, -1, -1)]
    sums += [grad_conv * raw_ref[...].astype(f32), grad_conv]
    totals_scratch[...] = jnp.zeros_like(totals_scratch)
    for k, each in enumerate(sums):
        each = jnp.sum(each, axis=0, keepdims=True)
        for j in range(LANE_BLOCKS):
            at = k * LANE_BLOCKS + j
            totals_scratch[at : at + 1] = each[:, j * 128 : (j + 1) * 128]

    states_ref[:tok, :INNER] = seen
    states_ref[:tok, INNER:] = back
    through = jnp.sum(prior * after, axis=0, keepdims=True)
    grad_bias = jnp.sum(seen * weights_ref[:, 2 * INNER : 3 * INNER] + back * weights_ref[:, 3 * INNER :], axis=0, keepdims=True)
    grad_alog = jnp.sum(seen * weights_ref[:, :INNER] + back * weights_ref[:, INNER : 2 * INNER], axis=0, keepdims=True)
    selector = head_selector(HEAD_ROWS * 2)[:HEAD_ROWS].astype(f32)
    grad_bias, grad_alog, through = (
        jnp.sum(selector * each, axis=1, keepdims=True) for each in (grad_bias, grad_alog, through)
    )
    through = through * rows_ref[24:32][:, tok - 1 : tok]
    states_ref[tok:] = jnp.broadcast_to(through, (HEAD_ROWS, 2 * INNER))
    fixed = sums_ref[16:24]
    row, lane = iota((HEAD_ROWS, 128), 0), iota((HEAD_ROWS, 128), 1)
    small = jnp.zeros((HEAD_ROWS, 128), f32)
    for i, column in enumerate((
        fixed[:, 0:1] + grad_bias + through * fixed[:, 3:4],
        fixed[:, 1:2] + grad_alog + through * fixed[:, 4:5],
        fixed[:, 2:3],
    )):
        small = jnp.where((row < H) & (lane == row + i * H), column, small)
    totals_scratch[SMALL_ROW : SMALL_ROW + 1] = jnp.sum(small, axis=0, keepdims=True)
    totals_ref[...] = pack_totals(totals_scratch[...])


def input_kernel(
    conv_ref, weight_ref, states_ref, xbc_ref, scaled_ref, rows_ref, sums_ref, until_ref, out_hbm, dt_out_ref, end_ref, out_ref, sem
):
    grad_conv = conv_ref[...]
    tok, channels = grad_conv.shape
    grad_in = weight_ref[K - 1 : K] * grad_conv
    row8 = iota((8, channels), 0)
    for ahead in range(1, K):
        tap = weight_ref[K - 1 - ahead : K - ahead]
        moved = pltpu.roll(grad_conv, tok - ahead, 0)
        last8 = moved[tok - 8 :]
        inside = row8 < 8 - ahead
        grad_in = grad_in + tap * jnp.concatenate([moved[: tok - 8], jnp.where(inside, last8, 0.0)], 0)
    out_ref[...] = grad_in.astype(bf16)
    copy = pltpu.make_async_copy(out_ref, out_hbm, sem)
    copy.start()
    end_ref[...] = grad_in[tok - END_ROWS :]

    step, left, gate, decay_rate = rows_ref[8:16], rows_ref[16:24], rows_ref[32:40], rows_ref[40:48]
    scaled_f = scaled_ref[:, :INNER].astype(f32) + scaled_ref[:, INNER:].astype(f32)
    seen_rows = head_sums(scaled_f * states_ref[:tok, :INNER])
    tail_rows = head_sums(xbc_ref[:, :INNER].astype(f32) * states_ref[:tok, INNER:])
    tail_term = tail_rows * left * step
    last_extra = jnp.sum(tail_term, axis=1, keepdims=True) + states_ref[tok:][:, :1]
    grad_cum = sums_ref[0:8] + seen_rows - tail_term
    grad_log = unstacked(dot(stacked(grad_cum), until_ref[...], 1, 1)) + last_extra
    grad_step = sums_ref[8:16] + tail_rows * left + decay_rate * grad_log
    dt_out_ref[...] = (grad_step * gate)[0:H]
    copy.wait()


def end_kernel(end_ref, spilled_ref, places_ref, main_hbm, out_hbm, rows_ref, sem):
    end = end_ref[...]
    last = places_ref[places_ref.shape[0] - 8 :][:1, :1]
    fixed = end[END_ROWS - 8 :] + jnp.where(last > 0.5, 0.0, spilled_ref[...])
    rows_ref[...] = jnp.concatenate([end[: END_ROWS - 8], fixed], 0).astype(bf16)
    tok = out_hbm.shape[0]
    copy = pltpu.make_async_copy(rows_ref, out_hbm.at[pl.ds(tok - END_ROWS, END_ROWS)], sem)
    copy.start()
    copy.wait()


def summed(parts):
    large = jnp.sum(parts * jnp.exp(parts[:, SMALL_ROW + 1 : SMALL_ROW + 2]), axis=0)
    small = parts[:, SMALL_ROW : SMALL_ROW + 1] + parts[:, SMALL_ROW + 3 : SMALL_ROW + 4] * (1 / 256.0)
    small = small * jnp.exp(parts[:, SMALL_ROW + 2 : SMALL_ROW + 3])
    return large, jnp.sum(small, axis=0)


def repack_kernel(parts_ref, out_ref):
    large, small = summed(parts_ref[...])
    out_ref[...] = pack_totals(jnp.where(iota(large.shape, 0) == SMALL_ROW, small, large))


def finish_kernel(parts_ref, weight_ref, bias_ref, dt_bias_ref, alog_ref, skip_ref):
    large, small = summed(parts_ref[...])
    for k in range(K + 1):
        for j in range(LANE_BLOCKS):
            at = k * LANE_BLOCKS + j
            if k < K:
                weight_ref[k : k + 1, j * 128 : (j + 1) * 128] = large[at : at + 1]
            else:
                bias_ref[:, j * 128 : (j + 1) * 128] = large[at : at + 1]
    for i, ref in enumerate((dt_bias_ref, alog_ref, skip_ref)):
        ref[...] = small[:, i * H : (i + 1) * H]


def call(kernel, outs, in_specs, out_specs=None, scratch=(), flops=0, limit=16 << 20, aliases=None):
    return pl.pallas_call(
        kernel,
        out_shape=outs,
        in_specs=in_specs,
        out_specs=out_specs or jax.tree.map(lambda _: VMEM, outs),
        scratch_shapes=list(scratch),
        input_output_aliases=aliases or {},
        compiler_params=pltpu.CompilerParams(vmem_limit_bytes=limit),
        cost_estimate=pl.CostEstimate(flops=flops, bytes_accessed=1 << 20, transcendentals=0),
    )


def struct(shape, dtype=f32):
    return jax.ShapeDtypeStruct(shape, dtype)


def from_groups(messages, slabs, size, radix):
    got = []
    for s in range(1, radix):
        message = messages[s - 1 if len(messages) > 1 else 0]
        route = [(p, p - p % (size * radix) + (p + s * size) % (size * radix)) for p in range(slabs)]
        got.append(lax.ppermute(message, "ctx", route))
    return got


def states_from_groups(messages, slabs, size, radix):
    got = from_groups([message.astype(jnp.float16) for message in messages], slabs, size, radix)
    return [each.astype(f32) for each in got]


def stages_of(slabs):
    stages, size = [], 1
    while size < slabs:
        radix = 2 if (slabs // size).bit_length() % 2 == 0 else 4
        stages.append((size, radix))
        size *= radix
    assert size == slabs and len(stages) > 1
    return stages


def everyones(packed, axes, count):
    packed = jnp.broadcast_to(packed.astype(jnp.float16)[None], (count, *packed.shape))
    return lax.all_to_all(packed, axes, 0, 0).astype(f32)


def on_device(xbc_raw, conv_weight, conv_bias, dt_raw, dt_bias, a_log, d_skip, grad_out):
    tok, channels = xbc_raw.shape[1:]
    slabs = lax.axis_size("ctx")
    contexts = lax.axis_size("dp")
    stages = stages_of(slabs)

    raw, cot, dt_rows = xbc_raw[0], grad_out[0], dt_raw[0].T
    until = call(triangle_kernel, struct((tok, tok), bf16), [], flops=10**11)()
    until, bias, heads = call(
        heads_kernel,
        (struct((tok, tok), bf16), struct((1, channels)), struct((3 * HEAD_ROWS, tok))),
        [VMEM] * 5,
        aliases={4: 0},
    )(conv_bias[None], dt_bias[None], a_log[None], d_skip[None], until)
    early_raw, until = lax.optimization_barrier((raw, until))
    halo = lax.ppermute(early_raw[tok - HALO_ROWS :], "ctx", [(i, (i + 1) % slabs) for i in range(slabs)])

    def last_radix(t):
        return stages[t][1] if t == len(stages) - 1 else 0

    def messages(t):
        if last_radix(t):
            return (struct((N + TAIL_ROWS, INNER)),) * (last_radix(t) - 1)
        return (struct((2 * N + TAIL_ROWS, INNER)),)

    state_like = struct((N, INNER))
    logs_like = struct((8, INNER))
    pre, xbc, weighted, scaled, tail, rows, logs, places, state, grad, *outgoing = call(
        functools.partial(start_kernel, stages),
        (
            struct((tok, channels)), struct((tok, channels), bf16), struct((tok, 2 * INNER), bf16),
            struct((tok, 2 * INNER), bf16), struct((tok, INNER)), struct((6 * HEAD_ROWS, tok)),
            logs_like, struct((8 * len(stages) + 16, INNER)), state_like, state_like, *messages(0),
        ),
        [VMEM] * 7,
        scratch=[pltpu.VMEM((HEAD_ROWS, tok), f32)],
        flops=10**11,
    )(raw, cot, conv_weight, bias, dt_rows, heads, until)
    pre, xbc, weighted, factors = call(
        fix_kernel,
        (
            struct((tok, channels)), struct((tok, channels), bf16), struct((tok, 2 * INNER), bf16),
            struct((FIX_ROWS, 2 * INNER + 2 * N), bf16),
        ),
        [VMEM] * 8,
        flops=1_000_000,
        aliases={5: 0, 6: 1, 7: 2},
    )(halo, conv_weight, scaled, tail, places, pre, xbc, weighted)

    local, sums, weights, moved, slope, state, grad = call(
        local_kernel,
        (
            struct((tok, channels)), struct((3 * HEAD_ROWS, tok)), struct((tok, 4 * INNER)), struct(((K - 1) * tok, channels)),
            struct((tok, channels)), state_like, state_like,
        ),
        [VMEM] * 13,
        flops=10**11,
        aliases={11: 5, 12: 6},
    )(xbc, cot, rows, logs, raw, halo, places, scaled, until, pre, factors, state, grad)

    carried = ()
    for t, (size, radix) in enumerate(stages):
        got = states_from_groups(outgoing, slabs, size, radix)
        if t == 0:
            got, local, sums, weights, moved, slope = lax.optimization_barrier((got, local, sums, weights, moved, slope))
            carried = from_groups([factors], slabs, size, radix)
        if t == len(stages) - 1:
            break
        last = last_radix(t + 1)
        outs = (logs_like, state_like, state_like) + (() if last else (state_like, state_like))
        logs, *outgoing = call(
            functools.partial(merge_kernel, t, radix, last),
            outs + messages(t + 1),
            [VMEM] * (4 + len(got) + len(carried)),
            flops=1_000_000,
        )(state, grad, logs, places, *got, *carried)
        carried, outgoing = outgoing[:2], outgoing[2:]
        if not last:
            (state, grad), outgoing = outgoing[:2], outgoing[2:]

    grad_conv, states, packed, spill = call(
        functools.partial(totals_kernel, len(stages) - 1, radix),
        (struct((tok, channels)), struct((tok + HEAD_ROWS, 2 * INNER)), struct((TOTAL_ROWS, 128)), struct((8, channels))),
        [VMEM] * (14 + len(got) + len(carried)),
        scratch=[pltpu.VMEM((TOTAL_ROWS, 128), f32)],
        flops=200_000_000,
    )(raw, moved, xbc, slope, scaled, weighted, tail, rows, local, sums, weights, logs, places, conv_weight, *got, *carried)

    spilled = lax.ppermute(spill, "ctx", [((i + 1) % slabs, i) for i in range(slabs)])
    if slabs * contexts <= 64:
        parts = everyones(packed, ("ctx", "dp"), slabs * contexts)
    else:
        packed = call(repack_kernel, struct((TOTAL_ROWS, 128)), [VMEM])(everyones(packed, "ctx", slabs))
        parts = everyones(packed, "dp", contexts)

    grad_main, grad_dt, end = call(
        input_kernel,
        (struct((tok, channels), bf16), struct((H, tok)), struct((END_ROWS, channels))),
        [VMEM] * 8,
        (HBM, VMEM, VMEM),
        [pltpu.VMEM((tok, channels), bf16), pltpu.SemaphoreType.DMA],
        flops=1_000_000,
    )(grad_conv, conv_weight, states, xbc, scaled, rows, sums, until)
    grad_input = call(
        end_kernel,
        struct((tok, channels), bf16),
        [VMEM] * 3 + [HBM],
        HBM,
        [pltpu.VMEM((END_ROWS, channels), bf16), pltpu.SemaphoreType.DMA],
        aliases={3: 0},
    )(end, spilled, places, grad_main)

    grad_weight, grad_bias, *small = call(
        finish_kernel,
        (struct((K, channels)), struct((1, channels)), struct((1, H)), struct((1, H)), struct((1, H))),
        [VMEM],
    )(parts)
    return (grad_input[None], grad_dt.T[None], grad_weight, grad_bias[0], *(each[0] for each in small))


def solution(mesh):
    in_specs = (
        P("dp", "ctx", None),
        P(),
        P(),
        P("dp", "ctx", None),
        P(),
        P(),
        P(),
        P("dp", "ctx", None),
    )
    out_specs = (P("dp", "ctx", None), P("dp", "ctx", None), P(), P(), P(), P(), P())
    return jax.shard_map(
        on_device, mesh=mesh, in_specs=in_specs, out_specs=out_specs, check_vma=False
    )
```

```python
import functools

import jax
import jax.numpy as jnp
from jax import lax
from jax.experimental import pallas as pl
from jax.experimental.pallas import tpu as pltpu
from jax.sharding import PartitionSpec as P

H = 4
P_SIZE = 64
N = 128
K = 4
INNER = H * P_SIZE
HEAD_ROWS = 8
TAIL_ROWS = 8
HALO_ROWS = 8
FIX_ROWS = 16
FACTOR_ROWS = 8
END_ROWS = 16
LANE_BLOCKS = (INNER + 2 * N) // 128
SMALL_ROW = (K + 1) * LANE_BLOCKS
TOTAL_ROWS = 24

f32 = jnp.float32
bf16 = jnp.bfloat16

VMEM = pl.BlockSpec(memory_space=pltpu.VMEM)
HBM = pl.BlockSpec(memory_space=pltpu.HBM)


def dot(a, b, a_dim=1, b_dim=0):
    return lax.dot_general(a, b, (((a_dim,), (b_dim,)), ((), ())), preferred_element_type=f32)


def split2(x):
    high = x.astype(bf16)
    return high, (x - high.astype(f32)).astype(bf16)


def split3(x):
    high = x.astype(bf16).astype(f32)
    rest = x - high
    middle = rest.astype(bf16).astype(f32)
    return high, middle, rest - middle


def iota(shape, dim):
    return lax.broadcasted_iota(jnp.int32, shape, dim)


def stacked(rows):
    return jnp.concatenate([*split3(rows), jnp.zeros_like(rows)], 0).astype(bf16)


def unstacked(rows):
    return rows[0:8] + rows[8:16] + rows[16:24]


def head_selector(rows):
    shape = (rows, INNER)
    return jnp.where(iota(shape, 1) // P_SIZE == iota(shape, 0) % HEAD_ROWS, 1.0, 0.0).astype(bf16)


def over_channels(rows):
    return dot(stacked(rows), head_selector(4 * HEAD_ROWS), 0, 0)


def head_sums(x):
    high, low = split2(x)
    selector = head_selector(HEAD_ROWS * 2)
    return (dot(selector, high, 1, 1) + dot(selector, low, 1, 1))[:HEAD_ROWS]


def by_head(ref, width):
    row = iota((HEAD_ROWS, width), 0)
    out = jnp.zeros((HEAD_ROWS, width), f32)
    for h in range(H):
        out = jnp.where(row == h, ref[:, h : h + 1], out)
    return out


def shifted_down(x, first, count):
    moved = pltpu.roll(x, count, 0)
    top = jnp.where(iota(first.shape, 0) < count, pltpu.roll(first, count, 0), moved[:8])
    return jnp.concatenate([top, moved[8:]], 0)


def quantized_log(size):
    return jnp.log(jnp.maximum(size, 1e-30)).astype(bf16).astype(f32)


def scaled_columns(x):
    log_size = quantized_log(jnp.max(jnp.abs(x), axis=0, keepdims=True))
    return x * jnp.exp(-log_size), log_size


def write_messages(msg_refs, state, grad, log_total, place, radix):
    row = iota((TAIL_ROWS, INNER), 0)
    high, middle, low = split3(log_total)
    tail = jnp.where(row == 4, high, jnp.where(row == 5, middle * 256.0, jnp.where(row == 6, low * 65536.0, 0.0)))
    state, state_size = scaled_columns(state)
    grad, grad_size = scaled_columns(grad)
    if radix:
        for s, msg_ref in enumerate(msg_refs, 1):
            on = place + s < radix
            msg_ref[0:N] = jnp.where(on, state, grad)
            msg_ref[N : N + TAIL_ROWS] = jnp.where(row == 0, jnp.where(on, state_size, grad_size), tail)
    else:
        (msg_ref,) = msg_refs
        msg_ref[0:N] = state
        msg_ref[N : 2 * N] = grad
        msg_ref[2 * N : 2 * N + TAIL_ROWS] = jnp.where(row == 0, state_size, jnp.where(row == 1, grad_size, tail))


def message_log(got_ref):
    rows = got_ref.shape[0] - TAIL_ROWS
    tail = got_ref[rows : rows + 8]
    return tail[4:5] + tail[5:6] * (1 / 256.0) + tail[6:7] * (1 / 65536.0)


def message_block(got_ref, which=0):
    rows = got_ref.shape[0] - TAIL_ROWS
    return got_ref[which * N : (which + 1) * N] * jnp.exp(got_ref[rows + which : rows + which + 1])


def chained(blocks, logs, used):
    total, log_sum = 0.0, 0.0
    for block, log, use in zip(blocks, logs, used):
        total = total + jnp.where(use, jnp.exp(log_sum) * block, 0.0)
        log_sum = log_sum + jnp.where(use, log, 0.0)
    return total, log_sum


def pack_totals(x):
    row = iota(x.shape, 0)
    large = jnp.where(row < SMALL_ROW, x, 0.0)
    large_size = quantized_log(jnp.max(jnp.abs(large), axis=0, keepdims=True))
    small = x[SMALL_ROW : SMALL_ROW + 1]
    small_size = quantized_log(jnp.abs(small))
    small = small * jnp.exp(-small_size)
    small_high = small.astype(bf16).astype(f32)
    out = jnp.where(row == SMALL_ROW, small_high, large * jnp.exp(-large_size))
    out = jnp.where(row == SMALL_ROW + 3, (small - small_high) * 256.0, out)
    return jnp.where(row == SMALL_ROW + 1, large_size, jnp.where(row == SMALL_ROW + 2, small_size, out))


def triangle_kernel(until_ref):
    shape = until_ref.shape
    until_ref[...] = jnp.where(iota(shape, 0) <= iota(shape, 1), 1.0, 0.0).astype(bf16)


def heads_kernel(bias_ref, dt_bias_ref, alog_ref, skip_ref, until_in, until_ref, bias_out, heads_ref):
    bias_out[...] = bias_ref[...]
    for i, ref in enumerate((dt_bias_ref, alog_ref, skip_ref)):
        heads_ref[8 * i : 8 * i + 8] = by_head(ref, until_ref.shape[1])


def mask_first(x):
    top = jnp.where(iota((FIX_ROWS, x.shape[1]), 0) < K - 1, 0.0, x[:FIX_ROWS].astype(f32))
    return jnp.concatenate([top.astype(x.dtype), x[FIX_ROWS:]], 0)


def start_kernel(
    stages, raw_ref, cot_ref, weight_ref, bias_ref, dt_ref, heads_ref, until_ref,
    pre_ref, xbc_ref, weighted_ref, scaled_ref, tail_ref, rows_ref, logs_ref, places_ref, state_ref, grad_ref, msg_ref, dt8_ref,
):
    tok = raw_ref.shape[0]
    place = lax.axis_index("ctx")
    for t, (size, radix) in enumerate(stages):
        places_ref[8 * t : 8 * t + 8] = jnp.full((8, INNER), lax.rem(lax.div(place, size), radix), jnp.int32).astype(f32)
    at = 8 * len(stages)
    slabs = stages[-1][0] * stages[-1][1]
    places_ref[at : at + 8] = jnp.full((8, INNER), jnp.where(place == 0, 1, 0), jnp.int32).astype(f32)
    places_ref[at + 8 : at + 16] = jnp.full((8, INNER), jnp.where(place == slabs - 1, 1, 0), jnp.int32).astype(f32)
    dt8_ref[...] = jnp.zeros_like(dt8_ref)
    dt8_ref[0:H] = dt_ref[...]
    dt_pre = dt8_ref[...] + heads_ref[0:8]
    step = jnp.maximum(dt_pre, 0.0) + jnp.log1p(jnp.exp(-jnp.abs(dt_pre)))
    real = iota((HEAD_ROWS, tok), 0) < H
    decay_rate = jnp.where(real, -jnp.exp(heads_ref[8:16]), 0.0)
    cum = unstacked(dot(stacked(step * decay_rate), until_ref[...]))
    left = jnp.exp(cum[:, tok - 1 : tok] - cum)
    reach = jnp.exp(cum)
    rows_ref[0:8] = cum
    rows_ref[8:16] = step
    rows_ref[16:24] = left
    rows_ref[24:32] = reach
    rows_ref[32:40] = 1.0 / (1.0 + jnp.exp(-dt_pre))
    rows_ref[40:48] = decay_rate
    tail = over_channels(left * step)
    tail_ref[...] = tail
    log_total = over_channels(cum)[tok - 1 : tok]
    skip = over_channels(heads_ref[16:24])[0:1]
    row = iota((8, INNER), 0)
    logs_ref[...] = jnp.where(row == 2, log_total, jnp.where(row == 3, skip, 0.0))
    scaled = jnp.concatenate(split2(cot_ref[...].astype(f32) * over_channels(reach)), 1)
    scaled_ref[...] = scaled

    raw = raw_ref[...].astype(f32)
    zeros = jnp.zeros((8, raw.shape[1]), f32)
    pre = bias_ref[...] + weight_ref[K - 1 : K] * raw
    for back in range(1, K):
        pre = pre + weight_ref[K - 1 - back : K - back] * shifted_down(raw, zeros, back)
    pre_ref[...] = pre
    gate = 1.0 / (1.0 + jnp.exp(-pre))
    xbc = (pre * gate).astype(bf16)
    xbc_ref[...] = xbc
    weighted = jnp.concatenate(split2(xbc[:, :INNER].astype(f32) * tail), 1)
    weighted_ref[...] = weighted
    later = mask_first(xbc[:, INNER:])
    state = dot(later[:, :N], weighted, 0, 0)
    state = state[:, :INNER] + state[:, INNER:]
    grad = dot(later[:, N:], scaled, 0, 0)
    grad = grad[:, :INNER] + grad[:, INNER:]
    state_ref[...] = state
    grad_ref[...] = grad
    write_messages((msg_ref,), state, grad, log_total, places_ref[0:1], 0)


def real_halo(halo_ref, places_ref):
    first = places_ref[places_ref.shape[0] - 16 :][:1, :1]
    return jnp.where(first > 0.5, 0.0, halo_ref[HALO_ROWS - 8 :].astype(f32))


def fix_kernel(
    halo_ref, weight_ref, scaled_ref, tail_ref, places_ref, pre_in, xbc_in, weighted_in,
    pre_ref, xbc_ref, weighted_ref, factors_ref,
):
    halo = real_halo(halo_ref, places_ref)
    top = pre_in[0:8]
    for back in range(1, K):
        tap = weight_ref[K - 1 - back : K - back]
        top = top + jnp.where(iota(top.shape, 0) < back, tap * pltpu.roll(halo, back, 0), 0.0)
    pre = jnp.concatenate([top, pre_in[8:FIX_ROWS]], 0)
    pre_ref[0:FIX_ROWS] = pre
    gate = 1.0 / (1.0 + jnp.exp(-pre))
    xbc = (pre * gate).astype(bf16)
    xbc_ref[0:FIX_ROWS] = xbc
    xbc = xbc.astype(f32)
    weighted = jnp.concatenate([each.astype(f32) for each in split2(xbc[:, :INNER] * tail_ref[0:FIX_ROWS])], 1)
    weighted_ref[0:FIX_ROWS] = weighted.astype(bf16)
    scaled = scaled_ref[0:FIX_ROWS].astype(f32)

    def placed(low, high):
        row = iota((FACTOR_ROWS, low.shape[1]), 0)
        moved = pltpu.roll(high[:FACTOR_ROWS], 4, 0)
        return jnp.where(row < K - 1, low[:FACTOR_ROWS], jnp.where((row >= 4) & (row < 4 + K - 1), moved, 0.0)).astype(bf16)

    zero = jnp.zeros((FACTOR_ROWS, N), f32)
    factors_ref[:, : 2 * INNER] = placed(weighted, scaled)
    factors_ref[:, 2 * INNER : 2 * INNER + N] = placed(xbc[:, INNER : INNER + N], zero)
    factors_ref[:, 2 * INNER + N :] = placed(zero, xbc[:, INNER + N :])


def first_parts(factors_ref):
    both = dot(factors_ref[:, 2 * INNER :], factors_ref[:, : 2 * INNER], 0, 0)
    both = both[:, :INNER] + both[:, INNER:]
    return both[:N], both[N:]


def merge_kernel(t, radix, next_radix, state_ref, grad_ref, logs_ref, places_ref, *refs):
    got, refs = refs[: radix - 1], refs[radix - 1 :]
    prior = after = 0.0
    if t > 0:
        prior, after = refs[0][...], refs[1][...]
        refs = refs[2:]
    else:
        parts, refs = [first_parts(ref) for ref in refs[: radix - 1]], refs[radix - 1 :]
    logs_out, prior_out, after_out, *refs = refs
    if not next_radix:
        state_out, grad_out, *refs = refs
    place = places_ref[8 * t : 8 * t + 1]
    log_prior, log_after, log_total = logs_ref[0:1], logs_ref[1:2], logs_ref[2:3]
    states = [message_block(ref, 0) for ref in got]
    grads = [message_block(ref, 1) for ref in got]
    logs = [message_log(ref) for ref in got]
    own_state, own_grad = state_ref[...], grad_ref[...]
    if t == 0:
        states = [each + part[0] for each, part in zip(states, parts)]
        grads = [each + part[1] for each, part in zip(grads, parts)]
    earlier = [s <= place for s in range(1, radix)]
    later = [s > place for s in range(1, radix)]
    before, log_before = chained(states, logs, earlier)
    beyond, log_beyond = chained(grads[::-1], logs[::-1], later[::-1])
    above, _ = chained(states, logs, later)
    below, _ = chained(grads[::-1], logs[::-1], earlier[::-1])
    mine = jnp.exp(log_total)
    state = above + jnp.exp(log_beyond) * (own_state + mine * before)
    grad = below + jnp.exp(log_before) * (own_grad + mine * beyond)
    prior_out[...] = prior + jnp.exp(log_prior) * before
    after_out[...] = after + jnp.exp(log_after) * beyond
    log_prior = log_prior + log_before
    log_after = log_after + log_beyond
    log_total = log_total + log_before + log_beyond
    row = iota((8, INNER), 0)
    logs_out[...] = jnp.where(row == 0, log_prior, jnp.where(row == 1, log_after, jnp.where(row == 2, log_total, 0.0)))
    if not next_radix:
        state_out[...] = state
        grad_out[...] = grad
    write_messages(refs, state, grad, log_total, places_ref[8 * t + 8 : 8 * t + 9], next_radix)


def local_kernel(
    xbc_ref, cot_ref, rows_ref, logs_ref, raw_ref, halo_ref, places_ref, scaled_ref, until_ref, pre_ref, factors_ref, state_in, grad_in,
    local_ref, sums_ref, weights_ref, moved_ref, slope_ref, state_ref, grad_ref,
):
    state, grad = first_parts(factors_ref)
    state_ref[...] = state_in[...] + state
    grad_ref[...] = grad_in[...] + grad
    pre = pre_ref[...]
    sigmoid = 1.0 / (1.0 + jnp.exp(-pre))
    slope_ref[...] = sigmoid * (1.0 + pre * (1.0 - sigmoid))
    tok = xbc_ref.shape[0]
    cot = cot_ref[...]
    values = xbc_ref[:, :INNER]
    b_proj = xbc_ref[:, INNER : INNER + N]
    c_proj = xbc_ref[:, INNER + N :]
    cum, step = rows_ref[0:8], rows_ref[8:16]
    step_wide = over_channels(step)
    values_f = values.astype(f32)
    cot_f = cot.astype(f32)
    stepped = split2(values_f * step_wide)
    gram = dot(b_proj, c_proj, 1, 1)
    reached = iota((tok, tok), 0) <= iota((tok, tok), 1)
    pieces = stacked(cum)
    piece_head = iota((4 * HEAD_ROWS, tok), 0) % HEAD_ROWS
    dgram = jnp.zeros((tok, tok), f32)
    grads, sums = [], []
    for h in range(H):
        of = slice(h * P_SIZE, (h + 1) * P_SIZE)
        column = dot(pieces, jnp.where(piece_head == h, 1.0, 0.0).astype(bf16), 0, 0)
        within = jnp.exp(jnp.where(reached, cum[h : h + 1] - column, -1e30))
        cot_h = cot[:, of]
        high, low = split2(gram * within)
        grads.append(dot(high, cot_h) + dot(low, cot_h))
        dmix = dot(stepped[0][:, of], cot_h, 1, 1) + dot(stepped[1][:, of], cot_h, 1, 1)
        dmix = dmix * within
        dgram = dgram + dmix
        sums.append(jnp.sum(dmix * gram, axis=0, keepdims=True))
    grad_stepped = jnp.concatenate(grads, 1)
    local_ref[:, :INNER] = grad_stepped * step_wide + logs_ref[3:4] * cot_f
    high, low = split2(dgram)
    local_ref[:, INNER : INNER + N] = dot(high, c_proj) + dot(low, c_proj)
    local_ref[:, INNER + N :] = dot(high, b_proj, 0, 0) + dot(low, b_proj, 0, 0)
    row = iota((HEAD_ROWS, tok), 0)
    pairs = jnp.zeros((HEAD_ROWS, tok), f32)
    for h in range(H):
        pairs = jnp.where(row == h, sums[h], pairs)
    left, gate, decay_rate = rows_ref[16:24], rows_ref[32:40], rows_ref[40:48]
    from_values = head_sums(values_f * grad_stepped)
    skip_rows = head_sums(values_f * cot_f)
    base = pairs - from_values * step
    sums_ref[0:8] = base
    sums_ref[8:16] = from_values

    bias_weight = decay_rate * unstacked(dot(stacked(gate), until_ref[...]))
    cum_last, bias_last = cum[:, tok - 1 : tok], bias_weight[:, tok - 1 : tok]
    tail = left * step
    scaled_f = scaled_ref[:, :INNER].astype(f32) + scaled_ref[:, INNER:].astype(f32)
    weights_ref[:, :INNER] = scaled_f * over_channels(cum)
    weights_ref[:, INNER : 2 * INNER] = values_f * over_channels(tail * (cum_last - cum))
    weights_ref[:, 2 * INNER : 3 * INNER] = scaled_f * over_channels(bias_weight)
    weights_ref[:, 3 * INNER :] = values_f * over_channels(left * gate + tail * (bias_last - bias_weight))
    lane = iota((HEAD_ROWS, tok), 1)
    fixed = jnp.zeros((HEAD_ROWS, tok), f32)
    for i, column in enumerate((
        jnp.sum(from_values * gate + base * bias_weight, axis=1, keepdims=True),
        jnp.sum(base * cum, axis=1, keepdims=True),
        jnp.sum(skip_rows, axis=1, keepdims=True),
        bias_last, cum_last,
    )):
        fixed = jnp.where(lane == i, column, fixed)
    sums_ref[16:24] = fixed
    raw = raw_ref[...].astype(f32)
    halo = real_halo(halo_ref, places_ref)
    for back in range(1, K):
        moved_ref[(back - 1) * tok : back * tok] = shifted_down(raw, halo, back)


def totals_kernel(
    t, radix, raw_ref, moved_ref, xbc_ref, slope_ref, scaled_ref, weighted_ref, tail_ref, rows_ref, local_ref, sums_ref, weights_ref,
    logs_ref, places_ref, weight_ref, *refs
):
    got, refs = refs[: radix - 1], refs[radix - 1 :]
    prior = after = 0.0
    if t > 0:
        prior, after = refs[0][...], refs[1][...]
        refs = refs[2:]
    conv_ref, states_ref, totals_ref, spill_ref, totals_scratch = refs
    tok = raw_ref.shape[0]
    place = places_ref[8 * t : 8 * t + 1]
    blocks = [message_block(ref) for ref in got]
    logs = [message_log(ref) for ref in got]
    before, _ = chained(blocks, logs, [s <= place for s in range(1, radix)])
    beyond, _ = chained(blocks[::-1], logs[::-1], [s > place for s in range(radix - 1, 0, -1)])
    prior = prior + jnp.exp(logs_ref[0:1]) * before
    after = after + jnp.exp(logs_ref[1:2]) * beyond

    b_proj = xbc_ref[:, INNER : INNER + N]
    c_proj = xbc_ref[:, INNER + N :]
    prior2 = jnp.concatenate(split2(prior), 0)
    after2 = jnp.concatenate(split2(after), 0)
    seen = dot(jnp.concatenate([c_proj, c_proj], 1), prior2)
    back = dot(jnp.concatenate([b_proj, b_proj], 1), after2)
    grad_c = dot(scaled_ref[:, :INNER], prior2, 1, 1)
    grad_c = grad_c[:, :N] + grad_c[:, N:] + dot(scaled_ref[:, INNER:], prior2[:N], 1, 1)
    grad_b = dot(weighted_ref[:, :INNER], after2, 1, 1)
    grad_b = grad_b[:, :N] + grad_b[:, N:] + dot(weighted_ref[:, INNER:], after2[:N], 1, 1)
    grad_low = (local_ref[...] + jnp.concatenate([tail_ref[...] * back, grad_b, grad_c], 1)).astype(bf16)
    grad_conv = grad_low.astype(f32) * slope_ref[...]
    conv_ref[...] = grad_conv
    top = grad_conv[:8]
    spill = jnp.zeros_like(top)
    for ahead in range(1, K):
        tap = weight_ref[K - 1 - ahead : K - ahead]
        spill = spill + tap * jnp.where(iota(top.shape, 0) < 8 - ahead, 0.0, pltpu.roll(top, 8 - ahead, 0))
    spill_ref[...] = spill

    sums = [grad_conv * moved_ref[back * tok : (back + 1) * tok] for back in range(K - 2, -1, -1)]
    sums += [grad_conv * raw_ref[...].astype(f32), grad_conv]
    totals_scratch[...] = jnp.zeros_like(totals_scratch)
    for k, each in enumerate(sums):
        each = jnp.sum(each, axis=0, keepdims=True)
        for j in range(LANE_BLOCKS):
            at = k * LANE_BLOCKS + j
            totals_scratch[at : at + 1] = each[:, j * 128 : (j + 1) * 128]

    states_ref[:tok, :INNER] = seen
    states_ref[:tok, INNER:] = back
    through = jnp.sum(prior * after, axis=0, keepdims=True)
    grad_bias = jnp.sum(seen * weights_ref[:, 2 * INNER : 3 * INNER] + back * weights_ref[:, 3 * INNER :], axis=0, keepdims=True)
    grad_alog = jnp.sum(seen * weights_ref[:, :INNER] + back * weights_ref[:, INNER : 2 * INNER], axis=0, keepdims=True)
    selector = head_selector(HEAD_ROWS * 2)[:HEAD_ROWS].astype(f32)
    grad_bias, grad_alog, through = (
        jnp.sum(selector * each, axis=1, keepdims=True) for each in (grad_bias, grad_alog, through)
    )
    through = through * rows_ref[24:32][:, tok - 1 : tok]
    states_ref[tok:] = jnp.broadcast_to(through, (HEAD_ROWS, 2 * INNER))
    fixed = sums_ref[16:24]
    row, lane = iota((HEAD_ROWS, 128), 0), iota((HEAD_ROWS, 128), 1)
    small = jnp.zeros((HEAD_ROWS, 128), f32)
    for i, column in enumerate((
        fixed[:, 0:1] + grad_bias + through * fixed[:, 3:4],
        fixed[:, 1:2] + grad_alog + through * fixed[:, 4:5],
        fixed[:, 2:3],
    )):
        small = jnp.where((row < H) & (lane == row + i * H), column, small)
    totals_scratch[SMALL_ROW : SMALL_ROW + 1] = jnp.sum(small, axis=0, keepdims=True)
    totals_ref[...] = pack_totals(totals_scratch[...])


def input_kernel(
    conv_ref, weight_ref, states_ref, xbc_ref, scaled_ref, rows_ref, sums_ref, until_ref, out_hbm, dt_out_ref, end_ref, out_ref, sem
):
    grad_conv = conv_ref[...]
    tok, channels = grad_conv.shape
    grad_in = weight_ref[K - 1 : K] * grad_conv
    row8 = iota((8, channels), 0)
    for ahead in range(1, K):
        tap = weight_ref[K - 1 - ahead : K - ahead]
        moved = pltpu.roll(grad_conv, tok - ahead, 0)
        last8 = moved[tok - 8 :]
        inside = row8 < 8 - ahead
        grad_in = grad_in + tap * jnp.concatenate([moved[: tok - 8], jnp.where(inside, last8, 0.0)], 0)
    out_ref[...] = grad_in.astype(bf16)
    copy = pltpu.make_async_copy(out_ref, out_hbm, sem)
    copy.start()
    end_ref[...] = grad_in[tok - END_ROWS :]

    step, left, gate, decay_rate = rows_ref[8:16], rows_ref[16:24], rows_ref[32:40], rows_ref[40:48]
    scaled_f = scaled_ref[:, :INNER].astype(f32) + scaled_ref[:, INNER:].astype(f32)
    seen_rows = head_sums(scaled_f * states_ref[:tok, :INNER])
    tail_rows = head_sums(xbc_ref[:, :INNER].astype(f32) * states_ref[:tok, INNER:])
    tail_term = tail_rows * left * step
    last_extra = jnp.sum(tail_term, axis=1, keepdims=True) + states_ref[tok:][:, :1]
    grad_cum = sums_ref[0:8] + seen_rows - tail_term
    grad_log = unstacked(dot(stacked(grad_cum), until_ref[...], 1, 1)) + last_extra
    grad_step = sums_ref[8:16] + tail_rows * left + decay_rate * grad_log
    dt_out_ref[...] = (grad_step * gate)[0:H]
    copy.wait()


def end_kernel(end_ref, spilled_ref, places_ref, main_hbm, out_hbm, rows_ref, sem):
    end = end_ref[...]
    last = places_ref[places_ref.shape[0] - 8 :][:1, :1]
    fixed = end[END_ROWS - 8 :] + jnp.where(last > 0.5, 0.0, spilled_ref[...])
    rows_ref[...] = jnp.concatenate([end[: END_ROWS - 8], fixed], 0).astype(bf16)
    tok = out_hbm.shape[0]
    copy = pltpu.make_async_copy(rows_ref, out_hbm.at[pl.ds(tok - END_ROWS, END_ROWS)], sem)
    copy.start()
    copy.wait()


def summed(parts):
    large = jnp.sum(parts * jnp.exp(parts[:, SMALL_ROW + 1 : SMALL_ROW + 2]), axis=0)
    small = parts[:, SMALL_ROW : SMALL_ROW + 1] + parts[:, SMALL_ROW + 3 : SMALL_ROW + 4] * (1 / 256.0)
    small = small * jnp.exp(parts[:, SMALL_ROW + 2 : SMALL_ROW + 3])
    return large, jnp.sum(small, axis=0)


def repack_kernel(parts_ref, out_ref):
    large, small = summed(parts_ref[...])
    out_ref[...] = pack_totals(jnp.where(iota(large.shape, 0) == SMALL_ROW, small, large))


def finish_kernel(parts_ref, weight_ref, bias_ref, dt_bias_ref, alog_ref, skip_ref):
    large, small = summed(parts_ref[...])
    for k in range(K + 1):
        for j in range(LANE_BLOCKS):
            at = k * LANE_BLOCKS + j
            if k < K:
                weight_ref[k : k + 1, j * 128 : (j + 1) * 128] = large[at : at + 1]
            else:
                bias_ref[:, j * 128 : (j + 1) * 128] = large[at : at + 1]
    for i, ref in enumerate((dt_bias_ref, alog_ref, skip_ref)):
        ref[...] = small[:, i * H : (i + 1) * H]


def call(kernel, outs, in_specs, out_specs=None, scratch=(), flops=0, limit=16 << 20, aliases=None):
    return pl.pallas_call(
        kernel,
        out_shape=outs,
        in_specs=in_specs,
        out_specs=out_specs or jax.tree.map(lambda _: VMEM, outs),
        scratch_shapes=list(scratch),
        input_output_aliases=aliases or {},
        compiler_params=pltpu.CompilerParams(vmem_limit_bytes=limit),
        cost_estimate=pl.CostEstimate(flops=flops, bytes_accessed=1 << 20, transcendentals=0),
    )


def struct(shape, dtype=f32):
    return jax.ShapeDtypeStruct(shape, dtype)


def from_groups(messages, slabs, size, radix):
    got = []
    for s in range(1, radix):
        message = messages[s - 1 if len(messages) > 1 else 0]
        route = [(p, p - p % (size * radix) + (p + s * size) % (size * radix)) for p in range(slabs)]
        got.append(lax.ppermute(message, "ctx", route))
    return got


def states_from_groups(messages, slabs, size, radix):
    got = from_groups([message.astype(jnp.float16) for message in messages], slabs, size, radix)
    return [each.astype(f32) for each in got]


def stages_of(slabs):
    stages, size = [], 1
    while size < slabs:
        radix = 2 if (slabs // size).bit_length() % 2 == 0 else 4
        stages.append((size, radix))
        size *= radix
    assert size == slabs and len(stages) > 1
    return stages


def everyones(packed, axes, count):
    packed = jnp.broadcast_to(packed.astype(jnp.float16)[None], (count, *packed.shape))
    return lax.all_to_all(packed, axes, 0, 0).astype(f32)


def on_device(xbc_raw, conv_weight, conv_bias, dt_raw, dt_bias, a_log, d_skip, grad_out):
    tok, channels = xbc_raw.shape[1:]
    slabs = lax.axis_size("ctx")
    contexts = lax.axis_size("dp")
    stages = stages_of(slabs)

    raw, cot, dt_rows = xbc_raw[0], grad_out[0], dt_raw[0].T
    until = call(triangle_kernel, struct((tok, tok), bf16), [], flops=10**11)()
    until, bias, heads = call(
        heads_kernel,
        (struct((tok, tok), bf16), struct((1, channels)), struct((3 * HEAD_ROWS, tok))),
        [VMEM] * 5,
        aliases={4: 0},
    )(conv_bias[None], dt_bias[None], a_log[None], d_skip[None], until)
    early_raw, until = lax.optimization_barrier((raw, until))
    halo = lax.ppermute(early_raw[tok - HALO_ROWS :], "ctx", [(i, (i + 1) % slabs) for i in range(slabs)])

    def last_radix(t):
        return stages[t][1] if t == len(stages) - 1 else 0

    def messages(t):
        if last_radix(t):
            return (struct((N + TAIL_ROWS, INNER)),) * (last_radix(t) - 1)
        return (struct((2 * N + TAIL_ROWS, INNER)),)

    state_like = struct((N, INNER))
    logs_like = struct((8, INNER))
    pre, xbc, weighted, scaled, tail, rows, logs, places, state, grad, *outgoing = call(
        functools.partial(start_kernel, stages),
        (
            struct((tok, channels)), struct((tok, channels), bf16), struct((tok, 2 * INNER), bf16),
            struct((tok, 2 * INNER), bf16), struct((tok, INNER)), struct((6 * HEAD_ROWS, tok)),
            logs_like, struct((8 * len(stages) + 16, INNER)), state_like, state_like, *messages(0),
        ),
        [VMEM] * 7,
        scratch=[pltpu.VMEM((HEAD_ROWS, tok), f32)],
        flops=10**11,
    )(raw, cot, conv_weight, bias, dt_rows, heads, until)
    pre, xbc, weighted, factors = call(
        fix_kernel,
        (
            struct((tok, channels)), struct((tok, channels), bf16), struct((tok, 2 * INNER), bf16),
            struct((FACTOR_ROWS, 2 * INNER + 2 * N), bf16),
        ),
        [VMEM] * 8,
        flops=1_000_000,
        aliases={5: 0, 6: 1, 7: 2},
    )(halo, conv_weight, scaled, tail, places, pre, xbc, weighted)

    local, sums, weights, moved, slope, state, grad = call(
        local_kernel,
        (
            struct((tok, channels)), struct((3 * HEAD_ROWS, tok)), struct((tok, 4 * INNER)), struct(((K - 1) * tok, channels)),
            struct((tok, channels)), state_like, state_like,
        ),
        [VMEM] * 13,
        flops=10**11,
        aliases={11: 5, 12: 6},
    )(xbc, cot, rows, logs, raw, halo, places, scaled, until, pre, factors, state, grad)

    carried = ()
    for t, (size, radix) in enumerate(stages):
        got = states_from_groups(outgoing, slabs, size, radix)
        if t == 0:
            got, local, sums, weights, moved, slope = lax.optimization_barrier((got, local, sums, weights, moved, slope))
            carried = from_groups([factors], slabs, size, radix)
        if t == len(stages) - 1:
            break
        last = last_radix(t + 1)
        outs = (logs_like, state_like, state_like) + (() if last else (state_like, state_like))
        logs, *outgoing = call(
            functools.partial(merge_kernel, t, radix, last),
            outs + messages(t + 1),
            [VMEM] * (4 + len(got) + len(carried)),
            flops=1_000_000,
        )(state, grad, logs, places, *got, *carried)
        carried, outgoing = outgoing[:2], outgoing[2:]
        if not last:
            (state, grad), outgoing = outgoing[:2], outgoing[2:]

    grad_conv, states, packed, spill = call(
        functools.partial(totals_kernel, len(stages) - 1, radix),
        (struct((tok, channels)), struct((tok + HEAD_ROWS, 2 * INNER)), struct((TOTAL_ROWS, 128)), struct((8, channels))),
        [VMEM] * (14 + len(got) + len(carried)),
        scratch=[pltpu.VMEM((TOTAL_ROWS, 128), f32)],
        flops=200_000_000,
    )(raw, moved, xbc, slope, scaled, weighted, tail, rows, local, sums, weights, logs, places, conv_weight, *got, *carried)

    spilled = lax.ppermute(spill, "ctx", [((i + 1) % slabs, i) for i in range(slabs)])
    if slabs * contexts <= 64:
        parts = everyones(packed, ("ctx", "dp"), slabs * contexts)
    else:
        packed = call(repack_kernel, struct((TOTAL_ROWS, 128)), [VMEM])(everyones(packed, "ctx", slabs))
        parts = everyones(packed, "dp", contexts)

    grad_main, grad_dt, end = call(
        input_kernel,
        (struct((tok, channels), bf16), struct((H, tok)), struct((END_ROWS, channels))),
        [VMEM] * 8,
        (HBM, VMEM, VMEM),
        [pltpu.VMEM((tok, channels), bf16), pltpu.SemaphoreType.DMA],
        flops=1_000_000,
    )(grad_conv, conv_weight, states, xbc, scaled, rows, sums, until)
    grad_input = call(
        end_kernel,
        struct((tok, channels), bf16),
        [VMEM] * 3 + [HBM],
        HBM,
        [pltpu.VMEM((END_ROWS, channels), bf16), pltpu.SemaphoreType.DMA],
        aliases={3: 0},
    )(end, spilled, places, grad_main)

    grad_weight, grad_bias, *small = call(
        finish_kernel,
        (struct((K, channels)), struct((1, channels)), struct((1, H)), struct((1, H)), struct((1, H))),
        [VMEM],
    )(parts)
    return (grad_input[None], grad_dt.T[None], grad_weight, grad_bias[0], *(each[0] for each in small))


def solution(mesh):
    in_specs = (
        P("dp", "ctx", None),
        P(),
        P(),
        P("dp", "ctx", None),
        P(),
        P(),
        P(),
        P("dp", "ctx", None),
    )
    out_specs = (P("dp", "ctx", None), P("dp", "ctx", None), P(), P(), P(), P(), P())
    return jax.shard_map(
        on_device, mesh=mesh, in_specs=in_specs, out_specs=out_specs, check_vma=False
    )
```

```python
import functools

import jax
import jax.numpy as jnp
from jax import lax
from jax.experimental import pallas as pl
from jax.experimental.pallas import tpu as pltpu
from jax.sharding import PartitionSpec as P

H = 4
P_SIZE = 64
N = 128
K = 4
INNER = H * P_SIZE
HEAD_ROWS = 8
TAIL_ROWS = 8
HALO_ROWS = 16
FIX_ROWS = 16
END_ROWS = 16
LANE_BLOCKS = (INNER + 2 * N) // 128
SMALL_ROW = (K + 1) * LANE_BLOCKS
TOTAL_ROWS = 24

f32 = jnp.float32
bf16 = jnp.bfloat16

VMEM = pl.BlockSpec(memory_space=pltpu.VMEM)
HBM = pl.BlockSpec(memory_space=pltpu.HBM)


def dot(a, b, a_dim=1, b_dim=0):
    return lax.dot_general(a, b, (((a_dim,), (b_dim,)), ((), ())), preferred_element_type=f32)


def split2(x):
    high = x.astype(bf16)
    return high, (x - high.astype(f32)).astype(bf16)


def split3(x):
    high = x.astype(bf16).astype(f32)
    rest = x - high
    middle = rest.astype(bf16).astype(f32)
    return high, middle, rest - middle


def iota(shape, dim):
    return lax.broadcasted_iota(jnp.int32, shape, dim)


def stacked(rows):
    return jnp.concatenate([*split3(rows), jnp.zeros_like(rows)], 0).astype(bf16)


def unstacked(rows):
    return rows[0:8] + rows[8:16] + rows[16:24]


def head_selector(rows):
    shape = (rows, INNER)
    return jnp.where(iota(shape, 1) // P_SIZE == iota(shape, 0) % HEAD_ROWS, 1.0, 0.0).astype(bf16)


def over_channels(rows):
    return dot(stacked(rows), head_selector(4 * HEAD_ROWS), 0, 0)


def pieces3(x):
    return [each.astype(bf16) for each in split3(x)]


def head_sums(x, split=split2):
    selector = head_selector(HEAD_ROWS * 2)
    return sum(dot(selector, each, 1, 1) for each in split(x))[:HEAD_ROWS]


def by_head(ref, width):
    row = iota((HEAD_ROWS, width), 0)
    out = jnp.zeros((HEAD_ROWS, width), f32)
    for h in range(H):
        out = jnp.where(row == h, ref[:, h : h + 1], out)
    return out


def shifted_down(x, first, count):
    moved = pltpu.roll(x, count, 0)
    top = jnp.where(iota(first.shape, 0) < count, pltpu.roll(first, count, 0), moved[:8])
    return jnp.concatenate([top, moved[8:]], 0)


def quantized_log(size):
    return jnp.log(jnp.maximum(size, 1e-30)).astype(bf16).astype(f32)


def scaled_columns(x):
    log_size = quantized_log(jnp.max(jnp.abs(x), axis=0, keepdims=True))
    return x * jnp.exp(-log_size), log_size


def write_messages(msg_refs, state, grad, log_total, place, radix):
    row = iota((TAIL_ROWS, INNER), 0)
    high, middle, low = split3(log_total)
    tail = jnp.where(row == 4, high, jnp.where(row == 5, middle * 256.0, jnp.where(row == 6, low * 65536.0, 0.0)))
    state, state_size = scaled_columns(state)
    grad, grad_size = scaled_columns(grad)
    if radix:
        for s, msg_ref in enumerate(msg_refs, 1):
            on = place + s < radix
            msg_ref[0:N] = jnp.where(on, state, grad)
            msg_ref[N : N + TAIL_ROWS] = jnp.where(row == 0, jnp.where(on, state_size, grad_size), tail)
    else:
        (msg_ref,) = msg_refs
        msg_ref[0:N] = state
        msg_ref[N : 2 * N] = grad
        msg_ref[2 * N : 2 * N + TAIL_ROWS] = jnp.where(row == 0, state_size, jnp.where(row == 1, grad_size, tail))


def message_log(got_ref):
    rows = got_ref.shape[0] - TAIL_ROWS
    tail = got_ref[rows : rows + 8]
    return tail[4:5] + tail[5:6] * (1 / 256.0) + tail[6:7] * (1 / 65536.0)


def message_block(got_ref, which=0):
    rows = got_ref.shape[0] - TAIL_ROWS
    return got_ref[which * N : (which + 1) * N] * jnp.exp(got_ref[rows + which : rows + which + 1])


def chained(blocks, logs, used):
    total, log_sum = 0.0, 0.0
    for block, log, use in zip(blocks, logs, used):
        total = total + jnp.where(use, jnp.exp(log_sum) * block, 0.0)
        log_sum = log_sum + jnp.where(use, log, 0.0)
    return total, log_sum


def pack_totals(x):
    row = iota(x.shape, 0)
    large = jnp.where(row < SMALL_ROW, x, 0.0)
    large_size = quantized_log(jnp.max(jnp.abs(large), axis=0, keepdims=True))
    small = x[SMALL_ROW : SMALL_ROW + 1]
    small_size = quantized_log(jnp.abs(small))
    small = small * jnp.exp(-small_size)
    small_high = small.astype(bf16).astype(f32)
    out = jnp.where(row == SMALL_ROW, small_high, large * jnp.exp(-large_size))
    out = jnp.where(row == SMALL_ROW + 3, (small - small_high) * 256.0, out)
    return jnp.where(row == SMALL_ROW + 1, large_size, jnp.where(row == SMALL_ROW + 2, small_size, out))


def triangle_kernel(until_ref):
    shape = until_ref.shape
    until_ref[...] = jnp.where(iota(shape, 0) <= iota(shape, 1), 1.0, 0.0).astype(bf16)


def heads_kernel(bias_ref, dt_bias_ref, alog_ref, skip_ref, until_in, until_ref, bias_out, heads_ref):
    bias_out[...] = bias_ref[...]
    for i, ref in enumerate((dt_bias_ref, alog_ref, skip_ref)):
        heads_ref[8 * i : 8 * i + 8] = by_head(ref, until_ref.shape[1])


def mask_first(x):
    top = jnp.where(iota((FIX_ROWS, x.shape[1]), 0) < K - 1, 0.0, x[:FIX_ROWS].astype(f32))
    return jnp.concatenate([top.astype(x.dtype), x[FIX_ROWS:]], 0)


def start_kernel(
    stages, raw_ref, cot_ref, weight_ref, bias_ref, dt_ref, heads_ref, until_ref,
    pre_ref, xbc_ref, weighted_ref, scaled_ref, tail_ref, rows_ref, logs_ref, places_ref, state_ref, grad_ref, msg_ref, dt8_ref,
):
    tok = raw_ref.shape[0]
    place = lax.axis_index("ctx")
    for t, (size, radix) in enumerate(stages):
        places_ref[8 * t : 8 * t + 8] = jnp.full((8, INNER), lax.rem(lax.div(place, size), radix), jnp.int32).astype(f32)
    at = 8 * len(stages)
    slabs = stages[-1][0] * stages[-1][1]
    places_ref[at : at + 8] = jnp.full((8, INNER), jnp.where(place == 0, 1, 0), jnp.int32).astype(f32)
    places_ref[at + 8 : at + 16] = jnp.full((8, INNER), jnp.where(place == slabs - 1, 1, 0), jnp.int32).astype(f32)
    dt8_ref[...] = jnp.zeros_like(dt8_ref)
    dt8_ref[0:H] = dt_ref[...]
    dt_pre = dt8_ref[...] + heads_ref[0:8]
    step = jnp.maximum(dt_pre, 0.0) + jnp.log1p(jnp.exp(-jnp.abs(dt_pre)))
    real = iota((HEAD_ROWS, tok), 0) < H
    decay_rate = jnp.where(real, -jnp.exp(heads_ref[8:16]), 0.0)
    cum = unstacked(dot(stacked(step * decay_rate), until_ref[...]))
    left = jnp.exp(cum[:, tok - 1 : tok] - cum)
    reach = jnp.exp(cum)
    rows_ref[0:8] = cum
    rows_ref[8:16] = step
    rows_ref[16:24] = left
    rows_ref[24:32] = reach
    rows_ref[32:40] = 1.0 / (1.0 + jnp.exp(-dt_pre))
    rows_ref[40:48] = decay_rate
    tail = over_channels(left * step)
    tail_ref[...] = tail
    log_total = over_channels(cum)[tok - 1 : tok]
    skip = over_channels(heads_ref[16:24])[0:1]
    row = iota((8, INNER), 0)
    logs_ref[...] = jnp.where(row == 2, log_total, jnp.where(row == 3, skip, 0.0))
    scaled = jnp.concatenate(split2(cot_ref[...].astype(f32) * over_channels(reach)), 1)
    scaled_ref[...] = scaled

    raw = raw_ref[...].astype(f32)
    zeros = jnp.zeros((8, raw.shape[1]), f32)
    pre = bias_ref[...] + weight_ref[K - 1 : K] * raw
    for back in range(1, K):
        pre = pre + weight_ref[K - 1 - back : K - back] * shifted_down(raw, zeros, back)
    pre_ref[...] = pre
    gate = 1.0 / (1.0 + jnp.exp(-pre))
    xbc = (pre * gate).astype(bf16)
    xbc_ref[...] = xbc
    weighted = jnp.concatenate(split2(xbc[:, :INNER].astype(f32) * tail), 1)
    weighted_ref[...] = weighted
    later = mask_first(xbc[:, INNER:])
    state = dot(later[:, :N], weighted, 0, 0)
    state = state[:, :INNER] + state[:, INNER:]
    grad = dot(later[:, N:], scaled, 0, 0)
    grad = grad[:, :INNER] + grad[:, INNER:]
    state_ref[...] = state
    grad_ref[...] = grad
    write_messages((msg_ref,), state, grad, log_total, places_ref[0:1], 0)


def real_halo(halo_ref, places_ref):
    first = places_ref[places_ref.shape[0] - 16 :][:1, :1]
    return jnp.where(first > 0.5, 0.0, halo_ref[HALO_ROWS - 8 :].astype(f32))


def fix_kernel(
    halo_ref, weight_ref, scaled_ref, tail_ref, places_ref, pre_in, xbc_in, weighted_in,
    pre_ref, xbc_ref, weighted_ref, factors_ref,
):
    halo = real_halo(halo_ref, places_ref)
    top = pre_in[0:8]
    for back in range(1, K):
        tap = weight_ref[K - 1 - back : K - back]
        top = top + jnp.where(iota(top.shape, 0) < back, tap * pltpu.roll(halo, back, 0), 0.0)
    pre = jnp.concatenate([top, pre_in[8:FIX_ROWS]], 0)
    pre_ref[0:FIX_ROWS] = pre
    gate = 1.0 / (1.0 + jnp.exp(-pre))
    xbc = (pre * gate).astype(bf16)
    xbc_ref[0:FIX_ROWS] = xbc
    xbc = xbc.astype(f32)
    weighted = jnp.concatenate([each.astype(f32) for each in split2(xbc[:, :INNER] * tail_ref[0:FIX_ROWS])], 1)
    weighted_ref[0:FIX_ROWS] = weighted.astype(bf16)
    scaled = scaled_ref[0:FIX_ROWS].astype(f32)

    def placed(low, high):
        row = iota(low.shape, 0)
        moved = jnp.concatenate([high[8:], high[:8]], 0)
        return jnp.where(row < K - 1, low, jnp.where((row >= 8) & (row < 8 + K - 1), moved, 0.0)).astype(bf16)

    zero = jnp.zeros((FIX_ROWS, N), f32)
    factors_ref[:, : 2 * INNER] = placed(weighted, scaled)
    factors_ref[:, 2 * INNER : 2 * INNER + N] = placed(xbc[:, INNER : INNER + N], zero)
    factors_ref[:, 2 * INNER + N :] = placed(zero, xbc[:, INNER + N :])


def first_parts(factors_ref):
    both = dot(factors_ref[:, 2 * INNER :], factors_ref[:, : 2 * INNER], 0, 0)
    both = both[:, :INNER] + both[:, INNER:]
    return both[:N], both[N:]


def merge_kernel(t, radix, next_radix, state_ref, grad_ref, logs_ref, places_ref, *refs):
    got, refs = refs[: radix - 1], refs[radix - 1 :]
    prior = after = 0.0
    if t > 0:
        prior, after = refs[0][...], refs[1][...]
        refs = refs[2:]
    else:
        parts, refs = [first_parts(ref) for ref in refs[: radix - 1]], refs[radix - 1 :]
    logs_out, prior_out, after_out, *refs = refs
    if not next_radix:
        state_out, grad_out, *refs = refs
    place = places_ref[8 * t : 8 * t + 1]
    log_prior, log_after, log_total = logs_ref[0:1], logs_ref[1:2], logs_ref[2:3]
    states = [message_block(ref, 0) for ref in got]
    grads = [message_block(ref, 1) for ref in got]
    logs = [message_log(ref) for ref in got]
    own_state, own_grad = state_ref[...], grad_ref[...]
    if t == 0:
        states = [each + part[0] for each, part in zip(states, parts)]
        grads = [each + part[1] for each, part in zip(grads, parts)]
    earlier = [s <= place for s in range(1, radix)]
    later = [s > place for s in range(1, radix)]
    before, log_before = chained(states, logs, earlier)
    beyond, log_beyond = chained(grads[::-1], logs[::-1], later[::-1])
    above, _ = chained(states, logs, later)
    below, _ = chained(grads[::-1], logs[::-1], earlier[::-1])
    mine = jnp.exp(log_total)
    state = above + jnp.exp(log_beyond) * (own_state + mine * before)
    grad = below + jnp.exp(log_before) * (own_grad + mine * beyond)
    prior_out[...] = prior + jnp.exp(log_prior) * before
    after_out[...] = after + jnp.exp(log_after) * beyond
    log_prior = log_prior + log_before
    log_after = log_after + log_beyond
    log_total = log_total + log_before + log_beyond
    row = iota((8, INNER), 0)
    logs_out[...] = jnp.where(row == 0, log_prior, jnp.where(row == 1, log_after, jnp.where(row == 2, log_total, 0.0)))
    if not next_radix:
        state_out[...] = state
        grad_out[...] = grad
    write_messages(refs, state, grad, log_total, places_ref[8 * t + 8 : 8 * t + 9], next_radix)


def local_kernel(
    xbc_ref, cot_ref, rows_ref, logs_ref, raw_ref, halo_ref, places_ref, scaled_ref, until_ref, pre_ref, factors_ref, state_in, grad_in,
    local_ref, sums_ref, weights_ref, moved_ref, slope_ref, state_ref, grad_ref,
):
    state, grad = first_parts(factors_ref)
    state_ref[...] = state_in[...] + state
    grad_ref[...] = grad_in[...] + grad
    pre = pre_ref[...]
    sigmoid = 1.0 / (1.0 + jnp.exp(-pre))
    slope_ref[...] = sigmoid * (1.0 + pre * (1.0 - sigmoid))
    tok = xbc_ref.shape[0]
    cot = cot_ref[...]
    values = xbc_ref[:, :INNER]
    b_proj = xbc_ref[:, INNER : INNER + N]
    c_proj = xbc_ref[:, INNER + N :]
    cum, step = rows_ref[0:8], rows_ref[8:16]
    step_wide = over_channels(step)
    values_f = values.astype(f32)
    cot_f = cot.astype(f32)
    stepped = pieces3(values_f * step_wide)
    gram = dot(b_proj, c_proj, 1, 1)
    reached = iota((tok, tok), 0) <= iota((tok, tok), 1)
    pieces = stacked(cum)
    piece_head = iota((4 * HEAD_ROWS, tok), 0) % HEAD_ROWS
    dgram = jnp.zeros((tok, tok), f32)
    grads, sums = [], []
    for h in range(H):
        of = slice(h * P_SIZE, (h + 1) * P_SIZE)
        column = dot(pieces, jnp.where(piece_head == h, 1.0, 0.0).astype(bf16), 0, 0)
        within = jnp.exp(jnp.where(reached, cum[h : h + 1] - column, -1e30))
        cot_h = cot[:, of]
        grads.append(sum(dot(each, cot_h) for each in pieces3(gram * within)))
        dmix = sum(dot(each[:, of], cot_h, 1, 1) for each in stepped) * within
        dgram = dgram + dmix
        sums.append(jnp.sum(dmix * gram, axis=0, keepdims=True))
    grad_stepped = jnp.concatenate(grads, 1)
    local_ref[:, :INNER] = grad_stepped * step_wide + logs_ref[3:4] * cot_f
    high, low = split2(dgram)
    local_ref[:, INNER : INNER + N] = dot(high, c_proj) + dot(low, c_proj)
    local_ref[:, INNER + N :] = dot(high, b_proj, 0, 0) + dot(low, b_proj, 0, 0)
    row = iota((HEAD_ROWS, tok), 0)
    pairs = jnp.zeros((HEAD_ROWS, tok), f32)
    for h in range(H):
        pairs = jnp.where(row == h, sums[h], pairs)
    left, gate, decay_rate = rows_ref[16:24], rows_ref[32:40], rows_ref[40:48]
    from_values = head_sums(values_f * grad_stepped, pieces3)
    skip_rows = head_sums(values_f * cot_f)
    base = pairs - from_values * step
    sums_ref[0:8] = base
    sums_ref[8:16] = from_values

    bias_weight = decay_rate * unstacked(dot(stacked(gate), until_ref[...]))
    cum_last, bias_last = cum[:, tok - 1 : tok], bias_weight[:, tok - 1 : tok]
    tail = left * step
    scaled_f = scaled_ref[:, :INNER].astype(f32) + scaled_ref[:, INNER:].astype(f32)
    weights_ref[:, :INNER] = scaled_f * over_channels(cum)
    weights_ref[:, INNER : 2 * INNER] = values_f * over_channels(tail * (cum_last - cum))
    weights_ref[:, 2 * INNER : 3 * INNER] = scaled_f * over_channels(bias_weight)
    weights_ref[:, 3 * INNER :] = values_f * over_channels(left * gate + tail * (bias_last - bias_weight))
    lane = iota((HEAD_ROWS, tok), 1)
    fixed = jnp.zeros((HEAD_ROWS, tok), f32)
    for i, column in enumerate((
        jnp.sum(from_values * gate + base * bias_weight, axis=1, keepdims=True),
        jnp.sum(base * cum, axis=1, keepdims=True),
        jnp.sum(skip_rows, axis=1, keepdims=True),
        bias_last, cum_last,
    )):
        fixed = jnp.where(lane == i, column, fixed)
    sums_ref[16:24] = fixed
    raw = raw_ref[...].astype(f32)
    halo = real_halo(halo_ref, places_ref)
    for back in range(1, K):
        moved_ref[(back - 1) * tok : back * tok] = shifted_down(raw, halo, back)


def totals_kernel(
    t, radix, raw_ref, moved_ref, xbc_ref, slope_ref, scaled_ref, weighted_ref, tail_ref, rows_ref, local_ref, sums_ref, weights_ref,
    logs_ref, places_ref, weight_ref, *refs
):
    got, refs = refs[: radix - 1], refs[radix - 1 :]
    prior = after = 0.0
    if t > 0:
        prior, after = refs[0][...], refs[1][...]
        refs = refs[2:]
    conv_ref, states_ref, totals_ref, spill_ref, totals_scratch = refs
    tok = raw_ref.shape[0]
    place = places_ref[8 * t : 8 * t + 1]
    blocks = [message_block(ref) for ref in got]
    logs = [message_log(ref) for ref in got]
    before, _ = chained(blocks, logs, [s <= place for s in range(1, radix)])
    beyond, _ = chained(blocks[::-1], logs[::-1], [s > place for s in range(radix - 1, 0, -1)])
    prior = prior + jnp.exp(logs_ref[0:1]) * before
    after = after + jnp.exp(logs_ref[1:2]) * beyond

    b_proj = xbc_ref[:, INNER : INNER + N]
    c_proj = xbc_ref[:, INNER + N :]
    prior2 = jnp.concatenate(split2(prior), 0)
    after2 = jnp.concatenate(split2(after), 0)
    seen = dot(jnp.concatenate([c_proj, c_proj], 1), prior2)
    back = dot(jnp.concatenate([b_proj, b_proj], 1), after2)
    grad_c = dot(scaled_ref[:, :INNER], prior2, 1, 1)
    grad_c = grad_c[:, :N] + grad_c[:, N:] + dot(scaled_ref[:, INNER:], prior2[:N], 1, 1)
    grad_b = dot(weighted_ref[:, :INNER], after2, 1, 1)
    grad_b = grad_b[:, :N] + grad_b[:, N:] + dot(weighted_ref[:, INNER:], after2[:N], 1, 1)
    grad_low = (local_ref[...] + jnp.concatenate([tail_ref[...] * back, grad_b, grad_c], 1)).astype(bf16)
    grad_conv = grad_low.astype(f32) * slope_ref[...]
    conv_ref[...] = grad_conv
    top = grad_conv[:8]
    spill = jnp.zeros_like(top)
    for ahead in range(1, K):
        tap = weight_ref[K - 1 - ahead : K - ahead]
        spill = spill + tap * jnp.where(iota(top.shape, 0) < 8 - ahead, 0.0, pltpu.roll(top, 8 - ahead, 0))
    spill_ref[...] = spill

    sums = [grad_conv * moved_ref[back * tok : (back + 1) * tok] for back in range(K - 2, -1, -1)]
    sums += [grad_conv * raw_ref[...].astype(f32), grad_conv]
    totals_scratch[...] = jnp.zeros_like(totals_scratch)
    for k, each in enumerate(sums):
        each = jnp.sum(each, axis=0, keepdims=True)
        for j in range(LANE_BLOCKS):
            at = k * LANE_BLOCKS + j
            totals_scratch[at : at + 1] = each[:, j * 128 : (j + 1) * 128]

    states_ref[:tok, :INNER] = seen
    states_ref[:tok, INNER:] = back
    through = jnp.sum(prior * after, axis=0, keepdims=True)
    grad_bias = jnp.sum(seen * weights_ref[:, 2 * INNER : 3 * INNER] + back * weights_ref[:, 3 * INNER :], axis=0, keepdims=True)
    grad_alog = jnp.sum(seen * weights_ref[:, :INNER] + back * weights_ref[:, INNER : 2 * INNER], axis=0, keepdims=True)
    selector = head_selector(HEAD_ROWS * 2)[:HEAD_ROWS].astype(f32)
    grad_bias, grad_alog, through = (
        jnp.sum(selector * each, axis=1, keepdims=True) for each in (grad_bias, grad_alog, through)
    )
    through = through * rows_ref[24:32][:, tok - 1 : tok]
    states_ref[tok:] = jnp.broadcast_to(through, (HEAD_ROWS, 2 * INNER))
    fixed = sums_ref[16:24]
    row, lane = iota((HEAD_ROWS, 128), 0), iota((HEAD_ROWS, 128), 1)
    small = jnp.zeros((HEAD_ROWS, 128), f32)
    for i, column in enumerate((
        fixed[:, 0:1] + grad_bias + through * fixed[:, 3:4],
        fixed[:, 1:2] + grad_alog + through * fixed[:, 4:5],
        fixed[:, 2:3],
    )):
        small = jnp.where((row < H) & (lane == row + i * H), column, small)
    totals_scratch[SMALL_ROW : SMALL_ROW + 1] = jnp.sum(small, axis=0, keepdims=True)
    totals_ref[...] = pack_totals(totals_scratch[...])


def input_kernel(
    conv_ref, weight_ref, states_ref, xbc_ref, scaled_ref, rows_ref, sums_ref, until_ref, out_hbm, dt_out_ref, end_ref, out_ref, sem
):
    grad_conv = conv_ref[...]
    tok, channels = grad_conv.shape
    grad_in = weight_ref[K - 1 : K] * grad_conv
    row8 = iota((8, channels), 0)
    for ahead in range(1, K):
        tap = weight_ref[K - 1 - ahead : K - ahead]
        moved = pltpu.roll(grad_conv, tok - ahead, 0)
        last8 = moved[tok - 8 :]
        inside = row8 < 8 - ahead
        grad_in = grad_in + tap * jnp.concatenate([moved[: tok - 8], jnp.where(inside, last8, 0.0)], 0)
    out_ref[...] = grad_in.astype(bf16)
    copy = pltpu.make_async_copy(out_ref, out_hbm, sem)
    copy.start()
    end_ref[...] = grad_in[tok - END_ROWS :]

    step, left, gate, decay_rate = rows_ref[8:16], rows_ref[16:24], rows_ref[32:40], rows_ref[40:48]
    scaled_f = scaled_ref[:, :INNER].astype(f32) + scaled_ref[:, INNER:].astype(f32)
    seen_rows = head_sums(scaled_f * states_ref[:tok, :INNER])
    tail_rows = head_sums(xbc_ref[:, :INNER].astype(f32) * states_ref[:tok, INNER:])
    tail_term = tail_rows * left * step
    last_extra = jnp.sum(tail_term, axis=1, keepdims=True) + states_ref[tok:][:, :1]
    grad_cum = sums_ref[0:8] + seen_rows - tail_term
    grad_log = unstacked(dot(stacked(grad_cum), until_ref[...], 1, 1)) + last_extra
    grad_step = sums_ref[8:16] + tail_rows * left + decay_rate * grad_log
    dt_out_ref[...] = (grad_step * gate)[0:H]
    copy.wait()


def end_kernel(end_ref, spilled_ref, places_ref, main_hbm, out_hbm, rows_ref, sem):
    end = end_ref[...]
    last = places_ref[places_ref.shape[0] - 8 :][:1, :1]
    fixed = end[END_ROWS - 8 :] + jnp.where(last > 0.5, 0.0, spilled_ref[...])
    rows_ref[...] = jnp.concatenate([end[: END_ROWS - 8], fixed], 0).astype(bf16)
    tok = out_hbm.shape[0]
    copy = pltpu.make_async_copy(rows_ref, out_hbm.at[pl.ds(tok - END_ROWS, END_ROWS)], sem)
    copy.start()
    copy.wait()


def summed(parts):
    large = jnp.sum(parts * jnp.exp(parts[:, SMALL_ROW + 1 : SMALL_ROW + 2]), axis=0)
    small = parts[:, SMALL_ROW : SMALL_ROW + 1] + parts[:, SMALL_ROW + 3 : SMALL_ROW + 4] * (1 / 256.0)
    small = small * jnp.exp(parts[:, SMALL_ROW + 2 : SMALL_ROW + 3])
    return large, jnp.sum(small, axis=0)


def repack_kernel(parts_ref, out_ref):
    large, small = summed(parts_ref[...])
    out_ref[...] = pack_totals(jnp.where(iota(large.shape, 0) == SMALL_ROW, small, large))


def finish_kernel(parts_ref, weight_ref, bias_ref, dt_bias_ref, alog_ref, skip_ref):
    large, small = summed(parts_ref[...])
    for k in range(K + 1):
        for j in range(LANE_BLOCKS):
            at = k * LANE_BLOCKS + j
            if k < K:
                weight_ref[k : k + 1, j * 128 : (j + 1) * 128] = large[at : at + 1]
            else:
                bias_ref[:, j * 128 : (j + 1) * 128] = large[at : at + 1]
    for i, ref in enumerate((dt_bias_ref, alog_ref, skip_ref)):
        ref[...] = small[:, i * H : (i + 1) * H]


def call(kernel, outs, in_specs, out_specs=None, scratch=(), flops=0, limit=16 << 20, aliases=None):
    return pl.pallas_call(
        kernel,
        out_shape=outs,
        in_specs=in_specs,
        out_specs=out_specs or jax.tree.map(lambda _: VMEM, outs),
        scratch_shapes=list(scratch),
        input_output_aliases=aliases or {},
        compiler_params=pltpu.CompilerParams(vmem_limit_bytes=limit),
        cost_estimate=pl.CostEstimate(flops=flops, bytes_accessed=1 << 20, transcendentals=0),
    )


def struct(shape, dtype=f32):
    return jax.ShapeDtypeStruct(shape, dtype)


def from_groups(messages, slabs, size, radix):
    got = []
    for s in range(1, radix):
        message = messages[s - 1 if len(messages) > 1 else 0]
        route = [(p, p - p % (size * radix) + (p + s * size) % (size * radix)) for p in range(slabs)]
        got.append(lax.ppermute(message, "ctx", route))
    return got


def states_from_groups(messages, slabs, size, radix):
    got = from_groups([message.astype(jnp.float16) for message in messages], slabs, size, radix)
    return [each.astype(f32) for each in got]


def stages_of(slabs):
    stages, size = [], 1
    while size < slabs:
        radix = 2 if (slabs // size).bit_length() % 2 == 0 else 4
        stages.append((size, radix))
        size *= radix
    assert size == slabs and len(stages) > 1
    return stages


def everyones(packed, axes, count):
    packed = jnp.broadcast_to(packed.astype(jnp.float16)[None], (count, *packed.shape))
    return lax.all_to_all(packed, axes, 0, 0).astype(f32)


def on_device(xbc_raw, conv_weight, conv_bias, dt_raw, dt_bias, a_log, d_skip, grad_out):
    tok, channels = xbc_raw.shape[1:]
    slabs = lax.axis_size("ctx")
    contexts = lax.axis_size("dp")
    stages = stages_of(slabs)

    raw, cot, dt_rows = xbc_raw[0], grad_out[0], dt_raw[0].T
    until = call(triangle_kernel, struct((tok, tok), bf16), [], flops=10**11)()
    until, bias, heads = call(
        heads_kernel,
        (struct((tok, tok), bf16), struct((1, channels)), struct((3 * HEAD_ROWS, tok))),
        [VMEM] * 5,
        aliases={4: 0},
    )(conv_bias[None], dt_bias[None], a_log[None], d_skip[None], until)
    early_raw, until = lax.optimization_barrier((raw, until))
    halo = lax.ppermute(early_raw[tok - HALO_ROWS :], "ctx", [(i, (i + 1) % slabs) for i in range(slabs)])

    def last_radix(t):
        return stages[t][1] if t == len(stages) - 1 else 0

    def messages(t):
        if last_radix(t):
            return (struct((N + TAIL_ROWS, INNER)),) * (last_radix(t) - 1)
        return (struct((2 * N + TAIL_ROWS, INNER)),)

    state_like = struct((N, INNER))
    logs_like = struct((8, INNER))
    pre, xbc, weighted, scaled, tail, rows, logs, places, state, grad, *outgoing = call(
        functools.partial(start_kernel, stages),
        (
            struct((tok, channels)), struct((tok, channels), bf16), struct((tok, 2 * INNER), bf16),
            struct((tok, 2 * INNER), bf16), struct((tok, INNER)), struct((6 * HEAD_ROWS, tok)),
            logs_like, struct((8 * len(stages) + 16, INNER)), state_like, state_like, *messages(0),
        ),
        [VMEM] * 7,
        scratch=[pltpu.VMEM((HEAD_ROWS, tok), f32)],
        flops=10**11,
    )(raw, cot, conv_weight, bias, dt_rows, heads, until)
    pre, xbc, weighted, factors = call(
        fix_kernel,
        (
            struct((tok, channels)), struct((tok, channels), bf16), struct((tok, 2 * INNER), bf16),
            struct((FIX_ROWS, 2 * INNER + 2 * N), bf16),
        ),
        [VMEM] * 8,
        flops=1_000_000,
        aliases={5: 0, 6: 1, 7: 2},
    )(halo, conv_weight, scaled, tail, places, pre, xbc, weighted)

    local, sums, weights, moved, slope, state, grad = call(
        local_kernel,
        (
            struct((tok, channels)), struct((3 * HEAD_ROWS, tok)), struct((tok, 4 * INNER)), struct(((K - 1) * tok, channels)),
            struct((tok, channels)), state_like, state_like,
        ),
        [VMEM] * 13,
        flops=10**11,
        aliases={11: 5, 12: 6},
    )(xbc, cot, rows, logs, raw, halo, places, scaled, until, pre, factors, state, grad)

    carried = ()
    for t, (size, radix) in enumerate(stages):
        got = states_from_groups(outgoing, slabs, size, radix)
        if t == 0:
            got, local, sums, weights, moved, slope = lax.optimization_barrier((got, local, sums, weights, moved, slope))
            carried = from_groups([factors], slabs, size, radix)
        if t == len(stages) - 1:
            break
        last = last_radix(t + 1)
        outs = (logs_like, state_like, state_like) + (() if last else (state_like, state_like))
        logs, *outgoing = call(
            functools.partial(merge_kernel, t, radix, last),
            outs + messages(t + 1),
            [VMEM] * (4 + len(got) + len(carried)),
            flops=1_000_000,
        )(state, grad, logs, places, *got, *carried)
        carried, outgoing = outgoing[:2], outgoing[2:]
        if not last:
            (state, grad), outgoing = outgoing[:2], outgoing[2:]

    grad_conv, states, packed, spill = call(
        functools.partial(totals_kernel, len(stages) - 1, radix),
        (struct((tok, channels)), struct((tok + HEAD_ROWS, 2 * INNER)), struct((TOTAL_ROWS, 128)), struct((8, channels))),
        [VMEM] * (14 + len(got) + len(carried)),
        scratch=[pltpu.VMEM((TOTAL_ROWS, 128), f32)],
        flops=200_000_000,
    )(raw, moved, xbc, slope, scaled, weighted, tail, rows, local, sums, weights, logs, places, conv_weight, *got, *carried)

    spilled = lax.ppermute(spill, "ctx", [((i + 1) % slabs, i) for i in range(slabs)])
    if slabs * contexts <= 64:
        parts = everyones(packed, ("ctx", "dp"), slabs * contexts)
    else:
        packed = call(repack_kernel, struct((TOTAL_ROWS, 128)), [VMEM])(everyones(packed, "ctx", slabs))
        parts = everyones(packed, "dp", contexts)

    grad_main, grad_dt, end = call(
        input_kernel,
        (struct((tok, channels), bf16), struct((H, tok)), struct((END_ROWS, channels))),
        [VMEM] * 8,
        (HBM, VMEM, VMEM),
        [pltpu.VMEM((tok, channels), bf16), pltpu.SemaphoreType.DMA],
        flops=1_000_000,
    )(grad_conv, conv_weight, states, xbc, scaled, rows, sums, until)
    grad_input = call(
        end_kernel,
        struct((tok, channels), bf16),
        [VMEM] * 3 + [HBM],
        HBM,
        [pltpu.VMEM((END_ROWS, channels), bf16), pltpu.SemaphoreType.DMA],
        aliases={3: 0},
    )(end, spilled, places, grad_main)

    grad_weight, grad_bias, *small = call(
        finish_kernel,
        (struct((K, channels)), struct((1, channels)), struct((1, H)), struct((1, H)), struct((1, H))),
        [VMEM],
    )(parts)
    return (grad_input[None], grad_dt.T[None], grad_weight, grad_bias[0], *(each[0] for each in small))


def solution(mesh):
    in_specs = (
        P("dp", "ctx", None),
        P(),
        P(),
        P("dp", "ctx", None),
        P(),
        P(),
        P(),
        P("dp", "ctx", None),
    )
    out_specs = (P("dp", "ctx", None), P("dp", "ctx", None), P(), P(), P(), P(), P())
    return jax.shard_map(
        on_device, mesh=mesh, in_specs=in_specs, out_specs=out_specs, check_vma=False
    )
```

```python
import functools

import jax
import jax.numpy as jnp
from jax import lax
from jax.experimental import pallas as pl
from jax.experimental.pallas import tpu as pltpu
from jax.sharding import PartitionSpec as P

H = 4
P_SIZE = 64
N = 128
K = 4
INNER = H * P_SIZE
HEAD_ROWS = 8
TAIL_ROWS = 8
HALO_ROWS = 16
FIX_ROWS = 16
END_ROWS = 16
LANE_BLOCKS = (INNER + 2 * N) // 128
SMALL_ROW = (K + 1) * LANE_BLOCKS
TOTAL_ROWS = 24

f32 = jnp.float32
bf16 = jnp.bfloat16

VMEM = pl.BlockSpec(memory_space=pltpu.VMEM)
HBM = pl.BlockSpec(memory_space=pltpu.HBM)


def dot(a, b, a_dim=1, b_dim=0):
    return lax.dot_general(a, b, (((a_dim,), (b_dim,)), ((), ())), preferred_element_type=f32)


def split2(x):
    high = x.astype(bf16)
    return high, (x - high.astype(f32)).astype(bf16)


def split3(x):
    high = x.astype(bf16).astype(f32)
    rest = x - high
    middle = rest.astype(bf16).astype(f32)
    return high, middle, rest - middle


def iota(shape, dim):
    return lax.broadcasted_iota(jnp.int32, shape, dim)


def stacked(rows):
    return jnp.concatenate([*split3(rows), jnp.zeros_like(rows)], 0).astype(bf16)


def unstacked(rows):
    return rows[0:8] + rows[8:16] + rows[16:24]


def head_selector(rows):
    shape = (rows, INNER)
    return jnp.where(iota(shape, 1) // P_SIZE == iota(shape, 0) % HEAD_ROWS, 1.0, 0.0).astype(bf16)


def over_channels(rows):
    return dot(stacked(rows), head_selector(4 * HEAD_ROWS), 0, 0)


def pieces3(x):
    return [each.astype(bf16) for each in split3(x)]


def head_sums(x, split=split2):
    selector = head_selector(HEAD_ROWS * 2)
    return sum(dot(selector, each, 1, 1) for each in split(x))[:HEAD_ROWS]


def by_head(ref, width):
    row = iota((HEAD_ROWS, width), 0)
    out = jnp.zeros((HEAD_ROWS, width), f32)
    for h in range(H):
        out = jnp.where(row == h, ref[:, h : h + 1], out)
    return out


def shifted_down(x, first, count):
    moved = pltpu.roll(x, count, 0)
    top = jnp.where(iota(first.shape, 0) < count, pltpu.roll(first, count, 0), moved[:8])
    return jnp.concatenate([top, moved[8:]], 0)


def quantized_log(size):
    return jnp.log(jnp.maximum(size, 1e-30)).astype(bf16).astype(f32)


def scaled_columns(x):
    log_size = quantized_log(jnp.max(jnp.abs(x), axis=0, keepdims=True))
    return x * jnp.exp(-log_size), log_size


def write_messages(msg_refs, state, grad, log_total, place, radix):
    row = iota((TAIL_ROWS, INNER), 0)
    high, middle, low = split3(log_total)
    tail = jnp.where(row == 4, high, jnp.where(row == 5, middle * 256.0, jnp.where(row == 6, low * 65536.0, 0.0)))
    state, state_size = scaled_columns(state)
    grad, grad_size = scaled_columns(grad)
    if radix:
        for s, msg_ref in enumerate(msg_refs, 1):
            on = place + s < radix
            msg_ref[0:N] = jnp.where(on, state, grad)
            msg_ref[N : N + TAIL_ROWS] = jnp.where(row == 0, jnp.where(on, state_size, grad_size), tail)
    else:
        (msg_ref,) = msg_refs
        msg_ref[0:N] = state
        msg_ref[N : 2 * N] = grad
        msg_ref[2 * N : 2 * N + TAIL_ROWS] = jnp.where(row == 0, state_size, jnp.where(row == 1, grad_size, tail))


def message_log(got_ref):
    rows = got_ref.shape[0] - TAIL_ROWS
    tail = got_ref[rows : rows + 8]
    return tail[4:5] + tail[5:6] * (1 / 256.0) + tail[6:7] * (1 / 65536.0)


def message_block(got_ref, which=0):
    rows = got_ref.shape[0] - TAIL_ROWS
    return got_ref[which * N : (which + 1) * N] * jnp.exp(got_ref[rows + which : rows + which + 1])


def chained(blocks, logs, used):
    total, log_sum = 0.0, 0.0
    for block, log, use in zip(blocks, logs, used):
        total = total + jnp.where(use, jnp.exp(log_sum) * block, 0.0)
        log_sum = log_sum + jnp.where(use, log, 0.0)
    return total, log_sum


def pack_totals(x):
    row = iota(x.shape, 0)
    large = jnp.where(row < SMALL_ROW, x, 0.0)
    large_size = quantized_log(jnp.max(jnp.abs(large), axis=0, keepdims=True))
    small = x[SMALL_ROW : SMALL_ROW + 1]
    small_size = quantized_log(jnp.abs(small))
    small = small * jnp.exp(-small_size)
    small_high = small.astype(bf16).astype(f32)
    out = jnp.where(row == SMALL_ROW, small_high, large * jnp.exp(-large_size))
    out = jnp.where(row == SMALL_ROW + 3, (small - small_high) * 256.0, out)
    return jnp.where(row == SMALL_ROW + 1, large_size, jnp.where(row == SMALL_ROW + 2, small_size, out))


def triangle_kernel(until_ref):
    shape = until_ref.shape
    until_ref[...] = jnp.where(iota(shape, 0) <= iota(shape, 1), 1.0, 0.0).astype(bf16)


def heads_kernel(bias_ref, dt_bias_ref, alog_ref, skip_ref, until_in, until_ref, bias_out, heads_ref):
    bias_out[...] = bias_ref[...]
    for i, ref in enumerate((dt_bias_ref, alog_ref, skip_ref)):
        heads_ref[8 * i : 8 * i + 8] = by_head(ref, until_ref.shape[1])


def mask_first(x):
    top = jnp.where(iota((FIX_ROWS, x.shape[1]), 0) < K - 1, 0.0, x[:FIX_ROWS].astype(f32))
    return jnp.concatenate([top.astype(x.dtype), x[FIX_ROWS:]], 0)


def start_kernel(
    stages, raw_ref, cot_ref, weight_ref, bias_ref, dt_ref, heads_ref, until_ref,
    pre_ref, xbc_ref, weighted_ref, scaled_ref, tail_ref, rows_ref, logs_ref, places_ref, state_ref, grad_ref, msg_ref, dt8_ref,
):
    tok = raw_ref.shape[0]
    place = lax.axis_index("ctx")
    for t, (size, radix) in enumerate(stages):
        places_ref[8 * t : 8 * t + 8] = jnp.full((8, INNER), lax.rem(lax.div(place, size), radix), jnp.int32).astype(f32)
    at = 8 * len(stages)
    slabs = stages[-1][0] * stages[-1][1]
    places_ref[at : at + 8] = jnp.full((8, INNER), jnp.where(place == 0, 1, 0), jnp.int32).astype(f32)
    places_ref[at + 8 : at + 16] = jnp.full((8, INNER), jnp.where(place == slabs - 1, 1, 0), jnp.int32).astype(f32)
    dt8_ref[...] = jnp.zeros_like(dt8_ref)
    dt8_ref[0:H] = dt_ref[...]
    dt_pre = dt8_ref[...] + heads_ref[0:8]
    step = jnp.maximum(dt_pre, 0.0) + jnp.log1p(jnp.exp(-jnp.abs(dt_pre)))
    real = iota((HEAD_ROWS, tok), 0) < H
    decay_rate = jnp.where(real, -jnp.exp(heads_ref[8:16]), 0.0)
    cum = unstacked(dot(stacked(step * decay_rate), until_ref[...]))
    left = jnp.exp(cum[:, tok - 1 : tok] - cum)
    reach = jnp.exp(cum)
    rows_ref[0:8] = cum
    rows_ref[8:16] = step
    rows_ref[16:24] = left
    rows_ref[24:32] = reach
    rows_ref[32:40] = 1.0 / (1.0 + jnp.exp(-dt_pre))
    rows_ref[40:48] = decay_rate
    tail = over_channels(left * step)
    tail_ref[...] = tail
    log_total = over_channels(cum)[tok - 1 : tok]
    skip = over_channels(heads_ref[16:24])[0:1]
    row = iota((8, INNER), 0)
    logs_ref[...] = jnp.where(row == 2, log_total, jnp.where(row == 3, skip, 0.0))
    scaled = jnp.concatenate(split2(cot_ref[...].astype(f32) * over_channels(reach)), 1)
    scaled_ref[...] = scaled

    raw = raw_ref[...].astype(f32)
    zeros = jnp.zeros((8, raw.shape[1]), f32)
    pre = bias_ref[...] + weight_ref[K - 1 : K] * raw
    for back in range(1, K):
        pre = pre + weight_ref[K - 1 - back : K - back] * shifted_down(raw, zeros, back)
    pre_ref[...] = pre
    gate = 1.0 / (1.0 + jnp.exp(-pre))
    xbc = (pre * gate).astype(bf16)
    xbc_ref[...] = xbc
    weighted = jnp.concatenate(split2(xbc[:, :INNER].astype(f32) * tail), 1)
    weighted_ref[...] = weighted
    later = mask_first(xbc[:, INNER:])
    state = dot(later[:, :N], weighted, 0, 0)
    state = state[:, :INNER] + state[:, INNER:]
    grad = dot(later[:, N:], scaled, 0, 0)
    grad = grad[:, :INNER] + grad[:, INNER:]
    state_ref[...] = state
    grad_ref[...] = grad
    write_messages((msg_ref,), state, grad, log_total, places_ref[0:1], 0)


def real_halo(halo_ref, places_ref):
    first = places_ref[places_ref.shape[0] - 16 :][:1, :1]
    return jnp.where(first > 0.5, 0.0, halo_ref[HALO_ROWS - 8 :].astype(f32))


def fix_kernel(
    halo_ref, weight_ref, scaled_ref, tail_ref, places_ref, pre_in, xbc_in, weighted_in,
    pre_ref, xbc_ref, weighted_ref, factors_ref,
):
    halo = real_halo(halo_ref, places_ref)
    top = pre_in[0:8]
    for back in range(1, K):
        tap = weight_ref[K - 1 - back : K - back]
        top = top + jnp.where(iota(top.shape, 0) < back, tap * pltpu.roll(halo, back, 0), 0.0)
    pre = jnp.concatenate([top, pre_in[8:FIX_ROWS]], 0)
    pre_ref[0:FIX_ROWS] = pre
    gate = 1.0 / (1.0 + jnp.exp(-pre))
    xbc = (pre * gate).astype(bf16)
    xbc_ref[0:FIX_ROWS] = xbc
    xbc = xbc.astype(f32)
    weighted = jnp.concatenate([each.astype(f32) for each in split2(xbc[:, :INNER] * tail_ref[0:FIX_ROWS])], 1)
    weighted_ref[0:FIX_ROWS] = weighted.astype(bf16)
    scaled = scaled_ref[0:FIX_ROWS].astype(f32)

    def packed(*parts):
        row = iota((FIX_ROWS, parts[0].shape[1]), 0)
        out = jnp.zeros(row.shape, f32)
        for at, part in enumerate(parts):
            part = pltpu.roll(part, at * (K - 1), 0) if at else part
            out = jnp.where((row >= at * (K - 1)) & (row < (at + 1) * (K - 1)), part, out)
        return out.astype(bf16)

    b_proj, c_proj = xbc[:, INNER : INNER + N], xbc[:, INNER + N :]
    factors_ref[:, :INNER] = packed(weighted[:, :INNER], weighted[:, INNER:], scaled[:, :INNER], scaled[:, INNER:])
    factors_ref[:, INNER:] = packed(b_proj, b_proj, c_proj, c_proj)


def first_parts(factors_ref):
    rows = factors_ref[:, INNER:].astype(f32)
    of_state = iota(rows.shape, 0) < 2 * (K - 1)
    rows = jnp.concatenate([jnp.where(of_state, rows, 0.0), jnp.where(of_state, 0.0, rows)], 1).astype(bf16)
    both = dot(rows, factors_ref[:, :INNER], 0, 0)
    return both[:N], both[N:]


def merge_kernel(t, radix, next_radix, state_ref, grad_ref, logs_ref, places_ref, *refs):
    got, refs = refs[: radix - 1], refs[radix - 1 :]
    prior = after = 0.0
    if t > 0:
        prior, after = refs[0][...], refs[1][...]
        refs = refs[2:]
    else:
        parts, refs = [first_parts(ref) for ref in refs[: radix - 1]], refs[radix - 1 :]
    logs_out, prior_out, after_out, *refs = refs
    if not next_radix:
        state_out, grad_out, *refs = refs
    place = places_ref[8 * t : 8 * t + 1]
    log_prior, log_after, log_total = logs_ref[0:1], logs_ref[1:2], logs_ref[2:3]
    states = [message_block(ref, 0) for ref in got]
    grads = [message_block(ref, 1) for ref in got]
    logs = [message_log(ref) for ref in got]
    own_state, own_grad = state_ref[...], grad_ref[...]
    if t == 0:
        states = [each + part[0] for each, part in zip(states, parts)]
        grads = [each + part[1] for each, part in zip(grads, parts)]
    earlier = [s <= place for s in range(1, radix)]
    later = [s > place for s in range(1, radix)]
    before, log_before = chained(states, logs, earlier)
    beyond, log_beyond = chained(grads[::-1], logs[::-1], later[::-1])
    above, _ = chained(states, logs, later)
    below, _ = chained(grads[::-1], logs[::-1], earlier[::-1])
    mine = jnp.exp(log_total)
    state = above + jnp.exp(log_beyond) * (own_state + mine * before)
    grad = below + jnp.exp(log_before) * (own_grad + mine * beyond)
    prior_out[...] = prior + jnp.exp(log_prior) * before
    after_out[...] = after + jnp.exp(log_after) * beyond
    log_prior = log_prior + log_before
    log_after = log_after + log_beyond
    log_total = log_total + log_before + log_beyond
    row = iota((8, INNER), 0)
    logs_out[...] = jnp.where(row == 0, log_prior, jnp.where(row == 1, log_after, jnp.where(row == 2, log_total, 0.0)))
    if not next_radix:
        state_out[...] = state
        grad_out[...] = grad
    write_messages(refs, state, grad, log_total, places_ref[8 * t + 8 : 8 * t + 9], next_radix)


def local_kernel(
    xbc_ref, cot_ref, rows_ref, logs_ref, factors_ref, state_in, grad_in, local_ref, sums_ref, state_ref, grad_ref,
):
    state, grad = first_parts(factors_ref)
    state_ref[...] = state_in[...] + state
    grad_ref[...] = grad_in[...] + grad
    tok = xbc_ref.shape[0]
    cot = cot_ref[...]
    values = xbc_ref[:, :INNER]
    b_proj = xbc_ref[:, INNER : INNER + N]
    c_proj = xbc_ref[:, INNER + N :]
    cum, step = rows_ref[0:8], rows_ref[8:16]
    step_wide = over_channels(step)
    values_f = values.astype(f32)
    cot_f = cot.astype(f32)
    stepped = pieces3(values_f * step_wide)
    gram = dot(b_proj, c_proj, 1, 1)
    reached = iota((tok, tok), 0) <= iota((tok, tok), 1)
    pieces = stacked(cum)
    piece_head = iota((4 * HEAD_ROWS, tok), 0) % HEAD_ROWS
    dgram = jnp.zeros((tok, tok), f32)
    grads, sums = [], []
    for h in range(H):
        of = slice(h * P_SIZE, (h + 1) * P_SIZE)
        column = dot(pieces, jnp.where(piece_head == h, 1.0, 0.0).astype(bf16), 0, 0)
        within = jnp.exp(jnp.where(reached, cum[h : h + 1] - column, -1e30))
        cot_h = cot[:, of]
        grads.append(sum(dot(each, cot_h) for each in pieces3(gram * within)))
        dmix = sum(dot(each[:, of], cot_h, 1, 1) for each in stepped) * within
        dgram = dgram + dmix
        sums.append(jnp.sum(dmix * gram, axis=0, keepdims=True))
    grad_stepped = jnp.concatenate(grads, 1)
    local_ref[:, :INNER] = grad_stepped * step_wide + logs_ref[3:4] * cot_f
    high, low = split2(dgram)
    local_ref[:, INNER : INNER + N] = dot(high, c_proj) + dot(low, c_proj)
    local_ref[:, INNER + N :] = dot(high, b_proj, 0, 0) + dot(low, b_proj, 0, 0)
    row = iota((HEAD_ROWS, tok), 0)
    pairs = jnp.zeros((HEAD_ROWS, tok), f32)
    for h in range(H):
        pairs = jnp.where(row == h, sums[h], pairs)
    from_values = head_sums(values_f * grad_stepped, pieces3)
    sums_ref[0:8] = pairs - from_values * step
    sums_ref[8:16] = from_values


def weights_kernel(
    xbc_ref, cot_ref, rows_ref, raw_ref, halo_ref, places_ref, scaled_ref, until_ref, pre_ref, sums_ref, logs_ref,
    weights_ref, fixed_ref, moved_ref, slope_ref,
):
    tok = xbc_ref.shape[0]
    pre = pre_ref[...]
    sigmoid = 1.0 / (1.0 + jnp.exp(-pre))
    slope_ref[...] = sigmoid * (1.0 + pre * (1.0 - sigmoid))
    values_f = xbc_ref[:, :INNER].astype(f32)
    cum, step, left = rows_ref[0:8], rows_ref[8:16], rows_ref[16:24]
    gate, decay_rate = rows_ref[32:40], rows_ref[40:48]
    base, from_values = sums_ref[0:8], sums_ref[8:16]
    skip_rows = head_sums(values_f * cot_ref[...].astype(f32))

    bias_weight = decay_rate * unstacked(dot(stacked(gate), until_ref[...]))
    cum_last, bias_last = cum[:, tok - 1 : tok], bias_weight[:, tok - 1 : tok]
    tail = left * step
    scaled_f = scaled_ref[:, :INNER].astype(f32) + scaled_ref[:, INNER:].astype(f32)
    weights_ref[:, :INNER] = scaled_f * over_channels(cum)
    weights_ref[:, INNER : 2 * INNER] = values_f * over_channels(tail * (cum_last - cum))
    weights_ref[:, 2 * INNER : 3 * INNER] = scaled_f * over_channels(bias_weight)
    weights_ref[:, 3 * INNER :] = values_f * over_channels(left * gate + tail * (bias_last - bias_weight))
    lane = iota((HEAD_ROWS, tok), 1)
    fixed = jnp.zeros((HEAD_ROWS, tok), f32)
    for i, column in enumerate((
        jnp.sum(from_values * gate + base * bias_weight, axis=1, keepdims=True),
        jnp.sum(base * cum, axis=1, keepdims=True),
        jnp.sum(skip_rows, axis=1, keepdims=True),
        bias_last, cum_last,
    )):
        fixed = jnp.where(lane == i, column, fixed)
    fixed_ref[...] = fixed
    raw = raw_ref[...].astype(f32)
    halo = real_halo(halo_ref, places_ref)
    for back in range(1, K):
        moved_ref[(back - 1) * tok : back * tok] = shifted_down(raw, halo, back)


def totals_kernel(
    t, radix, raw_ref, moved_ref, xbc_ref, slope_ref, scaled_ref, weighted_ref, tail_ref, rows_ref, local_ref, fixed_ref, weights_ref,
    logs_ref, places_ref, weight_ref, *refs
):
    got, refs = refs[: radix - 1], refs[radix - 1 :]
    prior = after = 0.0
    if t > 0:
        prior, after = refs[0][...], refs[1][...]
        refs = refs[2:]
    conv_ref, states_ref, totals_ref, spill_ref, totals_scratch = refs
    tok = raw_ref.shape[0]
    place = places_ref[8 * t : 8 * t + 1]
    blocks = [message_block(ref) for ref in got]
    logs = [message_log(ref) for ref in got]
    before, _ = chained(blocks, logs, [s <= place for s in range(1, radix)])
    beyond, _ = chained(blocks[::-1], logs[::-1], [s > place for s in range(radix - 1, 0, -1)])
    prior = prior + jnp.exp(logs_ref[0:1]) * before
    after = after + jnp.exp(logs_ref[1:2]) * beyond

    b_proj = xbc_ref[:, INNER : INNER + N]
    c_proj = xbc_ref[:, INNER + N :]
    prior2 = jnp.concatenate(split2(prior), 0)
    after2 = jnp.concatenate(split2(after), 0)
    seen = dot(jnp.concatenate([c_proj, c_proj], 1), prior2)
    back = dot(jnp.concatenate([b_proj, b_proj], 1), after2)
    grad_c = dot(scaled_ref[:, :INNER], prior2, 1, 1)
    grad_c = grad_c[:, :N] + grad_c[:, N:] + dot(scaled_ref[:, INNER:], prior2[:N], 1, 1)
    grad_b = dot(weighted_ref[:, :INNER], after2, 1, 1)
    grad_b = grad_b[:, :N] + grad_b[:, N:] + dot(weighted_ref[:, INNER:], after2[:N], 1, 1)
    grad_low = (local_ref[...] + jnp.concatenate([tail_ref[...] * back, grad_b, grad_c], 1)).astype(bf16)
    grad_conv = grad_low.astype(f32) * slope_ref[...]
    conv_ref[...] = grad_conv
    top = grad_conv[:8]
    spill = jnp.zeros_like(top)
    for ahead in range(1, K):
        tap = weight_ref[K - 1 - ahead : K - ahead]
        spill = spill + tap * jnp.where(iota(top.shape, 0) < 8 - ahead, 0.0, pltpu.roll(top, 8 - ahead, 0))
    spill_ref[...] = spill

    sums = [grad_conv * moved_ref[back * tok : (back + 1) * tok] for back in range(K - 2, -1, -1)]
    sums += [grad_conv * raw_ref[...].astype(f32), grad_conv]
    totals_scratch[...] = jnp.zeros_like(totals_scratch)
    for k, each in enumerate(sums):
        each = jnp.sum(each, axis=0, keepdims=True)
        for j in range(LANE_BLOCKS):
            at = k * LANE_BLOCKS + j
            totals_scratch[at : at + 1] = each[:, j * 128 : (j + 1) * 128]

    states_ref[:tok, :INNER] = seen
    states_ref[:tok, INNER:] = back
    through = jnp.sum(prior * after, axis=0, keepdims=True)
    grad_bias = jnp.sum(seen * weights_ref[:, 2 * INNER : 3 * INNER] + back * weights_ref[:, 3 * INNER :], axis=0, keepdims=True)
    grad_alog = jnp.sum(seen * weights_ref[:, :INNER] + back * weights_ref[:, INNER : 2 * INNER], axis=0, keepdims=True)
    selector = head_selector(HEAD_ROWS * 2)[:HEAD_ROWS].astype(f32)
    grad_bias, grad_alog, through = (
        jnp.sum(selector * each, axis=1, keepdims=True) for each in (grad_bias, grad_alog, through)
    )
    through = through * rows_ref[24:32][:, tok - 1 : tok]
    states_ref[tok:] = jnp.broadcast_to(through, (HEAD_ROWS, 2 * INNER))
    fixed = fixed_ref[...]
    row, lane = iota((HEAD_ROWS, 128), 0), iota((HEAD_ROWS, 128), 1)
    small = jnp.zeros((HEAD_ROWS, 128), f32)
    for i, column in enumerate((
        fixed[:, 0:1] + grad_bias + through * fixed[:, 3:4],
        fixed[:, 1:2] + grad_alog + through * fixed[:, 4:5],
        fixed[:, 2:3],
    )):
        small = jnp.where((row < H) & (lane == row + i * H), column, small)
    totals_scratch[SMALL_ROW : SMALL_ROW + 1] = jnp.sum(small, axis=0, keepdims=True)
    totals_ref[...] = pack_totals(totals_scratch[...])


def input_kernel(
    conv_ref, weight_ref, states_ref, xbc_ref, scaled_ref, rows_ref, sums_ref, until_ref, out_hbm, dt_out_ref, end_ref, out_ref, sem
):
    grad_conv = conv_ref[...]
    tok, channels = grad_conv.shape
    grad_in = weight_ref[K - 1 : K] * grad_conv
    row8 = iota((8, channels), 0)
    for ahead in range(1, K):
        tap = weight_ref[K - 1 - ahead : K - ahead]
        moved = pltpu.roll(grad_conv, tok - ahead, 0)
        last8 = moved[tok - 8 :]
        inside = row8 < 8 - ahead
        grad_in = grad_in + tap * jnp.concatenate([moved[: tok - 8], jnp.where(inside, last8, 0.0)], 0)
    out_ref[...] = grad_in.astype(bf16)
    copy = pltpu.make_async_copy(out_ref, out_hbm, sem)
    copy.start()
    end_ref[...] = grad_in[tok - END_ROWS :]

    step, left, gate, decay_rate = rows_ref[8:16], rows_ref[16:24], rows_ref[32:40], rows_ref[40:48]
    scaled_f = scaled_ref[:, :INNER].astype(f32) + scaled_ref[:, INNER:].astype(f32)
    seen_rows = head_sums(scaled_f * states_ref[:tok, :INNER])
    tail_rows = head_sums(xbc_ref[:, :INNER].astype(f32) * states_ref[:tok, INNER:])
    tail_term = tail_rows * left * step
    last_extra = jnp.sum(tail_term, axis=1, keepdims=True) + states_ref[tok:][:, :1]
    grad_cum = sums_ref[0:8] + seen_rows - tail_term
    grad_log = unstacked(dot(stacked(grad_cum), until_ref[...], 1, 1)) + last_extra
    grad_step = sums_ref[8:16] + tail_rows * left + decay_rate * grad_log
    dt_out_ref[...] = (grad_step * gate)[0:H]
    copy.wait()


def end_kernel(end_ref, spilled_ref, places_ref, main_hbm, out_hbm, rows_ref, sem):
    end = end_ref[...]
    last = places_ref[places_ref.shape[0] - 8 :][:1, :1]
    fixed = end[END_ROWS - 8 :] + jnp.where(last > 0.5, 0.0, spilled_ref[...])
    rows_ref[...] = jnp.concatenate([end[: END_ROWS - 8], fixed], 0).astype(bf16)
    tok = out_hbm.shape[0]
    copy = pltpu.make_async_copy(rows_ref, out_hbm.at[pl.ds(tok - END_ROWS, END_ROWS)], sem)
    copy.start()
    copy.wait()


def summed(parts):
    large = jnp.sum(parts * jnp.exp(parts[:, SMALL_ROW + 1 : SMALL_ROW + 2]), axis=0)
    small = parts[:, SMALL_ROW : SMALL_ROW + 1] + parts[:, SMALL_ROW + 3 : SMALL_ROW + 4] * (1 / 256.0)
    small = small * jnp.exp(parts[:, SMALL_ROW + 2 : SMALL_ROW + 3])
    return large, jnp.sum(small, axis=0)


def repack_kernel(parts_ref, out_ref):
    large, small = summed(parts_ref[...])
    out_ref[...] = pack_totals(jnp.where(iota(large.shape, 0) == SMALL_ROW, small, large))


def finish_kernel(parts_ref, weight_ref, bias_ref, dt_bias_ref, alog_ref, skip_ref):
    large, small = summed(parts_ref[...])
    for k in range(K + 1):
        for j in range(LANE_BLOCKS):
            at = k * LANE_BLOCKS + j
            if k < K:
                weight_ref[k : k + 1, j * 128 : (j + 1) * 128] = large[at : at + 1]
            else:
                bias_ref[:, j * 128 : (j + 1) * 128] = large[at : at + 1]
    for i, ref in enumerate((dt_bias_ref, alog_ref, skip_ref)):
        ref[...] = small[:, i * H : (i + 1) * H]


def call(kernel, outs, in_specs, out_specs=None, scratch=(), flops=0, limit=16 << 20, aliases=None):
    return pl.pallas_call(
        kernel,
        out_shape=outs,
        in_specs=in_specs,
        out_specs=out_specs or jax.tree.map(lambda _: VMEM, outs),
        scratch_shapes=list(scratch),
        input_output_aliases=aliases or {},
        compiler_params=pltpu.CompilerParams(vmem_limit_bytes=limit),
        cost_estimate=pl.CostEstimate(flops=flops, bytes_accessed=1 << 20, transcendentals=0),
    )


def struct(shape, dtype=f32):
    return jax.ShapeDtypeStruct(shape, dtype)


def from_groups(messages, slabs, size, radix):
    got = []
    for s in range(1, radix):
        message = messages[s - 1 if len(messages) > 1 else 0]
        route = [(p, p - p % (size * radix) + (p + s * size) % (size * radix)) for p in range(slabs)]
        got.append(lax.ppermute(message, "ctx", route))
    return got


def states_from_groups(messages, slabs, size, radix):
    got = from_groups([message.astype(jnp.float16) for message in messages], slabs, size, radix)
    return [each.astype(f32) for each in got]


def stages_of(slabs):
    stages, size = [], 1
    while size < slabs:
        radix = 2 if (slabs // size).bit_length() % 2 == 0 else 4
        stages.append((size, radix))
        size *= radix
    assert size == slabs and len(stages) > 1
    return stages


def everyones(packed, axes, count):
    packed = jnp.broadcast_to(packed.astype(jnp.float16)[None], (count, *packed.shape))
    return lax.all_to_all(packed, axes, 0, 0).astype(f32)


def on_device(xbc_raw, conv_weight, conv_bias, dt_raw, dt_bias, a_log, d_skip, grad_out):
    tok, channels = xbc_raw.shape[1:]
    slabs = lax.axis_size("ctx")
    contexts = lax.axis_size("dp")
    stages = stages_of(slabs)

    raw, cot, dt_rows = xbc_raw[0], grad_out[0], dt_raw[0].T
    until = call(triangle_kernel, struct((tok, tok), bf16), [], flops=10**11)()
    until, bias, heads = call(
        heads_kernel,
        (struct((tok, tok), bf16), struct((1, channels)), struct((3 * HEAD_ROWS, tok))),
        [VMEM] * 5,
        aliases={4: 0},
    )(conv_bias[None], dt_bias[None], a_log[None], d_skip[None], until)
    early_raw, until = lax.optimization_barrier((raw, until))
    halo = lax.ppermute(early_raw[tok - HALO_ROWS :], "ctx", [(i, (i + 1) % slabs) for i in range(slabs)])

    def last_radix(t):
        return stages[t][1] if t == len(stages) - 1 else 0

    def messages(t):
        if last_radix(t):
            return (struct((N + TAIL_ROWS, INNER)),) * (last_radix(t) - 1)
        return (struct((2 * N + TAIL_ROWS, INNER)),)

    state_like = struct((N, INNER))
    logs_like = struct((8, INNER))
    pre, xbc, weighted, scaled, tail, rows, logs, places, state, grad, *outgoing = call(
        functools.partial(start_kernel, stages),
        (
            struct((tok, channels)), struct((tok, channels), bf16), struct((tok, 2 * INNER), bf16),
            struct((tok, 2 * INNER), bf16), struct((tok, INNER)), struct((6 * HEAD_ROWS, tok)),
            logs_like, struct((8 * len(stages) + 16, INNER)), state_like, state_like, *messages(0),
        ),
        [VMEM] * 7,
        scratch=[pltpu.VMEM((HEAD_ROWS, tok), f32)],
        flops=10**11,
    )(raw, cot, conv_weight, bias, dt_rows, heads, until)
    pre, xbc, weighted, factors = call(
        fix_kernel,
        (
            struct((tok, channels)), struct((tok, channels), bf16), struct((tok, 2 * INNER), bf16),
            struct((FIX_ROWS, INNER + N), bf16),
        ),
        [VMEM] * 8,
        flops=1_000_000,
        aliases={5: 0, 6: 1, 7: 2},
    )(halo, conv_weight, scaled, tail, places, pre, xbc, weighted)

    local, sums, state, grad = call(
        local_kernel,
        (struct((tok, channels)), struct((2 * HEAD_ROWS, tok)), state_like, state_like),
        [VMEM] * 7,
        flops=10**11,
        aliases={5: 2, 6: 3},
    )(xbc, cot, rows, logs, factors, state, grad)

    carried = ()
    for t, (size, radix) in enumerate(stages):
        got = states_from_groups(outgoing, slabs, size, radix)
        if t == 0:
            got, local, sums = lax.optimization_barrier((got, local, sums))
            carried = from_groups([factors], slabs, size, radix)
        if t == len(stages) - 1:
            got, weights, fixed, moved, slope = lax.optimization_barrier((got, weights, fixed, moved, slope))
            break
        last = last_radix(t + 1)
        outs = (logs_like, state_like, state_like) + (() if last else (state_like, state_like))
        logs, *outgoing = call(
            functools.partial(merge_kernel, t, radix, last),
            outs + messages(t + 1),
            [VMEM] * (4 + len(got) + len(carried)),
            flops=1_000_000,
        )(state, grad, logs, places, *got, *carried)
        carried, outgoing = outgoing[:2], outgoing[2:]
        if not last:
            (state, grad), outgoing = outgoing[:2], outgoing[2:]
        if t == 0:
            weights, fixed, moved, slope = call(
                weights_kernel,
                (
                    struct((tok, 4 * INNER)), struct((HEAD_ROWS, tok)), struct(((K - 1) * tok, channels)), struct((tok, channels)),
                ),
                [VMEM] * 11,
                flops=10**11,
            )(xbc, cot, rows, raw, halo, places, scaled, until, pre, sums, logs)

    grad_conv, states, packed, spill = call(
        functools.partial(totals_kernel, len(stages) - 1, radix),
        (struct((tok, channels)), struct((tok + HEAD_ROWS, 2 * INNER)), struct((TOTAL_ROWS, 128)), struct((8, channels))),
        [VMEM] * (14 + len(got) + len(carried)),
        scratch=[pltpu.VMEM((TOTAL_ROWS, 128), f32)],
        flops=200_000_000,
    )(raw, moved, xbc, slope, scaled, weighted, tail, rows, local, fixed, weights, logs, places, conv_weight, *got, *carried)

    spilled = lax.ppermute(spill, "ctx", [((i + 1) % slabs, i) for i in range(slabs)])
    if slabs * contexts <= 64:
        parts = everyones(packed, ("ctx", "dp"), slabs * contexts)
    else:
        packed = call(repack_kernel, struct((TOTAL_ROWS, 128)), [VMEM])(everyones(packed, "ctx", slabs))
        parts = everyones(packed, "dp", contexts)

    grad_main, grad_dt, end = call(
        input_kernel,
        (struct((tok, channels), bf16), struct((H, tok)), struct((END_ROWS, channels))),
        [VMEM] * 8,
        (HBM, VMEM, VMEM),
        [pltpu.VMEM((tok, channels), bf16), pltpu.SemaphoreType.DMA],
        flops=1_000_000,
    )(grad_conv, conv_weight, states, xbc, scaled, rows, sums, until)
    grad_input = call(
        end_kernel,
        struct((tok, channels), bf16),
        [VMEM] * 3 + [HBM],
        HBM,
        [pltpu.VMEM((END_ROWS, channels), bf16), pltpu.SemaphoreType.DMA],
        aliases={3: 0},
    )(end, spilled, places, grad_main)

    grad_weight, grad_bias, *small = call(
        finish_kernel,
        (struct((K, channels)), struct((1, channels)), struct((1, H)), struct((1, H)), struct((1, H))),
        [VMEM],
    )(parts)
    return (grad_input[None], grad_dt.T[None], grad_weight, grad_bias[0], *(each[0] for each in small))


def solution(mesh):
    in_specs = (
        P("dp", "ctx", None),
        P(),
        P(),
        P("dp", "ctx", None),
        P(),
        P(),
        P(),
        P("dp", "ctx", None),
    )
    out_specs = (P("dp", "ctx", None), P("dp", "ctx", None), P(), P(), P(), P(), P())
    return jax.shard_map(
        on_device, mesh=mesh, in_specs=in_specs, out_specs=out_specs, check_vma=False
    )
```

```python
import functools

import jax
import jax.numpy as jnp
from jax import lax
from jax.experimental import pallas as pl
from jax.experimental.pallas import tpu as pltpu
from jax.sharding import PartitionSpec as P

H = 4
P_SIZE = 64
N = 128
K = 4
INNER = H * P_SIZE
HEAD_ROWS = 8
TAIL_ROWS = 8
HALO_ROWS = 16
FIX_ROWS = 16
END_ROWS = 16
LANE_BLOCKS = (INNER + 2 * N) // 128
SMALL_ROW = (K + 1) * LANE_BLOCKS
TOTAL_ROWS = 24

f32 = jnp.float32
bf16 = jnp.bfloat16

VMEM = pl.BlockSpec(memory_space=pltpu.VMEM)
HBM = pl.BlockSpec(memory_space=pltpu.HBM)


def dot(a, b, a_dim=1, b_dim=0):
    return lax.dot_general(a, b, (((a_dim,), (b_dim,)), ((), ())), preferred_element_type=f32)


def split2(x):
    high = x.astype(bf16)
    return high, (x - high.astype(f32)).astype(bf16)


def split3(x):
    high = x.astype(bf16).astype(f32)
    rest = x - high
    middle = rest.astype(bf16).astype(f32)
    return high, middle, rest - middle


def iota(shape, dim):
    return lax.broadcasted_iota(jnp.int32, shape, dim)


def stacked(rows):
    return jnp.concatenate([*split3(rows), jnp.zeros_like(rows)], 0).astype(bf16)


def unstacked(rows):
    return rows[0:8] + rows[8:16] + rows[16:24]


def head_selector(rows):
    shape = (rows, INNER)
    return jnp.where(iota(shape, 1) // P_SIZE == iota(shape, 0) % HEAD_ROWS, 1.0, 0.0).astype(bf16)


def over_channels(rows):
    return dot(stacked(rows), head_selector(4 * HEAD_ROWS), 0, 0)


def channel_row(column):
    return jnp.sum(head_selector(HEAD_ROWS * 2)[:HEAD_ROWS].astype(f32) * column, axis=0, keepdims=True)


def pieces3(x):
    return [each.astype(bf16) for each in split3(x)]


def head_sums(x, split=split2):
    selector = head_selector(HEAD_ROWS * 2)
    return sum(dot(selector, each, 1, 1) for each in split(x))[:HEAD_ROWS]


def by_head(ref, width):
    row = iota((HEAD_ROWS, width), 0)
    out = jnp.zeros((HEAD_ROWS, width), f32)
    for h in range(H):
        out = jnp.where(row == h, ref[:, h : h + 1], out)
    return out


def shifted_down(x, first, count):
    moved = pltpu.roll(x, count, 0)
    top = jnp.where(iota(first.shape, 0) < count, pltpu.roll(first, count, 0), moved[:8])
    return jnp.concatenate([top, moved[8:]], 0)


def quantized_log(size):
    return jnp.log(jnp.maximum(size, 1e-30)).astype(bf16).astype(f32)


def scaled_columns(x):
    log_size = quantized_log(jnp.max(jnp.abs(x), axis=0, keepdims=True))
    return x * jnp.exp(-log_size), log_size


def write_messages(msg_refs, state, grad, log_total, place, radix):
    row = iota((TAIL_ROWS, INNER), 0)
    high, middle, low = split3(log_total)
    tail = jnp.where(row == 4, high, jnp.where(row == 5, middle * 256.0, jnp.where(row == 6, low * 65536.0, 0.0)))
    state, state_size = scaled_columns(state)
    grad, grad_size = scaled_columns(grad)
    if radix:
        for s, msg_ref in enumerate(msg_refs, 1):
            on = place + s < radix
            msg_ref[0:N] = jnp.where(on, state, grad)
            msg_ref[N : N + TAIL_ROWS] = jnp.where(row == 0, jnp.where(on, state_size, grad_size), tail)
    else:
        (msg_ref,) = msg_refs
        msg_ref[0:N] = state
        msg_ref[N : 2 * N] = grad
        msg_ref[2 * N : 2 * N + TAIL_ROWS] = jnp.where(row == 0, state_size, jnp.where(row == 1, grad_size, tail))


def message_log(got_ref):
    rows = got_ref.shape[0] - TAIL_ROWS
    tail = got_ref[rows : rows + 8]
    return tail[4:5] + tail[5:6] * (1 / 256.0) + tail[6:7] * (1 / 65536.0)


def message_block(got_ref, which=0):
    rows = got_ref.shape[0] - TAIL_ROWS
    return got_ref[which * N : (which + 1) * N] * jnp.exp(got_ref[rows + which : rows + which + 1])


def chained(blocks, logs, used):
    total, log_sum = 0.0, 0.0
    for block, log, use in zip(blocks, logs, used):
        total = total + jnp.where(use, jnp.exp(log_sum) * block, 0.0)
        log_sum = log_sum + jnp.where(use, log, 0.0)
    return total, log_sum


def pack_totals(x):
    row = iota(x.shape, 0)
    large = jnp.where(row < SMALL_ROW, x, 0.0)
    large_size = quantized_log(jnp.max(jnp.abs(large), axis=0, keepdims=True))
    small = x[SMALL_ROW : SMALL_ROW + 1]
    small_size = quantized_log(jnp.abs(small))
    small = small * jnp.exp(-small_size)
    small_high = small.astype(bf16).astype(f32)
    out = jnp.where(row == SMALL_ROW, small_high, large * jnp.exp(-large_size))
    out = jnp.where(row == SMALL_ROW + 3, (small - small_high) * 256.0, out)
    return jnp.where(row == SMALL_ROW + 1, large_size, jnp.where(row == SMALL_ROW + 2, small_size, out))


def triangle_kernel(until_ref):
    shape = until_ref.shape
    until_ref[...] = jnp.where(iota(shape, 0) <= iota(shape, 1), 1.0, 0.0).astype(bf16)


def heads_kernel(bias_ref, dt_bias_ref, alog_ref, skip_ref, until_in, until_ref, bias_out, heads_ref):
    bias_out[...] = bias_ref[...]
    for i, ref in enumerate((dt_bias_ref, alog_ref, skip_ref)):
        heads_ref[8 * i : 8 * i + 8] = by_head(ref, until_ref.shape[1])


def mask_first(x):
    top = jnp.where(iota((FIX_ROWS, x.shape[1]), 0) < K - 1, 0.0, x[:FIX_ROWS].astype(f32))
    return jnp.concatenate([top.astype(x.dtype), x[FIX_ROWS:]], 0)


def start_kernel(
    stages, raw_ref, cot_ref, weight_ref, bias_ref, dt_ref, heads_ref, until_ref,
    pre_ref, xbc_ref, weighted_ref, scaled_ref, tail_ref, rows_ref, logs_ref, places_ref, state_ref, grad_ref, msg_ref, dt8_ref,
):
    tok = raw_ref.shape[0]
    place = lax.axis_index("ctx")
    for t, (size, radix) in enumerate(stages):
        places_ref[8 * t : 8 * t + 8] = jnp.full((8, INNER), lax.rem(lax.div(place, size), radix), jnp.int32).astype(f32)
    at = 8 * len(stages)
    slabs = stages[-1][0] * stages[-1][1]
    places_ref[at : at + 8] = jnp.full((8, INNER), jnp.where(place == 0, 1, 0), jnp.int32).astype(f32)
    places_ref[at + 8 : at + 16] = jnp.full((8, INNER), jnp.where(place == slabs - 1, 1, 0), jnp.int32).astype(f32)
    dt8_ref[...] = jnp.zeros_like(dt8_ref)
    dt8_ref[0:H] = dt_ref[...]
    dt_pre = dt8_ref[...] + heads_ref[0:8]
    step = jnp.maximum(dt_pre, 0.0) + jnp.log1p(jnp.exp(-jnp.abs(dt_pre)))
    real = iota((HEAD_ROWS, tok), 0) < H
    decay_rate = jnp.where(real, -jnp.exp(heads_ref[8:16]), 0.0)
    cum = unstacked(dot(stacked(step * decay_rate), until_ref[...]))
    left = jnp.exp(cum[:, tok - 1 : tok] - cum)
    reach = jnp.exp(cum)
    rows_ref[0:8] = cum
    rows_ref[8:16] = step
    rows_ref[16:24] = left
    rows_ref[24:32] = reach
    rows_ref[32:40] = 1.0 / (1.0 + jnp.exp(-dt_pre))
    rows_ref[40:48] = decay_rate
    tail = over_channels(left * step)
    tail_ref[...] = tail
    log_total = channel_row(cum[:, tok - 1 : tok])
    skip = channel_row(heads_ref[16:24][:, :1])
    row = iota((8, INNER), 0)
    logs_ref[...] = jnp.where(row == 2, log_total, jnp.where(row == 3, skip, 0.0))
    scaled = jnp.concatenate(split2(cot_ref[...].astype(f32) * over_channels(reach)), 1)
    scaled_ref[...] = scaled

    raw = raw_ref[...].astype(f32)
    zeros = jnp.zeros((8, raw.shape[1]), f32)
    pre = bias_ref[...] + weight_ref[K - 1 : K] * raw
    for back in range(1, K):
        pre = pre + weight_ref[K - 1 - back : K - back] * shifted_down(raw, zeros, back)
    pre_ref[...] = pre
    gate = 1.0 / (1.0 + jnp.exp(-pre))
    xbc = (pre * gate).astype(bf16)
    xbc_ref[...] = xbc
    weighted = jnp.concatenate(split2(xbc[:, :INNER].astype(f32) * tail), 1)
    weighted_ref[...] = weighted
    later = mask_first(xbc[:, INNER:])
    state = dot(later[:, :N], weighted, 0, 0)
    state = state[:, :INNER] + state[:, INNER:]
    grad = dot(later[:, N:], scaled, 0, 0)
    grad = grad[:, :INNER] + grad[:, INNER:]
    state_ref[...] = state
    grad_ref[...] = grad
    write_messages((msg_ref,), state, grad, log_total, places_ref[0:1], 0)


def real_halo(halo_ref, places_ref):
    first = places_ref[places_ref.shape[0] - 16 :][:1, :1]
    return jnp.where(first > 0.5, 0.0, halo_ref[HALO_ROWS - 8 :].astype(f32))


def fix_kernel(
    halo_ref, weight_ref, scaled_ref, tail_ref, places_ref, pre_in, xbc_in, weighted_in,
    pre_ref, xbc_ref, weighted_ref, factors_ref,
):
    halo = real_halo(halo_ref, places_ref)
    top = pre_in[0:8]
    for back in range(1, K):
        tap = weight_ref[K - 1 - back : K - back]
        top = top + jnp.where(iota(top.shape, 0) < back, tap * pltpu.roll(halo, back, 0), 0.0)
    pre = jnp.concatenate([top, pre_in[8:FIX_ROWS]], 0)
    pre_ref[0:FIX_ROWS] = pre
    gate = 1.0 / (1.0 + jnp.exp(-pre))
    xbc = (pre * gate).astype(bf16)
    xbc_ref[0:FIX_ROWS] = xbc
    xbc = xbc.astype(f32)
    weighted = jnp.concatenate([each.astype(f32) for each in split2(xbc[:, :INNER] * tail_ref[0:FIX_ROWS])], 1)
    weighted_ref[0:FIX_ROWS] = weighted.astype(bf16)
    scaled = scaled_ref[0:FIX_ROWS].astype(f32)

    def packed(*parts):
        row = iota((FIX_ROWS, parts[0].shape[1]), 0)
        out = jnp.zeros(row.shape, f32)
        for at, part in enumerate(parts):
            part = pltpu.roll(part, at * (K - 1), 0) if at else part
            out = jnp.where((row >= at * (K - 1)) & (row < (at + 1) * (K - 1)), part, out)
        return out.astype(bf16)

    b_proj, c_proj = xbc[:, INNER : INNER + N], xbc[:, INNER + N :]
    factors_ref[:, :INNER] = packed(weighted[:, :INNER], weighted[:, INNER:], scaled[:, :INNER], scaled[:, INNER:])
    factors_ref[:, INNER:] = packed(b_proj, b_proj, c_proj, c_proj)


def first_parts(factors_ref):
    rows = factors_ref[:, INNER:].astype(f32)
    of_state = iota(rows.shape, 0) < 2 * (K - 1)
    rows = jnp.concatenate([jnp.where(of_state, rows, 0.0), jnp.where(of_state, 0.0, rows)], 1).astype(bf16)
    both = dot(rows, factors_ref[:, :INNER], 0, 0)
    return both[:N], both[N:]


def merge_kernel(t, radix, next_radix, state_ref, grad_ref, logs_ref, places_ref, *refs):
    got, refs = refs[: radix - 1], refs[radix - 1 :]
    prior = after = 0.0
    if t > 0:
        prior, after = refs[0][...], refs[1][...]
        refs = refs[2:]
    else:
        parts, refs = [first_parts(ref) for ref in refs[: radix - 1]], refs[radix - 1 :]
    logs_out, prior_out, after_out, *refs = refs
    if not next_radix:
        state_out, grad_out, *refs = refs
    place = places_ref[8 * t : 8 * t + 1]
    log_prior, log_after, log_total = logs_ref[0:1], logs_ref[1:2], logs_ref[2:3]
    states = [message_block(ref, 0) for ref in got]
    grads = [message_block(ref, 1) for ref in got]
    logs = [message_log(ref) for ref in got]
    own_state, own_grad = state_ref[...], grad_ref[...]
    if t == 0:
        states = [each + part[0] for each, part in zip(states, parts)]
        grads = [each + part[1] for each, part in zip(grads, parts)]
    earlier = [s <= place for s in range(1, radix)]
    later = [s > place for s in range(1, radix)]
    before, log_before = chained(states, logs, earlier)
    beyond, log_beyond = chained(grads[::-1], logs[::-1], later[::-1])
    above, _ = chained(states, logs, later)
    below, _ = chained(grads[::-1], logs[::-1], earlier[::-1])
    mine = jnp.exp(log_total)
    state = above + jnp.exp(log_beyond) * (own_state + mine * before)
    grad = below + jnp.exp(log_before) * (own_grad + mine * beyond)
    prior_out[...] = prior + jnp.exp(log_prior) * before
    after_out[...] = after + jnp.exp(log_after) * beyond
    log_prior = log_prior + log_before
    log_after = log_after + log_beyond
    log_total = log_total + log_before + log_beyond
    row = iota((8, INNER), 0)
    logs_out[...] = jnp.where(row == 0, log_prior, jnp.where(row == 1, log_after, jnp.where(row == 2, log_total, 0.0)))
    if not next_radix:
        state_out[...] = state
        grad_out[...] = grad
    write_messages(refs, state, grad, log_total, places_ref[8 * t + 8 : 8 * t + 9], next_radix)


def local_kernel(
    xbc_ref, cot_ref, rows_ref, logs_ref, factors_ref, state_in, grad_in, local_ref, sums_ref, state_ref, grad_ref,
):
    state, grad = first_parts(factors_ref)
    state_ref[...] = state_in[...] + state
    grad_ref[...] = grad_in[...] + grad
    tok = xbc_ref.shape[0]
    cot = cot_ref[...]
    values = xbc_ref[:, :INNER]
    b_proj = xbc_ref[:, INNER : INNER + N]
    c_proj = xbc_ref[:, INNER + N :]
    cum, step = rows_ref[0:8], rows_ref[8:16]
    step_wide = over_channels(step)
    values_f = values.astype(f32)
    cot_f = cot.astype(f32)
    stepped = pieces3(values_f * step_wide)
    gram = dot(b_proj, c_proj, 1, 1)
    reached = iota((tok, tok), 0) <= iota((tok, tok), 1)
    pieces = stacked(cum)
    piece_head = iota((4 * HEAD_ROWS, tok), 0) % HEAD_ROWS
    dgram = jnp.zeros((tok, tok), f32)
    grads, sums = [], []
    for h in range(H):
        of = slice(h * P_SIZE, (h + 1) * P_SIZE)
        column = dot(pieces, jnp.where(piece_head == h, 1.0, 0.0).astype(bf16), 0, 0)
        within = jnp.exp(jnp.where(reached, cum[h : h + 1] - column, -1e30))
        cot_h = cot[:, of]
        grads.append(sum(dot(each, cot_h) for each in pieces3(gram * within)))
        dmix = sum(dot(each[:, of], cot_h, 1, 1) for each in stepped) * within
        dgram = dgram + dmix
        sums.append(jnp.sum(dmix * gram, axis=0, keepdims=True))
    grad_stepped = jnp.concatenate(grads, 1)
    local_ref[:, :INNER] = grad_stepped * step_wide + logs_ref[3:4] * cot_f
    high, low = split2(dgram)
    local_ref[:, INNER : INNER + N] = dot(high, c_proj) + dot(low, c_proj)
    local_ref[:, INNER + N :] = dot(high, b_proj, 0, 0) + dot(low, b_proj, 0, 0)
    row = iota((HEAD_ROWS, tok), 0)
    pairs = jnp.zeros((HEAD_ROWS, tok), f32)
    for h in range(H):
        pairs = jnp.where(row == h, sums[h], pairs)
    from_values = head_sums(values_f * grad_stepped, pieces3)
    sums_ref[0:8] = pairs - from_values * step
    sums_ref[8:16] = from_values


def weights_kernel(
    xbc_ref, cot_ref, rows_ref, raw_ref, halo_ref, places_ref, scaled_ref, until_ref, pre_ref, sums_ref, logs_ref,
    weights_ref, fixed_ref, moved_ref, slope_ref,
):
    tok = xbc_ref.shape[0]
    pre = pre_ref[...]
    sigmoid = 1.0 / (1.0 + jnp.exp(-pre))
    slope_ref[...] = sigmoid * (1.0 + pre * (1.0 - sigmoid))
    values_f = xbc_ref[:, :INNER].astype(f32)
    cum, step, left = rows_ref[0:8], rows_ref[8:16], rows_ref[16:24]
    gate, decay_rate = rows_ref[32:40], rows_ref[40:48]
    base, from_values = sums_ref[0:8], sums_ref[8:16]
    skip_rows = head_sums(values_f * cot_ref[...].astype(f32))

    bias_weight = decay_rate * unstacked(dot(stacked(gate), until_ref[...]))
    cum_last, bias_last = cum[:, tok - 1 : tok], bias_weight[:, tok - 1 : tok]
    tail = left * step
    scaled_f = scaled_ref[:, :INNER].astype(f32) + scaled_ref[:, INNER:].astype(f32)
    weights_ref[:, :INNER] = scaled_f * over_channels(cum)
    weights_ref[:, INNER : 2 * INNER] = values_f * over_channels(tail * (cum_last - cum))
    weights_ref[:, 2 * INNER : 3 * INNER] = scaled_f * over_channels(bias_weight)
    weights_ref[:, 3 * INNER :] = values_f * over_channels(left * gate + tail * (bias_last - bias_weight))
    lane = iota((HEAD_ROWS, tok), 1)
    fixed = jnp.zeros((HEAD_ROWS, tok), f32)
    for i, column in enumerate((
        jnp.sum(from_values * gate + base * bias_weight, axis=1, keepdims=True),
        jnp.sum(base * cum, axis=1, keepdims=True),
        jnp.sum(skip_rows, axis=1, keepdims=True),
        bias_last, cum_last,
    )):
        fixed = jnp.where(lane == i, column, fixed)
    fixed_ref[...] = fixed
    raw = raw_ref[...].astype(f32)
    halo = real_halo(halo_ref, places_ref)
    for back in range(1, K):
        moved_ref[(back - 1) * tok : back * tok] = shifted_down(raw, halo, back)


def totals_kernel(
    t, radix, raw_ref, moved_ref, xbc_ref, slope_ref, scaled_ref, weighted_ref, tail_ref, rows_ref, local_ref, fixed_ref, weights_ref,
    logs_ref, places_ref, weight_ref, *refs
):
    got, refs = refs[: radix - 1], refs[radix - 1 :]
    prior = after = 0.0
    if t > 0:
        prior, after = refs[0][...], refs[1][...]
        refs = refs[2:]
    conv_ref, states_ref, totals_ref, spill_ref, totals_scratch = refs
    tok = raw_ref.shape[0]
    place = places_ref[8 * t : 8 * t + 1]
    blocks = [message_block(ref) for ref in got]
    logs = [message_log(ref) for ref in got]
    before, _ = chained(blocks, logs, [s <= place for s in range(1, radix)])
    beyond, _ = chained(blocks[::-1], logs[::-1], [s > place for s in range(radix - 1, 0, -1)])
    prior = prior + jnp.exp(logs_ref[0:1]) * before
    after = after + jnp.exp(logs_ref[1:2]) * beyond

    b_proj = xbc_ref[:, INNER : INNER + N]
    c_proj = xbc_ref[:, INNER + N :]
    prior2 = jnp.concatenate(split2(prior), 0)
    after2 = jnp.concatenate(split2(after), 0)
    seen = dot(jnp.concatenate([c_proj, c_proj], 1), prior2)
    back = dot(jnp.concatenate([b_proj, b_proj], 1), after2)
    grad_c = dot(scaled_ref[:, :INNER], prior2, 1, 1)
    grad_c = grad_c[:, :N] + grad_c[:, N:] + dot(scaled_ref[:, INNER:], prior2[:N], 1, 1)
    grad_b = dot(weighted_ref[:, :INNER], after2, 1, 1)
    grad_b = grad_b[:, :N] + grad_b[:, N:] + dot(weighted_ref[:, INNER:], after2[:N], 1, 1)
    grad_low = (local_ref[...] + jnp.concatenate([tail_ref[...] * back, grad_b, grad_c], 1)).astype(bf16)
    grad_conv = grad_low.astype(f32) * slope_ref[...]
    conv_ref[...] = grad_conv
    top = grad_conv[:8]
    spill = jnp.zeros_like(top)
    for ahead in range(1, K):
        tap = weight_ref[K - 1 - ahead : K - ahead]
        spill = spill + tap * jnp.where(iota(top.shape, 0) < 8 - ahead, 0.0, pltpu.roll(top, 8 - ahead, 0))
    spill_ref[...] = spill

    sums = [grad_conv * moved_ref[back * tok : (back + 1) * tok] for back in range(K - 2, -1, -1)]
    sums += [grad_conv * raw_ref[...].astype(f32), grad_conv]
    totals_scratch[...] = jnp.zeros_like(totals_scratch)
    for k, each in enumerate(sums):
        each = jnp.sum(each, axis=0, keepdims=True)
        for j in range(LANE_BLOCKS):
            at = k * LANE_BLOCKS + j
            totals_scratch[at : at + 1] = each[:, j * 128 : (j + 1) * 128]

    states_ref[:tok, :INNER] = seen
    states_ref[:tok, INNER:] = back
    through = jnp.sum(prior * after, axis=0, keepdims=True)
    grad_bias = jnp.sum(seen * weights_ref[:, 2 * INNER : 3 * INNER] + back * weights_ref[:, 3 * INNER :], axis=0, keepdims=True)
    grad_alog = jnp.sum(seen * weights_ref[:, :INNER] + back * weights_ref[:, INNER : 2 * INNER], axis=0, keepdims=True)
    selector = head_selector(HEAD_ROWS * 2)[:HEAD_ROWS].astype(f32)
    grad_bias, grad_alog, through = (
        jnp.sum(selector * each, axis=1, keepdims=True) for each in (grad_bias, grad_alog, through)
    )
    through = through * rows_ref[24:32][:, tok - 1 : tok]
    states_ref[tok:] = jnp.broadcast_to(through, (HEAD_ROWS, 2 * INNER))
    fixed = fixed_ref[...]
    row, lane = iota((HEAD_ROWS, 128), 0), iota((HEAD_ROWS, 128), 1)
    small = jnp.zeros((HEAD_ROWS, 128), f32)
    for i, column in enumerate((
        fixed[:, 0:1] + grad_bias + through * fixed[:, 3:4],
        fixed[:, 1:2] + grad_alog + through * fixed[:, 4:5],
        fixed[:, 2:3],
    )):
        small = jnp.where((row < H) & (lane == row + i * H), column, small)
    totals_scratch[SMALL_ROW : SMALL_ROW + 1] = jnp.sum(small, axis=0, keepdims=True)
    totals_ref[...] = pack_totals(totals_scratch[...])


def input_kernel(
    conv_ref, weight_ref, states_ref, xbc_ref, scaled_ref, rows_ref, sums_ref, until_ref, out_hbm, dt_out_ref, end_ref, out_ref, sem
):
    grad_conv = conv_ref[...]
    tok, channels = grad_conv.shape
    grad_in = weight_ref[K - 1 : K] * grad_conv
    row8 = iota((8, channels), 0)
    for ahead in range(1, K):
        tap = weight_ref[K - 1 - ahead : K - ahead]
        moved = pltpu.roll(grad_conv, tok - ahead, 0)
        last8 = moved[tok - 8 :]
        inside = row8 < 8 - ahead
        grad_in = grad_in + tap * jnp.concatenate([moved[: tok - 8], jnp.where(inside, last8, 0.0)], 0)
    out_ref[...] = grad_in.astype(bf16)
    copy = pltpu.make_async_copy(out_ref, out_hbm, sem)
    copy.start()
    end_ref[...] = grad_in[tok - END_ROWS :]

    step, left, gate, decay_rate = rows_ref[8:16], rows_ref[16:24], rows_ref[32:40], rows_ref[40:48]
    scaled_f = scaled_ref[:, :INNER].astype(f32) + scaled_ref[:, INNER:].astype(f32)
    seen_rows = head_sums(scaled_f * states_ref[:tok, :INNER])
    tail_rows = head_sums(xbc_ref[:, :INNER].astype(f32) * states_ref[:tok, INNER:])
    tail_term = tail_rows * left * step
    last_extra = jnp.sum(tail_term, axis=1, keepdims=True) + states_ref[tok:][:, :1]
    grad_cum = sums_ref[0:8] + seen_rows - tail_term
    grad_log = unstacked(dot(stacked(grad_cum), until_ref[...], 1, 1)) + last_extra
    grad_step = sums_ref[8:16] + tail_rows * left + decay_rate * grad_log
    dt_out_ref[...] = (grad_step * gate)[0:H]
    copy.wait()


def end_kernel(end_ref, spilled_ref, places_ref, main_hbm, out_hbm, rows_ref, sem):
    end = end_ref[...]
    last = places_ref[places_ref.shape[0] - 8 :][:1, :1]
    fixed = end[END_ROWS - 8 :] + jnp.where(last > 0.5, 0.0, spilled_ref[...])
    rows_ref[...] = jnp.concatenate([end[: END_ROWS - 8], fixed], 0).astype(bf16)
    tok = out_hbm.shape[0]
    copy = pltpu.make_async_copy(rows_ref, out_hbm.at[pl.ds(tok - END_ROWS, END_ROWS)], sem)
    copy.start()
    copy.wait()


def summed(parts):
    large = jnp.sum(parts * jnp.exp(parts[:, SMALL_ROW + 1 : SMALL_ROW + 2]), axis=0)
    small = parts[:, SMALL_ROW : SMALL_ROW + 1] + parts[:, SMALL_ROW + 3 : SMALL_ROW + 4] * (1 / 256.0)
    small = small * jnp.exp(parts[:, SMALL_ROW + 2 : SMALL_ROW + 3])
    return large, jnp.sum(small, axis=0)


def repack_kernel(parts_ref, out_ref):
    large, small = summed(parts_ref[...])
    out_ref[...] = pack_totals(jnp.where(iota(large.shape, 0) == SMALL_ROW, small, large))


def finish_kernel(parts_ref, weight_ref, bias_ref, dt_bias_ref, alog_ref, skip_ref):
    large, small = summed(parts_ref[...])
    for k in range(K + 1):
        for j in range(LANE_BLOCKS):
            at = k * LANE_BLOCKS + j
            if k < K:
                weight_ref[k : k + 1, j * 128 : (j + 1) * 128] = large[at : at + 1]
            else:
                bias_ref[:, j * 128 : (j + 1) * 128] = large[at : at + 1]
    for i, ref in enumerate((dt_bias_ref, alog_ref, skip_ref)):
        ref[...] = small[:, i * H : (i + 1) * H]


def call(kernel, outs, in_specs, out_specs=None, scratch=(), flops=0, limit=16 << 20, aliases=None):
    return pl.pallas_call(
        kernel,
        out_shape=outs,
        in_specs=in_specs,
        out_specs=out_specs or jax.tree.map(lambda _: VMEM, outs),
        scratch_shapes=list(scratch),
        input_output_aliases=aliases or {},
        compiler_params=pltpu.CompilerParams(vmem_limit_bytes=limit),
        cost_estimate=pl.CostEstimate(flops=flops, bytes_accessed=1 << 20, transcendentals=0),
    )


def struct(shape, dtype=f32):
    return jax.ShapeDtypeStruct(shape, dtype)


def from_groups(messages, slabs, size, radix):
    got = []
    for s in range(1, radix):
        message = messages[s - 1 if len(messages) > 1 else 0]
        route = [(p, p - p % (size * radix) + (p + s * size) % (size * radix)) for p in range(slabs)]
        got.append(lax.ppermute(message, "ctx", route))
    return got


def states_from_groups(messages, slabs, size, radix):
    got = from_groups([message.astype(jnp.float16) for message in messages], slabs, size, radix)
    return [each.astype(f32) for each in got]


def stages_of(slabs):
    stages, size = [], 1
    while size < slabs:
        radix = 2 if (slabs // size).bit_length() % 2 == 0 else 4
        stages.append((size, radix))
        size *= radix
    assert size == slabs and len(stages) > 1
    return stages


def everyones(packed, axes, count):
    packed = jnp.broadcast_to(packed.astype(jnp.float16)[None], (count, *packed.shape))
    return lax.all_to_all(packed, axes, 0, 0).astype(f32)


def on_device(xbc_raw, conv_weight, conv_bias, dt_raw, dt_bias, a_log, d_skip, grad_out):
    tok, channels = xbc_raw.shape[1:]
    slabs = lax.axis_size("ctx")
    contexts = lax.axis_size("dp")
    stages = stages_of(slabs)

    raw, cot, dt_rows = xbc_raw[0], grad_out[0], dt_raw[0].T
    until = call(triangle_kernel, struct((tok, tok), bf16), [], flops=10**11)()
    until, bias, heads = call(
        heads_kernel,
        (struct((tok, tok), bf16), struct((1, channels)), struct((3 * HEAD_ROWS, tok))),
        [VMEM] * 5,
        aliases={4: 0},
    )(conv_bias[None], dt_bias[None], a_log[None], d_skip[None], until)
    early_raw, until = lax.optimization_barrier((raw, until))
    halo = lax.ppermute(early_raw[tok - HALO_ROWS :], "ctx", [(i, (i + 1) % slabs) for i in range(slabs)])

    def last_radix(t):
        return stages[t][1] if t == len(stages) - 1 else 0

    def messages(t):
        if last_radix(t):
            return (struct((N + TAIL_ROWS, INNER)),) * (last_radix(t) - 1)
        return (struct((2 * N + TAIL_ROWS, INNER)),)

    state_like = struct((N, INNER))
    logs_like = struct((8, INNER))
    pre, xbc, weighted, scaled, tail, rows, logs, places, state, grad, *outgoing = call(
        functools.partial(start_kernel, stages),
        (
            struct((tok, channels)), struct((tok, channels), bf16), struct((tok, 2 * INNER), bf16),
            struct((tok, 2 * INNER), bf16), struct((tok, INNER)), struct((6 * HEAD_ROWS, tok)),
            logs_like, struct((8 * len(stages) + 16, INNER)), state_like, state_like, *messages(0),
        ),
        [VMEM] * 7,
        scratch=[pltpu.VMEM((HEAD_ROWS, tok), f32)],
        flops=10**11,
    )(raw, cot, conv_weight, bias, dt_rows, heads, until)
    pre, xbc, weighted, factors = call(
        fix_kernel,
        (
            struct((tok, channels)), struct((tok, channels), bf16), struct((tok, 2 * INNER), bf16),
            struct((FIX_ROWS, INNER + N), bf16),
        ),
        [VMEM] * 8,
        flops=1_000_000,
        aliases={5: 0, 6: 1, 7: 2},
    )(halo, conv_weight, scaled, tail, places, pre, xbc, weighted)

    local, sums, state, grad = call(
        local_kernel,
        (struct((tok, channels)), struct((2 * HEAD_ROWS, tok)), state_like, state_like),
        [VMEM] * 7,
        flops=10**11,
        aliases={5: 2, 6: 3},
    )(xbc, cot, rows, logs, factors, state, grad)

    carried = ()
    for t, (size, radix) in enumerate(stages):
        got = states_from_groups(outgoing, slabs, size, radix)
        if t == 0:
            got, local, sums = lax.optimization_barrier((got, local, sums))
            carried = from_groups([factors], slabs, size, radix)
        if t == len(stages) - 1:
            got, weights, fixed, moved, slope = lax.optimization_barrier((got, weights, fixed, moved, slope))
            break
        last = last_radix(t + 1)
        outs = (logs_like, state_like, state_like) + (() if last else (state_like, state_like))
        logs, *outgoing = call(
            functools.partial(merge_kernel, t, radix, last),
            outs + messages(t + 1),
            [VMEM] * (4 + len(got) + len(carried)),
            flops=1_000_000,
        )(state, grad, logs, places, *got, *carried)
        carried, outgoing = outgoing[:2], outgoing[2:]
        if not last:
            (state, grad), outgoing = outgoing[:2], outgoing[2:]
        if t == 0:
            weights, fixed, moved, slope = call(
                weights_kernel,
                (
                    struct((tok, 4 * INNER)), struct((HEAD_ROWS, tok)), struct(((K - 1) * tok, channels)), struct((tok, channels)),
                ),
                [VMEM] * 11,
                flops=10**11,
            )(xbc, cot, rows, raw, halo, places, scaled, until, pre, sums, logs)

    grad_conv, states, packed, spill = call(
        functools.partial(totals_kernel, len(stages) - 1, radix),
        (struct((tok, channels)), struct((tok + HEAD_ROWS, 2 * INNER)), struct((TOTAL_ROWS, 128)), struct((8, channels))),
        [VMEM] * (14 + len(got) + len(carried)),
        scratch=[pltpu.VMEM((TOTAL_ROWS, 128), f32)],
        flops=200_000_000,
    )(raw, moved, xbc, slope, scaled, weighted, tail, rows, local, fixed, weights, logs, places, conv_weight, *got, *carried)

    spilled = lax.ppermute(spill, "ctx", [((i + 1) % slabs, i) for i in range(slabs)])
    if slabs * contexts <= 64:
        parts = everyones(packed, ("ctx", "dp"), slabs * contexts)
    else:
        packed = call(repack_kernel, struct((TOTAL_ROWS, 128)), [VMEM])(everyones(packed, "ctx", slabs))
        parts = everyones(packed, "dp", contexts)

    grad_main, grad_dt, end = call(
        input_kernel,
        (struct((tok, channels), bf16), struct((H, tok)), struct((END_ROWS, channels))),
        [VMEM] * 8,
        (HBM, VMEM, VMEM),
        [pltpu.VMEM((tok, channels), bf16), pltpu.SemaphoreType.DMA],
        flops=1_000_000,
    )(grad_conv, conv_weight, states, xbc, scaled, rows, sums, until)
    grad_input = call(
        end_kernel,
        struct((tok, channels), bf16),
        [VMEM] * 3 + [HBM],
        HBM,
        [pltpu.VMEM((END_ROWS, channels), bf16), pltpu.SemaphoreType.DMA],
        aliases={3: 0},
    )(end, spilled, places, grad_main)

    grad_weight, grad_bias, *small = call(
        finish_kernel,
        (struct((K, channels)), struct((1, channels)), struct((1, H)), struct((1, H)), struct((1, H))),
        [VMEM],
    )(parts)
    return (grad_input[None], grad_dt.T[None], grad_weight, grad_bias[0], *(each[0] for each in small))


def solution(mesh):
    in_specs = (
        P("dp", "ctx", None),
        P(),
        P(),
        P("dp", "ctx", None),
        P(),
        P(),
        P(),
        P("dp", "ctx", None),
    )
    out_specs = (P("dp", "ctx", None), P("dp", "ctx", None), P(), P(), P(), P(), P())
    return jax.shard_map(
        on_device, mesh=mesh, in_specs=in_specs, out_specs=out_specs, check_vma=False
    )
```

```python
import functools

import jax
import jax.numpy as jnp
from jax import lax
from jax.experimental import pallas as pl
from jax.experimental.pallas import tpu as pltpu
from jax.sharding import PartitionSpec as P

H = 4
P_SIZE = 64
N = 128
K = 4
INNER = H * P_SIZE
HEAD_ROWS = 8
TAIL_ROWS = 8
HALO_ROWS = 16
FIX_ROWS = 16
END_ROWS = 16
LANE_BLOCKS = (INNER + 2 * N) // 128
SMALL_ROW = (K + 1) * LANE_BLOCKS
TOTAL_ROWS = 24

f32 = jnp.float32
bf16 = jnp.bfloat16

VMEM = pl.BlockSpec(memory_space=pltpu.VMEM)
HBM = pl.BlockSpec(memory_space=pltpu.HBM)


def dot(a, b, a_dim=1, b_dim=0):
    return lax.dot_general(a, b, (((a_dim,), (b_dim,)), ((), ())), preferred_element_type=f32)


def split2(x):
    high = x.astype(bf16)
    return high, (x - high.astype(f32)).astype(bf16)


def split3(x):
    high = x.astype(bf16).astype(f32)
    rest = x - high
    middle = rest.astype(bf16).astype(f32)
    return high, middle, rest - middle


def iota(shape, dim):
    return lax.broadcasted_iota(jnp.int32, shape, dim)


def stacked(rows):
    return jnp.concatenate([*split3(rows), jnp.zeros_like(rows)], 0).astype(bf16)


def unstacked(rows):
    return rows[0:8] + rows[8:16] + rows[16:24]


def head_selector(rows):
    shape = (rows, INNER)
    return jnp.where(iota(shape, 1) // P_SIZE == iota(shape, 0) % HEAD_ROWS, 1.0, 0.0).astype(bf16)


def over_channels(rows):
    return dot(stacked(rows), head_selector(4 * HEAD_ROWS), 0, 0)


def channel_row(column):
    return jnp.sum(head_selector(HEAD_ROWS * 2)[:HEAD_ROWS].astype(f32) * column, axis=0, keepdims=True)


def pieces3(x):
    return [each.astype(bf16) for each in split3(x)]


def head_sums(x, split=split2):
    selector = head_selector(HEAD_ROWS * 2)
    return sum(dot(selector, each, 1, 1) for each in split(x))[:HEAD_ROWS]


def by_head(ref, width):
    row = iota((HEAD_ROWS, width), 0)
    out = jnp.zeros((HEAD_ROWS, width), f32)
    for h in range(H):
        out = jnp.where(row == h, ref[:, h : h + 1], out)
    return out


def shifted_down(x, first, count):
    moved = pltpu.roll(x, count, 0)
    top = jnp.where(iota(first.shape, 0) < count, pltpu.roll(first, count, 0), moved[:8])
    return jnp.concatenate([top, moved[8:]], 0)


def quantized_log(size):
    return jnp.log(jnp.maximum(size, 1e-30)).astype(bf16).astype(f32)


def scaled_columns(x):
    log_size = quantized_log(jnp.max(jnp.abs(x), axis=0, keepdims=True))
    return x * jnp.exp(-log_size), log_size


def write_messages(msg_refs, state, grad, log_total, place, radix):
    row = iota((TAIL_ROWS, INNER), 0)
    high, middle, low = split3(log_total)
    tail = jnp.where(row == 4, high, jnp.where(row == 5, middle * 256.0, jnp.where(row == 6, low * 65536.0, 0.0)))
    state, state_size = scaled_columns(state)
    grad, grad_size = scaled_columns(grad)
    if radix:
        for s, msg_ref in enumerate(msg_refs, 1):
            on = place + s < radix
            msg_ref[0:N] = jnp.where(on, state, grad)
            msg_ref[N : N + TAIL_ROWS] = jnp.where(row == 0, jnp.where(on, state_size, grad_size), tail)
    else:
        (msg_ref,) = msg_refs
        msg_ref[0:N] = state
        msg_ref[N : 2 * N] = grad
        msg_ref[2 * N : 2 * N + TAIL_ROWS] = jnp.where(row == 0, state_size, jnp.where(row == 1, grad_size, tail))


def message_log(got_ref):
    rows = got_ref.shape[0] - TAIL_ROWS
    tail = got_ref[rows : rows + 8]
    return tail[4:5] + tail[5:6] * (1 / 256.0) + tail[6:7] * (1 / 65536.0)


def message_block(got_ref, which=0):
    rows = got_ref.shape[0] - TAIL_ROWS
    return got_ref[which * N : (which + 1) * N] * jnp.exp(got_ref[rows + which : rows + which + 1])


def chained(blocks, logs, used):
    total, log_sum = 0.0, 0.0
    for block, log, use in zip(blocks, logs, used):
        total = total + jnp.where(use, jnp.exp(log_sum) * block, 0.0)
        log_sum = log_sum + jnp.where(use, log, 0.0)
    return total, log_sum


def pack_totals(x):
    row = iota(x.shape, 0)
    large = jnp.where(row < SMALL_ROW, x, 0.0)
    large_size = quantized_log(jnp.max(jnp.abs(large), axis=0, keepdims=True))
    small = x[SMALL_ROW : SMALL_ROW + 1]
    small_size = quantized_log(jnp.abs(small))
    small = small * jnp.exp(-small_size)
    small_high = small.astype(bf16).astype(f32)
    out = jnp.where(row == SMALL_ROW, small_high, large * jnp.exp(-large_size))
    out = jnp.where(row == SMALL_ROW + 3, (small - small_high) * 256.0, out)
    return jnp.where(row == SMALL_ROW + 1, large_size, jnp.where(row == SMALL_ROW + 2, small_size, out))


def triangle_kernel(until_ref):
    shape = until_ref.shape
    until_ref[...] = jnp.where(iota(shape, 0) <= iota(shape, 1), 1.0, 0.0).astype(bf16)


def heads_kernel(bias_ref, dt_bias_ref, alog_ref, skip_ref, until_in, until_ref, bias_out, heads_ref):
    bias_out[...] = bias_ref[...]
    for i, ref in enumerate((dt_bias_ref, alog_ref, skip_ref)):
        heads_ref[8 * i : 8 * i + 8] = by_head(ref, until_ref.shape[1])


def mask_first(x):
    top = jnp.where(iota((FIX_ROWS, x.shape[1]), 0) < K - 1, 0.0, x[:FIX_ROWS].astype(f32))
    return jnp.concatenate([top.astype(x.dtype), x[FIX_ROWS:]], 0)


def start_kernel(
    stages, raw_ref, cot_ref, weight_ref, bias_ref, dt_ref, heads_ref, until_ref,
    pre_ref, xbc_ref, weighted_ref, scaled_ref, tail_ref, rows_ref, logs_ref, places_ref, state_ref, grad_ref, msg_ref, dt8_ref,
):
    tok = raw_ref.shape[0]
    place = lax.axis_index("ctx")
    for t, (size, radix) in enumerate(stages):
        places_ref[8 * t : 8 * t + 8] = jnp.full((8, INNER), lax.rem(lax.div(place, size), radix), jnp.int32).astype(f32)
    at = 8 * len(stages)
    slabs = stages[-1][0] * stages[-1][1]
    places_ref[at : at + 8] = jnp.full((8, INNER), jnp.where(place == 0, 1, 0), jnp.int32).astype(f32)
    places_ref[at + 8 : at + 16] = jnp.full((8, INNER), jnp.where(place == slabs - 1, 1, 0), jnp.int32).astype(f32)
    dt8_ref[...] = jnp.zeros_like(dt8_ref)
    dt8_ref[0:H] = dt_ref[...]
    dt_pre = dt8_ref[...] + heads_ref[0:8]
    step = jnp.maximum(dt_pre, 0.0) + jnp.log1p(jnp.exp(-jnp.abs(dt_pre)))
    real = iota((HEAD_ROWS, tok), 0) < H
    decay_rate = jnp.where(real, -jnp.exp(heads_ref[8:16]), 0.0)
    cum = unstacked(dot(stacked(step * decay_rate), until_ref[...]))
    left = jnp.exp(cum[:, tok - 1 : tok] - cum)
    reach = jnp.exp(cum)
    rows_ref[0:8] = cum
    rows_ref[8:16] = step
    rows_ref[16:24] = left
    rows_ref[24:32] = reach
    rows_ref[32:40] = 1.0 / (1.0 + jnp.exp(-dt_pre))
    rows_ref[40:48] = decay_rate
    tail = over_channels(left * step)
    tail_ref[...] = tail
    log_total = channel_row(cum[:, tok - 1 : tok])
    skip = channel_row(heads_ref[16:24][:, :1])
    row = iota((8, INNER), 0)
    logs_ref[...] = jnp.where(row == 2, log_total, jnp.where(row == 3, skip, 0.0))
    scaled = jnp.concatenate(split2(cot_ref[...].astype(f32) * over_channels(reach)), 1)
    scaled_ref[...] = scaled

    raw = raw_ref[...].astype(f32)
    zeros = jnp.zeros((8, raw.shape[1]), f32)
    pre = bias_ref[...] + weight_ref[K - 1 : K] * raw
    for back in range(1, K):
        pre = pre + weight_ref[K - 1 - back : K - back] * shifted_down(raw, zeros, back)
    pre_ref[...] = pre
    gate = 1.0 / (1.0 + jnp.exp(-pre))
    xbc = (pre * gate).astype(bf16)
    xbc_ref[...] = xbc
    weighted = jnp.concatenate(split2(xbc[:, :INNER].astype(f32) * tail), 1)
    weighted_ref[...] = weighted
    later = mask_first(xbc[:, INNER:])
    state = dot(later[:, :N], weighted, 0, 0)
    state = state[:, :INNER] + state[:, INNER:]
    grad = dot(later[:, N:], scaled, 0, 0)
    grad = grad[:, :INNER] + grad[:, INNER:]
    state_ref[...] = state
    grad_ref[...] = grad
    write_messages((msg_ref,), state, grad, log_total, places_ref[0:1], 0)


def real_halo(halo_ref, places_ref):
    first = places_ref[places_ref.shape[0] - 16 :][:1, :1]
    return jnp.where(first > 0.5, 0.0, halo_ref[HALO_ROWS - 8 :].astype(f32))


def fix_kernel(
    halo_ref, weight_ref, scaled_ref, tail_ref, places_ref, pre_in, xbc_in, weighted_in,
    pre_ref, xbc_ref, weighted_ref, factors_ref,
):
    halo = real_halo(halo_ref, places_ref)
    top = pre_in[0:8]
    for back in range(1, K):
        tap = weight_ref[K - 1 - back : K - back]
        top = top + jnp.where(iota(top.shape, 0) < back, tap * pltpu.roll(halo, back, 0), 0.0)
    pre = jnp.concatenate([top, pre_in[8:FIX_ROWS]], 0)
    pre_ref[0:FIX_ROWS] = pre
    gate = 1.0 / (1.0 + jnp.exp(-pre))
    xbc = (pre * gate).astype(bf16)
    xbc_ref[0:FIX_ROWS] = xbc
    xbc = xbc.astype(f32)
    weighted = jnp.concatenate([each.astype(f32) for each in split2(xbc[:, :INNER] * tail_ref[0:FIX_ROWS])], 1)
    weighted_ref[0:FIX_ROWS] = weighted.astype(bf16)
    scaled = scaled_ref[0:FIX_ROWS].astype(f32)

    def packed(*parts):
        row = iota((FIX_ROWS, parts[0].shape[1]), 0)
        out = jnp.zeros(row.shape, f32)
        for at, part in enumerate(parts):
            part = pltpu.roll(part, at * (K - 1), 0) if at else part
            out = jnp.where((row >= at * (K - 1)) & (row < (at + 1) * (K - 1)), part, out)
        return out.astype(bf16)

    b_proj, c_proj = xbc[:, INNER : INNER + N], xbc[:, INNER + N :]
    factors_ref[:, :INNER] = packed(weighted[:, :INNER], weighted[:, INNER:], scaled[:, :INNER], scaled[:, INNER:])
    factors_ref[:, INNER:] = packed(b_proj, b_proj, c_proj, c_proj)


def first_parts(factors_ref):
    rows = factors_ref[:, INNER:].astype(f32)
    of_state = iota(rows.shape, 0) < 2 * (K - 1)
    rows = jnp.concatenate([jnp.where(of_state, rows, 0.0), jnp.where(of_state, 0.0, rows)], 1).astype(bf16)
    both = dot(rows, factors_ref[:, :INNER], 0, 0)
    return both[:N], both[N:]


def merge_kernel(t, radix, next_radix, state_ref, grad_ref, logs_ref, places_ref, *refs):
    got, refs = refs[: radix - 1], refs[radix - 1 :]
    prior = after = 0.0
    if t > 0:
        prior, after = refs[0][...], refs[1][...]
        refs = refs[2:]
    else:
        parts, refs = [first_parts(ref) for ref in refs[:radix]], refs[radix:]
    logs_out, prior_out, after_out, *refs = refs
    if not next_radix:
        state_out, grad_out, *refs = refs
    place = places_ref[8 * t : 8 * t + 1]
    log_prior, log_after, log_total = logs_ref[0:1], logs_ref[1:2], logs_ref[2:3]
    states = [message_block(ref, 0) for ref in got]
    grads = [message_block(ref, 1) for ref in got]
    logs = [message_log(ref) for ref in got]
    own_state, own_grad = state_ref[...], grad_ref[...]
    if t == 0:
        own_state, own_grad = own_state + parts[0][0], own_grad + parts[0][1]
        states = [each + part[0] for each, part in zip(states, parts[1:])]
        grads = [each + part[1] for each, part in zip(grads, parts[1:])]
    earlier = [s <= place for s in range(1, radix)]
    later = [s > place for s in range(1, radix)]
    before, log_before = chained(states, logs, earlier)
    beyond, log_beyond = chained(grads[::-1], logs[::-1], later[::-1])
    above, _ = chained(states, logs, later)
    below, _ = chained(grads[::-1], logs[::-1], earlier[::-1])
    mine = jnp.exp(log_total)
    state = above + jnp.exp(log_beyond) * (own_state + mine * before)
    grad = below + jnp.exp(log_before) * (own_grad + mine * beyond)
    prior_out[...] = prior + jnp.exp(log_prior) * before
    after_out[...] = after + jnp.exp(log_after) * beyond
    log_prior = log_prior + log_before
    log_after = log_after + log_beyond
    log_total = log_total + log_before + log_beyond
    row = iota((8, INNER), 0)
    logs_out[...] = jnp.where(row == 0, log_prior, jnp.where(row == 1, log_after, jnp.where(row == 2, log_total, 0.0)))
    if not next_radix:
        state_out[...] = state
        grad_out[...] = grad
    write_messages(refs, state, grad, log_total, places_ref[8 * t + 8 : 8 * t + 9], next_radix)


def local_kernel(
    xbc_ref, cot_ref, rows_ref, logs_ref, merged_logs_ref, local_ref, sums_ref,
):
    tok = xbc_ref.shape[0]
    cot = cot_ref[...]
    values = xbc_ref[:, :INNER]
    b_proj = xbc_ref[:, INNER : INNER + N]
    c_proj = xbc_ref[:, INNER + N :]
    cum, step = rows_ref[0:8], rows_ref[8:16]
    step_wide = over_channels(step)
    values_f = values.astype(f32)
    cot_f = cot.astype(f32)
    stepped = pieces3(values_f * step_wide)
    gram = dot(b_proj, c_proj, 1, 1)
    reached = iota((tok, tok), 0) <= iota((tok, tok), 1)
    pieces = stacked(cum)
    piece_head = iota((4 * HEAD_ROWS, tok), 0) % HEAD_ROWS
    dgram = jnp.zeros((tok, tok), f32)
    grads, sums = [], []
    for h in range(H):
        of = slice(h * P_SIZE, (h + 1) * P_SIZE)
        column = dot(pieces, jnp.where(piece_head == h, 1.0, 0.0).astype(bf16), 0, 0)
        within = jnp.exp(jnp.where(reached, cum[h : h + 1] - column, -1e30))
        cot_h = cot[:, of]
        grads.append(sum(dot(each, cot_h) for each in pieces3(gram * within)))
        dmix = sum(dot(each[:, of], cot_h, 1, 1) for each in stepped) * within
        dgram = dgram + dmix
        sums.append(jnp.sum(dmix * gram, axis=0, keepdims=True))
    grad_stepped = jnp.concatenate(grads, 1)
    local_ref[:, :INNER] = grad_stepped * step_wide + logs_ref[3:4] * cot_f
    high, low = split2(dgram)
    local_ref[:, INNER : INNER + N] = dot(high, c_proj) + dot(low, c_proj)
    local_ref[:, INNER + N :] = dot(high, b_proj, 0, 0) + dot(low, b_proj, 0, 0)
    row = iota((HEAD_ROWS, tok), 0)
    pairs = jnp.zeros((HEAD_ROWS, tok), f32)
    for h in range(H):
        pairs = jnp.where(row == h, sums[h], pairs)
    from_values = head_sums(values_f * grad_stepped, pieces3)
    sums_ref[0:8] = pairs - from_values * step
    sums_ref[8:16] = from_values


def weights_kernel(
    xbc_ref, cot_ref, rows_ref, raw_ref, halo_ref, places_ref, scaled_ref, until_ref, pre_ref, sums_ref, logs_ref,
    weights_ref, fixed_ref, moved_ref, slope_ref,
):
    tok = xbc_ref.shape[0]
    pre = pre_ref[...]
    sigmoid = 1.0 / (1.0 + jnp.exp(-pre))
    slope_ref[...] = sigmoid * (1.0 + pre * (1.0 - sigmoid))
    values_f = xbc_ref[:, :INNER].astype(f32)
    cum, step, left = rows_ref[0:8], rows_ref[8:16], rows_ref[16:24]
    gate, decay_rate = rows_ref[32:40], rows_ref[40:48]
    base, from_values = sums_ref[0:8], sums_ref[8:16]
    skip_rows = head_sums(values_f * cot_ref[...].astype(f32))

    bias_weight = decay_rate * unstacked(dot(stacked(gate), until_ref[...]))
    cum_last, bias_last = cum[:, tok - 1 : tok], bias_weight[:, tok - 1 : tok]
    tail = left * step
    scaled_f = scaled_ref[:, :INNER].astype(f32) + scaled_ref[:, INNER:].astype(f32)
    weights_ref[:, :INNER] = scaled_f * over_channels(cum)
    weights_ref[:, INNER : 2 * INNER] = values_f * over_channels(tail * (cum_last - cum))
    weights_ref[:, 2 * INNER : 3 * INNER] = scaled_f * over_channels(bias_weight)
    weights_ref[:, 3 * INNER :] = values_f * over_channels(left * gate + tail * (bias_last - bias_weight))
    lane = iota((HEAD_ROWS, tok), 1)
    fixed = jnp.zeros((HEAD_ROWS, tok), f32)
    for i, column in enumerate((
        jnp.sum(from_values * gate + base * bias_weight, axis=1, keepdims=True),
        jnp.sum(base * cum, axis=1, keepdims=True),
        jnp.sum(skip_rows, axis=1, keepdims=True),
        bias_last, cum_last,
    )):
        fixed = jnp.where(lane == i, column, fixed)
    fixed_ref[...] = fixed
    raw = raw_ref[...].astype(f32)
    halo = real_halo(halo_ref, places_ref)
    for back in range(1, K):
        moved_ref[(back - 1) * tok : back * tok] = shifted_down(raw, halo, back)


def totals_kernel(
    t, radix, raw_ref, moved_ref, xbc_ref, slope_ref, scaled_ref, weighted_ref, tail_ref, rows_ref, local_ref, fixed_ref, weights_ref,
    logs_ref, places_ref, weight_ref, *refs
):
    got, refs = refs[: radix - 1], refs[radix - 1 :]
    prior = after = 0.0
    if t > 0:
        prior, after = refs[0][...], refs[1][...]
        refs = refs[2:]
    conv_ref, states_ref, totals_ref, spill_ref, totals_scratch = refs
    tok = raw_ref.shape[0]
    place = places_ref[8 * t : 8 * t + 1]
    blocks = [message_block(ref) for ref in got]
    logs = [message_log(ref) for ref in got]
    before, _ = chained(blocks, logs, [s <= place for s in range(1, radix)])
    beyond, _ = chained(blocks[::-1], logs[::-1], [s > place for s in range(radix - 1, 0, -1)])
    prior = prior + jnp.exp(logs_ref[0:1]) * before
    after = after + jnp.exp(logs_ref[1:2]) * beyond

    b_proj = xbc_ref[:, INNER : INNER + N]
    c_proj = xbc_ref[:, INNER + N :]
    prior2 = jnp.concatenate(split2(prior), 0)
    after2 = jnp.concatenate(split2(after), 0)
    seen = dot(jnp.concatenate([c_proj, c_proj], 1), prior2)
    back = dot(jnp.concatenate([b_proj, b_proj], 1), after2)
    grad_c = dot(scaled_ref[:, :INNER], prior2, 1, 1)
    grad_c = grad_c[:, :N] + grad_c[:, N:] + dot(scaled_ref[:, INNER:], prior2[:N], 1, 1)
    grad_b = dot(weighted_ref[:, :INNER], after2, 1, 1)
    grad_b = grad_b[:, :N] + grad_b[:, N:] + dot(weighted_ref[:, INNER:], after2[:N], 1, 1)
    grad_low = (local_ref[...] + jnp.concatenate([tail_ref[...] * back, grad_b, grad_c], 1)).astype(bf16)
    grad_conv = grad_low.astype(f32) * slope_ref[...]
    conv_ref[...] = grad_conv
    top = grad_conv[:8]
    spill = jnp.zeros_like(top)
    for ahead in range(1, K):
        tap = weight_ref[K - 1 - ahead : K - ahead]
        spill = spill + tap * jnp.where(iota(top.shape, 0) < 8 - ahead, 0.0, pltpu.roll(top, 8 - ahead, 0))
    spill_ref[...] = spill

    sums = [grad_conv * moved_ref[back * tok : (back + 1) * tok] for back in range(K - 2, -1, -1)]
    sums += [grad_conv * raw_ref[...].astype(f32), grad_conv]
    totals_scratch[...] = jnp.zeros_like(totals_scratch)
    for k, each in enumerate(sums):
        each = jnp.sum(each, axis=0, keepdims=True)
        for j in range(LANE_BLOCKS):
            at = k * LANE_BLOCKS + j
            totals_scratch[at : at + 1] = each[:, j * 128 : (j + 1) * 128]

    states_ref[:tok, :INNER] = seen
    states_ref[:tok, INNER:] = back
    through = jnp.sum(prior * after, axis=0, keepdims=True)
    grad_bias = jnp.sum(seen * weights_ref[:, 2 * INNER : 3 * INNER] + back * weights_ref[:, 3 * INNER :], axis=0, keepdims=True)
    grad_alog = jnp.sum(seen * weights_ref[:, :INNER] + back * weights_ref[:, INNER : 2 * INNER], axis=0, keepdims=True)
    selector = head_selector(HEAD_ROWS * 2)[:HEAD_ROWS].astype(f32)
    grad_bias, grad_alog, through = (
        jnp.sum(selector * each, axis=1, keepdims=True) for each in (grad_bias, grad_alog, through)
    )
    through = through * rows_ref[24:32][:, tok - 1 : tok]
    states_ref[tok:] = jnp.broadcast_to(through, (HEAD_ROWS, 2 * INNER))
    fixed = fixed_ref[...]
    row, lane = iota((HEAD_ROWS, 128), 0), iota((HEAD_ROWS, 128), 1)
    small = jnp.zeros((HEAD_ROWS, 128), f32)
    for i, column in enumerate((
        fixed[:, 0:1] + grad_bias + through * fixed[:, 3:4],
        fixed[:, 1:2] + grad_alog + through * fixed[:, 4:5],
        fixed[:, 2:3],
    )):
        small = jnp.where((row < H) & (lane == row + i * H), column, small)
    totals_scratch[SMALL_ROW : SMALL_ROW + 1] = jnp.sum(small, axis=0, keepdims=True)
    totals_ref[...] = pack_totals(totals_scratch[...])


def input_kernel(
    conv_ref, weight_ref, states_ref, xbc_ref, scaled_ref, rows_ref, sums_ref, until_ref, out_hbm, dt_out_ref, end_ref, out_ref, sem
):
    grad_conv = conv_ref[...]
    tok, channels = grad_conv.shape
    grad_in = weight_ref[K - 1 : K] * grad_conv
    row8 = iota((8, channels), 0)
    for ahead in range(1, K):
        tap = weight_ref[K - 1 - ahead : K - ahead]
        moved = pltpu.roll(grad_conv, tok - ahead, 0)
        last8 = moved[tok - 8 :]
        inside = row8 < 8 - ahead
        grad_in = grad_in + tap * jnp.concatenate([moved[: tok - 8], jnp.where(inside, last8, 0.0)], 0)
    out_ref[...] = grad_in.astype(bf16)
    copy = pltpu.make_async_copy(out_ref, out_hbm, sem)
    copy.start()
    end_ref[...] = grad_in[tok - END_ROWS :]

    step, left, gate, decay_rate = rows_ref[8:16], rows_ref[16:24], rows_ref[32:40], rows_ref[40:48]
    scaled_f = scaled_ref[:, :INNER].astype(f32) + scaled_ref[:, INNER:].astype(f32)
    seen_rows = head_sums(scaled_f * states_ref[:tok, :INNER])
    tail_rows = head_sums(xbc_ref[:, :INNER].astype(f32) * states_ref[:tok, INNER:])
    tail_term = tail_rows * left * step
    last_extra = jnp.sum(tail_term, axis=1, keepdims=True) + states_ref[tok:][:, :1]
    grad_cum = sums_ref[0:8] + seen_rows - tail_term
    grad_log = unstacked(dot(stacked(grad_cum), until_ref[...], 1, 1)) + last_extra
    grad_step = sums_ref[8:16] + tail_rows * left + decay_rate * grad_log
    dt_out_ref[...] = (grad_step * gate)[0:H]
    copy.wait()


def end_kernel(end_ref, spilled_ref, places_ref, main_hbm, out_hbm, rows_ref, sem):
    end = end_ref[...]
    last = places_ref[places_ref.shape[0] - 8 :][:1, :1]
    fixed = end[END_ROWS - 8 :] + jnp.where(last > 0.5, 0.0, spilled_ref[...])
    rows_ref[...] = jnp.concatenate([end[: END_ROWS - 8], fixed], 0).astype(bf16)
    tok = out_hbm.shape[0]
    copy = pltpu.make_async_copy(rows_ref, out_hbm.at[pl.ds(tok - END_ROWS, END_ROWS)], sem)
    copy.start()
    copy.wait()


def summed(parts):
    large = jnp.sum(parts * jnp.exp(parts[:, SMALL_ROW + 1 : SMALL_ROW + 2]), axis=0)
    small = parts[:, SMALL_ROW : SMALL_ROW + 1] + parts[:, SMALL_ROW + 3 : SMALL_ROW + 4] * (1 / 256.0)
    small = small * jnp.exp(parts[:, SMALL_ROW + 2 : SMALL_ROW + 3])
    return large, jnp.sum(small, axis=0)


def repack_kernel(parts_ref, out_ref):
    large, small = summed(parts_ref[...])
    out_ref[...] = pack_totals(jnp.where(iota(large.shape, 0) == SMALL_ROW, small, large))


def finish_kernel(parts_ref, weight_ref, bias_ref, dt_bias_ref, alog_ref, skip_ref):
    large, small = summed(parts_ref[...])
    for k in range(K + 1):
        for j in range(LANE_BLOCKS):
            at = k * LANE_BLOCKS + j
            if k < K:
                weight_ref[k : k + 1, j * 128 : (j + 1) * 128] = large[at : at + 1]
            else:
                bias_ref[:, j * 128 : (j + 1) * 128] = large[at : at + 1]
    for i, ref in enumerate((dt_bias_ref, alog_ref, skip_ref)):
        ref[...] = small[:, i * H : (i + 1) * H]


def call(kernel, outs, in_specs, out_specs=None, scratch=(), flops=0, limit=16 << 20, aliases=None):
    return pl.pallas_call(
        kernel,
        out_shape=outs,
        in_specs=in_specs,
        out_specs=out_specs or jax.tree.map(lambda _: VMEM, outs),
        scratch_shapes=list(scratch),
        input_output_aliases=aliases or {},
        compiler_params=pltpu.CompilerParams(vmem_limit_bytes=limit),
        cost_estimate=pl.CostEstimate(flops=flops, bytes_accessed=1 << 20, transcendentals=0),
    )


def struct(shape, dtype=f32):
    return jax.ShapeDtypeStruct(shape, dtype)


def from_groups(messages, slabs, size, radix):
    got = []
    for s in range(1, radix):
        message = messages[s - 1 if len(messages) > 1 else 0]
        route = [(p, p - p % (size * radix) + (p + s * size) % (size * radix)) for p in range(slabs)]
        got.append(lax.ppermute(message, "ctx", route))
    return got


def states_from_groups(messages, slabs, size, radix):
    got = from_groups([message.astype(jnp.float16) for message in messages], slabs, size, radix)
    return [each.astype(f32) for each in got]


def stages_of(slabs):
    stages, size = [], 1
    while size < slabs:
        radix = 2 if (slabs // size).bit_length() % 2 == 0 else 4
        stages.append((size, radix))
        size *= radix
    assert size == slabs and len(stages) > 1
    return stages


def everyones(packed, axes, count):
    packed = jnp.broadcast_to(packed.astype(jnp.float16)[None], (count, *packed.shape))
    return lax.all_to_all(packed, axes, 0, 0).astype(f32)


def on_device(xbc_raw, conv_weight, conv_bias, dt_raw, dt_bias, a_log, d_skip, grad_out):
    tok, channels = xbc_raw.shape[1:]
    slabs = lax.axis_size("ctx")
    contexts = lax.axis_size("dp")
    stages = stages_of(slabs)

    raw, cot, dt_rows = xbc_raw[0], grad_out[0], dt_raw[0].T
    until = call(triangle_kernel, struct((tok, tok), bf16), [], flops=10**11)()
    until, bias, heads = call(
        heads_kernel,
        (struct((tok, tok), bf16), struct((1, channels)), struct((3 * HEAD_ROWS, tok))),
        [VMEM] * 5,
        aliases={4: 0},
    )(conv_bias[None], dt_bias[None], a_log[None], d_skip[None], until)
    early_raw, until = lax.optimization_barrier((raw, until))
    halo = lax.ppermute(early_raw[tok - HALO_ROWS :], "ctx", [(i, (i + 1) % slabs) for i in range(slabs)])

    def last_radix(t):
        return stages[t][1] if t == len(stages) - 1 else 0

    def messages(t):
        if last_radix(t):
            return (struct((N + TAIL_ROWS, INNER)),) * (last_radix(t) - 1)
        return (struct((2 * N + TAIL_ROWS, INNER)),)

    state_like = struct((N, INNER))
    logs_like = struct((8, INNER))
    pre, xbc, weighted, scaled, tail, rows, logs, places, state, grad, *outgoing = call(
        functools.partial(start_kernel, stages),
        (
            struct((tok, channels)), struct((tok, channels), bf16), struct((tok, 2 * INNER), bf16),
            struct((tok, 2 * INNER), bf16), struct((tok, INNER)), struct((6 * HEAD_ROWS, tok)),
            logs_like, struct((8 * len(stages) + 16, INNER)), state_like, state_like, *messages(0),
        ),
        [VMEM] * 7,
        scratch=[pltpu.VMEM((HEAD_ROWS, tok), f32)],
        flops=10**11,
    )(raw, cot, conv_weight, bias, dt_rows, heads, until)
    pre, xbc, weighted, factors = call(
        fix_kernel,
        (
            struct((tok, channels)), struct((tok, channels), bf16), struct((tok, 2 * INNER), bf16),
            struct((FIX_ROWS, INNER + N), bf16),
        ),
        [VMEM] * 8,
        flops=5 * 10**9,
        aliases={5: 0, 6: 1, 7: 2},
    )(halo, conv_weight, scaled, tail, places, pre, xbc, weighted)

    first_logs = logs
    carried = ()
    for t, (size, radix) in enumerate(stages):
        got = states_from_groups(outgoing, slabs, size, radix)
        if t == 0:
            carried = [factors] + from_groups([factors], slabs, size, radix)
        if t == len(stages) - 1:
            got, local, weights, fixed, moved, slope = lax.optimization_barrier((got, local, weights, fixed, moved, slope))
            break
        last = last_radix(t + 1)
        outs = (logs_like, state_like, state_like) + (() if last else (state_like, state_like))
        logs, *outgoing = call(
            functools.partial(merge_kernel, t, radix, last),
            outs + messages(t + 1),
            [VMEM] * (4 + len(got) + len(carried)),
            flops=1_000_000,
        )(state, grad, logs, places, *got, *carried)
        carried, outgoing = outgoing[:2], outgoing[2:]
        if not last:
            (state, grad), outgoing = outgoing[:2], outgoing[2:]
        if t == 0:
            local, sums = call(
                local_kernel,
                (struct((tok, channels)), struct((2 * HEAD_ROWS, tok))),
                [VMEM] * 5,
                flops=2 * 10**9,
            )(xbc, cot, rows, first_logs, logs)
            weights, fixed, moved, slope = call(
                weights_kernel,
                (
                    struct((tok, 4 * INNER)), struct((HEAD_ROWS, tok)), struct(((K - 1) * tok, channels)), struct((tok, channels)),
                ),
                [VMEM] * 11,
                flops=10**11,
            )(xbc, cot, rows, raw, halo, places, scaled, until, pre, sums, logs)

    grad_conv, states, packed, spill = call(
        functools.partial(totals_kernel, len(stages) - 1, radix),
        (struct((tok, channels)), struct((tok + HEAD_ROWS, 2 * INNER)), struct((TOTAL_ROWS, 128)), struct((8, channels))),
        [VMEM] * (14 + len(got) + len(carried)),
        scratch=[pltpu.VMEM((TOTAL_ROWS, 128), f32)],
        flops=200_000_000,
    )(raw, moved, xbc, slope, scaled, weighted, tail, rows, local, fixed, weights, logs, places, conv_weight, *got, *carried)

    spilled = lax.ppermute(spill, "ctx", [((i + 1) % slabs, i) for i in range(slabs)])
    if slabs * contexts <= 64:
        parts = everyones(packed, ("ctx", "dp"), slabs * contexts)
    else:
        packed = call(repack_kernel, struct((TOTAL_ROWS, 128)), [VMEM])(everyones(packed, "ctx", slabs))
        parts = everyones(packed, "dp", contexts)

    grad_main, grad_dt, end = call(
        input_kernel,
        (struct((tok, channels), bf16), struct((H, tok)), struct((END_ROWS, channels))),
        [VMEM] * 8,
        (HBM, VMEM, VMEM),
        [pltpu.VMEM((tok, channels), bf16), pltpu.SemaphoreType.DMA],
        flops=1_000_000,
    )(grad_conv, conv_weight, states, xbc, scaled, rows, sums, until)
    grad_input = call(
        end_kernel,
        struct((tok, channels), bf16),
        [VMEM] * 3 + [HBM],
        HBM,
        [pltpu.VMEM((END_ROWS, channels), bf16), pltpu.SemaphoreType.DMA],
        aliases={3: 0},
    )(end, spilled, places, grad_main)

    grad_weight, grad_bias, *small = call(
        finish_kernel,
        (struct((K, channels)), struct((1, channels)), struct((1, H)), struct((1, H)), struct((1, H))),
        [VMEM],
    )(parts)
    return (grad_input[None], grad_dt.T[None], grad_weight, grad_bias[0], *(each[0] for each in small))


def solution(mesh):
    in_specs = (
        P("dp", "ctx", None),
        P(),
        P(),
        P("dp", "ctx", None),
        P(),
        P(),
        P(),
        P("dp", "ctx", None),
    )
    out_specs = (P("dp", "ctx", None), P("dp", "ctx", None), P(), P(), P(), P(), P())
    return jax.shard_map(
        on_device, mesh=mesh, in_specs=in_specs, out_specs=out_specs, check_vma=False
    )
```

```python
import functools

import jax
import jax.numpy as jnp
from jax import lax
from jax.experimental import pallas as pl
from jax.experimental.pallas import tpu as pltpu
from jax.sharding import PartitionSpec as P

H = 4
P_SIZE = 64
N = 128
K = 4
INNER = H * P_SIZE
HEAD_ROWS = 8
TAIL_ROWS = 8
HALO_ROWS = 16
FIX_ROWS = 16
END_ROWS = 16
LANE_BLOCKS = (INNER + 2 * N) // 128
SMALL_ROW = (K + 1) * LANE_BLOCKS
TOTAL_ROWS = 24

f32 = jnp.float32
bf16 = jnp.bfloat16

VMEM = pl.BlockSpec(memory_space=pltpu.VMEM)
HBM = pl.BlockSpec(memory_space=pltpu.HBM)


def dot(a, b, a_dim=1, b_dim=0):
    return lax.dot_general(a, b, (((a_dim,), (b_dim,)), ((), ())), preferred_element_type=f32)


def split2(x):
    high = x.astype(bf16)
    return high, (x - high.astype(f32)).astype(bf16)


def split3(x):
    high = x.astype(bf16).astype(f32)
    rest = x - high
    middle = rest.astype(bf16).astype(f32)
    return high, middle, rest - middle


def iota(shape, dim):
    return lax.broadcasted_iota(jnp.int32, shape, dim)


def stacked(rows):
    return jnp.concatenate([*split3(rows), jnp.zeros_like(rows)], 0).astype(bf16)


def unstacked(rows):
    return rows[0:8] + rows[8:16] + rows[16:24]


def head_selector(rows):
    shape = (rows, INNER)
    return jnp.where(iota(shape, 1) // P_SIZE == iota(shape, 0) % HEAD_ROWS, 1.0, 0.0).astype(bf16)


def over_channels(rows):
    return dot(stacked(rows), head_selector(4 * HEAD_ROWS), 0, 0)


def channel_row(column):
    return jnp.sum(head_selector(HEAD_ROWS * 2)[:HEAD_ROWS].astype(f32) * column, axis=0, keepdims=True)


def pieces3(x):
    return [each.astype(bf16) for each in split3(x)]


def head_sums(x, split=split2):
    selector = head_selector(HEAD_ROWS * 2)
    return sum(dot(selector, each, 1, 1) for each in split(x))[:HEAD_ROWS]


def by_head(ref, width):
    row = iota((HEAD_ROWS, width), 0)
    out = jnp.zeros((HEAD_ROWS, width), f32)
    for h in range(H):
        out = jnp.where(row == h, ref[:, h : h + 1], out)
    return out


def shifted_down(x, first, count):
    moved = pltpu.roll(x, count, 0)
    top = jnp.where(iota(first.shape, 0) < count, pltpu.roll(first, count, 0), moved[:8])
    return jnp.concatenate([top, moved[8:]], 0)


def quantized_log(size):
    return jnp.log(jnp.maximum(size, 1e-30)).astype(bf16).astype(f32)


def scaled_columns(x):
    log_size = quantized_log(jnp.max(jnp.abs(x), axis=0, keepdims=True))
    return x * jnp.exp(-log_size), log_size


def write_messages(msg_refs, state, grad, log_total, place, radix):
    row = iota((TAIL_ROWS, INNER), 0)
    high, middle, low = split3(log_total)
    tail = jnp.where(row == 4, high, jnp.where(row == 5, middle * 256.0, jnp.where(row == 6, low * 65536.0, 0.0)))
    state, state_size = scaled_columns(state)
    grad, grad_size = scaled_columns(grad)
    if radix:
        for s, msg_ref in enumerate(msg_refs, 1):
            on = place + s < radix
            msg_ref[0:N] = jnp.where(on, state, grad)
            msg_ref[N : N + TAIL_ROWS] = jnp.where(row == 0, jnp.where(on, state_size, grad_size), tail)
    else:
        (msg_ref,) = msg_refs
        msg_ref[0:N] = state
        msg_ref[N : 2 * N] = grad
        msg_ref[2 * N : 2 * N + TAIL_ROWS] = jnp.where(row == 0, state_size, jnp.where(row == 1, grad_size, tail))


def message_log(got_ref):
    rows = got_ref.shape[0] - TAIL_ROWS
    tail = got_ref[rows : rows + 8]
    return tail[4:5] + tail[5:6] * (1 / 256.0) + tail[6:7] * (1 / 65536.0)


def message_block(got_ref, which=0):
    rows = got_ref.shape[0] - TAIL_ROWS
    return got_ref[which * N : (which + 1) * N] * jnp.exp(got_ref[rows + which : rows + which + 1])


def chained(blocks, logs, used):
    total, log_sum = 0.0, 0.0
    for block, log, use in zip(blocks, logs, used):
        total = total + jnp.where(use, jnp.exp(log_sum) * block, 0.0)
        log_sum = log_sum + jnp.where(use, log, 0.0)
    return total, log_sum


def pack_totals(x):
    row = iota(x.shape, 0)
    large = jnp.where(row < SMALL_ROW, x, 0.0)
    large_size = quantized_log(jnp.max(jnp.abs(large), axis=0, keepdims=True))
    small = x[SMALL_ROW : SMALL_ROW + 1]
    small_size = quantized_log(jnp.abs(small))
    small = small * jnp.exp(-small_size)
    small_high = small.astype(bf16).astype(f32)
    out = jnp.where(row == SMALL_ROW, small_high, large * jnp.exp(-large_size))
    out = jnp.where(row == SMALL_ROW + 3, (small - small_high) * 256.0, out)
    return jnp.where(row == SMALL_ROW + 1, large_size, jnp.where(row == SMALL_ROW + 2, small_size, out))


def triangle_kernel(until_ref):
    shape = until_ref.shape
    until_ref[...] = jnp.where(iota(shape, 0) <= iota(shape, 1), 1.0, 0.0).astype(bf16)


def heads_kernel(bias_ref, dt_bias_ref, alog_ref, skip_ref, until_in, until_ref, bias_out, heads_ref):
    bias_out[...] = bias_ref[...]
    for i, ref in enumerate((dt_bias_ref, alog_ref, skip_ref)):
        heads_ref[8 * i : 8 * i + 8] = by_head(ref, until_ref.shape[1])


def mask_first(x):
    top = jnp.where(iota((FIX_ROWS, x.shape[1]), 0) < K - 1, 0.0, x[:FIX_ROWS].astype(f32))
    return jnp.concatenate([top.astype(x.dtype), x[FIX_ROWS:]], 0)


def start_kernel(
    stages, raw_ref, cot_ref, weight_ref, bias_ref, dt_ref, heads_ref, until_ref,
    pre_ref, xbc_ref, weighted_ref, scaled_ref, tail_ref, rows_ref, logs_ref, places_ref, state_ref, grad_ref, msg_ref, dt8_ref,
):
    tok = raw_ref.shape[0]
    place = lax.axis_index("ctx")
    for t, (size, radix) in enumerate(stages):
        places_ref[8 * t : 8 * t + 8] = jnp.full((8, INNER), lax.rem(lax.div(place, size), radix), jnp.int32).astype(f32)
    at = 8 * len(stages)
    slabs = stages[-1][0] * stages[-1][1]
    places_ref[at : at + 8] = jnp.full((8, INNER), jnp.where(place == 0, 1, 0), jnp.int32).astype(f32)
    places_ref[at + 8 : at + 16] = jnp.full((8, INNER), jnp.where(place == slabs - 1, 1, 0), jnp.int32).astype(f32)
    dt8_ref[...] = jnp.zeros_like(dt8_ref)
    dt8_ref[0:H] = dt_ref[...]
    dt_pre = dt8_ref[...] + heads_ref[0:8]
    step = jnp.maximum(dt_pre, 0.0) + jnp.log1p(jnp.exp(-jnp.abs(dt_pre)))
    real = iota((HEAD_ROWS, tok), 0) < H
    decay_rate = jnp.where(real, -jnp.exp(heads_ref[8:16]), 0.0)
    cum = unstacked(dot(stacked(step * decay_rate), until_ref[...]))
    left = jnp.exp(cum[:, tok - 1 : tok] - cum)
    reach = jnp.exp(cum)
    rows_ref[0:8] = cum
    rows_ref[8:16] = step
    rows_ref[16:24] = left
    rows_ref[24:32] = reach
    rows_ref[32:40] = 1.0 / (1.0 + jnp.exp(-dt_pre))
    rows_ref[40:48] = decay_rate
    tail = over_channels(left * step)
    tail_ref[...] = tail
    log_total = channel_row(cum[:, tok - 1 : tok])
    skip = channel_row(heads_ref[16:24][:, :1])
    row = iota((8, INNER), 0)
    logs_ref[...] = jnp.where(row == 2, log_total, jnp.where(row == 3, skip, 0.0))
    scaled = jnp.concatenate(split2(cot_ref[...].astype(f32) * over_channels(reach)), 1)
    scaled_ref[...] = scaled

    raw = raw_ref[...].astype(f32)
    zeros = jnp.zeros((8, raw.shape[1]), f32)
    pre = bias_ref[...] + weight_ref[K - 1 : K] * raw
    for back in range(1, K):
        pre = pre + weight_ref[K - 1 - back : K - back] * shifted_down(raw, zeros, back)
    pre_ref[...] = pre
    gate = 1.0 / (1.0 + jnp.exp(-pre))
    xbc = (pre * gate).astype(bf16)
    xbc_ref[...] = xbc
    weighted = jnp.concatenate(split2(xbc[:, :INNER].astype(f32) * tail), 1)
    weighted_ref[...] = weighted
    later = mask_first(xbc[:, INNER:])
    state = dot(later[:, :N], weighted, 0, 0)
    state = state[:, :INNER] + state[:, INNER:]
    grad = dot(later[:, N:], scaled, 0, 0)
    grad = grad[:, :INNER] + grad[:, INNER:]
    state_ref[...] = state
    grad_ref[...] = grad
    write_messages((msg_ref,), state, grad, log_total, places_ref[0:1], 0)


def real_halo(halo_ref, places_ref):
    first = places_ref[places_ref.shape[0] - 16 :][:1, :1]
    return jnp.where(first > 0.5, 0.0, halo_ref[HALO_ROWS - 8 :].astype(f32))


def fix_kernel(
    halo_ref, weight_ref, scaled_ref, tail_ref, places_ref, pre_in, xbc_in, weighted_in,
    pre_ref, xbc_ref, weighted_ref, factors_ref,
):
    halo = real_halo(halo_ref, places_ref)
    top = pre_in[0:8]
    for back in range(1, K):
        tap = weight_ref[K - 1 - back : K - back]
        top = top + jnp.where(iota(top.shape, 0) < back, tap * pltpu.roll(halo, back, 0), 0.0)
    pre = jnp.concatenate([top, pre_in[8:FIX_ROWS]], 0)
    pre_ref[0:FIX_ROWS] = pre
    gate = 1.0 / (1.0 + jnp.exp(-pre))
    xbc = (pre * gate).astype(bf16)
    xbc_ref[0:FIX_ROWS] = xbc
    xbc = xbc.astype(f32)
    weighted = jnp.concatenate([each.astype(f32) for each in split2(xbc[:, :INNER] * tail_ref[0:FIX_ROWS])], 1)
    weighted_ref[0:FIX_ROWS] = weighted.astype(bf16)
    scaled = scaled_ref[0:FIX_ROWS].astype(f32)

    def packed(*parts):
        row = iota((FIX_ROWS, parts[0].shape[1]), 0)
        out = jnp.zeros(row.shape, f32)
        for at, part in enumerate(parts):
            part = pltpu.roll(part, at * (K - 1), 0) if at else part
            out = jnp.where((row >= at * (K - 1)) & (row < (at + 1) * (K - 1)), part, out)
        return out.astype(bf16)

    b_proj, c_proj = xbc[:, INNER : INNER + N], xbc[:, INNER + N :]
    factors_ref[:, :INNER] = packed(weighted[:, :INNER], weighted[:, INNER:], scaled[:, :INNER], scaled[:, INNER:])
    factors_ref[:, INNER:] = packed(b_proj, b_proj, c_proj, c_proj)


def first_parts(factors_ref):
    rows = factors_ref[:, INNER:].astype(f32)
    of_state = iota(rows.shape, 0) < 2 * (K - 1)
    rows = jnp.concatenate([jnp.where(of_state, rows, 0.0), jnp.where(of_state, 0.0, rows)], 1).astype(bf16)
    both = dot(rows, factors_ref[:, :INNER], 0, 0)
    return both[:N], both[N:]


def merge_kernel(t, radix, next_radix, state_ref, grad_ref, logs_ref, places_ref, *refs):
    got, refs = refs[: radix - 1], refs[radix - 1 :]
    prior = after = 0.0
    if t > 0:
        prior, after = refs[0][...], refs[1][...]
        refs = refs[2:]
    else:
        parts, refs = [first_parts(ref) for ref in refs[: radix - 1]], refs[radix - 1 :]
    logs_out, prior_out, after_out, *refs = refs
    if not next_radix:
        state_out, grad_out, *refs = refs
    place = places_ref[8 * t : 8 * t + 1]
    log_prior, log_after, log_total = logs_ref[0:1], logs_ref[1:2], logs_ref[2:3]
    states = [message_block(ref, 0) for ref in got]
    grads = [message_block(ref, 1) for ref in got]
    logs = [message_log(ref) for ref in got]
    own_state, own_grad = state_ref[...], grad_ref[...]
    if t == 0:
        states = [each + part[0] for each, part in zip(states, parts)]
        grads = [each + part[1] for each, part in zip(grads, parts)]
    earlier = [s <= place for s in range(1, radix)]
    later = [s > place for s in range(1, radix)]
    before, log_before = chained(states, logs, earlier)
    beyond, log_beyond = chained(grads[::-1], logs[::-1], later[::-1])
    above, _ = chained(states, logs, later)
    below, _ = chained(grads[::-1], logs[::-1], earlier[::-1])
    mine = jnp.exp(log_total)
    state = above + jnp.exp(log_beyond) * (own_state + mine * before)
    grad = below + jnp.exp(log_before) * (own_grad + mine * beyond)
    prior_out[...] = prior + jnp.exp(log_prior) * before
    after_out[...] = after + jnp.exp(log_after) * beyond
    log_prior = log_prior + log_before
    log_after = log_after + log_beyond
    log_total = log_total + log_before + log_beyond
    row = iota((8, INNER), 0)
    logs_out[...] = jnp.where(row == 0, log_prior, jnp.where(row == 1, log_after, jnp.where(row == 2, log_total, 0.0)))
    if not next_radix:
        state_out[...] = state
        grad_out[...] = grad
    write_messages(refs, state, grad, log_total, places_ref[8 * t + 8 : 8 * t + 9], next_radix)


def local_kernel(
    xbc_ref, cot_ref, rows_ref, logs_ref, factors_ref, state_in, grad_in, local_ref, sums_ref, state_ref, grad_ref,
):
    state, grad = first_parts(factors_ref)
    state_ref[...] = state_in[...] + state
    grad_ref[...] = grad_in[...] + grad
    tok = xbc_ref.shape[0]
    cot = cot_ref[...]
    values = xbc_ref[:, :INNER]
    b_proj = xbc_ref[:, INNER : INNER + N]
    c_proj = xbc_ref[:, INNER + N :]
    cum, step = rows_ref[0:8], rows_ref[8:16]
    step_wide = over_channels(step)
    values_f = values.astype(f32)
    cot_f = cot.astype(f32)
    stepped = pieces3(values_f * step_wide)
    gram = dot(b_proj, c_proj, 1, 1)
    reached = iota((tok, tok), 0) <= iota((tok, tok), 1)
    pieces = stacked(cum)
    piece_head = iota((4 * HEAD_ROWS, tok), 0) % HEAD_ROWS
    dgram = jnp.zeros((tok, tok), f32)
    grads, sums = [], []
    for h in range(H):
        of = slice(h * P_SIZE, (h + 1) * P_SIZE)
        column = dot(pieces, jnp.where(piece_head == h, 1.0, 0.0).astype(bf16), 0, 0)
        within = jnp.exp(jnp.where(reached, cum[h : h + 1] - column, -1e30))
        cot_h = cot[:, of]
        grads.append(sum(dot(each, cot_h) for each in pieces3(gram * within)))
        dmix = sum(dot(each[:, of], cot_h, 1, 1) for each in stepped) * within
        dgram = dgram + dmix
        sums.append(jnp.sum(dmix * gram, axis=0, keepdims=True))
    grad_stepped = jnp.concatenate(grads, 1)
    local_ref[:, :INNER] = grad_stepped * step_wide + logs_ref[3:4] * cot_f
    high, low = split2(dgram)
    local_ref[:, INNER : INNER + N] = dot(high, c_proj) + dot(low, c_proj)
    local_ref[:, INNER + N :] = dot(high, b_proj, 0, 0) + dot(low, b_proj, 0, 0)
    row = iota((HEAD_ROWS, tok), 0)
    pairs = jnp.zeros((HEAD_ROWS, tok), f32)
    for h in range(H):
        pairs = jnp.where(row == h, sums[h], pairs)
    from_values = head_sums(values_f * grad_stepped, pieces3)
    sums_ref[0:8] = pairs - from_values * step
    sums_ref[8:16] = from_values


def weights_kernel(
    xbc_ref, cot_ref, rows_ref, raw_ref, halo_ref, places_ref, scaled_ref, until_ref, pre_ref, sums_ref, logs_ref,
    weights_ref, fixed_ref, moved_ref, slope_ref,
):
    tok = xbc_ref.shape[0]
    pre = pre_ref[...]
    sigmoid = 1.0 / (1.0 + jnp.exp(-pre))
    slope_ref[...] = sigmoid * (1.0 + pre * (1.0 - sigmoid))
    values_f = xbc_ref[:, :INNER].astype(f32)
    cum, step, left = rows_ref[0:8], rows_ref[8:16], rows_ref[16:24]
    gate, decay_rate = rows_ref[32:40], rows_ref[40:48]
    base, from_values = sums_ref[0:8], sums_ref[8:16]
    skip_rows = head_sums(values_f * cot_ref[...].astype(f32))

    bias_weight = decay_rate * unstacked(dot(stacked(gate), until_ref[...]))
    cum_last, bias_last = cum[:, tok - 1 : tok], bias_weight[:, tok - 1 : tok]
    tail = left * step
    scaled_f = scaled_ref[:, :INNER].astype(f32) + scaled_ref[:, INNER:].astype(f32)
    weights_ref[:, :INNER] = scaled_f * over_channels(cum)
    weights_ref[:, INNER : 2 * INNER] = values_f * over_channels(tail * (cum_last - cum))
    weights_ref[:, 2 * INNER : 3 * INNER] = scaled_f * over_channels(bias_weight)
    weights_ref[:, 3 * INNER :] = values_f * over_channels(left * gate + tail * (bias_last - bias_weight))
    lane = iota((HEAD_ROWS, tok), 1)
    fixed = jnp.zeros((HEAD_ROWS, tok), f32)
    for i, column in enumerate((
        jnp.sum(from_values * gate + base * bias_weight, axis=1, keepdims=True),
        jnp.sum(base * cum, axis=1, keepdims=True),
        jnp.sum(skip_rows, axis=1, keepdims=True),
        bias_last, cum_last,
    )):
        fixed = jnp.where(lane == i, column, fixed)
    fixed_ref[...] = fixed
    raw = raw_ref[...].astype(f32)
    halo = real_halo(halo_ref, places_ref)
    for back in range(1, K):
        moved_ref[(back - 1) * tok : back * tok] = shifted_down(raw, halo, back)


def totals_kernel(
    t, radix, raw_ref, moved_ref, xbc_ref, slope_ref, scaled_ref, weighted_ref, tail_ref, rows_ref, local_ref, fixed_ref, weights_ref,
    logs_ref, places_ref, weight_ref, *refs
):
    got, refs = refs[: radix - 1], refs[radix - 1 :]
    prior = after = 0.0
    if t > 0:
        prior, after = refs[0][...], refs[1][...]
        refs = refs[2:]
    conv_ref, states_ref, totals_ref, spill_ref, totals_scratch = refs
    tok = raw_ref.shape[0]
    place = places_ref[8 * t : 8 * t + 1]
    blocks = [message_block(ref) for ref in got]
    logs = [message_log(ref) for ref in got]
    before, _ = chained(blocks, logs, [s <= place for s in range(1, radix)])
    beyond, _ = chained(blocks[::-1], logs[::-1], [s > place for s in range(radix - 1, 0, -1)])
    prior = prior + jnp.exp(logs_ref[0:1]) * before
    after = after + jnp.exp(logs_ref[1:2]) * beyond

    b_proj = xbc_ref[:, INNER : INNER + N]
    c_proj = xbc_ref[:, INNER + N :]
    prior2 = jnp.concatenate(split2(prior), 0)
    after2 = jnp.concatenate(split2(after), 0)
    seen = dot(jnp.concatenate([c_proj, c_proj], 1), prior2)
    back = dot(jnp.concatenate([b_proj, b_proj], 1), after2)
    grad_c = dot(scaled_ref[:, :INNER], prior2, 1, 1)
    grad_c = grad_c[:, :N] + grad_c[:, N:] + dot(scaled_ref[:, INNER:], prior2[:N], 1, 1)
    grad_b = dot(weighted_ref[:, :INNER], after2, 1, 1)
    grad_b = grad_b[:, :N] + grad_b[:, N:] + dot(weighted_ref[:, INNER:], after2[:N], 1, 1)
    grad_low = (local_ref[...] + jnp.concatenate([tail_ref[...] * back, grad_b, grad_c], 1)).astype(bf16)
    grad_conv = grad_low.astype(f32) * slope_ref[...]
    conv_ref[...] = grad_conv
    top = grad_conv[:8]
    spill = jnp.zeros_like(top)
    for ahead in range(1, K):
        tap = weight_ref[K - 1 - ahead : K - ahead]
        spill = spill + tap * jnp.where(iota(top.shape, 0) < 8 - ahead, 0.0, pltpu.roll(top, 8 - ahead, 0))
    spill_ref[...] = spill

    sums = [grad_conv * moved_ref[back * tok : (back + 1) * tok] for back in range(K - 2, -1, -1)]
    sums += [grad_conv * raw_ref[...].astype(f32), grad_conv]
    totals_scratch[...] = jnp.zeros_like(totals_scratch)
    for k, each in enumerate(sums):
        each = jnp.sum(each, axis=0, keepdims=True)
        for j in range(LANE_BLOCKS):
            at = k * LANE_BLOCKS + j
            totals_scratch[at : at + 1] = each[:, j * 128 : (j + 1) * 128]

    states_ref[:tok, :INNER] = seen
    states_ref[:tok, INNER:] = back
    through = jnp.sum(prior * after, axis=0, keepdims=True)
    grad_bias = jnp.sum(seen * weights_ref[:, 2 * INNER : 3 * INNER] + back * weights_ref[:, 3 * INNER :], axis=0, keepdims=True)
    grad_alog = jnp.sum(seen * weights_ref[:, :INNER] + back * weights_ref[:, INNER : 2 * INNER], axis=0, keepdims=True)
    selector = head_selector(HEAD_ROWS * 2)[:HEAD_ROWS].astype(f32)
    grad_bias, grad_alog, through = (
        jnp.sum(selector * each, axis=1, keepdims=True) for each in (grad_bias, grad_alog, through)
    )
    through = through * rows_ref[24:32][:, tok - 1 : tok]
    states_ref[tok:] = jnp.broadcast_to(through, (HEAD_ROWS, 2 * INNER))
    fixed = fixed_ref[...]
    row, lane = iota((HEAD_ROWS, 128), 0), iota((HEAD_ROWS, 128), 1)
    small = jnp.zeros((HEAD_ROWS, 128), f32)
    for i, column in enumerate((
        fixed[:, 0:1] + grad_bias + through * fixed[:, 3:4],
        fixed[:, 1:2] + grad_alog + through * fixed[:, 4:5],
        fixed[:, 2:3],
    )):
        small = jnp.where((row < H) & (lane == row + i * H), column, small)
    totals_scratch[SMALL_ROW : SMALL_ROW + 1] = jnp.sum(small, axis=0, keepdims=True)
    totals_ref[...] = pack_totals(totals_scratch[...])


def input_kernel(
    conv_ref, weight_ref, states_ref, xbc_ref, scaled_ref, rows_ref, sums_ref, until_ref, out_hbm, dt_out_ref, end_ref, out_ref, sem
):
    grad_conv = conv_ref[...]
    tok, channels = grad_conv.shape
    grad_in = weight_ref[K - 1 : K] * grad_conv
    row8 = iota((8, channels), 0)
    for ahead in range(1, K):
        tap = weight_ref[K - 1 - ahead : K - ahead]
        moved = pltpu.roll(grad_conv, tok - ahead, 0)
        last8 = moved[tok - 8 :]
        inside = row8 < 8 - ahead
        grad_in = grad_in + tap * jnp.concatenate([moved[: tok - 8], jnp.where(inside, last8, 0.0)], 0)
    out_ref[...] = grad_in.astype(bf16)
    copy = pltpu.make_async_copy(out_ref, out_hbm, sem)
    copy.start()
    end_ref[...] = grad_in[tok - END_ROWS :]

    step, left, gate, decay_rate = rows_ref[8:16], rows_ref[16:24], rows_ref[32:40], rows_ref[40:48]
    scaled_f = scaled_ref[:, :INNER].astype(f32) + scaled_ref[:, INNER:].astype(f32)
    seen_rows = head_sums(scaled_f * states_ref[:tok, :INNER])
    tail_rows = head_sums(xbc_ref[:, :INNER].astype(f32) * states_ref[:tok, INNER:])
    tail_term = tail_rows * left * step
    last_extra = jnp.sum(tail_term, axis=1, keepdims=True) + states_ref[tok:][:, :1]
    grad_cum = sums_ref[0:8] + seen_rows - tail_term
    grad_log = unstacked(dot(stacked(grad_cum), until_ref[...], 1, 1)) + last_extra
    grad_step = sums_ref[8:16] + tail_rows * left + decay_rate * grad_log
    dt_out_ref[...] = (grad_step * gate)[0:H]
    copy.wait()


def end_kernel(end_ref, spilled_ref, places_ref, main_hbm, out_hbm, rows_ref, sem):
    end = end_ref[...]
    last = places_ref[places_ref.shape[0] - 8 :][:1, :1]
    fixed = end[END_ROWS - 8 :] + jnp.where(last > 0.5, 0.0, spilled_ref[...])
    rows_ref[...] = jnp.concatenate([end[: END_ROWS - 8], fixed], 0).astype(bf16)
    tok = out_hbm.shape[0]
    copy = pltpu.make_async_copy(rows_ref, out_hbm.at[pl.ds(tok - END_ROWS, END_ROWS)], sem)
    copy.start()
    copy.wait()


def summed(parts):
    large = jnp.sum(parts * jnp.exp(parts[:, SMALL_ROW + 1 : SMALL_ROW + 2]), axis=0)
    small = parts[:, SMALL_ROW : SMALL_ROW + 1] + parts[:, SMALL_ROW + 3 : SMALL_ROW + 4] * (1 / 256.0)
    small = small * jnp.exp(parts[:, SMALL_ROW + 2 : SMALL_ROW + 3])
    return large, jnp.sum(small, axis=0)


def repack_kernel(parts_ref, out_ref):
    large, small = summed(parts_ref[...])
    out_ref[...] = pack_totals(jnp.where(iota(large.shape, 0) == SMALL_ROW, small, large))


def finish_kernel(parts_ref, weight_ref, bias_ref, dt_bias_ref, alog_ref, skip_ref):
    large, small = summed(parts_ref[...])
    for k in range(K + 1):
        for j in range(LANE_BLOCKS):
            at = k * LANE_BLOCKS + j
            if k < K:
                weight_ref[k : k + 1, j * 128 : (j + 1) * 128] = large[at : at + 1]
            else:
                bias_ref[:, j * 128 : (j + 1) * 128] = large[at : at + 1]
    for i, ref in enumerate((dt_bias_ref, alog_ref, skip_ref)):
        ref[...] = small[:, i * H : (i + 1) * H]


def call(kernel, outs, in_specs, out_specs=None, scratch=(), flops=0, limit=16 << 20, aliases=None):
    return pl.pallas_call(
        kernel,
        out_shape=outs,
        in_specs=in_specs,
        out_specs=out_specs or jax.tree.map(lambda _: VMEM, outs),
        scratch_shapes=list(scratch),
        input_output_aliases=aliases or {},
        compiler_params=pltpu.CompilerParams(vmem_limit_bytes=limit),
        cost_estimate=pl.CostEstimate(flops=flops, bytes_accessed=1 << 20, transcendentals=0),
    )


def struct(shape, dtype=f32):
    return jax.ShapeDtypeStruct(shape, dtype)


def from_groups(messages, slabs, size, radix):
    got = []
    for s in range(1, radix):
        message = messages[s - 1 if len(messages) > 1 else 0]
        route = [(p, p - p % (size * radix) + (p + s * size) % (size * radix)) for p in range(slabs)]
        got.append(lax.ppermute(message, "ctx", route))
    return got


def states_from_groups(messages, slabs, size, radix):
    got = from_groups([message.astype(jnp.float16) for message in messages], slabs, size, radix)
    return [each.astype(f32) for each in got]


def stages_of(slabs):
    stages, size = [], 1
    while size < slabs:
        radix = 2 if (slabs // size).bit_length() % 2 == 0 else 4
        stages.append((size, radix))
        size *= radix
    assert size == slabs and len(stages) > 1
    return stages


def everyones(packed, axes, count):
    packed = jnp.broadcast_to(packed.astype(jnp.float16)[None], (count, *packed.shape))
    return lax.all_to_all(packed, axes, 0, 0).astype(f32)


def on_device(xbc_raw, conv_weight, conv_bias, dt_raw, dt_bias, a_log, d_skip, grad_out):
    tok, channels = xbc_raw.shape[1:]
    slabs = lax.axis_size("ctx")
    contexts = lax.axis_size("dp")
    stages = stages_of(slabs)

    raw, cot, dt_rows = xbc_raw[0], grad_out[0], dt_raw[0].T
    until = call(triangle_kernel, struct((tok, tok), bf16), [], flops=10**11)()
    until, bias, heads = call(
        heads_kernel,
        (struct((tok, tok), bf16), struct((1, channels)), struct((3 * HEAD_ROWS, tok))),
        [VMEM] * 5,
        aliases={4: 0},
    )(conv_bias[None], dt_bias[None], a_log[None], d_skip[None], until)
    early_raw, until = lax.optimization_barrier((raw, until))
    halo = lax.ppermute(early_raw[tok - HALO_ROWS :], "ctx", [(i, (i + 1) % slabs) for i in range(slabs)])

    def last_radix(t):
        return stages[t][1] if t == len(stages) - 1 else 0

    def messages(t):
        if last_radix(t):
            return (struct((N + TAIL_ROWS, INNER)),) * (last_radix(t) - 1)
        return (struct((2 * N + TAIL_ROWS, INNER)),)

    state_like = struct((N, INNER))
    logs_like = struct((8, INNER))
    pre, xbc, weighted, scaled, tail, rows, logs, places, state, grad, *outgoing = call(
        functools.partial(start_kernel, stages),
        (
            struct((tok, channels)), struct((tok, channels), bf16), struct((tok, 2 * INNER), bf16),
            struct((tok, 2 * INNER), bf16), struct((tok, INNER)), struct((6 * HEAD_ROWS, tok)),
            logs_like, struct((8 * len(stages) + 16, INNER)), state_like, state_like, *messages(0),
        ),
        [VMEM] * 7,
        scratch=[pltpu.VMEM((HEAD_ROWS, tok), f32)],
        flops=10**11,
    )(raw, cot, conv_weight, bias, dt_rows, heads, until)
    pre, xbc, weighted, factors = call(
        fix_kernel,
        (
            struct((tok, channels)), struct((tok, channels), bf16), struct((tok, 2 * INNER), bf16),
            struct((FIX_ROWS, INNER + N), bf16),
        ),
        [VMEM] * 8,
        flops=1_000_000,
        aliases={5: 0, 6: 1, 7: 2},
    )(halo, conv_weight, scaled, tail, places, pre, xbc, weighted)

    local, sums, state, grad = call(
        local_kernel,
        (struct((tok, channels)), struct((2 * HEAD_ROWS, tok)), state_like, state_like),
        [VMEM] * 7,
        flops=10**11,
        aliases={5: 2, 6: 3},
    )(xbc, cot, rows, logs, factors, state, grad)

    carried = ()
    for t, (size, radix) in enumerate(stages):
        got = states_from_groups(outgoing, slabs, size, radix)
        if t == 0:
            got, local, sums = lax.optimization_barrier((got, local, sums))
            carried = from_groups([factors], slabs, size, radix)
        if t == len(stages) - 1:
            got, weights, fixed, moved, slope = lax.optimization_barrier((got, weights, fixed, moved, slope))
            break
        last = last_radix(t + 1)
        outs = (logs_like, state_like, state_like) + (() if last else (state_like, state_like))
        logs, *outgoing = call(
            functools.partial(merge_kernel, t, radix, last),
            outs + messages(t + 1),
            [VMEM] * (4 + len(got) + len(carried)),
            flops=1_000_000,
        )(state, grad, logs, places, *got, *carried)
        carried, outgoing = outgoing[:2], outgoing[2:]
        if not last:
            (state, grad), outgoing = outgoing[:2], outgoing[2:]
        if t == 0:
            weights, fixed, moved, slope = call(
                weights_kernel,
                (
                    struct((tok, 4 * INNER)), struct((HEAD_ROWS, tok)), struct(((K - 1) * tok, channels)), struct((tok, channels)),
                ),
                [VMEM] * 11,
                flops=10**11,
            )(xbc, cot, rows, raw, halo, places, scaled, until, pre, sums, logs)

    grad_conv, states, packed, spill = call(
        functools.partial(totals_kernel, len(stages) - 1, radix),
        (struct((tok, channels)), struct((tok + HEAD_ROWS, 2 * INNER)), struct((TOTAL_ROWS, 128)), struct((8, channels))),
        [VMEM] * (14 + len(got) + len(carried)),
        scratch=[pltpu.VMEM((TOTAL_ROWS, 128), f32)],
        flops=200_000_000,
    )(raw, moved, xbc, slope, scaled, weighted, tail, rows, local, fixed, weights, logs, places, conv_weight, *got, *carried)

    spilled = lax.ppermute(spill, "ctx", [((i + 1) % slabs, i) for i in range(slabs)])
    if slabs * contexts <= 64:
        parts = everyones(packed, ("dp", "ctx"), slabs * contexts)
    else:
        packed = call(repack_kernel, struct((TOTAL_ROWS, 128)), [VMEM])(everyones(packed, "ctx", slabs))
        parts = everyones(packed, "dp", contexts)

    grad_main, grad_dt, end = call(
        input_kernel,
        (struct((tok, channels), bf16), struct((H, tok)), struct((END_ROWS, channels))),
        [VMEM] * 8,
        (HBM, VMEM, VMEM),
        [pltpu.VMEM((tok, channels), bf16), pltpu.SemaphoreType.DMA],
        flops=1_000_000,
    )(grad_conv, conv_weight, states, xbc, scaled, rows, sums, until)
    grad_input = call(
        end_kernel,
        struct((tok, channels), bf16),
        [VMEM] * 3 + [HBM],
        HBM,
        [pltpu.VMEM((END_ROWS, channels), bf16), pltpu.SemaphoreType.DMA],
        aliases={3: 0},
    )(end, spilled, places, grad_main)

    grad_weight, grad_bias, *small = call(
        finish_kernel,
        (struct((K, channels)), struct((1, channels)), struct((1, H)), struct((1, H)), struct((1, H))),
        [VMEM],
    )(parts)
    return (grad_input[None], grad_dt.T[None], grad_weight, grad_bias[0], *(each[0] for each in small))


def solution(mesh):
    in_specs = (
        P("dp", "ctx", None),
        P(),
        P(),
        P("dp", "ctx", None),
        P(),
        P(),
        P(),
        P("dp", "ctx", None),
    )
    out_specs = (P("dp", "ctx", None), P("dp", "ctx", None), P(), P(), P(), P(), P())
    return jax.shard_map(
        on_device, mesh=mesh, in_specs=in_specs, out_specs=out_specs, check_vma=False
    )
```
